128 devices in a mesh: section: 2 (over y_lo), dp: 64 (over z, y_hi, x, core).
Axes of the slice: x: 4, y: 4 (y_hi: 2, y_lo: 2; y = y_hi * 2 + y_lo), z: 4, core: 2. Of those that a mesh axis runs over, the one named last changes fastest.
Arguments:
- hidden_in: bfloat16 [128, 128, 768], P('dp'), may hold values from -6 to 6
- cotangent: bfloat16 [128, 128, 768], P('dp'), may hold values from -6 to 6
- segment_ids: int32 [128, 128], P('dp'), may hold values from 0 to 3, never falling along the last dimension, each value on 1 to 64 neighbouring positions
- positions: int32 [128, 128], P('dp'), may hold values from 0 to 511, as said below
- w_in: bfloat16 [2, 768, 2304], P('section'), may hold values from -0.3125 to 0.3125
- b_in: bfloat16 [2, 2304], P('section'), may hold values from -1.1953125 to 1.1953125
- w_out: bfloat16 [2, 768, 768], P('section'), may hold values from -0.625 to 0.625
- w_up: bfloat16 [2, 768, 3072], P('section'), may hold values from -0.21875 to 0.21875
- b_up: bfloat16 [2, 3072], P('section'), may hold values from -1.1953125 to 1.1953125
- w_down: bfloat16 [2, 3072, 768], P('section'), may hold values from -0.15625 to 0.15625
- gains: bfloat16 [2, 2, 768], P('section'), may hold values from 0.5 to 1.5
- biases: bfloat16 [2, 4, 768], P('section'), may hold values from -1.1953125 to 1.1953125
- rel_table: bfloat16 [512, 768], replicated, may hold values from -6 to 6
- abs_table: bfloat16 [512, 768], replicated, may hold values from -3 to 3
Outputs:
- section_out: bfloat16 [2, 128, 128, 768], P('section', 'dp')
- input_grad: bfloat16 [2, 128, 128, 768], P('section', 'dp')
- g_w_in: float32 [2, 768, 2304], P('section')
- g_b_in: float32 [2, 2304], P('section')
- g_w_out: float32 [2, 768, 768], P('section')
- g_w_up: float32 [2, 768, 3072], P('section')
- g_b_up: float32 [2, 3072], P('section')
- g_w_down: float32 [2, 3072, 768], P('section')
- g_gains: float32 [2, 2, 768], P('section')
- g_biases: float32 [2, 4, 768], P('section')
- g_rel_table: float32 [512, 768], replicated
- g_abs_table: float32 [512, 768], replicated
The draws below stay inside these ranges and needn't reach their ends.
Inputs may be any that keep to these rules, and one draw needn't show every extreme that they name: Each row holds 128 consecutive positions from a start of its own; one row ends at 511. `segment_ids`: ids never fall along a row; a document holds at most 64 tokens.
All inputs are finite; a program needn't handle non-finite values.
Results may differ from the reference program's by a relative error of at most 0.035.
The reference program's roundings to bfloat16 on the way count: a program that leaves them out, or rounds other values in their place, can miss the bound.
Values may be sent and summed in bfloat16 or wider, within the bound.
No kernel may reach another device: no remote copies, remote signals or barrier semaphores. Data moves between devices by JAX's collectives and lax.ppermute only.
A program may use at most 256 MiB of HBM per device.

```python
import math
import jax
import jax.numpy as jnp
import numpy as np
from jax import lax

D = 768
HEADS = 12
HEAD_DIM = 64
FF = 3072
SPAN = 256
ABS_POS = 512
SEQ_LEN = 128
ROWS = 128


def draw_positions(key, part):
    key = jax.random.fold_in(key, 7)
    starts = jax.random.randint(key, (ROWS, 1), 0, ABS_POS - SEQ_LEN + 1)
    row_index = lax.broadcasted_iota(jnp.int32, (ROWS, 1), 0)
    starts = jnp.where(row_index == 0, ABS_POS - SEQ_LEN, starts)
    return (starts + lax.broadcasted_iota(jnp.int32, (ROWS, SEQ_LEN), 1)).astype(jnp.int32)


def level_of(own_key, dims, split, low, high):
    def one(position, blocks):
        heights = jax.random.uniform(jax.random.fold_in(jax.random.fold_in(own_key, 6), position), (blocks,), jnp.float32, low / len(split), high / len(split))
        return jnp.repeat(jnp.exp(heights), dims[position] // blocks).reshape((-1,) + (1,) * (len(dims) - position - 1))

    level = one(*split[0])
    for cut in split[1:]:
        level = level * one(*cut)
    return level


def profile(count, total, limit, lean):
    portions = [(1 << 20) // math.isqrt(grade ** lean) + 1 for grade in range(2, count + 1)]
    surplus, holding = total - limit - (count - 1), [1] * (count - 1)
    while surplus > 0:
        free = [i for i in range(count - 1) if holding[i] < limit]
        whole, left = sum([portions[i] for i in free]), surplus
        for i in free:
            addition = min(limit - holding[i], max(1, left * portions[i] // whole), surplus)
            holding[i] = holding[i] + addition
            surplus = surplus - addition
    return np.array([limit] + holding)


def ragged_sizes(stream_key, amount, total, reach, slope):
    if amount == 2:
        one = jax.random.randint(stream_key, (), max(1, total - reach), min(reach, total - 1) + 1)
        return jnp.stack([one, total - one])
    sizes = jnp.asarray(profile(amount, total, reach, slope), jnp.int32)
    pairs = (amount - 1) // 2
    source_of, sink = sizes[1:1 + 2 * pairs:2], sizes[2:2 + 2 * pairs:2]
    slack = jnp.minimum(source_of - 1, reach - sink)
    moved = jax.random.randint(jax.random.fold_in(stream_key, 1), (pairs,), 0, 1 << 20) % (slack + 1)
    sizes = sizes.at[1:1 + 2 * pairs:2].set(source_of - moved).at[2:2 + 2 * pairs:2].set(sink + moved)
    return sizes[jax.random.permutation(jax.random.fold_in(stream_key, 2), amount)]


def bell_draw(stream_key, shape, scale, limit, shards=(), dtype=jnp.bfloat16):
    values = jax.random.normal(stream_key, shape, jnp.float32) * scale
    if len(shards) > 0:
        values = level_of(stream_key, shape, shards, -0.22, 0.18) * values
    return jnp.clip(values, min=-limit, max=limit).astype(dtype)


def setup_inputs(seed: int = 0) -> dict:
    seeds = jax.random.split(jax.random.key(seed), 15)
    return {
        "hidden_in": bell_draw(seeds[0], (ROWS, SEQ_LEN, D), 1.0, 6.0, ((0, 64),)),
        "cotangent": bell_draw(seeds[1], (ROWS, SEQ_LEN, D), 1.0, 6.0, ((0, 64),)),
        "segment_ids": jax.vmap(lambda own: jnp.searchsorted(jnp.cumsum(ragged_sizes(own, 4, SEQ_LEN, SEQ_LEN // 2, 1)), jnp.arange(SEQ_LEN), side="right"))(jax.random.split(seeds[2], ROWS)).reshape((ROWS, SEQ_LEN)).astype(jnp.int32),
        "positions": draw_positions(jax.random.fold_in(seeds[14], 71), 0),
        "w_in": bell_draw(seeds[4], (2, D, 3 * D), (D // 2) ** -0.5, 0.3125, ((0, 2),)),
        "b_in": bell_draw(seeds[5], (2, 3 * D), 0.2, 1.1953125, ((0, 2),)),
        "w_out": bell_draw(seeds[6], (2, D, D), (D // 8) ** -0.5, 0.625, ((0, 2),)),
        "w_up": bell_draw(seeds[7], (2, D, FF), D ** -0.5, 0.21875, ((0, 2),)),
        "b_up": bell_draw(seeds[8], (2, FF), 0.2, 1.1953125, ((0, 2),)),
        "w_down": bell_draw(seeds[9], (2, FF, D), (FF // 2) ** -0.5, 0.15625, ((0, 2),)),
        "gains": jnp.clip(1.0 + 0.1 * jax.random.normal(seeds[10], (2, 2, D), jnp.float32), 0.5, 1.5).astype(jnp.bfloat16),
        "biases": bell_draw(seeds[11], (2, 4, D), 0.2, 1.1953125, ((0, 2),)),
        "rel_table": bell_draw(seeds[12], (2 * SPAN, D), 1.0, 6.0),
        "abs_table": bell_draw(seeds[13], (ABS_POS, D), 0.5, 3.0),
    }


@jax.custom_vjp
def low(v):
    return lax.optimization_barrier(v.astype(jnp.bfloat16)).astype(jnp.float32)

@jax.custom_vjp
def lower_backward(v):
    return v

def low_keep(v):
    return (low(v), None)

def low_pass(kept, grad):
    return (grad,)

def back_keep(v):
    return (v, None)

def back_low(kept, grad):
    return (low(grad),)
low.defvjp(low_keep, low_pass)
lower_backward.defvjp(back_keep, back_low)
highest_precision = lax.Precision.HIGHEST
norm_eps = 1e-06
negative = -1e+30

def matmul(left, right):
    return jnp.dot(left, right, precision=highest_precision)

def layer_norm(value, gain, shift):
    centered = value - lax.optimization_barrier(jnp.mean(value, axis=-1, keepdims=True))
    spread = lax.optimization_barrier(jnp.mean(centered * centered, axis=-1, keepdims=True))
    return centered * lax.rsqrt(spread + norm_eps) * gain + shift

def split_heads(value):
    return value.reshape(value.shape[0], HEADS, HEAD_DIM)

def offset_table(length):
    rows_at = lax.broadcasted_iota(jnp.int32, (length, length), 0)
    cols_at = lax.broadcasted_iota(jnp.int32, (length, length), 1)
    return cols_at + length - rows_at

def select_index(length):
    return jnp.clip(length - lax.iota(jnp.int32, 2 * length), -SPAN, SPAN - 1) + SPAN

def take_rows(table, offsets):
    return jnp.take_along_axis(table, jnp.broadcast_to(offsets, (table.shape[0],) + offsets.shape), axis=2)

def layer(inputs, extra_rows, segment, params, rel_float):
    w_in, b_in, w_out, w_up, b_up, w_down, gains, biases = params
    length = inputs.shape[0]
    start_rows = inputs + extra_rows
    queries = low(lower_backward(matmul(low(start_rows), w_in[:, :D]) + b_in[:D]))
    key_value = low(lower_backward(matmul(low(inputs), w_in[:, D:]) + b_in[D:]))
    rel_proj = low(matmul(rel_float[select_index(length)], w_in[:, :2 * D]) + b_in[:2 * D])
    query_head_split = split_heads(queries)
    key_head_split = split_heads(key_value[:, :D])
    v_heads = split_heads(key_value[:, D:])
    relative_query = split_heads(rel_proj[:, :D])
    relative_key = split_heads(rel_proj[:, D:])
    content = jnp.einsum('ihd,jhd->hij', query_head_split, key_head_split, precision=highest_precision)
    distant_content_position = lower_backward(jnp.einsum('ywt,nwt->wyn', query_head_split, relative_key, precision=highest_precision))
    distant_position_content = lower_backward(jnp.einsum('ntr,ctr->tnc', key_head_split, relative_query, precision=highest_precision))
    offsets = offset_table(length)
    summed = content + take_rows(distant_content_position, offsets) + jnp.swapaxes(take_rows(distant_position_content, offsets), 1, 2)
    scores = lower_backward(summed * (1.0 / math.sqrt(3 * HEAD_DIM)))
    same_doc = (segment[:, None] == segment[None, :])[None]
    scores = jnp.where(same_doc, scores, negative)
    row_max = lax.optimization_barrier(jnp.max(scores, axis=2, keepdims=True))
    exponent = jnp.exp(scores - row_max)
    attn_probs = exponent / lax.optimization_barrier(jnp.sum(exponent, axis=2, keepdims=True))
    context = jnp.einsum('hij,jhd->ihd', low(attn_probs), v_heads, precision=highest_precision).reshape(length, D)
    context = low(lower_backward(context))
    attended = lower_backward(matmul(context, w_out) + biases[0])
    hidden = layer_norm(start_rows + attended, gains[0], biases[1])
    gate_pre = lower_backward(matmul(low(hidden), w_up) + b_up)
    active = low(jax.nn.gelu(gate_pre, approximate=False))
    down_rows = lower_backward(matmul(active, w_down) + biases[2])
    return layer_norm(hidden + down_rows, gains[1], biases[3])

def reference(hidden_in, cotangent, segment_ids, positions, w_in, b_in, w_out, w_up, b_up, w_down, gains, biases, rel_table, abs_table):
    stacked = tuple((weight_array.astype(jnp.float32) for weight_array in (w_in, b_in, w_out, w_up, b_up, w_down, gains, biases)))
    params_one = tuple((weight_array[0] for weight_array in stacked))
    params_two = tuple((weight_array[1] for weight_array in stacked))
    rel_float = rel_table.astype(jnp.float32)
    abs_float = abs_table.astype(jnp.float32)
    group_size = math.gcd(ROWS, 32)
    group_count = ROWS // group_size

    def regroup(array):
        return array.reshape((group_count, group_size) + array.shape[1:])
    batches = (regroup(hidden_in), regroup(cotangent), regroup(segment_ids), regroup(positions))
    run_layer = jax.vmap(layer, in_axes=(0, 0, 0, None, None))

    def one_group(totals, group_batch):
        inputs, cot_rows, segment, place_ids = group_batch

        def first_section(values, params, rel_values):
            return run_layer(values, jnp.zeros_like(values), segment, params, rel_values)

        def second_section(values, params, rel_values, absolute):
            return run_layer(values, absolute[place_ids], segment, params, rel_values)
        middle, first_back = jax.vjp(first_section, inputs.astype(jnp.float32), params_one, rel_float)
        sent_rows = low(middle)
        final, second_back = jax.vjp(second_section, sent_rows, params_two, rel_float, abs_float)
        d_sent, grads_two, rel_two, abs_grad = second_back(cot_rows.astype(jnp.float32))
        sent_grad = d_sent.astype(jnp.bfloat16)
        d_inputs, grads_one, rel_one = first_back(sent_grad.astype(jnp.float32))
        layer_sums = tuple((total_item + jnp.stack([first_item, second_item]) for total_item, first_item, second_item in zip(totals[0], grads_one, grads_two)))
        new_totals = (layer_sums, totals[1] + rel_one + rel_two, totals[2] + abs_grad)
        return (new_totals, (middle.astype(jnp.bfloat16), final.astype(jnp.bfloat16), d_inputs.astype(jnp.bfloat16), sent_grad))
    init = (tuple((jnp.zeros_like(weight_array) for weight_array in stacked)), jnp.zeros_like(rel_float), jnp.zeros_like(abs_float))
    totals, results = lax.scan(one_group, init, batches)

    def ungroup(array):
        return array.reshape((ROWS,) + array.shape[2:])
    middle_all, final_all, d_in_all, sent_all = (ungroup(item_array) for item_array in results)
    section_out = jnp.stack([middle_all, final_all])
    input_grad = jnp.stack([d_in_all, sent_all])
    g_w_in, g_b_in, g_w_out, g_w_up, g_b_up, g_w_down, g_gains, g_biases = totals[0]
    return (section_out, input_grad, g_w_in, g_b_in, g_w_out, g_w_up, g_b_up, g_w_down, g_gains, g_biases, totals[1], totals[2])
```

```python
from functools import partial
import math

import jax
import jax.numpy as jnp
from jax import lax
from jax.sharding import PartitionSpec as P

HEADS = 12


norm_eps = 1e-06
negative = -1e30
highest_precision = lax.Precision.HIGHEST


def from_behind(value, axis, by):
    peers = lax.axis_size(axis)
    pairs = [(i, i + by) for i in range(peers) if 0 <= i + by < peers]
    return lax.ppermute(value, axis, pairs)


SQUARE = ((0, 0), (1, 0), (1, 1), (0, 1))
ROTATION = ("x0", "z0", "x1", "z1", "y")
COLUMN_BLOCK = 768
PIECES = 5


def dp_place(index):
    return {"core": index % 2, "x": index // 2 % 4, "y": index // 8 % 2, "z": index // 16}


def dp_index(place):
    return ((place["z"] * 2 + place["y"]) * 4 + place["x"]) * 2 + place["core"]


def partner(index, dim):
    place = dp_place(index)
    if len(dim) == 2:
        bits = list(SQUARE[place[dim[0]]])
        bits[int(dim[1])] ^= 1
        place[dim[0]] = SQUARE.index(tuple(bits))
    else:
        place[dim] ^= 1
    return dp_index(place)


def swap(value, dim):
    peers = lax.axis_size("dp")
    return lax.ppermute(value, "dp", [(i, partner(i, dim)) for i in range(peers)])


def side(dim):
    place = dp_place(lax.axis_index("dp"))
    if len(dim) == 1 or dim == "core":
        return place[dim].astype(jnp.int32)
    at = place[dim[0]]
    if dim[1] == "0":
        return ((at == 1) | (at == 2)).astype(jnp.int32)
    return (at >= 2).astype(jnp.int32)


def order_of(piece):
    return [ROTATION[(piece + step) % len(ROTATION)] for step in range(len(ROTATION))]


def scatter_sums(pieces, orders):
    for step in range(len(ROTATION)):
        summed = []
        for piece, order in zip(pieces, orders):
            at, half = side(order[step]), piece.shape[0] // 2
            sent = lax.dynamic_slice_in_dim(piece, (1 - at) * half, half, 0)
            summed.append((piece, at, half, swap(sent, order[step])))
        pieces = [
            lax.dynamic_slice_in_dim(piece, at * half, half, 0) + received
            for piece, at, half, received in summed
        ]
    return pieces


def in_order(at, own, other, axis):
    return jnp.where(
        at == 0,
        jnp.concatenate([own, other], axis=axis),
        jnp.concatenate([other, own], axis=axis),
    )


def gather_pieces(pieces, orders):
    for step in reversed(range(len(ROTATION))):
        received = [swap(piece, order[step]) for piece, order in zip(pieces, orders)]
        pieces = [
            in_order(side(order[step]), piece, other, 0)
            for piece, other, order in zip(pieces, received, orders)
        ]
    return pieces


def cut_columns(value):
    rows, width = value.shape
    return [value[:, at : at + COLUMN_BLOCK] for at in range(0, width, COLUMN_BLOCK)]


def cut_rows(value):
    return [value[at : at + COLUMN_BLOCK] for at in range(0, value.shape[0], COLUMN_BLOCK)]


def core_sum(blocks):
    core = side("core")
    half = COLUMN_BLOCK // 2
    low = jnp.concatenate([block.astype(jnp.bfloat16) for block in blocks], axis=0)
    own = lax.dynamic_slice_in_dim(low, core * half, half, 1)
    other = lax.dynamic_slice_in_dim(low, (1 - core) * half, half, 1)
    return own + swap(other, "core")


def sum_over_rows(ffn_blocks, attn_blocks, tables, vectors):
    table_rows = tables.shape[0]
    rest = 1024 - table_rows - vectors.shape[0]
    tail = jnp.pad(jnp.concatenate([tables, vectors], axis=0), ((0, rest), (0, 0)))
    held = core_sum(ffn_blocks + attn_blocks + [tail])
    size = held.shape[0] // PIECES
    pieces = [held[at * size : (at + 1) * size] for at in range(PIECES)]
    orders = [order_of(piece) for piece in range(PIECES)]
    pieces = scatter_sums(pieces, orders)
    first_row, span = 0, size
    for dim in orders[-1]:
        span //= 2
        first_row = first_row + side(dim) * span
    row_at = first_row + lax.broadcasted_iota(jnp.int32, pieces[-1].shape, 0) - (size - 1024)
    is_table = (row_at >= 0) & (row_at < table_rows)
    elsewhere = lax.ppermute(pieces[-1], "section", [(0, 1), (1, 0)])
    pieces[-1] = jnp.where(is_table, pieces[-1] + elsewhere, pieces[-1])
    pieces = gather_pieces(pieces, orders)
    held = jnp.concatenate(pieces, axis=0)
    return in_order(side("core"), held, swap(held, "core"), 1)


def matmul(left, right):
    return jnp.dot(left, right, preferred_element_type=jnp.float32)


def exact_dot(left, right):
    return jnp.dot(left, right, precision=highest_precision, preferred_element_type=jnp.float32)


def layer_norm(value, gain, shift):
    centered = value - jnp.mean(value, axis=-1, keepdims=True)
    spread = jnp.mean(centered * centered, axis=-1, keepdims=True)
    return centered * lax.rsqrt(spread + norm_eps) * gain + shift


def split_heads(value):
    return value.reshape(value.shape[0], HEADS, value.shape[1] // HEADS)


def skew_rows(table):
    head_count, length, width = table.shape
    flat = table.reshape(head_count, length * width)[:, length:]
    return flat.reshape(head_count, length, width - 1)[:, :, :length]


def unskew_rows(grid):
    head_count = grid.shape[0]
    length = grid.shape[1]
    padded = jnp.pad(grid, ((0, 0), (0, 0), (0, length - 1)))
    flat = jnp.pad(padded.reshape(head_count, length * (2 * length - 1)), ((0, 0), (length, 0)))
    return flat.reshape(head_count, length, 2 * length)


def masked_scores(
    query_head_split, key_head_split, relative_query, relative_key, same_doc, score_scale
):
    content = jnp.einsum(
        "ihd,jhd->hij", query_head_split, key_head_split, preferred_element_type=jnp.float32
    )
    distant_content_position = jnp.einsum(
        "ywt,nwt->wyn", query_head_split, relative_key, preferred_element_type=jnp.float32
    )
    distant_position_content = jnp.einsum(
        "ntr,ctr->tnc", key_head_split, relative_query, preferred_element_type=jnp.float32
    )
    summed = (
        content
        + skew_rows(distant_content_position)
        + jnp.swapaxes(skew_rows(distant_position_content), 1, 2)
    )
    return jnp.where(same_doc, summed * score_scale, negative)


def forward(inputs, extra_rows, segment, weights, relative_query, relative_key, score_scale):
    w_in, b_in, w_out, w_up, b_up, w_down, gains, biases = weights
    model_width = inputs.shape[1]
    gains_float = gains.astype(jnp.float32)
    biases_float = biases.astype(jnp.float32)
    start_rows = inputs.astype(jnp.float32) + extra_rows
    query_in = start_rows.astype(jnp.bfloat16)
    queries = (
        matmul(query_in, w_in[:, :model_width]) + b_in[:model_width].astype(jnp.float32)
    ).astype(jnp.bfloat16)
    key_value = (
        matmul(inputs, w_in[:, model_width:]) + b_in[model_width:].astype(jnp.float32)
    ).astype(jnp.bfloat16)
    same_doc = (segment[:, None] == segment[None, :])[None]
    scores = masked_scores(
        split_heads(queries),
        split_heads(key_value[:, :model_width]),
        relative_query,
        relative_key,
        same_doc,
        score_scale,
    )
    row_max = jnp.max(scores, axis=2, keepdims=True)
    exponent = jnp.exp(scores - row_max)
    row_total = jnp.sum(exponent, axis=2, keepdims=True)
    attn_probs = (exponent / row_total).astype(jnp.bfloat16)
    log_total = row_max + jnp.log(row_total)
    context = jnp.einsum(
        "hij,jhd->ihd",
        attn_probs,
        split_heads(key_value[:, model_width:]),
        preferred_element_type=jnp.float32,
    )
    context = context.reshape(inputs.shape[0], model_width).astype(jnp.bfloat16)
    resid_one = start_rows + matmul(context, w_out) + biases_float[0]
    hidden = layer_norm(resid_one, gains_float[0], biases_float[1])
    hidden_low = hidden.astype(jnp.bfloat16)
    gate_pre = matmul(hidden_low, w_up) + b_up.astype(jnp.float32)
    active = jax.nn.gelu(gate_pre, approximate=False).astype(jnp.bfloat16)
    resid_two = hidden + matmul(active, w_down) + biases_float[2]
    output = layer_norm(resid_two, gains_float[1], biases_float[3])
    return (
        output,
        (
            query_in,
            queries,
            key_value,
            same_doc,
            log_total,
            context,
            resid_one,
            hidden_low,
            gate_pre,
            active,
            resid_two,
        ),
    )


def backward_ffn(grad_out, saved_state, weights):
    w_in, b_in, w_out, w_up, b_up, w_down, gains, biases = weights
    resid_one, hidden_low, gate_pre, active, resid_two = saved_state[6:]
    gains_float = gains.astype(jnp.float32)
    biases_float = biases.astype(jnp.float32)
    unused_two, norm_two_back = jax.vjp(layer_norm, resid_two, gains_float[1], biases_float[3])
    d_resid_two, d_gain_two, d_shift_two = norm_two_back(grad_out)
    d_down = d_resid_two.astype(jnp.bfloat16)
    d_w_down = matmul(active.T, d_down)
    d_active = matmul(d_down, w_down.T)
    unused_gate, gelu_back = jax.vjp(partial(jax.nn.gelu, approximate=False), gate_pre)
    d_gate = gelu_back(d_active)[0].astype(jnp.bfloat16)
    d_w_up = matmul(hidden_low.T, d_gate)
    d_hidden = d_resid_two + matmul(d_gate, w_up.T)
    unused_one, norm_one_back = jax.vjp(layer_norm, resid_one, gains_float[0], biases_float[1])
    d_resid_one, d_gain_one, d_shift_one = norm_one_back(d_hidden)
    ffn_grads = (d_w_up, jnp.sum(d_gate.astype(jnp.float32), axis=0), d_w_down)
    d_gains = jnp.stack([d_gain_one, d_gain_two])
    norm_rows = (d_shift_one, jnp.sum(d_down.astype(jnp.float32), axis=0), d_shift_two)
    return (d_resid_one, ffn_grads, d_gains, norm_rows)


def backward_attention(
    d_resid_one, inputs, saved_state, weights, relative_query, relative_key, score_scale
):
    w_in, b_in, w_out = weights[:3]
    query_in, queries, key_value, same_doc, log_total, context = saved_state[:6]
    length, model_width = inputs.shape
    d_attended = d_resid_one.astype(jnp.bfloat16)
    d_w_out = matmul(context.T, d_attended)
    d_context = split_heads(matmul(d_attended, w_out.T).astype(jnp.bfloat16))
    query_head_split = split_heads(queries)
    key_head_split = split_heads(key_value[:, :model_width])
    v_heads = split_heads(key_value[:, model_width:])
    scores = masked_scores(
        query_head_split, key_head_split, relative_query, relative_key, same_doc, score_scale
    )
    attn_probs = jnp.exp(scores - log_total)
    d_probs = jnp.einsum("ihd,jhd->hij", d_context, v_heads, preferred_element_type=jnp.float32)
    d_value = jnp.einsum(
        "hij,ihd->jhd",
        attn_probs.astype(jnp.bfloat16),
        d_context,
        preferred_element_type=jnp.float32,
    )
    d_scores = (
        attn_probs * (d_probs - jnp.sum(d_probs * attn_probs, axis=2, keepdims=True))
    ).astype(jnp.bfloat16)
    distant_content_position_gradient = (
        score_scale * unskew_rows(d_scores).astype(jnp.float32)
    ).astype(jnp.bfloat16)
    distant_position_content_gradient = (
        score_scale * unskew_rows(jnp.swapaxes(d_scores, 1, 2)).astype(jnp.float32)
    ).astype(jnp.bfloat16)
    d_query = score_scale * jnp.einsum(
        "hij,jhd->ihd", d_scores, key_head_split, preferred_element_type=jnp.float32
    )
    d_query = d_query + jnp.einsum(
        "owg,goc->woc",
        distant_content_position_gradient,
        relative_key,
        preferred_element_type=jnp.float32,
    )
    key_gradient_rows = score_scale * jnp.einsum(
        "hij,ihd->jhd", d_scores, query_head_split, preferred_element_type=jnp.float32
    )
    key_gradient_rows = key_gradient_rows + jnp.einsum(
        "qol,lqc->oqc",
        distant_position_content_gradient,
        relative_query,
        preferred_element_type=jnp.float32,
    )
    table_rows = relative_key.shape[0]
    d_rel_k = jnp.einsum(
        "oba,bor->aor",
        distant_content_position_gradient,
        query_head_split,
        preferred_element_type=jnp.float32,
    ).reshape(table_rows, model_width)
    d_rel_q = jnp.einsum(
        "kay,ake->yke",
        distant_position_content_gradient,
        key_head_split,
        preferred_element_type=jnp.float32,
    ).reshape(table_rows, model_width)
    d_query = d_query.reshape(length, model_width).astype(jnp.bfloat16)
    d_key_value = jnp.concatenate(
        [key_gradient_rows.reshape(length, model_width), d_value.reshape(length, model_width)],
        axis=1,
    ).astype(jnp.bfloat16)
    d_start = d_resid_one + matmul(d_query, w_in[:, :model_width].T)
    d_inputs = d_start + matmul(d_key_value, w_in[:, model_width:].T)
    d_w_in = jnp.concatenate([matmul(query_in.T, d_query), matmul(inputs.T, d_key_value)], axis=1)
    d_b_in = jnp.concatenate(
        [
            jnp.sum(d_query.astype(jnp.float32), axis=0),
            jnp.sum(d_key_value.astype(jnp.float32), axis=0),
        ]
    )
    attended_sum = jnp.sum(d_attended.astype(jnp.float32), axis=0)
    return (d_inputs, (d_w_in, d_b_in, d_w_out), attended_sum, d_rel_q, d_rel_k, d_start)


def per_device(
    hidden_in,
    cotangent,
    segment_ids,
    positions,
    w_in,
    b_in,
    w_out,
    w_up,
    b_up,
    w_down,
    gains,
    biases,
    rel_table,
    abs_table,
):
    weights = (w_in[0], b_in[0], w_out[0], w_up[0], b_up[0], w_down[0], gains[0], biases[0])
    micro_count, length, model_width = hidden_in.shape
    half_table = rel_table.shape[0] // 2
    score_scale = 1.0 / math.sqrt(3 * (model_width // HEADS))
    section_index = lax.axis_index("section")
    is_last = section_index == 1
    last_flag = is_last.astype(jnp.float32)
    select_at = lax.broadcasted_iota(jnp.int32, (2 * length, 2 * half_table), 0)
    table_at = lax.broadcasted_iota(jnp.int32, (2 * length, 2 * half_table), 1)
    select_rows = (
        jnp.clip(length - select_at, -half_table, half_table - 1) + half_table == table_at
    ).astype(jnp.bfloat16)
    rel_rows = matmul(select_rows, rel_table).astype(jnp.bfloat16)
    rel_proj = (
        matmul(rel_rows, w_in[0][:, : 2 * model_width])
        + b_in[0][: 2 * model_width].astype(jnp.float32)
    ).astype(jnp.bfloat16)
    relative_query = split_heads(rel_proj[:, :model_width])
    relative_key = split_heads(rel_proj[:, model_width:])
    table_index = lax.broadcasted_iota(jnp.int32, (1, abs_table.shape[0]), 1)

    def choose(late_value, early_value):
        return jnp.where(is_last, late_value, early_value)

    received = jnp.zeros((length, model_width), jnp.bfloat16)
    stored = []
    outputs = []
    for tick_index in range(micro_count + 1):
        micro_slot = jnp.clip(tick_index - section_index, 0, micro_count - 1)
        inputs = choose(received, hidden_in[min(tick_index, micro_count - 1)])
        segment = lax.dynamic_index_in_dim(segment_ids, micro_slot, 0, keepdims=False)
        place_ids = lax.dynamic_index_in_dim(positions, micro_slot, 0, keepdims=False)
        onehot = (place_ids[:, None] == table_index).astype(jnp.bfloat16)
        extra_rows = last_flag * matmul(onehot, abs_table)
        output, saved_state = forward(
            inputs, extra_rows, segment, weights, relative_query, relative_key, score_scale
        )
        sent_rows = output.astype(jnp.bfloat16)
        outputs.append(sent_rows)
        stored.append((inputs, extra_rows, segment, onehot, saved_state))
        if tick_index < micro_count:
            received = from_behind(sent_rows, "section", 1)
    ffn_sums = (
        jnp.zeros(w_up[0].shape, jnp.float32),
        jnp.zeros(b_up[0].shape, jnp.float32),
        jnp.zeros(w_down[0].shape, jnp.float32),
    )
    attn_sums = (
        jnp.zeros(w_in[0].shape, jnp.float32),
        jnp.zeros(b_in[0].shape, jnp.float32),
        jnp.zeros(w_out[0].shape, jnp.float32),
    )
    gain_sum = jnp.zeros(gains[0].shape, jnp.float32)
    bias_sum = jnp.zeros(biases[0].shape, jnp.float32)
    rel_q_sum = jnp.zeros((2 * length, model_width), jnp.float32)
    rel_k_sum = jnp.zeros((2 * length, model_width), jnp.float32)
    abs_sum = jnp.zeros(abs_table.shape, jnp.float32)
    received = jnp.zeros((length, model_width), jnp.bfloat16)
    returned = []
    for tick_index in range(micro_count + 1):
        late_entry = stored[min(tick_index + 1, micro_count)]
        early_entry = stored[max(tick_index - 1, 0)]
        inputs, extra_rows, segment, onehot, saved_state = jax.tree.map(
            choose, late_entry, early_entry
        )
        if tick_index < micro_count:
            own_grad = cotangent[tick_index]
        else:
            own_grad = jnp.zeros((length, model_width), jnp.bfloat16)
        grad_out = choose(own_grad, received).astype(jnp.float32)
        d_resid_one, ffn_grads, d_gains, norm_rows = backward_ffn(grad_out, saved_state, weights)
        ffn_sums = jax.tree.map(jnp.add, ffn_sums, ffn_grads)
        if tick_index == micro_count:
            ffn_total = ffn_sums
        d_inputs, attn_grads, attended_sum, d_rel_q, d_rel_k, d_start = backward_attention(
            d_resid_one, inputs, saved_state, weights, relative_query, relative_key, score_scale
        )
        attn_sums = jax.tree.map(jnp.add, attn_sums, attn_grads)
        gain_sum = gain_sum + d_gains
        bias_sum = bias_sum + jnp.stack([attended_sum, norm_rows[0], norm_rows[1], norm_rows[2]])
        rel_q_sum = rel_q_sum + d_rel_q
        rel_k_sum = rel_k_sum + d_rel_k
        abs_sum = abs_sum + last_flag * exact_dot(onehot.astype(jnp.float32).T, d_start)
        sent_back = d_inputs.astype(jnp.bfloat16)
        returned.append(sent_back)
        if tick_index < micro_count:
            received = from_behind(sent_back, "section", -1)
    rel_pair = jnp.concatenate([rel_q_sum, rel_k_sum], axis=1)
    d_rel_rows = exact_dot(rel_pair, w_in[0][:, : 2 * model_width].astype(jnp.float32).T)
    d_rel_table = exact_dot(select_rows.astype(jnp.float32).T, d_rel_rows)
    d_w_in = (
        attn_sums[0]
        .at[:, : 2 * model_width]
        .add(exact_dot(rel_rows.astype(jnp.float32).T, rel_pair))
    )
    d_b_in = attn_sums[1].at[: 2 * model_width].add(jnp.sum(rel_pair, axis=0))
    d_w_out = attn_sums[2]
    vectors = jnp.concatenate(
        [d_b_in, ffn_total[1], gain_sum.reshape(-1), bias_sum.reshape(-1)]
    ).reshape(-1, model_width)
    rel_used = half_table - length
    total = sum_over_rows(
        cut_columns(ffn_total[0]) + cut_rows(ffn_total[2]),
        cut_columns(d_w_in) + [d_w_out],
        jnp.concatenate([d_rel_table[rel_used:], abs_sum], axis=0),
        vectors,
    ).astype(jnp.float32)
    blocks = cut_rows(total[: 12 * COLUMN_BLOCK])
    g_w_up = jnp.concatenate(blocks[:4], axis=1)
    g_w_down = jnp.concatenate(blocks[4:8], axis=0)
    g_w_in = jnp.concatenate(blocks[8:11], axis=1)
    g_w_out = blocks[11]
    tail = total[12 * COLUMN_BLOCK :]
    table_rows = rel_table.shape[0] - rel_used
    rel_total = jnp.pad(tail[:table_rows], ((rel_used, 0), (0, 0)))
    abs_total = tail[table_rows : table_rows + abs_table.shape[0]]
    flat = tail[table_rows + abs_table.shape[0] :][: vectors.shape[0]].reshape(-1)
    ends = (b_in.shape[1], b_up.shape[1], 2 * model_width, 4 * model_width)
    starts = [sum(ends[:at]) for at in range(4)]
    g_b_in, g_b_up, g_gains, g_biases = [flat[at : at + n] for at, n in zip(starts, ends)]
    g_gains = g_gains.reshape(2, model_width)
    g_biases = g_biases.reshape(4, model_width)
    section_out = jnp.stack(
        [choose(outputs[row_index + 1], outputs[row_index]) for row_index in range(micro_count)]
    )
    input_grad = jnp.stack(
        [choose(returned[row_index], returned[row_index + 1]) for row_index in range(micro_count)]
    )
    return (
        section_out[None],
        input_grad[None],
        g_w_in[None],
        g_b_in[None],
        g_w_out[None],
        g_w_up[None],
        g_b_up[None],
        g_w_down[None],
        g_gains[None],
        g_biases[None],
        rel_total,
        abs_total,
    )


def solution(mesh):
    in_specs = (
        P("dp", None, None),
        P("dp", None, None),
        P("dp", None),
        P("dp", None),
        P("section", None, None),
        P("section", None),
        P("section", None, None),
        P("section", None, None),
        P("section", None),
        P("section", None, None),
        P("section", None, None),
        P("section", None, None),
        P(),
        P(),
    )
    out_specs = (
        P("section", "dp", None, None),
        P("section", "dp", None, None),
        P("section", None, None),
        P("section", None),
        P("section", None, None),
        P("section", None, None),
        P("section", None),
        P("section", None, None),
        P("section", None, None),
        P("section", None, None),
        P(),
        P(),
    )
    return jax.shard_map(
        per_device, mesh=mesh, in_specs=in_specs, out_specs=out_specs, check_vma=False
    )
```

```python
from functools import partial
import math

import jax
import jax.numpy as jnp
from jax import lax
from jax.experimental import pallas as pl
from jax.experimental.pallas import tpu as pltpu
from jax.sharding import PartitionSpec as P

HEADS = 12
L = 128
D = 768
FF = 3072
PAIRS = HEADS // 2
ROWS = 2
EPS = 1e-06
SPAN = 256
PIECES = 5
NEG = -1e30
SCALE = 1.0 / math.sqrt(3 * 64)
VMEM_LIMIT = 56 * 1024 * 1024
f32, bf16 = jnp.float32, jnp.bfloat16


def nn(a, b):
    return lax.dot_general(a, b, (((1,), (0,)), ((), ())), preferred_element_type=f32)


def nt(a, b):
    return lax.dot_general(a, b, (((1,), (1,)), ((), ())), preferred_element_type=f32)


def tn(a, b):
    return lax.dot_general(a, b, (((0,), (0,)), ((), ())), preferred_element_type=f32)


def norm_parts(value):
    centered = value - jnp.mean(value, axis=1, keepdims=True)
    rstd = lax.rsqrt(jnp.mean(centered * centered, axis=1, keepdims=True) + EPS)
    return centered * rstd, rstd


def norm_backward(normed, rstd, gain, grad):
    scaled = grad * gain
    mean_one = jnp.mean(scaled, axis=1, keepdims=True)
    mean_two = jnp.mean(scaled * normed, axis=1, keepdims=True)
    return (scaled - mean_one - normed * mean_two) * rstd


def column_sums(value):
    return jnp.sum(value, axis=0, keepdims=True)


def lane_halves():
    lane = lax.broadcasted_iota(jnp.int32, (1, L), 1)
    low = (lane < 64).astype(f32).astype(bf16)
    high = (lane >= 64).astype(f32).astype(bf16)
    return low, high


def stacked(value, halves):
    return jnp.concatenate([value * halves[0], value * halves[1]], axis=0)


def skew(table):
    return pltpu.roll(table, L, 1, stride=1, stride_axis=0)[:, :L]


def unskew(turned):
    wide = jnp.concatenate([turned, jnp.zeros_like(turned)], axis=1)
    return pltpu.roll(wide, 1, 1, stride=1, stride_axis=0)


def start_all(copies):
    for copy in copies:
        copy.start()


def wait_all(copies):
    for copy in copies:
        copy.wait()


def slot_of(ctl, tick, backward):
    section = ctl[0]
    return tick - (1 - section) if backward else tick - section


A_START, A_X, A_CTX, A_HID, A_ACT, A_ALL = 0, 768, 1536, 2304, 3072, 6144
K_QKV, K_P, K_GP, K_ALL = 0, 2304, 3840, 6912


def forward_kernel(tick, n_alias, *refs):
    (ctl, hidden_in, received, seg, w_in, w_out, w_up, w_down, b_in, b_up, gains, biases, rel, abs_table) = refs[:14]
    out, acts, keep, resid, sec_out = refs[14 + n_alias : 19 + n_alias]
    (x_v, wi, wo, wu, wd, acts_v, keep_v, resid_v, sems) = refs[19 + n_alias :]
    slot = slot_of(ctl, tick, False)

    @pl.when((slot >= 0) & (slot < ROWS))
    def _():
        loads = [
            pltpu.make_async_copy(w_in, wi, sems.at[0]),
            pltpu.make_async_copy(w_out, wo, sems.at[1]),
            pltpu.make_async_copy(w_up, wu, sems.at[2]),
            pltpu.make_async_copy(w_down, wd, sems.at[3]),
        ]
        own_x = pltpu.make_async_copy(hidden_in.at[slot], x_v, sems.at[4])
        sent_x = pltpu.make_async_copy(received if tick > 0 else received.at[0], x_v, sems.at[4])

        @pl.when(ctl[0] == 0)
        def _():
            own_x.start()

        @pl.when(ctl[0] != 0)
        def _():
            sent_x.start()

        start_all(loads)
        sent_x.wait()
        halves = lane_halves()
        first = ctl[2 + slot]
        x = x_v[...]
        token = lax.broadcasted_iota(jnp.int32, (L, 512), 0)
        place = lax.broadcasted_iota(jnp.int32, (L, 512), 1)
        onehot = (place - token == first).astype(f32).astype(bf16)
        start = x.astype(f32) + nn(onehot, abs_table[...])
        query_in = start.astype(bf16)
        acts_v[:, A_START : A_START + D] = query_in
        acts_v[:, A_X : A_X + D] = x
        loads[0].wait()
        keep_v[:, :D] = (nn(query_in, wi[:, :D]) + b_in[:, :D].astype(f32)).astype(bf16)
        keep_v[:, D : 3 * D] = (nn(x, wi[:, D:]) + b_in[:, D:].astype(f32)).astype(bf16)
        seg_rows = jnp.broadcast_to(seg[pl.ds(slot, 1), :], (L, L)).astype(f32)
        same = seg_rows == seg_rows.T
        for pair in range(PAIRS):
            at = slice(pair * L, pair * L + L)
            query = keep_v[:, pair * L : pair * L + L]
            key = keep_v[:, D + pair * L : D + pair * L + L]
            value = keep_v[:, 2 * D + pair * L : 2 * D + pair * L + L]
            rel_q = rel[:, pair * L : pair * L + L]
            rel_k = rel[:, D + pair * L : D + pair * L + L]
            query_two, key_two = stacked(query, halves), stacked(key, halves)
            content = nt(query_two, key)
            far_query = nt(query_two, rel_k)
            far_key = nt(key_two, rel_q)
            probs = []
            for head in range(2):
                rows = slice(head * L, head * L + L)
                summed = content[rows] + skew(far_query[rows]) + skew(far_key[rows]).T
                scores = jnp.where(same, summed * SCALE, NEG)
                exponent = jnp.exp(scores - jnp.max(scores, axis=1, keepdims=True))
                total = jnp.sum(exponent, axis=1, keepdims=True)
                probs.append((exponent * (1.0 / total)).astype(bf16))
            probs = jnp.concatenate(probs, axis=1)
            keep_v[:, K_P + 2 * pair * L : K_P + 2 * (pair + 1) * L] = probs
            acts_v[:, A_CTX + pair * L : A_CTX + pair * L + L] = nn(probs, stacked(value, halves)).astype(bf16)
        loads[1].wait()
        gain = gains[...].astype(f32)
        shift = biases[...].astype(f32)
        resid_one = start + nn(acts_v[:, A_CTX : A_CTX + D], wo[...]) + shift[0:1]
        resid_v[:, :D] = resid_one
        hidden = norm_parts(resid_one)[0] * gain[0:1] + shift[1:2]
        hidden_low = hidden.astype(bf16)
        acts_v[:, A_HID : A_HID + D] = hidden_low
        loads[2].wait()
        loads[3].wait()
        total = hidden + shift[2:3]
        for part in range(4):
            at = slice(part * D, part * D + D)
            gate = nn(hidden_low, wu[:, at]) + b_up[:, at].astype(f32)
            below = 0.5 + 0.5 * lax.erf(gate * (1.0 / math.sqrt(2.0)))
            density = jnp.exp(gate * gate * -0.5) * (1.0 / math.sqrt(2.0 * math.pi))
            active = (gate * below).astype(bf16)
            acts_v[:, A_ACT + part * D : A_ACT + part * D + D] = active
            keep_v[:, K_GP + part * D : K_GP + part * D + D] = (below + gate * density).astype(bf16)
            total = total + nn(active, wd[at, :])
        resid_v[:, D:] = total
        result = norm_parts(total)[0] * gain[1:2] + shift[3:4]
        out[...] = result.astype(bf16)
        stores = [
            pltpu.make_async_copy(acts_v, acts.at[slot], sems.at[5]),
            pltpu.make_async_copy(keep_v, keep.at[slot], sems.at[6]),
            pltpu.make_async_copy(resid_v, resid.at[slot], sems.at[7]),
            pltpu.make_async_copy(out, sec_out.at[slot], sems.at[8]),
        ]
        start_all(stores)
        wait_all(stores)


ANY = pl.BlockSpec(memory_space=pl.ANY)
VMEM = pl.BlockSpec(memory_space=pltpu.VMEM)
SMEM = pl.BlockSpec(memory_space=pltpu.SMEM)


def forward_tick(tick, ctl, hidden_in, received, seg, w_in, w_out, w_up, w_down, b_in, b_up, gains, biases, rel, abs_table, held):
    held = tuple(held)
    shapes = (
        jax.ShapeDtypeStruct((L, D), bf16),
        jax.ShapeDtypeStruct((ROWS, L, A_ALL), bf16),
        jax.ShapeDtypeStruct((ROWS, L, K_ALL), bf16),
        jax.ShapeDtypeStruct((ROWS, L, 2 * D), f32),
        jax.ShapeDtypeStruct((ROWS, L, D), bf16),
    )
    return pl.pallas_call(
        partial(forward_kernel, tick, len(held)),
        out_shape=shapes,
        in_specs=[SMEM, ANY, ANY, VMEM, ANY, ANY, ANY, ANY, VMEM, VMEM, VMEM, VMEM, VMEM, VMEM] + [ANY] * len(held),
        out_specs=(VMEM, ANY, ANY, ANY, ANY),
        input_output_aliases={14 + i: 1 + i for i in range(len(held))},
        scratch_shapes=[
            pltpu.VMEM((L, D), bf16),
            pltpu.VMEM((D, 3 * D), bf16),
            pltpu.VMEM((D, D), bf16),
            pltpu.VMEM((D, FF), bf16),
            pltpu.VMEM((FF, D), bf16),
            pltpu.VMEM((L, A_ALL), bf16),
            pltpu.VMEM((L, K_ALL), bf16),
            pltpu.VMEM((L, 2 * D), f32),
            pltpu.SemaphoreType.DMA((9,)),
        ],
        compiler_params=pltpu.CompilerParams(vmem_limit_bytes=VMEM_LIMIT),
        cost_estimate=pl.CostEstimate(flops=2 * L * 7077888, bytes_accessed=18000000, transcendentals=L * FF),
    )(ctl, hidden_in, received, seg, w_in, w_out, w_up, w_down, b_in, b_up, gains, biases, rel, abs_table, *held)


def back_ffn_kernel(tick, n_alias, *refs):
    (ctl, cotangent, received, w_up, w_down, gains, keep, resid) = refs[:8]
    d_resid, other_rows, own_rows, vec = refs[8 + n_alias : 12 + n_alias]
    (g_v, wu, wd, gp_v, resid_v, d_v, vec_v, sems) = refs[12 + n_alias :]
    slot = slot_of(ctl, tick, True)

    @pl.when((slot >= 0) & (slot < ROWS))
    def _():
        loads = [
            pltpu.make_async_copy(resid.at[slot], resid_v, sems.at[0]),
            pltpu.make_async_copy(w_down, wd, sems.at[1]),
            pltpu.make_async_copy(keep.at[slot, :, pl.ds(K_GP, FF)], gp_v, sems.at[2]),
            pltpu.make_async_copy(w_up, wu, sems.at[3]),
        ]
        own_g = pltpu.make_async_copy(cotangent.at[slot], g_v, sems.at[4])
        sent_g = pltpu.make_async_copy(received if tick > 0 else received.at[0], g_v, sems.at[4])

        @pl.when(ctl[0] != 0)
        def _():
            own_g.start()

        @pl.when(ctl[0] == 0)
        def _():
            sent_g.start()

        start_all(loads)
        core = ctl[1]
        gain = gains[...].astype(f32)
        sent_g.wait()
        loads[0].wait()
        grad = g_v[...].astype(f32)
        normed, rstd = norm_parts(resid_v[:, D:])
        vec_v[...] = jnp.zeros_like(vec_v)
        vec_v[8:9] = column_sums(grad * normed)
        vec_v[12:13] = column_sums(grad)
        d_two = norm_backward(normed, rstd, gain[1:2], grad)
        d_down = d_two.astype(bf16)
        d_v[:, FF:] = d_down
        vec_v[11:12] = column_sums(d_down.astype(f32))
        loads[1].wait()
        loads[2].wait()
        loads[3].wait()
        d_hidden = d_two
        for part in range(4):
            at = slice(part * D, part * D + D)
            d_gate = (nt(d_down, wd[at, :]) * gp_v[:, at].astype(f32)).astype(bf16)
            d_v[:, at] = d_gate
            vec_v[3 + part : 4 + part] = column_sums(d_gate.astype(f32))
            d_hidden = d_hidden + nt(d_gate, wu[:, at])
        normed, rstd = norm_parts(resid_v[:, :D])
        vec_v[7:8] = column_sums(d_hidden * normed)
        vec_v[10:11] = column_sums(d_hidden)
        d_resid[...] = norm_backward(normed, rstd, gain[0:1], d_hidden)
        stores = [pltpu.make_async_copy(vec_v, vec.at[slot], sems.at[5])]
        for block in range(5):
            own_at = pl.multiple_of(block * D + core * 384, 128)
            other_at = pl.multiple_of(block * D + (1 - core) * 384, 128)
            stores.append(pltpu.make_async_copy(d_v.at[:, pl.ds(own_at, 384)], own_rows.at[block, slot], sems.at[6 + block]))
            stores.append(pltpu.make_async_copy(d_v.at[:, pl.ds(other_at, 384)], other_rows.at[block, slot], sems.at[11 + block]))
        start_all(stores)
        wait_all(stores)


def back_ffn_tick(tick, ctl, cotangent, received, w_up, w_down, gains, keep, resid, held):
    held = tuple(held)
    shapes = (
        jax.ShapeDtypeStruct((L, D), f32),
        jax.ShapeDtypeStruct((5, ROWS, L, 384), bf16),
        jax.ShapeDtypeStruct((5, ROWS, L, 384), bf16),
        jax.ShapeDtypeStruct((ROWS, 16, D), f32),
    )
    return pl.pallas_call(
        partial(back_ffn_kernel, tick, len(held)),
        out_shape=shapes,
        in_specs=[SMEM, ANY, ANY, ANY, ANY, VMEM, ANY, ANY] + [ANY] * len(held),
        out_specs=(VMEM, ANY, ANY, ANY),
        input_output_aliases={8 + i: 1 + i for i in range(len(held))},
        scratch_shapes=[
            pltpu.VMEM((L, D), bf16),
            pltpu.VMEM((D, FF), bf16),
            pltpu.VMEM((FF, D), bf16),
            pltpu.VMEM((L, FF), bf16),
            pltpu.VMEM((L, 2 * D), f32),
            pltpu.VMEM((L, FF + D), bf16),
            pltpu.VMEM((16, D), f32),
            pltpu.SemaphoreType.DMA((16,)),
        ],
        compiler_params=pltpu.CompilerParams(vmem_limit_bytes=VMEM_LIMIT),
        cost_estimate=pl.CostEstimate(flops=2 * L * 4718592, bytes_accessed=12000000, transcendentals=0),
    )(ctl, cotangent, received, w_up, w_down, gains, keep, resid, *held)


def back_att_kernel(tick, n_alias, *refs):
    (ctl, d_resid_in, w_in, w_out, rel, keep) = refs[:6]
    d_in, other_rows, own_rows, vec, d_start_out, d_rel_out, in_grad = refs[6 + n_alias : 13 + n_alias]
    (wi, wo, keep_v, d_v, vec_v, ds_v, rel_v, rel_old, rel_low, sems) = refs[13 + n_alias :]
    slot = slot_of(ctl, tick, True)

    @pl.when((slot >= 0) & (slot < ROWS))
    def _():
        loads = [
            pltpu.make_async_copy(w_out, wo, sems.at[0]),
            pltpu.make_async_copy(keep.at[slot, :, pl.ds(0, K_GP)], keep_v, sems.at[1]),
            pltpu.make_async_copy(w_in, wi, sems.at[2]),
        ]
        start_all(loads)
        core = ctl[1]
        halves = lane_halves()
        row = lax.broadcasted_iota(jnp.int32, (L, L), 0)
        column = lax.broadcasted_iota(jnp.int32, (L, L), 1)
        turn = (row + column == L - 1).astype(f32).astype(bf16)
        d_resid = d_resid_in[...]
        d_att = d_resid.astype(bf16)
        vec_v[...] = jnp.zeros_like(vec_v)
        d_v[:, 3 * D :] = d_att
        vec_v[9:10] = column_sums(d_att.astype(f32))
        loads[0].wait()
        d_context = nt(d_att, wo[...]).astype(bf16)
        loads[1].wait()
        for pair in range(PAIRS):
            at = slice(pair * L, pair * L + L)
            query = keep_v[:, at]
            key = keep_v[:, D + pair * L : D + pair * L + L]
            value = keep_v[:, 2 * D + pair * L : 2 * D + pair * L + L]
            probs = keep_v[:, K_P + 2 * pair * L : K_P + 2 * (pair + 1) * L]
            probs_two = jnp.concatenate([probs[:, :L], probs[:, L:]], axis=0)
            rel_q, rel_k = rel[:, at], rel[:, D + pair * L : D + pair * L + L]
            context_two = stacked(d_context[:, at], halves)
            probs_f = probs_two.astype(f32)
            weighted = nt(context_two, value) * probs_f
            d_scores = (weighted - probs_f * jnp.sum(weighted, axis=1, keepdims=True)).astype(bf16)
            d_value = tn(probs_two, context_two)
            query_two, key_two = stacked(query, halves), stacked(key, halves)
            d_key = tn(d_scores, query_two)
            d_side = jnp.concatenate([d_scores[:L], d_scores[L:]], axis=1)
            d_query = nn(d_side, key_two)
            d_far = (d_side.astype(f32) * SCALE).astype(bf16)
            query_turned = nn(turn, query).astype(bf16)
            key_turned = nn(turn, key).astype(bf16)
            rows_turned = nn(turn, d_far)
            far_query, far_key = [], []
            for head in range(2):
                far_query.append(unskew(rows_turned[:, head * L : head * L + L]).astype(bf16))
                columns_turned = nt(turn, d_far[:, head * L : head * L + L])
                far_key.append(unskew(columns_turned).astype(bf16))
            d_query_turned = nn(jnp.concatenate(far_query, axis=1), stacked(rel_k, halves))
            d_key_turned = nn(jnp.concatenate(far_key, axis=1), stacked(rel_q, halves))
            rel_v[:, at] = tn(jnp.concatenate(far_key, axis=0), stacked(key_turned, halves))
            rel_v[:, D + pair * L : D + pair * L + L] = tn(
                jnp.concatenate(far_query, axis=0), stacked(query_turned, halves)
            )
            d_query = d_query * SCALE + nn(turn, d_query_turned.astype(bf16))
            d_key = d_key * SCALE + nn(turn, d_key_turned.astype(bf16))
            d_v[:, at] = d_query.astype(bf16)
            d_v[:, D + pair * L : D + pair * L + L] = d_key.astype(bf16)
            d_v[:, 2 * D + pair * L : 2 * D + pair * L + L] = d_value.astype(bf16)
        for part in range(3):
            rows = column_sums(d_v[:, part * D : part * D + D].astype(f32))
            if part < 2:
                rows = rows + column_sums(rel_v[:, part * D : part * D + D])
            vec_v[part : part + 1] = rows

        @pl.when(slot == ROWS - 1)
        def _():
            earlier = pltpu.make_async_copy(d_rel_out, rel_old, sems.at[19])
            earlier.start()
            earlier.wait()
            rel_v[...] = rel_v[...] + rel_old[...]

        rel_low[...] = rel_v[...].astype(bf16)
        loads[2].wait()
        d_start = d_resid + nt(d_v[:, :D], wi[:, :D])
        ds_v[...] = d_start.astype(bf16)
        result = d_start + nt(d_v[:, D : 3 * D], wi[:, D:])
        d_in[...] = result.astype(bf16)
        stores = [
            pltpu.make_async_copy(vec_v, vec.at[slot], sems.at[3]),
            pltpu.make_async_copy(ds_v, d_start_out.at[slot], sems.at[4]),
            pltpu.make_async_copy(rel_v, d_rel_out, sems.at[5]),
            pltpu.make_async_copy(d_in, in_grad.at[slot], sems.at[6]),
        ]
        for block in range(4):
            own_at = pl.multiple_of(block * D + core * 384, 128)
            other_at = pl.multiple_of(block * D + (1 - core) * 384, 128)
            stores.append(pltpu.make_async_copy(d_v.at[:, pl.ds(own_at, 384)], own_rows.at[block, slot], sems.at[7 + block]))
            stores.append(pltpu.make_async_copy(d_v.at[:, pl.ds(other_at, 384)], other_rows.at[block, slot], sems.at[11 + block]))
        for block in range(2):
            own_at = pl.multiple_of(block * D + core * 384, 128)
            other_at = pl.multiple_of(block * D + (1 - core) * 384, 128)
            for part in range(ROWS):
                rows = pl.ds(part * L, L)
                at = 2 * block + part
                stores.append(pltpu.make_async_copy(rel_low.at[rows, pl.ds(own_at, 384)], own_rows.at[4 + block, part], sems.at[15 + at]))
                stores.append(pltpu.make_async_copy(rel_low.at[rows, pl.ds(other_at, 384)], other_rows.at[4 + block, part], sems.at[20 + at]))
        start_all(stores)
        wait_all(stores)


def back_att_tick(tick, ctl, d_resid, w_in, w_out, rel, keep, held):
    held = tuple(held)
    shapes = (
        jax.ShapeDtypeStruct((L, D), bf16),
        jax.ShapeDtypeStruct((6, ROWS, L, 384), bf16),
        jax.ShapeDtypeStruct((6, ROWS, L, 384), bf16),
        jax.ShapeDtypeStruct((ROWS, 16, D), f32),
        jax.ShapeDtypeStruct((ROWS, L, D), bf16),
        jax.ShapeDtypeStruct((2 * L, 2 * D), f32),
        jax.ShapeDtypeStruct((ROWS, L, D), bf16),
    )
    return pl.pallas_call(
        partial(back_att_kernel, tick, len(held)),
        out_shape=shapes,
        in_specs=[SMEM, VMEM, ANY, ANY, VMEM, ANY] + [ANY] * len(held),
        out_specs=(VMEM, ANY, ANY, ANY, ANY, ANY, ANY),
        input_output_aliases={6 + i: 1 + i for i in range(len(held))},
        scratch_shapes=[
            pltpu.VMEM((D, 3 * D), bf16),
            pltpu.VMEM((D, D), bf16),
            pltpu.VMEM((L, K_GP), bf16),
            pltpu.VMEM((L, 4 * D), bf16),
            pltpu.VMEM((16, D), f32),
            pltpu.VMEM((L, D), bf16),
            pltpu.VMEM((2 * L, 2 * D), f32),
            pltpu.VMEM((2 * L, 2 * D), f32),
            pltpu.VMEM((2 * L, 2 * D), bf16),
            pltpu.SemaphoreType.DMA((24,)),
        ],
        compiler_params=pltpu.CompilerParams(vmem_limit_bytes=VMEM_LIMIT),
        cost_estimate=pl.CostEstimate(flops=2 * L * 2359296 + 400000000, bytes_accessed=8000000, transcendentals=0),
    )(ctl, d_resid, w_in, w_out, rel, keep, *held)


def relative_kernel(rel_table, w_in, b_in, rel_rows, rel, wi, sem):
    load = pltpu.make_async_copy(w_in.at[:, pl.ds(0, 2 * D)], wi, sem)
    load.start()
    shape = (2 * L, rel_table.shape[0])
    select = lax.broadcasted_iota(jnp.int32, shape, 0) + lax.broadcasted_iota(jnp.int32, shape, 1) == L + SPAN
    rows = nn(select.astype(f32).astype(bf16), rel_table[...]).astype(bf16)
    rel_rows[...] = rows
    load.wait()
    rel[...] = (nn(rows, wi[...]) + b_in[:, : 2 * D].astype(f32)).astype(bf16)


def relative_rows(rel_table, w_in, b_in):
    return pl.pallas_call(
        relative_kernel,
        out_shape=(jax.ShapeDtypeStruct((2 * L, D), bf16), jax.ShapeDtypeStruct((2 * L, 2 * D), bf16)),
        in_specs=[VMEM, ANY, VMEM],
        out_specs=(VMEM, VMEM),
        scratch_shapes=[pltpu.VMEM((D, 2 * D), bf16), pltpu.SemaphoreType.DMA],
        compiler_params=pltpu.CompilerParams(vmem_limit_bytes=VMEM_LIMIT),
        cost_estimate=pl.CostEstimate(flops=1000000000, bytes_accessed=5000000, transcendentals=0),
    )(rel_table, w_in, b_in)


TABLE_ROWS, VECTOR_ROWS, TAIL_ROWS = 896, 16, 1024
REL_FROM = 128


def tables_kernel(ctl, d_rel, d_start, vec_one, vec_two, w_in, own, other, wi, sem):
    load = pltpu.make_async_copy(w_in.at[:, pl.ds(0, 2 * D)], wi, sem)
    load.start()
    core = ctl[1]

    def put(rows, value):
        low, high = value[:, :384].astype(bf16), value[:, 384:].astype(bf16)
        own[rows] = jnp.where(core == 0, low, high)
        other[rows] = jnp.where(core == 0, high, low)

    place = lax.broadcasted_iota(jnp.int32, (512, L), 0) - lax.broadcasted_iota(jnp.int32, (512, L), 1)
    spots = [(place == ctl[2 + slot]).astype(f32).astype(bf16) for slot in range(ROWS)]
    put(slice(384, 896), nn(spots[0], d_start[0]) + nn(spots[1], d_start[1]))
    vectors = vec_one[0] + vec_one[1] + vec_two[0] + vec_two[1]
    put(slice(896, 912), vectors)
    put(slice(912, 1024), jnp.zeros((112, D), f32))
    load.wait()
    rows = nt(d_rel[...].astype(bf16), wi[...]).astype(bf16)
    shape = (384, 2 * L)
    select = lax.broadcasted_iota(jnp.int32, shape, 0) + lax.broadcasted_iota(jnp.int32, shape, 1) == L + SPAN - REL_FROM
    put(slice(0, 384), nn(select.astype(f32).astype(bf16), rows))


def tables(ctl, d_rel, d_start, vec_one, vec_two, w_in):
    shape = jax.ShapeDtypeStruct((TAIL_ROWS, 384), bf16)
    return pl.pallas_call(
        tables_kernel,
        out_shape=(shape, shape),
        in_specs=[SMEM, VMEM, VMEM, VMEM, VMEM, ANY],
        out_specs=(VMEM, VMEM),
        scratch_shapes=[pltpu.VMEM((D, 2 * D), bf16), pltpu.SemaphoreType.DMA],
        compiler_params=pltpu.CompilerParams(vmem_limit_bytes=VMEM_LIMIT),
        cost_estimate=pl.CostEstimate(flops=1000000000, bytes_accessed=7000000, transcendentals=0),
    )(ctl, d_rel, d_start, vec_one, vec_two, w_in)


def ffn_weight_kernel(acts, acts_sent, rows, rows_sent, out):
    total = tn(acts[...].reshape(2 * L, D), rows[...].reshape(2 * L, 384))
    total += tn(acts_sent[...].reshape(2 * L, D), rows_sent[...].reshape(2 * L, 384))
    out[...] = total.astype(bf16)


def ffn_weights(acts, acts_sent, rows, rows_sent):
    act_spec = pl.BlockSpec((ROWS, L, D), lambda b: (0, 0, jnp.maximum(b, 3)))
    row_spec = pl.BlockSpec((1, ROWS, L, 384), lambda b: (jnp.minimum(b, 4), 0, 0, 0))
    return pl.pallas_call(
        ffn_weight_kernel,
        grid=(8,),
        out_shape=jax.ShapeDtypeStruct((8 * D, 384), bf16),
        in_specs=[act_spec, act_spec, row_spec, row_spec],
        out_specs=pl.BlockSpec((D, 384), lambda b: (b, 0)),
        compiler_params=pltpu.CompilerParams(vmem_limit_bytes=VMEM_LIMIT),
        cost_estimate=pl.CostEstimate(flops=8 * 2 * 512 * 768 * 384, bytes_accessed=13000000, transcendentals=0),
    )(acts, acts_sent, rows, rows_sent)


def att_weight_kernel(acts, acts_sent, rows, rows_sent, table, d_table, d_table_sent, out):
    total = tn(acts[...].reshape(2 * L, D), rows[...].reshape(2 * L, 384))
    total += tn(acts_sent[...].reshape(2 * L, D), rows_sent[...].reshape(2 * L, 384))
    far = tn(table[...], d_table[...].reshape(2 * L, 384))
    far += tn(table[...], d_table_sent[...].reshape(2 * L, 384))
    out[...] = (total + far * jnp.where(pl.program_id(0) < 2, 1.0, 0.0)).astype(bf16)


def att_weights(acts, acts_sent, rows, rows_sent, table):
    act_spec = pl.BlockSpec((ROWS, L, D), lambda b: (0, 0, (b + 1) // 2))
    row_spec = pl.BlockSpec((1, ROWS, L, 384), lambda b: (b, 0, 0, 0))
    far_spec = pl.BlockSpec((1, ROWS, L, 384), lambda b: (4 + jnp.minimum(b, 1), 0, 0, 0))
    return pl.pallas_call(
        att_weight_kernel,
        grid=(4,),
        out_shape=jax.ShapeDtypeStruct((4 * D, 384), bf16),
        in_specs=[act_spec, act_spec, row_spec, row_spec, pl.BlockSpec((2 * L, D), lambda b: (0, 0)), far_spec, far_spec],
        out_specs=pl.BlockSpec((D, 384), lambda b: (b, 0)),
        compiler_params=pltpu.CompilerParams(vmem_limit_bytes=VMEM_LIMIT),
        cost_estimate=pl.CostEstimate(flops=4 * 2 * 1024 * 768 * 384, bytes_accessed=8000000, transcendentals=0),
    )(acts, acts_sent, rows, rows_sent, table, rows, rows_sent)


UNIT = 256
SLOTS = 4


def assemble_kernel(ctl, *refs):
    n = 2 * PIECES
    own, sent = refs[:n], refs[n : 2 * n]
    g_in, g_out, g_up, g_down, g_rel, g_abs, g_b_in, g_b_up, g_gains, g_biases = refs[2 * n : 2 * n + 10]
    low, wide, blank, in_sems, out_sems, blank_sem = refs[2 * n + 10 :]
    core = ctl[1]

    def targets(unit):
        block, part = unit // 3, unit % 3
        rows = pl.ds(part * UNIT, UNIT)
        every = pl.ds(0, UNIT)
        if block < 4:
            return [(every, g_up.at[rows, pl.ds(block * D, D)])]
        if block < 8:
            return [(every, g_down.at[pl.ds((block - 4) * D + part * UNIT, UNIT)])]
        if block < 11:
            return [(every, g_in.at[rows, pl.ds((block - 8) * D, D)])]
        if block < 12:
            return [(every, g_out.at[rows])]
        if unit == 36:
            return [(every, g_rel.at[pl.ds(REL_FROM, UNIT)])]
        if unit == 37:
            return [(pl.ds(0, L), g_rel.at[pl.ds(REL_FROM + UNIT, L)]), (pl.ds(L, L), g_abs.at[pl.ds(0, L)])]
        if unit == 38:
            return [(every, g_abs.at[pl.ds(L, UNIT)])]
        return [(pl.ds(0, L), g_abs.at[pl.ds(L + UNIT, L)])]

    def load(unit, start):
        piece, half, part = unit // 8, unit % 8 // 4, unit % 4
        at = unit % SLOTS
        rows = pl.ds(part * UNIT, UNIT)

        def copy(which, kind):
            column = pl.multiple_of((core if which == 0 else 1 - core) * 384, 128)
            array = (own, sent)[which][2 * piece + kind]
            return pltpu.make_async_copy(array.at[rows], low.at[at, :, pl.ds(column, 384)], in_sems.at[at, which])

        for which in range(2):
            if not start:
                copy(which, 0).wait()
                continue

            @pl.when(ctl[4 + piece] == half)
            def _():
                copy(which, 0).start()

            @pl.when(ctl[4 + piece] != half)
            def _():
                copy(which, 1).start()

    def stores(unit):
        at = unit % SLOTS
        return [
            pltpu.make_async_copy(wide.at[at, rows], target, out_sems.at[at, which])
            for which, (rows, target) in enumerate(targets(unit))
        ]

    units = 8 * PIECES
    for unit in range(SLOTS - 1):
        load(unit, True)
    blank[...] = jnp.zeros_like(blank)
    clear = pltpu.make_async_copy(blank, g_rel.at[pl.ds(0, REL_FROM)], blank_sem)
    clear.start()
    for unit in range(units):
        if unit + SLOTS - 1 < units:
            load(unit + SLOTS - 1, True)
        load(unit, False)
        if unit >= SLOTS:
            wait_all(stores(unit - SLOTS))
        wide[unit % SLOTS] = low[unit % SLOTS].astype(f32)
        start_all(stores(unit))
    vectors = wide[(units - 1) % SLOTS, L : L + VECTOR_ROWS, :]
    for part in range(3):
        g_b_in[:, part * D : part * D + D] = vectors[part : part + 1]
    for part in range(4):
        g_b_up[:, part * D : part * D + D] = vectors[3 + part : 4 + part]
    g_gains[...] = vectors[7:9]
    g_biases[...] = vectors[9:13]
    clear.wait()
    for unit in range(units - SLOTS, units):
        wait_all(stores(unit))


def assemble(ctl, own, sent):
    shapes = ((D, 3 * D), (D, D), (D, FF), (FF, D), (512, D), (512, D), (1, 3 * D), (1, FF), (2, D), (4, D))
    return pl.pallas_call(
        assemble_kernel,
        out_shape=tuple(jax.ShapeDtypeStruct(shape, f32) for shape in shapes),
        in_specs=[SMEM] + [ANY] * (4 * PIECES),
        out_specs=(ANY,) * 6 + (VMEM,) * 4,
        scratch_shapes=[
            pltpu.VMEM((SLOTS, UNIT, D), bf16),
            pltpu.VMEM((SLOTS, UNIT, D), f32),
            pltpu.VMEM((REL_FROM, D), f32),
            pltpu.SemaphoreType.DMA((SLOTS, 2)),
            pltpu.SemaphoreType.DMA((SLOTS, 2)),
            pltpu.SemaphoreType.DMA,
        ],
        compiler_params=pltpu.CompilerParams(vmem_limit_bytes=VMEM_LIMIT),
        cost_estimate=pl.CostEstimate(flops=0, bytes_accessed=48000000, transcendentals=0),
    )(ctl, *own, *sent)


SQUARE = ((0, 0), (1, 0), (1, 1), (0, 1))
ROTATION = ("x0", "z0", "x1", "z1", "y")


def dp_place(index):
    return {"core": index % 2, "x": index // 2 % 4, "y": index // 8 % 2, "z": index // 16}


def dp_index(place):
    return ((place["z"] * 2 + place["y"]) * 4 + place["x"]) * 2 + place["core"]


def partner(index, dim):
    place = dp_place(index)
    if len(dim) == 2:
        bits = list(SQUARE[place[dim[0]]])
        bits[int(dim[1])] ^= 1
        place[dim[0]] = SQUARE.index(tuple(bits))
    else:
        place[dim] ^= 1
    return dp_index(place)


def swap(value, dim):
    peers = lax.axis_size("dp")
    return lax.ppermute(value, "dp", [(i, partner(i, dim)) for i in range(peers)])


def side(dim):
    place = dp_place(lax.axis_index("dp"))
    if len(dim) == 1 or dim == "core":
        return place[dim].astype(jnp.int32)
    at = place[dim[0]]
    if dim[1] == "0":
        return ((at == 1) | (at == 2)).astype(jnp.int32)
    return (at >= 2).astype(jnp.int32)


def order_of(piece):
    return [ROTATION[(piece + step) % len(ROTATION)] for step in range(len(ROTATION))]


ORDERS = [order_of(piece) for piece in range(PIECES)]


def scatter_sums(pieces, orders):
    for step in range(len(ROTATION)):
        summed = []
        for piece, order in zip(pieces, orders):
            at, half = side(order[step]), piece.shape[0] // 2
            sent = lax.dynamic_slice_in_dim(piece, (1 - at) * half, half, 0)
            summed.append((piece, at, half, swap(sent, order[step])))
        pieces = [
            lax.dynamic_slice_in_dim(piece, at * half, half, 0) + received
            for piece, at, half, received in summed
        ]
    return pieces


def in_order(at, own, other):
    return jnp.where(
        at == 0,
        jnp.concatenate([own, other], axis=0),
        jnp.concatenate([other, own], axis=0),
    )


def gather_pieces(pieces, orders):
    for step in reversed(range(1, len(ROTATION))):
        received = [swap(piece, order[step]) for piece, order in zip(pieces, orders)]
        pieces = [
            in_order(side(order[step]), piece, other)
            for piece, other, order in zip(pieces, received, orders)
        ]
    received = [swap(piece, order[0]) for piece, order in zip(pieces, orders)]
    return [half for pair in zip(pieces, received) for half in pair]


def add_tables_of_both_sections(chunk, order):
    size = chunk.shape[0] * 2 ** len(order)
    first_row, span = 0, size
    for dim in order:
        span //= 2
        first_row = first_row + side(dim) * span
    row_at = first_row + lax.broadcasted_iota(jnp.int32, chunk.shape, 0) - (size - TAIL_ROWS)
    is_table = (row_at >= 0) & (row_at < TABLE_ROWS)
    elsewhere = lax.ppermute(chunk, "section", [(0, 1), (1, 0)])
    return jnp.where(is_table, chunk + elsewhere, chunk)


def per_device(
    hidden_in,
    cotangent,
    segment_ids,
    positions,
    w_in,
    b_in,
    w_out,
    w_up,
    b_up,
    w_down,
    gains,
    biases,
    rel_table,
    abs_table,
):
    w_in, w_out, w_up, w_down, gains, biases = w_in[0], w_out[0], w_up[0], w_down[0], gains[0], biases[0]
    section = lax.axis_index("section").astype(jnp.int32)
    firsts = jnp.where(section == 1, positions[:, 0], 8 * abs_table.shape[0])
    sides = [side(order[0]) for order in ORDERS]
    ctl = jnp.stack([section, side("core"), firsts[0], firsts[1], *sides])
    rel_rows, rel = relative_rows(rel_table, w_in, b_in)

    received, held = hidden_in, ()
    for tick in range(ROWS + 1):
        sent, *held = forward_tick(
            tick, ctl, hidden_in, received, segment_ids, w_in, w_out, w_up, w_down, b_in, b_up, gains, biases, rel, abs_table, held
        )
        if tick < ROWS:
            received = lax.ppermute(sent, "section", [(0, 1)])
    acts, keep, resid, section_out = held
    acts_sent = swap(acts, "core")

    received, ffn_held, att_held = cotangent, (), ()
    for tick in range(ROWS + 1):
        d_resid, *ffn_held = back_ffn_tick(tick, ctl, cotangent, received, w_up, w_down, gains, keep, resid, ffn_held)
        sent, *att_held = back_att_tick(tick, ctl, d_resid, w_in, w_out, rel, keep, att_held)
        if tick < ROWS:
            received = lax.ppermute(sent, "section", [(1, 0)])
    ffn_other, ffn_rows, ffn_vectors = ffn_held
    att_other, att_rows, att_vectors, d_start, d_rel, input_grad = att_held
    tail, tail_other = tables(ctl, d_rel, d_start, ffn_vectors, att_vectors, w_in)

    ffn = ffn_weights(acts, acts_sent, ffn_rows, swap(ffn_other, "core"))
    att = att_weights(acts, acts_sent, att_rows, swap(att_other, "core"), rel_rows)
    tail = tail + swap(tail_other, "core")
    size = (ffn.shape[0] + att.shape[0] + tail.shape[0]) // PIECES
    pieces = [ffn[at : at + size] for at in range(0, ffn.shape[0], size)]
    pieces += [att[:size], jnp.concatenate([att[size:], tail], axis=0)]
    pieces = scatter_sums(pieces, ORDERS)
    pieces[-1] = add_tables_of_both_sections(pieces[-1], ORDERS[-1])
    halves = gather_pieces(pieces, ORDERS)
    g_w_in, g_w_out, g_w_up, g_w_down, g_rel, g_abs, g_b_in, g_b_up, g_gains, g_biases = assemble(
        ctl, halves, [swap(half, "core") for half in halves]
    )
    return (
        section_out[None],
        input_grad[None],
        g_w_in[None],
        g_b_in,
        g_w_out[None],
        g_w_up[None],
        g_b_up,
        g_w_down[None],
        g_gains[None],
        g_biases[None],
        g_rel,
        g_abs,
    )


def solution(mesh):
    in_specs = (
        P("dp", None, None),
        P("dp", None, None),
        P("dp", None),
        P("dp", None),
        P("section", None, None),
        P("section", None),
        P("section", None, None),
        P("section", None, None),
        P("section", None),
        P("section", None, None),
        P("section", None, None),
        P("section", None, None),
        P(),
        P(),
    )
    out_specs = (
        P("section", "dp", None, None),
        P("section", "dp", None, None),
        P("section", None, None),
        P("section", None),
        P("section", None, None),
        P("section", None, None),
        P("section", None),
        P("section", None, None),
        P("section", None, None),
        P("section", None, None),
        P(),
        P(),
    )
    return jax.shard_map(
        per_device, mesh=mesh, in_specs=in_specs, out_specs=out_specs, check_vma=False
    )
```

```python
from functools import partial
import math
from types import SimpleNamespace

import jax
import jax.numpy as jnp
from jax import lax
from jax.experimental import pallas as pl
from jax.experimental.pallas import tpu as pltpu
from jax.sharding import PartitionSpec as P

HEADS = 12
L = 128
D = 768
FF = 3072
HALF = D // 2
PAIRS = HEADS // 2
ROWS = 2
SPAN = 256
PIECES = 5
EPS = 1e-06
NEG = -1e30
SCALE = 1.0 / math.sqrt(3 * 64)
VMEM_LIMIT = 56 * 1024 * 1024
f32, bf16 = jnp.float32, jnp.bfloat16

A_START, A_X, A_CTX, A_HID, A_ACT, A_ALL = 0, 768, 1536, 2304, 3072, 6144
K_P, K_GP, K_ALL = 2304, 3840, 6912
VECTOR_ROWS = 16
REL_FROM, REL_ROWS, ABS_ROWS, TAIL_ROWS = 128, 384, 512, 1024
TABLE_ROWS = REL_ROWS + ABS_ROWS
PIECE = 2048
UNIT = 256

ANY = pl.BlockSpec(memory_space=pl.ANY)
SMEM = pl.BlockSpec(memory_space=pltpu.SMEM)


def nn(a, b):
    return lax.dot_general(a, b, (((1,), (0,)), ((), ())), preferred_element_type=f32)


def nt(a, b):
    return lax.dot_general(a, b, (((1,), (1,)), ((), ())), preferred_element_type=f32)


def tn(a, b):
    return lax.dot_general(a, b, (((0,), (0,)), ((), ())), preferred_element_type=f32)


def norm_parts(value):
    centered = value - jnp.mean(value, axis=1, keepdims=True)
    rstd = lax.rsqrt(jnp.mean(centered * centered, axis=1, keepdims=True) + EPS)
    return centered * rstd, rstd


def norm_backward(normed, rstd, gain, grad):
    scaled = grad * gain
    mean_one = jnp.mean(scaled, axis=1, keepdims=True)
    mean_two = jnp.mean(scaled * normed, axis=1, keepdims=True)
    return (scaled - mean_one - normed * mean_two) * rstd


def column_sums(value):
    return jnp.sum(value, axis=0, keepdims=True)


def indicator(condition):
    return condition.astype(f32).astype(bf16)


def lane_halves():
    lane = lax.broadcasted_iota(jnp.int32, (1, L), 1)
    return indicator(lane < 64), indicator(lane >= 64)


def stacked(value, halves):
    return jnp.concatenate([value * halves[0], value * halves[1]], axis=0)


def skew(table):
    return pltpu.roll(table, L, 1, stride=1, stride_axis=0)[:, :L]


def unskew(turned):
    wide = jnp.concatenate([turned, jnp.zeros_like(turned)], axis=1)
    return pltpu.roll(wide, 1, 1, stride=1, stride_axis=0)


def pair_at(pair, base=0):
    return slice(base + pair * L, base + pair * L + L)


def block_at(block, base=0):
    return slice(base + block * D, base + block * D + D)


def shape(dims, dtype=bf16):
    return jax.ShapeDtypeStruct(dims, dtype)


class Copies:
    def __init__(self, sems):
        self.sems, self.used = sems, 0

    def make(self, source, target):
        self.used += 1
        return pltpu.make_async_copy(source, target, self.sems.at[self.used - 1])

    def start(self, source, target):
        copy = self.make(source, target)
        copy.start()
        return copy


def wait_all(copies):
    for copy in copies:
        copy.wait()


def run(body, ctl, ins, outs, held, scratch, copies, flops, traffic):
    names, out_names, scratch_names = list(ins), list(outs), list(scratch)
    kept = [name for name in out_names if name in held and name != "sent"]

    def kernel(*refs):
        ctl_ref, refs = refs[0], refs[1:]
        r = SimpleNamespace(ctl=ctl_ref, **dict(zip(names, refs)))
        refs = refs[len(names) + len(kept) :]
        for name, ref in zip(out_names + scratch_names, refs):
            setattr(r, name, ref)
        r.copies = Copies(refs[-1])
        body(r)

    results = pl.pallas_call(
        kernel,
        out_shape=tuple(outs.values()),
        in_specs=[SMEM] + [ANY] * (len(names) + len(kept)),
        out_specs=(ANY,) * len(out_names),
        input_output_aliases={1 + len(names) + i: out_names.index(name) for i, name in enumerate(kept)},
        scratch_shapes=[pltpu.VMEM(s.shape, s.dtype) for s in scratch.values()] + [pltpu.SemaphoreType.DMA((copies,))],
        compiler_params=pltpu.CompilerParams(vmem_limit_bytes=VMEM_LIMIT),
        cost_estimate=pl.CostEstimate(flops=flops, bytes_accessed=traffic, transcendentals=0),
    )(ctl, *ins.values(), *[held[name] for name in kept])
    return dict(zip(out_names, results))


def relative_part(r):
    loads = [r.copies.start(r.rel_table, r.table_v), r.copies.start(r.b_in, r.b_in_v), r.copies.start(r.w_in, r.wi)]
    dims = (2 * L, 2 * SPAN)
    select = indicator(lax.broadcasted_iota(jnp.int32, dims, 0) + lax.broadcasted_iota(jnp.int32, dims, 1) == L + SPAN)
    loads[0].wait()
    rows = nn(select, r.table_v[...]).astype(bf16)
    r.rel_rows_v[...] = rows
    loads[1].wait()
    loads[2].wait()
    r.rel_v[...] = (nn(rows, r.wi[:, : 2 * D]) + r.b_in_v[:, : 2 * D].astype(f32)).astype(bf16)
    return [r.copies.start(r.rel_rows_v, r.rel_rows), r.copies.start(r.rel_v, r.rel)]


def forward_body(row, section, first, r):
    start_copy = r.copies.start
    stores = relative_part(r) if first else []

    @pl.when(r.ctl[0] == section)
    def _():
        x_load = start_copy(r.hidden_in.at[row] if section == 0 else r.received, r.x_v)
        small = [start_copy(r.segment_ids, r.seg_v), start_copy(r.gains, r.gains_v), start_copy(r.biases, r.biases_v)]
        abs_load = start_copy(r.abs_table, r.table_v) if section == 1 else None
        in_loads = [] if first else [start_copy(r.b_in, r.b_in_v), start_copy(r.w_in, r.wi)]
        rel_load = None if first else start_copy(r.rel, r.rel_v)
        loads = [start_copy(r.w_out, r.wo), start_copy(r.b_up, r.b_up_v), start_copy(r.w_up, r.wu), start_copy(r.w_down, r.wd)]
        halves = lane_halves()
        x_load.wait()
        x = r.x_v[...]
        start = x.astype(f32)
        if section == 1:
            abs_load.wait()
            dims = (L, ABS_ROWS)
            place = lax.broadcasted_iota(jnp.int32, dims, 1) - lax.broadcasted_iota(jnp.int32, dims, 0)
            start = start + nn(indicator(place == r.ctl[2 + row]), r.table_v[...])
        query_in = start.astype(bf16)
        r.acts_v[:, block_at(0)] = query_in
        r.acts_v[:, block_at(1)] = x
        wait_all(in_loads)
        b_in = r.b_in_v[...].astype(f32)
        r.keep_v[:, :D] = (nn(query_in, r.wi[:, :D]) + b_in[:, :D]).astype(bf16)
        r.keep_v[:, D : 3 * D] = (nn(x, r.wi[:, D:]) + b_in[:, D:]).astype(bf16)
        wait_all(small)
        if rel_load is not None:
            rel_load.wait()
        seg_rows = jnp.broadcast_to(r.seg_v[row : row + 1, :], (L, L)).astype(f32)
        same = seg_rows == seg_rows.T
        for pair in range(PAIRS):
            query = r.keep_v[:, pair_at(pair)]
            key = r.keep_v[:, pair_at(pair, D)]
            value = r.keep_v[:, pair_at(pair, 2 * D)]
            query_two, key_two = stacked(query, halves), stacked(key, halves)
            content = nt(query_two, key)
            far_query = nt(query_two, r.rel_v[:, pair_at(pair, D)])
            far_key = nt(key_two, r.rel_v[:, pair_at(pair)])
            probs = []
            for head in range(2):
                rows = slice(head * L, head * L + L)
                summed = content[rows] + skew(far_query[rows]) + skew(far_key[rows]).T
                scores = jnp.where(same, summed * SCALE, NEG)
                exponent = jnp.exp(scores - jnp.max(scores, axis=1, keepdims=True))
                total = jnp.sum(exponent, axis=1, keepdims=True)
                probs.append((exponent * (1.0 / total)).astype(bf16))
            probs = jnp.concatenate(probs, axis=1)
            r.keep_v[:, K_P + 2 * pair * L : K_P + 2 * (pair + 1) * L] = probs
            r.acts_v[:, pair_at(pair, A_CTX)] = nn(probs, stacked(value, halves)).astype(bf16)
        loads[0].wait()
        gain = r.gains_v[...].astype(f32)
        shift = r.biases_v[...].astype(f32)
        resid_one = start + nn(r.acts_v[:, A_CTX : A_CTX + D], r.wo[...]) + shift[0:1]
        r.resid_v[:, :D] = resid_one
        hidden = norm_parts(resid_one)[0] * gain[0:1] + shift[1:2]
        hidden_low = hidden.astype(bf16)
        r.acts_v[:, A_HID : A_HID + D] = hidden_low
        early = [
            start_copy(r.acts_v.at[:, pl.ds(0, A_ACT)], r.acts.at[row, :, pl.ds(0, A_ACT)]),
            start_copy(r.keep_v.at[:, pl.ds(0, K_GP)], r.keep.at[row, :, pl.ds(0, K_GP)]),
        ]
        wait_all(loads[1:])
        total = hidden + shift[2:3]
        for part in range(4):
            gate = nn(hidden_low, r.wu[:, block_at(part)]) + r.b_up_v[:, block_at(part)].astype(f32)
            below = 0.5 + 0.5 * lax.erf(gate * (1.0 / math.sqrt(2.0)))
            density = jnp.exp(gate * gate * -0.5) * (1.0 / math.sqrt(2.0 * math.pi))
            active = (gate * below).astype(bf16)
            r.acts_v[:, block_at(part, A_ACT)] = active
            r.keep_v[:, block_at(part, K_GP)] = (below + gate * density).astype(bf16)
            total = total + nn(active, r.wd[block_at(part), :])
        r.resid_v[:, D:] = total
        late = [
            start_copy(r.acts_v.at[:, pl.ds(A_ACT, FF)], r.acts.at[row, :, pl.ds(A_ACT, FF)]),
            start_copy(r.keep_v.at[:, pl.ds(K_GP, FF)], r.keep.at[row, :, pl.ds(K_GP, FF)]),
            start_copy(r.resid_v, r.resid.at[row]),
        ]
        r.x_v[...] = (norm_parts(total)[0] * gain[1:2] + shift[3:4]).astype(bf16)
        late.append(start_copy(r.x_v, r.section_out.at[row]))
        if section == 0:
            late.append(start_copy(r.x_v, r.sent))
        wait_all(early + late)

    wait_all(stores)


def forward(row, section, ctl, ins, held):
    first = not held
    outs = {"sent": shape((L, D))} if section == 0 else {}
    if first:
        outs.update(rel_rows=shape((2 * L, D)), rel=shape((2 * L, 2 * D)))
    outs.update(
        acts=shape((ROWS, L, A_ALL)),
        keep=shape((ROWS, L, K_ALL)),
        resid=shape((ROWS, L, 2 * D), f32),
        section_out=shape((ROWS, L, D)),
    )
    scratch = dict(
        x_v=shape((L, D)), seg_v=shape((ROWS, L), jnp.int32), gains_v=shape((2, D)), biases_v=shape((4, D)),
        b_in_v=shape((1, 3 * D)), b_up_v=shape((1, FF)), table_v=shape((2 * SPAN, D)), rel_v=shape((2 * L, 2 * D)),
        wi=shape((D, 3 * D)), wo=shape((D, D)), wu=shape((D, FF)), wd=shape((FF, D)),
        acts_v=shape((L, A_ALL)), keep_v=shape((L, K_ALL)), resid_v=shape((L, 2 * D), f32),
    )
    if first:
        scratch.update(rel_rows_v=shape((2 * L, D)))
    return run(partial(forward_body, row, section, first), ctl, ins, outs, held, scratch, 24, 1900000000, 18000000)


def ffn_loads(row, section, r):
    return SimpleNamespace(
        grad=r.copies.start(r.cotangent.at[row] if section == 1 else r.received, r.grad_v),
        resid=r.copies.start(r.resid.at[row], r.resid_v),
        gains=r.copies.start(r.gains, r.gains_v),
        down=r.copies.start(r.w_down, r.wd),
        slope=r.copies.start(r.keep.at[row, :, pl.ds(K_GP, FF)], r.slope_v),
        up=r.copies.start(r.w_up, r.wu),
    )


def ffn_part(row, r, loads):
    wait_all([loads.grad, loads.resid, loads.gains])
    gain = r.gains_v[...].astype(f32)
    grad = r.grad_v[...].astype(f32)
    normed, rstd = norm_parts(r.resid_v[:, D:])
    r.ffn_vec_v[...] = jnp.zeros_like(r.ffn_vec_v)
    r.ffn_vec_v[8:9] = column_sums(grad * normed)
    r.ffn_vec_v[12:13] = column_sums(grad)
    d_two = norm_backward(normed, rstd, gain[1:2], grad)
    d_down = d_two.astype(bf16)
    r.ffn_v[:, FF:] = d_down
    r.ffn_vec_v[11:12] = column_sums(d_down.astype(f32))
    wait_all([loads.down, loads.slope, loads.up])
    d_hidden = d_two
    for part in range(4):
        d_gate = (nt(d_down, r.wd[block_at(part), :]) * r.slope_v[:, block_at(part)].astype(f32)).astype(bf16)
        r.ffn_v[:, block_at(part)] = d_gate
        r.ffn_vec_v[3 + part : 4 + part] = column_sums(d_gate.astype(f32))
        d_hidden = d_hidden + nt(d_gate, r.wu[:, block_at(part)])
    stores = store_blocks(row, r, r.ffn_v, r.ffn_own, r.ffn_other, 5)
    normed, rstd = norm_parts(r.resid_v[:, :D])
    r.ffn_vec_v[7:8] = column_sums(d_hidden * normed)
    r.ffn_vec_v[10:11] = column_sums(d_hidden)
    stores.append(r.copies.start(r.ffn_vec_v, r.ffn_vec.at[row]))
    return norm_backward(normed, rstd, gain[0:1], d_hidden), stores


def store_blocks(row, r, source, own, other, blocks):
    core, stores = r.ctl[1], []
    for block in range(blocks):
        own_at = pl.multiple_of(block * D + core * HALF, 128)
        other_at = pl.multiple_of(block * D + (1 - core) * HALF, 128)
        stores.append(r.copies.start(source.at[:, pl.ds(own_at, HALF)], own.at[block, row]))
        stores.append(r.copies.start(source.at[:, pl.ds(other_at, HALF)], other.at[block, row]))
    return stores


def att_loads(row, r):
    return SimpleNamespace(
        out=r.copies.start(r.w_out, r.wo),
        keep=r.copies.start(r.keep.at[row, :, pl.ds(0, K_GP)], r.keep_v),
        rel=r.copies.start(r.rel, r.rel_v),
        earlier=r.copies.start(r.d_rel, r.d_rel_old) if row > 0 else None,
        w_in=r.copies.start(r.w_in, r.wi),
    )


def att_part(row, section, r, loads, d_resid):
    halves = lane_halves()
    row_at = lax.broadcasted_iota(jnp.int32, (L, L), 0)
    column_at = lax.broadcasted_iota(jnp.int32, (L, L), 1)
    turn = indicator(row_at + column_at == L - 1)
    d_att = d_resid.astype(bf16)
    r.att_vec_v[...] = jnp.zeros_like(r.att_vec_v)
    r.att_v[:, block_at(3)] = d_att
    r.att_vec_v[9:10] = column_sums(d_att.astype(f32))
    loads.out.wait()
    d_context = nt(d_att, r.wo[...]).astype(bf16)
    loads.keep.wait()
    loads.rel.wait()
    for pair in range(PAIRS):
        query = r.keep_v[:, pair_at(pair)]
        key = r.keep_v[:, pair_at(pair, D)]
        value = r.keep_v[:, pair_at(pair, 2 * D)]
        probs = r.keep_v[:, K_P + 2 * pair * L : K_P + 2 * (pair + 1) * L]
        probs_two = jnp.concatenate([probs[:, :L], probs[:, L:]], axis=0)
        rel_q, rel_k = r.rel_v[:, pair_at(pair)], r.rel_v[:, pair_at(pair, D)]
        context_two = stacked(d_context[:, pair_at(pair)], halves)
        probs_f = probs_two.astype(f32)
        weighted = nt(context_two, value) * probs_f
        d_scores = (weighted - probs_f * jnp.sum(weighted, axis=1, keepdims=True)).astype(bf16)
        query_two, key_two = stacked(query, halves), stacked(key, halves)
        d_value = tn(probs_two, context_two)
        d_key = tn(d_scores, query_two)
        d_side = jnp.concatenate([d_scores[:L], d_scores[L:]], axis=1)
        d_query = nn(d_side, key_two)
        d_far = (d_side.astype(f32) * SCALE).astype(bf16)
        query_turned = nn(turn, query).astype(bf16)
        key_turned = nn(turn, key).astype(bf16)
        rows_turned = nn(turn, d_far)
        far_query, far_key = [], []
        for head in range(2):
            columns = slice(head * L, head * L + L)
            far_query.append(unskew(rows_turned[:, columns]).astype(bf16))
            far_key.append(unskew(nt(turn, d_far[:, columns])).astype(bf16))
        d_query_turned = nn(jnp.concatenate(far_query, axis=1), stacked(rel_k, halves))
        d_key_turned = nn(jnp.concatenate(far_key, axis=1), stacked(rel_q, halves))
        r.d_rel_v[:, pair_at(pair)] = tn(jnp.concatenate(far_key, axis=0), stacked(key_turned, halves))
        r.d_rel_v[:, pair_at(pair, D)] = tn(jnp.concatenate(far_query, axis=0), stacked(query_turned, halves))
        d_query = d_query * SCALE + nn(turn, d_query_turned.astype(bf16))
        d_key = d_key * SCALE + nn(turn, d_key_turned.astype(bf16))
        r.att_v[:, pair_at(pair)] = d_query.astype(bf16)
        r.att_v[:, pair_at(pair, D)] = d_key.astype(bf16)
        r.att_v[:, pair_at(pair, 2 * D)] = d_value.astype(bf16)
    stores = store_blocks(row, r, r.att_v, r.att_own, r.att_other, 4)
    loads.w_in.wait()
    d_start = d_resid + nt(r.att_v[:, :D], r.wi[:, :D])
    r.start_v[...] = d_start.astype(bf16)
    stores.append(r.copies.start(r.start_v, r.d_start.at[row]))
    r.grad_out_v[...] = (d_start + nt(r.att_v[:, D : 3 * D], r.wi[:, D:])).astype(bf16)
    stores.append(r.copies.start(r.grad_out_v, r.input_grad.at[row]))
    if section == 1:
        stores.append(r.copies.start(r.grad_out_v, r.sent))
    for part in range(3):
        rows = column_sums(r.att_v[:, block_at(part)].astype(f32))
        if part < 2:
            rows = rows + column_sums(r.d_rel_v[:, block_at(part)])
        r.att_vec_v[part : part + 1] = rows
    stores.append(r.copies.start(r.att_vec_v, r.att_vec.at[row]))
    if row > 0:
        loads.earlier.wait()
        r.d_rel_v[...] = r.d_rel_v[...] + r.d_rel_old[...]
    if row < ROWS - 1:
        stores.append(r.copies.start(r.d_rel_v, r.d_rel))
    else:
        r.rel_low[...] = r.d_rel_v[...].astype(bf16)
        stores.append(r.copies.start(r.rel_low, r.d_rel_low))
        core = r.ctl[1]
        for block in range(2):
            own_at = pl.multiple_of(block * D + core * HALF, 128)
            other_at = pl.multiple_of(block * D + (1 - core) * HALF, 128)
            for part in range(ROWS):
                rows = pl.ds(part * L, L)
                stores.append(r.copies.start(r.rel_low.at[rows, pl.ds(own_at, HALF)], r.att_own.at[4 + block, part]))
                stores.append(r.copies.start(r.rel_low.at[rows, pl.ds(other_at, HALF)], r.att_other.at[4 + block, part]))
    return stores


def backward_body(row, section, parts, r):
    @pl.when(r.ctl[0] == section)
    def _():
        if parts == "ffn":
            d_resid, stores = ffn_part(row, r, ffn_loads(row, section, r))
            r.resid_v[:, :D] = d_resid
            stores.append(r.copies.start(r.resid_v.at[:, pl.ds(0, D)], r.d_resid))
        elif parts == "att":
            load = r.copies.start(r.d_resid, r.d_resid_v)
            loads = att_loads(row, r)
            load.wait()
            stores = att_part(row, section, r, loads, r.d_resid_v[...])
        else:
            loads = ffn_loads(row, section, r)
            later = att_loads(row, r)
            d_resid, stores = ffn_part(row, r, loads)
            stores = stores + att_part(row, section, r, later, d_resid)
        wait_all(stores)


def backward(row, section, parts, ctl, ins, held):
    outs, scratch, flops, traffic = {}, {}, 0, 0
    if parts == "ffn":
        outs.update(d_resid=shape((L, D), f32))
    if parts != "att":
        outs.update(
            ffn_own=shape((5, ROWS, L, HALF)), ffn_other=shape((5, ROWS, L, HALF)), ffn_vec=shape((ROWS, VECTOR_ROWS, D), f32)
        )
        scratch.update(
            grad_v=shape((L, D)), resid_v=shape((L, 2 * D), f32), gains_v=shape((2, D)), slope_v=shape((L, FF)),
            wu=shape((D, FF)), wd=shape((FF, D)), ffn_v=shape((L, FF + D)), ffn_vec_v=shape((VECTOR_ROWS, D), f32),
        )
        flops, traffic = flops + 1300000000, traffic + 12000000
    if parts == "att":
        scratch.update(d_resid_v=shape((L, D), f32))
    if parts != "ffn":
        if section == 1:
            outs.update(sent=shape((L, D)))
        outs.update(
            att_own=shape((6, ROWS, L, HALF)), att_other=shape((6, ROWS, L, HALF)), att_vec=shape((ROWS, VECTOR_ROWS, D), f32),
            d_start=shape((ROWS, L, D)), d_rel=shape((2 * L, 2 * D), f32), d_rel_low=shape((2 * L, 2 * D)),
            input_grad=shape((ROWS, L, D)),
        )
        scratch.update(
            wi=shape((D, 3 * D)), wo=shape((D, D)), keep_v=shape((L, K_GP)), rel_v=shape((2 * L, 2 * D)),
            att_v=shape((L, 4 * D)), att_vec_v=shape((VECTOR_ROWS, D), f32), start_v=shape((L, D)), grad_out_v=shape((L, D)),
            d_rel_v=shape((2 * L, 2 * D), f32), d_rel_old=shape((2 * L, 2 * D), f32), rel_low=shape((2 * L, 2 * D)),
        )
        flops, traffic = flops + 1100000000, traffic + 8000000
    return run(partial(backward_body, row, section, parts), ctl, ins, outs, held, scratch, 48, flops, traffic)


def tables_body(r):
    loads = [
        r.copies.start(source, target)
        for source, target in (
            (r.d_start, r.start_v), (r.ffn_vec, r.ffn_vec_v), (r.att_vec, r.att_vec_v), (r.d_rel_low, r.d_rel_v),
            (r.w_in.at[:, pl.ds(0, 2 * D)], r.wi),
        )
    ]
    core, stores = r.ctl[1], []

    def put(first, rows, value):
        at = slice(first, first + rows)
        low, high = value[:, :HALF].astype(bf16), value[:, HALF:].astype(bf16)
        r.own_v[at] = jnp.where(core == 0, low, high)
        r.other_v[at] = jnp.where(core == 0, high, low)

    loads[0].wait()
    dims = (ABS_ROWS, L)
    place = lax.broadcasted_iota(jnp.int32, dims, 0) - lax.broadcasted_iota(jnp.int32, dims, 1)
    spots = [indicator(place == r.ctl[2 + row]) for row in range(ROWS)]
    put(REL_ROWS, ABS_ROWS, nn(spots[0], r.start_v[0]) + nn(spots[1], r.start_v[1]))
    wait_all(loads[1:3])
    put(TABLE_ROWS, VECTOR_ROWS, r.ffn_vec_v[0] + r.ffn_vec_v[1] + r.att_vec_v[0] + r.att_vec_v[1])
    rest = TAIL_ROWS - TABLE_ROWS - VECTOR_ROWS
    put(TABLE_ROWS + VECTOR_ROWS, rest, jnp.zeros((rest, D), f32))
    wait_all(loads[3:])
    rows = nt(r.d_rel_v[...], r.wi[...]).astype(bf16)
    dims = (REL_ROWS, 2 * L)
    select = lax.broadcasted_iota(jnp.int32, dims, 0) + lax.broadcasted_iota(jnp.int32, dims, 1) == L + SPAN - REL_FROM
    put(0, REL_ROWS, nn(indicator(select), rows))
    stores = [r.copies.start(r.own_v, r.own), r.copies.start(r.other_v, r.other)]
    wait_all(stores)


def tables(ctl, **ins):
    outs = dict(own=shape((TAIL_ROWS, HALF)), other=shape((TAIL_ROWS, HALF)))
    scratch = dict(
        start_v=shape((ROWS, L, D)), ffn_vec_v=shape((ROWS, VECTOR_ROWS, D), f32), att_vec_v=shape((ROWS, VECTOR_ROWS, D), f32),
        d_rel_v=shape((2 * L, 2 * D)), wi=shape((D, 2 * D)), own_v=shape((TAIL_ROWS, HALF)), other_v=shape((TAIL_ROWS, HALF)),
    )
    result = run(tables_body, ctl, ins, outs, {}, scratch, 8, 1000000000, 7000000)
    return result["own"], result["other"]


class Halves:
    def __init__(self, r, first_piece):
        self.r, self.first_piece, self.pending = r, first_piece, []

    def store(self, unit, source):
        piece, half, part = unit // 8, unit % 8 // 4, unit % 4
        rows = pl.ds(part * UNIT, UNIT)
        kept = self.r.copies.make(source, getattr(self.r, f"kept{piece}").at[rows])
        sent = pltpu.make_async_copy(source, getattr(self.r, f"sent{piece}").at[rows], self.r.copies.sems.at[self.r.copies.used - 1])
        mine = self.r.ctl[4 + self.first_piece + piece] == half

        @pl.when(mine)
        def _():
            kept.start()

        @pl.when(jnp.logical_not(mine))
        def _():
            sent.start()

        self.pending.append(kept)


def both_cores(r, block_rows, acts_at):
    own = tn(r.acts_v[:, acts_at], r.rows_v[block_rows].reshape(2 * L, HALF))
    return own + tn(r.acts_sent_v[:, acts_at], r.rows_sent_v[block_rows].reshape(2 * L, HALF))


def ffn_weights_body(r):
    start_copy = r.copies.start
    width = FF + D
    loads = [start_copy(r.rows, r.rows_v), start_copy(r.rows_sent, r.rows_sent_v)]
    for at, size in ((0, D), (D, FF)):
        for row in range(ROWS):
            for source, target in ((r.acts, r.acts_v), (r.acts_sent, r.acts_sent_v)):
                loads.append(
                    start_copy(source.at[row, :, pl.ds(A_HID + at, size)], target.at[pl.ds(row * L, L), pl.ds(at, size)])
                )
    halves = Halves(r, 0)
    wait_all(loads[:6])
    for block in range(8):
        if block == 4:
            wait_all(loads[6:])
        acts_at = block_at(0) if block < 4 else block_at(block - 3)
        r.out_v[block] = both_cores(r, min(block, 4), acts_at).astype(bf16)
        for part in range(3):
            halves.store(3 * block + part, r.out_v.at[block, pl.ds(part * UNIT, UNIT)])
    wait_all(halves.pending)


def half_outputs(pieces):
    return {f"{kind}{piece}": shape((PIECE // 2, HALF)) for piece in range(pieces) for kind in ("kept", "sent")}


def ffn_weights(ctl, **ins):
    scratch = dict(
        rows_v=shape((5, ROWS, L, HALF)), rows_sent_v=shape((5, ROWS, L, HALF)),
        acts_v=shape((ROWS * L, FF + D)), acts_sent_v=shape((ROWS * L, FF + D)), out_v=shape((8, D, HALF)),
    )
    return run(ffn_weights_body, ctl, ins, half_outputs(3), {}, scratch, 40, 8 * 2 * 512 * 768 * 384, 13000000)


def att_weights_body(r):
    start_copy = r.copies.start
    loads = [start_copy(r.rows, r.rows_v), start_copy(r.rows_sent, r.rows_sent_v), start_copy(r.table, r.table_v)]
    for row in range(ROWS):
        for source, target in ((r.acts, r.acts_v), (r.acts_sent, r.acts_sent_v)):
            loads.append(start_copy(source.at[row, :, pl.ds(0, A_HID)], target.at[pl.ds(row * L, L)]))
    tail_loads = [start_copy(r.tail, r.tail_v), start_copy(r.tail_sent, r.tail_sent_v)]
    halves = Halves(r, 3)
    wait_all(loads)
    for block in range(4):
        total = both_cores(r, block, block_at((block + 1) // 2))
        if block < 2:
            far = r.rows_v[4 + block].astype(f32) + r.rows_sent_v[4 + block].astype(f32)
            total = total + tn(r.table_v[...], far.reshape(2 * L, HALF).astype(bf16))
        r.out_v[block] = total.astype(bf16)
        for part in range(3):
            halves.store(3 * block + part, r.out_v.at[block, pl.ds(part * UNIT, UNIT)])
    wait_all(tail_loads)
    r.tail_v[...] = r.tail_v[...] + r.tail_sent_v[...]
    for part in range(TAIL_ROWS // UNIT):
        halves.store(12 + part, r.tail_v.at[pl.ds(part * UNIT, UNIT)])
    wait_all(halves.pending)


def att_weights(ctl, **ins):
    scratch = dict(
        rows_v=shape((6, ROWS, L, HALF)), rows_sent_v=shape((6, ROWS, L, HALF)), table_v=shape((2 * L, D)),
        acts_v=shape((ROWS * L, A_HID)), acts_sent_v=shape((ROWS * L, A_HID)), out_v=shape((4, D, HALF)),
        tail_v=shape((TAIL_ROWS, HALF)), tail_sent_v=shape((TAIL_ROWS, HALF)),
    )
    return run(att_weights_body, ctl, ins, half_outputs(2), {}, scratch, 32, 5 * 2 * 512 * 768 * 384, 10000000)


def ffn_targets(r, unit):
    block, rows = unit // 3, pl.ds(unit % 3 * UNIT, UNIT)
    if block < 4:
        return [(pl.ds(0, UNIT), r.g_up.at[rows, pl.ds(block * D, D)])]
    return [(pl.ds(0, UNIT), r.g_down.at[pl.ds((block - 4) * D + unit % 3 * UNIT, UNIT)])]


def att_targets(r, unit):
    block, rows, every = unit // 3, pl.ds(unit % 3 * UNIT, UNIT), pl.ds(0, UNIT)
    if block < 3:
        return [(every, r.g_in.at[rows, pl.ds(block * D, D)])]
    if block == 3:
        return [(every, r.g_out.at[rows])]
    if unit == 12:
        return [(every, r.g_rel.at[pl.ds(REL_FROM, UNIT)])]
    if unit == 13:
        return [(pl.ds(0, L), r.g_rel.at[pl.ds(REL_FROM + UNIT, L)]), (pl.ds(L, L), r.g_abs.at[pl.ds(0, L)])]
    if unit == 14:
        return [(every, r.g_abs.at[pl.ds(L, UNIT)])]
    return [(pl.ds(0, L), r.g_abs.at[pl.ds(L + UNIT, L)])]


def assemble_body(first_piece, pieces, kept, targets, r):
    start_copy = r.copies.start
    core = r.ctl[1]
    loads = []
    for piece in range(pieces):
        for part in range(4):
            at = 4 * piece + part
            rows = pl.ds(part * UNIT, UNIT)
            loads.append([
                start_copy(array.at[rows], r.low.at[at, :, pl.ds(pl.multiple_of(column * HALF, 128), HALF)])
                for array, column in ((getattr(r, f"own{piece}"), core), (getattr(r, f"sent{piece}"), 1 - core))
            ])
    blank = None
    if first_piece > 0 and kept:
        r.blank[...] = jnp.zeros_like(r.blank)
        blank = start_copy(r.blank, r.g_rel.at[pl.ds(0, REL_FROM)])
    stores = []
    for piece in range(pieces):
        side_bit = r.ctl[4 + first_piece + piece]
        for part in range(4):
            at = 4 * piece + part
            wait_all(loads[at])
            r.wide[at] = r.low[at].astype(f32)
            first_copy = r.copies.used
            for half in range(2):
                r.copies.used = first_copy
                copies = [
                    r.copies.make(r.wide.at[at, rows], target) for rows, target in targets(r, 8 * piece + 4 * half + part)
                ]
                stores.append((side_bit == (half if kept else 1 - half), copies))
            r.copies.used = first_copy + 2
            for mine, copies in stores[-2:]:

                @pl.when(mine)
                def _():
                    for copy in copies:
                        copy.start()

    if first_piece > 0:
        @pl.when(r.ctl[4 + PIECES - 1] == (1 if kept else 0))
        def _():
            vectors = r.wide[4 * pieces - 1, L : L + VECTOR_ROWS, :]
            for part in range(3):
                r.b_in_v[:, block_at(part)] = vectors[part : part + 1]
            for part in range(4):
                r.b_up_v[:, block_at(part)] = vectors[3 + part : 4 + part]
            r.gains_v[...] = vectors[7:9]
            r.biases_v[...] = vectors[9:13]
            wait_all([
                start_copy(r.b_in_v, r.g_b_in), start_copy(r.b_up_v, r.g_b_up),
                start_copy(r.gains_v, r.g_gains), start_copy(r.biases_v, r.g_biases),
            ])

    if blank is not None:
        blank.wait()
    for mine, copies in stores:

        @pl.when(mine)
        def _():
            wait_all(copies)


def assemble(first_piece, pieces, kept, targets, ctl, own, sent, shapes, held):
    ins = {f"own{i}": value for i, value in enumerate(own)}
    ins.update({f"sent{i}": value for i, value in enumerate(sent)})
    outs = {name: shape(dims, f32) for name, dims in shapes.items()}
    scratch = dict(low=shape((4 * pieces, UNIT, D)), wide=shape((4 * pieces, UNIT, D), f32))
    if first_piece > 0:
        scratch.update(
            blank=shape((REL_FROM, D), f32), b_in_v=shape((1, 3 * D), f32), b_up_v=shape((1, FF), f32),
            gains_v=shape((2, D), f32), biases_v=shape((4, D), f32),
        )
    body = partial(assemble_body, first_piece, pieces, kept, targets)
    return run(body, ctl, ins, outs, held, scratch, 16 * pieces + 8, 0, pieces * 4800000)


FFN_SHAPES = dict(g_up=(D, FF), g_down=(FF, D))
ATT_SHAPES = dict(
    g_in=(D, 3 * D), g_out=(D, D), g_rel=(2 * SPAN, D), g_abs=(ABS_ROWS, D),
    g_b_in=(1, 3 * D), g_b_up=(1, FF), g_gains=(2, D), g_biases=(4, D),
)


SQUARE = ((0, 0), (1, 0), (1, 1), (0, 1))
ROTATION = ("x0", "z0", "x1", "z1", "y")


def dp_place(index):
    return {"core": index % 2, "x": index // 2 % 4, "y": index // 8 % 2, "z": index // 16}


def dp_index(place):
    return ((place["z"] * 2 + place["y"]) * 4 + place["x"]) * 2 + place["core"]


def partner(index, dim):
    place = dp_place(index)
    if len(dim) == 2:
        bits = list(SQUARE[place[dim[0]]])
        bits[int(dim[1])] ^= 1
        place[dim[0]] = SQUARE.index(tuple(bits))
    else:
        place[dim] ^= 1
    return dp_index(place)


def swap(value, dim):
    peers = lax.axis_size("dp")
    return lax.ppermute(value, "dp", [(i, partner(i, dim)) for i in range(peers)])


def side(dim):
    place = dp_place(lax.axis_index("dp"))
    if len(dim) == 1 or dim == "core":
        return place[dim].astype(jnp.int32)
    at = place[dim[0]]
    if dim[1] == "0":
        return ((at == 1) | (at == 2)).astype(jnp.int32)
    return (at >= 2).astype(jnp.int32)


def order_of(piece):
    return [ROTATION[(piece + step) % len(ROTATION)] for step in range(len(ROTATION))]


ORDERS = [order_of(piece) for piece in range(PIECES)]


SPLIT_STEPS = 3


def summed_chunk(kept, sent, order):
    chunk = kept + swap(sent, order[0])
    for dim in order[1:SPLIT_STEPS]:
        at, half = side(dim), chunk.shape[0] // 2
        received = swap(lax.dynamic_slice_in_dim(chunk, (1 - at) * half, half, 0), dim)
        chunk = lax.dynamic_slice_in_dim(chunk, at * half, half, 0) + received
    for dim in order[SPLIT_STEPS:]:
        chunk = chunk + swap(chunk, dim)
    return chunk


def in_order(at, own, other):
    return jnp.where(
        at == 0,
        jnp.concatenate([own, other], axis=0),
        jnp.concatenate([other, own], axis=0),
    )


def gathered_half(chunk, order):
    for dim in reversed(order[1:SPLIT_STEPS]):
        chunk = in_order(side(dim), chunk, swap(chunk, dim))
    return chunk


def add_tables_of_both_sections(chunk, order):
    first_row, span = 0, PIECE
    for dim in order[:SPLIT_STEPS]:
        span //= 2
        first_row = first_row + side(dim) * span
    row_at = first_row + lax.broadcasted_iota(jnp.int32, chunk.shape, 0) - (PIECE - TAIL_ROWS)
    is_table = (row_at >= 0) & (row_at < TABLE_ROWS)
    elsewhere = lax.ppermute(chunk, "section", [(0, 1), (1, 0)])
    return jnp.where(is_table, chunk + elsewhere, chunk)


def per_device(
    hidden_in,
    cotangent,
    segment_ids,
    positions,
    w_in,
    b_in,
    w_out,
    w_up,
    b_up,
    w_down,
    gains,
    biases,
    rel_table,
    abs_table,
):
    section = lax.axis_index("section").astype(jnp.int32)
    firsts = jnp.where(section == 1, positions[:, 0], 8 * ABS_ROWS)
    ctl = jnp.stack([section, side("core"), firsts[0], firsts[1], *[side(order[0]) for order in ORDERS]])
    weights = dict(w_in=w_in[0], w_out=w_out[0], w_up=w_up[0], w_down=w_down[0], gains=gains[0])
    common = dict(
        weights, hidden_in=hidden_in, segment_ids=segment_ids, biases=biases[0], b_in=b_in, b_up=b_up, abs_table=abs_table
    )

    out = forward(0, 0, ctl, dict(common, rel_table=rel_table), {})
    rel, rel_rows = out["rel"], out["rel_rows"]
    common["rel"] = rel
    received = []
    for row in range(ROWS):
        if row > 0:
            out = forward(row, 0, ctl, common, out)
        received.append(lax.ppermute(out["sent"], "section", [(0, 1)]))
    for row in range(ROWS):
        out = forward(row, 1, ctl, dict(common, received=received[row]), out)
    acts, keep, resid, section_out = out["acts"], out["keep"], out["resid"], out["section_out"]
    acts_sent = swap(acts, "core")

    common = dict(weights, cotangent=cotangent, keep=keep, resid=resid, rel=rel)
    out, received = {}, []
    for row in range(ROWS):
        out = backward(row, 1, "both", ctl, common, out)
        received.append(lax.ppermute(out["sent"], "section", [(1, 0)]))
    out = backward(0, 0, "both", ctl, dict(common, received=received[0]), out)
    ffn = backward(1, 0, "ffn", ctl, dict(common, received=received[1]), out)
    ffn_pieces = ffn_weights(
        ctl, acts=acts, acts_sent=acts_sent, rows=ffn["ffn_own"], rows_sent=swap(ffn["ffn_other"], "core")
    )
    d_resid, ffn_pieces = lax.optimization_barrier((ffn["d_resid"], ffn_pieces))
    out = backward(1, 0, "att", ctl, dict(common, d_resid=d_resid), out)
    tail, tail_other = tables(
        ctl, d_start=out["d_start"], ffn_vec=ffn["ffn_vec"], att_vec=out["att_vec"], d_rel_low=out["d_rel_low"], w_in=weights["w_in"]
    )
    att_pieces = att_weights(
        ctl, acts=acts, acts_sent=acts_sent, rows=out["att_own"], rows_sent=swap(out["att_other"], "core"),
        table=rel_rows, tail=tail, tail_sent=swap(tail_other, "core"),
    )

    halves = [(ffn_pieces[f"kept{i}"], ffn_pieces[f"sent{i}"]) for i in range(3)]
    halves += [(att_pieces[f"kept{i}"], att_pieces[f"sent{i}"]) for i in range(2)]
    chunks = [summed_chunk(kept, sent, order) for (kept, sent), order in zip(halves, ORDERS)]
    chunks[-1] = add_tables_of_both_sections(chunks[-1], ORDERS[-1])
    mine = [gathered_half(chunk, order) for chunk, order in zip(chunks, ORDERS)]
    partners = [swap(half, order[0]) for half, order in zip(mine, ORDERS)]
    both = [(half, swap(half, "core")) for half in mine]
    other = [(half, swap(half, "core")) for half in partners]
    ffn, att = {}, {}
    for kept, pairs in ((True, both), (False, other)):
        own, sent = zip(*pairs)
        ffn = assemble(0, 3, kept, ffn_targets, ctl, own[:3], sent[:3], FFN_SHAPES, ffn)
        att = assemble(3, 2, kept, att_targets, ctl, own[3:], sent[3:], ATT_SHAPES, att)
    return (
        section_out[None],
        out["input_grad"][None],
        att["g_in"][None],
        att["g_b_in"],
        att["g_out"][None],
        ffn["g_up"][None],
        att["g_b_up"],
        ffn["g_down"][None],
        att["g_gains"][None],
        att["g_biases"][None],
        att["g_rel"],
        att["g_abs"],
    )


def solution(mesh):
    in_specs = (
        P("dp", None, None),
        P("dp", None, None),
        P("dp", None),
        P("dp", None),
        P("section", None, None),
        P("section", None),
        P("section", None, None),
        P("section", None, None),
        P("section", None),
        P("section", None, None),
        P("section", None, None),
        P("section", None, None),
        P(),
        P(),
    )
    out_specs = (
        P("section", "dp", None, None),
        P("section", "dp", None, None),
        P("section", None, None),
        P("section", None),
        P("section", None, None),
        P("section", None, None),
        P("section", None),
        P("section", None, None),
        P("section", None, None),
        P("section", None, None),
        P(),
        P(),
    )
    return jax.shard_map(
        per_device, mesh=mesh, in_specs=in_specs, out_specs=out_specs, check_vma=False
    )
```

```python
from functools import partial
import math
from types import SimpleNamespace

import jax
import jax.numpy as jnp
from jax import lax
from jax.experimental import pallas as pl
from jax.experimental.pallas import tpu as pltpu
from jax.sharding import PartitionSpec as P

HEADS = 12
L = 128
D = 768
FF = 3072
HALF = D // 2
PAIRS = HEADS // 2
ROWS = 2
SPAN = 256
EPS = 1e-06
NEG = -1e30
SCALE = 1.0 / math.sqrt(3 * 64)
f32, bf16 = jnp.float32, jnp.bfloat16

A_START, A_X, A_CTX, A_HID, A_ACT, A_ALL = 0, 768, 1536, 2304, 3072, 6144
K_P, K_GP, K_ALL = 2304, 3840, 6912
VECTOR_ROWS = 16
REL_FROM, REL_ROWS, ABS_ROWS, TAIL_ROWS = 128, 272, 512, 896
TABLE_ROWS = REL_ROWS + ABS_ROWS
FFN_LAYOUT = [("g_up", D, 0, block) for block in range(4)]
FFN_LAYOUT += [("g_down", D, block * D, 0) for block in range(4)] + [("g_out", D, 0, 0)]
ATT_LAYOUT = [("g_in", D, 0, block) for block in range(3)]
ATT_LAYOUT += [("g_rel", REL_ROWS, REL_FROM, 0), ("g_abs", ABS_ROWS, 0, 0), ("vectors", VECTOR_ROWS, 0, 0)]
ATT_LAYOUT += [("", TAIL_ROWS - TABLE_ROWS - VECTOR_ROWS, 0, 0)]
FFN_PIECES, ATT_PIECES = 3, 2
FFN_BLOCKS, ATT_BLOCKS = 6, 5
ATT_ROWS = ATT_BLOCKS * ROWS * L + TAIL_ROWS

ANY = pl.BlockSpec(memory_space=pl.ANY)
SMEM = pl.BlockSpec(memory_space=pltpu.SMEM)


def nn(a, b):
    return lax.dot_general(a, b, (((1,), (0,)), ((), ())), preferred_element_type=f32)


def nt(a, b):
    return lax.dot_general(a, b, (((1,), (1,)), ((), ())), preferred_element_type=f32)


def tn(a, b):
    return lax.dot_general(a, b, (((0,), (0,)), ((), ())), preferred_element_type=f32)


def norm_parts(value):
    centered = value - jnp.mean(value, axis=1, keepdims=True)
    rstd = lax.rsqrt(jnp.mean(centered * centered, axis=1, keepdims=True) + EPS)
    return centered * rstd, rstd


def norm_backward(normed, rstd, gain, grad):
    scaled = grad * gain
    mean_one = jnp.mean(scaled, axis=1, keepdims=True)
    mean_two = jnp.mean(scaled * normed, axis=1, keepdims=True)
    return (scaled - mean_one - normed * mean_two) * rstd


def column_sums(value):
    return jnp.sum(value, axis=0, keepdims=True)


def indicator(condition):
    return condition.astype(f32).astype(bf16)


def lane_halves():
    lane = lax.broadcasted_iota(jnp.int32, (1, L), 1)
    return indicator(lane < 64), indicator(lane >= 64)


def stacked(value, halves):
    return jnp.concatenate([value * halves[0], value * halves[1]], axis=0)


def skew(table):
    return pltpu.roll(table, L, 1, stride=1, stride_axis=0)[:, :L]


def unskew(turned):
    wide = jnp.concatenate([turned, jnp.zeros_like(turned)], axis=1)
    return pltpu.roll(wide, 1, 1, stride=1, stride_axis=0)


def pair_at(pair, base=0):
    return slice(base + pair * L, base + pair * L + L)


def block_at(block, base=0):
    return slice(base + block * D, base + block * D + D)


def shape(dims, dtype=bf16):
    return jax.ShapeDtypeStruct(dims, dtype)


class Copies:
    def __init__(self, sems):
        self.sems, self.used = sems, 0

    def make(self, source, target):
        self.used += 1
        return pltpu.make_async_copy(source, target, self.sems.at[self.used - 1])

    def start(self, source, target):
        copy = self.make(source, target)
        copy.start()
        return copy


def wait_all(copies):
    for copy in copies:
        copy.wait()


def run(body, ctl, ins, outs, held, scratch, copies, flops, traffic, room=12):
    names, out_names, scratch_names = list(ins), list(outs), list(scratch)
    kept = [name for name in out_names if name in held and name != "sent"]

    def kernel(*refs):
        ctl_ref, refs = refs[0], refs[1:]
        r = SimpleNamespace(ctl=ctl_ref, **dict(zip(names, refs)))
        refs = refs[len(names) + len(kept) :]
        for name, ref in zip(out_names + scratch_names, refs):
            setattr(r, name, ref)
        r.copies = Copies(refs[-1])
        body(r)

    size = sum(math.prod(s.shape) * s.dtype.itemsize for s in scratch.values()) + room * 2**20
    results = pl.pallas_call(
        kernel,
        out_shape=tuple(outs.values()),
        in_specs=[SMEM] + [ANY] * (len(names) + len(kept)),
        out_specs=(ANY,) * len(out_names),
        input_output_aliases={1 + len(names) + i: out_names.index(name) for i, name in enumerate(kept)},
        scratch_shapes=[pltpu.VMEM(s.shape, s.dtype) for s in scratch.values()] + [pltpu.SemaphoreType.DMA((copies,))],
        compiler_params=pltpu.CompilerParams(vmem_limit_bytes=size),
        cost_estimate=pl.CostEstimate(flops=flops, bytes_accessed=traffic, transcendentals=0),
    )(ctl, *ins.values(), *[held[name] for name in kept])
    return dict(zip(out_names, results))


def relative_part(r):
    loads = [r.copies.start(r.rel_table, r.table_v), r.copies.start(r.b_in, r.b_in_v), r.copies.start(r.w_in, r.wi)]
    dims = (2 * L, 2 * SPAN)
    select = indicator(lax.broadcasted_iota(jnp.int32, dims, 0) + lax.broadcasted_iota(jnp.int32, dims, 1) == L + SPAN)
    loads[0].wait()
    rows = nn(select, r.table_v[...]).astype(bf16)
    r.rel_rows_v[...] = rows
    loads[1].wait()
    loads[2].wait()
    r.rel_v[...] = (nn(rows, r.wi[:, : 2 * D]) + r.b_in_v[:, : 2 * D].astype(f32)).astype(bf16)
    return [r.copies.start(r.rel_rows_v, r.rel_rows), r.copies.start(r.rel_v, r.rel)]


def forward_body(row, section, first, r):
    start_copy = r.copies.start
    stores = relative_part(r) if first else []

    @pl.when(r.ctl[0] == section)
    def _():
        x_load = start_copy(r.hidden_in.at[row] if section == 0 else r.received, r.x_v)
        small = [start_copy(r.segment_ids, r.seg_v), start_copy(r.gains, r.gains_v), start_copy(r.biases, r.biases_v)]
        abs_load = start_copy(r.abs_table, r.table_v) if section == 1 else None
        in_loads = [] if first else [start_copy(r.b_in, r.b_in_v), start_copy(r.w_in, r.wi)]
        rel_load = None if first else start_copy(r.rel, r.rel_v)
        loads = [start_copy(r.w_out, r.wo), start_copy(r.b_up, r.b_up_v), start_copy(r.w_up, r.wu), start_copy(r.w_down, r.wd)]
        halves = lane_halves()
        x_load.wait()
        x = r.x_v[...]
        start = x.astype(f32)
        if section == 1:
            abs_load.wait()
            dims = (L, ABS_ROWS)
            place = lax.broadcasted_iota(jnp.int32, dims, 1) - lax.broadcasted_iota(jnp.int32, dims, 0)
            start = start + nn(indicator(place == r.ctl[2 + row]), r.table_v[...])
        query_in = start.astype(bf16)
        r.acts_v[:, block_at(0)] = query_in
        r.acts_v[:, block_at(1)] = x
        wait_all(in_loads)
        b_in = r.b_in_v[...].astype(f32)
        r.keep_v[:, :D] = (nn(query_in, r.wi[:, :D]) + b_in[:, :D]).astype(bf16)
        r.keep_v[:, D : 3 * D] = (nn(x, r.wi[:, D:]) + b_in[:, D:]).astype(bf16)
        wait_all(small)
        if rel_load is not None:
            rel_load.wait()
        seg_rows = jnp.broadcast_to(r.seg_v[row : row + 1, :], (L, L)).astype(f32)
        same = seg_rows == seg_rows.T
        for pair in range(PAIRS):
            query = r.keep_v[:, pair_at(pair)]
            key = r.keep_v[:, pair_at(pair, D)]
            value = r.keep_v[:, pair_at(pair, 2 * D)]
            query_two, key_two = stacked(query, halves), stacked(key, halves)
            content = nt(query_two, key)
            far_query = nt(query_two, r.rel_v[:, pair_at(pair, D)])
            far_key = nt(key_two, r.rel_v[:, pair_at(pair)])
            probs = []
            for head in range(2):
                rows = slice(head * L, head * L + L)
                summed = content[rows] + skew(far_query[rows]) + skew(far_key[rows]).T
                scores = jnp.where(same, summed * SCALE, NEG)
                exponent = jnp.exp(scores - jnp.max(scores, axis=1, keepdims=True))
                total = jnp.sum(exponent, axis=1, keepdims=True)
                probs.append((exponent * (1.0 / total)).astype(bf16))
            probs = jnp.concatenate(probs, axis=1)
            r.keep_v[:, K_P + 2 * pair * L : K_P + 2 * (pair + 1) * L] = probs
            r.acts_v[:, pair_at(pair, A_CTX)] = nn(probs, stacked(value, halves)).astype(bf16)
        loads[0].wait()
        gain = r.gains_v[...].astype(f32)
        shift = r.biases_v[...].astype(f32)
        resid_one = start + nn(r.acts_v[:, A_CTX : A_CTX + D], r.wo[...]) + shift[0:1]
        r.resid_v[:, :D] = resid_one
        hidden = norm_parts(resid_one)[0] * gain[0:1] + shift[1:2]
        hidden_low = hidden.astype(bf16)
        r.acts_v[:, A_HID : A_HID + D] = hidden_low
        early = [
            start_copy(r.acts_v.at[:, pl.ds(0, A_ACT)], r.acts.at[row, :, pl.ds(0, A_ACT)]),
            start_copy(r.keep_v.at[:, pl.ds(0, K_GP)], r.keep.at[row, :, pl.ds(0, K_GP)]),
        ]
        wait_all(loads[1:])
        total = hidden + shift[2:3]
        for part in range(4):
            gate = nn(hidden_low, r.wu[:, block_at(part)]) + r.b_up_v[:, block_at(part)].astype(f32)
            below = 0.5 + 0.5 * lax.erf(gate * (1.0 / math.sqrt(2.0)))
            density = jnp.exp(gate * gate * -0.5) * (1.0 / math.sqrt(2.0 * math.pi))
            active = (gate * below).astype(bf16)
            r.acts_v[:, block_at(part, A_ACT)] = active
            r.keep_v[:, block_at(part, K_GP)] = (below + gate * density).astype(bf16)
            total = total + nn(active, r.wd[block_at(part), :])
        r.resid_v[:, D:] = total
        late = [
            start_copy(r.acts_v.at[:, pl.ds(A_ACT, FF)], r.acts.at[row, :, pl.ds(A_ACT, FF)]),
            start_copy(r.keep_v.at[:, pl.ds(K_GP, FF)], r.keep.at[row, :, pl.ds(K_GP, FF)]),
            start_copy(r.resid_v, r.resid.at[row]),
        ]
        r.x_v[...] = (norm_parts(total)[0] * gain[1:2] + shift[3:4]).astype(bf16)
        late.append(start_copy(r.x_v, r.section_out.at[row]))
        if section == 0:
            late.append(start_copy(r.x_v, r.sent))
        wait_all(early + late)

    wait_all(stores)


def forward(row, section, ctl, ins, held):
    first = not held
    outs = {"sent": shape((L, D))} if section == 0 else {}
    if first:
        outs.update(rel_rows=shape((2 * L, D)), rel=shape((2 * L, 2 * D)))
    outs.update(
        acts=shape((ROWS, L, A_ALL)),
        keep=shape((ROWS, L, K_ALL)),
        resid=shape((ROWS, L, 2 * D), f32),
        section_out=shape((ROWS, L, D)),
    )
    scratch = dict(
        x_v=shape((L, D)), seg_v=shape((ROWS, L), jnp.int32), gains_v=shape((2, D)), biases_v=shape((4, D)),
        b_in_v=shape((1, 3 * D)), b_up_v=shape((1, FF)), table_v=shape((2 * SPAN, D)), rel_v=shape((2 * L, 2 * D)),
        wi=shape((D, 3 * D)), wo=shape((D, D)), wu=shape((D, FF)), wd=shape((FF, D)),
        acts_v=shape((L, A_ALL)), keep_v=shape((L, K_ALL)), resid_v=shape((L, 2 * D), f32),
    )
    if first:
        scratch.update(rel_rows_v=shape((2 * L, D)))
    return run(partial(forward_body, row, section, first), ctl, ins, outs, held, scratch, 24, 1900000000, 18000000)


def ffn_loads(row, section, r):
    return SimpleNamespace(
        grad=r.copies.start(r.cotangent.at[row] if section == 1 else r.received, r.grad_v),
        resid=r.copies.start(r.resid.at[row], r.resid_v),
        gains=r.copies.start(r.gains, r.gains_v),
        down=r.copies.start(r.w_down, r.wd),
        slope=r.copies.start(r.keep.at[row, :, pl.ds(K_GP, FF)], r.slope_v),
        up=r.copies.start(r.w_up, r.wu),
    )


def ffn_part(row, r, loads):
    wait_all([loads.grad, loads.resid, loads.gains])
    gain = r.gains_v[...].astype(f32)
    grad = r.grad_v[...].astype(f32)
    normed, rstd = norm_parts(r.resid_v[:, D:])
    r.ffn_vec_v[...] = jnp.zeros_like(r.ffn_vec_v)
    r.ffn_vec_v[8:9] = column_sums(grad * normed)
    r.ffn_vec_v[12:13] = column_sums(grad)
    d_two = norm_backward(normed, rstd, gain[1:2], grad)
    d_down = d_two.astype(bf16)
    r.ffn_v[:, FF : FF + D] = d_down
    r.ffn_vec_v[11:12] = column_sums(d_down.astype(f32))
    wait_all([loads.down, loads.slope, loads.up])
    d_hidden = d_two
    for part in range(4):
        d_gate = (nt(d_down, r.wd[block_at(part), :]) * r.slope_v[:, block_at(part)].astype(f32)).astype(bf16)
        r.ffn_v[:, block_at(part)] = d_gate
        r.ffn_vec_v[3 + part : 4 + part] = column_sums(d_gate.astype(f32))
        d_hidden = d_hidden + nt(d_gate, r.wu[:, block_at(part)])
    normed, rstd = norm_parts(r.resid_v[:, :D])
    r.ffn_vec_v[7:8] = column_sums(d_hidden * normed)
    r.ffn_vec_v[10:11] = column_sums(d_hidden)
    d_resid = norm_backward(normed, rstd, gain[0:1], d_hidden)
    d_att = d_resid.astype(bf16)
    r.ffn_v[:, FF + D :] = d_att
    r.ffn_vec_v[9:10] = column_sums(d_att.astype(f32))
    stores = store_blocks(row, r, r.ffn_v, r.ffn_own, r.ffn_other, FFN_BLOCKS)
    stores.append(r.copies.start(r.ffn_vec_v, r.ffn_vec.at[row]))
    return d_resid, stores


def store_blocks(row, r, source, own, other, blocks):
    core, stores = r.ctl[1], []
    for block in range(blocks):
        own_at = pl.multiple_of(block * D + core * HALF, 128)
        other_at = pl.multiple_of(block * D + (1 - core) * HALF, 128)
        rows = pl.ds((block * ROWS + row) * L, L)
        stores.append(r.copies.start(source.at[:, pl.ds(own_at, HALF)], own.at[rows]))
        stores.append(r.copies.start(source.at[:, pl.ds(other_at, HALF)], other.at[rows]))
    return stores


def att_loads(row, section, r):
    return SimpleNamespace(
        out=r.copies.start(r.w_out, r.wo),
        keep=r.copies.start(r.keep.at[row, :, pl.ds(0, K_GP)], r.keep_v),
        rel=r.copies.start(r.rel, r.rel_v),
        earlier=r.copies.start(r.d_rel, r.d_rel_old) if row > 0 else None,
        w_in=r.copies.start(r.w_in, r.wi),
        others=[
            r.copies.start(r.d_start.at[0], r.others_v),
            r.copies.start(r.att_vec.at[0], r.att_vec_old),
            r.copies.start(r.ffn_vec, r.ffn_vec_v),
        ]
        if row == ROWS - 1 and section == 0
        else [],
    )


def att_part(row, section, r, loads, d_resid):
    halves = lane_halves()
    row_at = lax.broadcasted_iota(jnp.int32, (L, L), 0)
    column_at = lax.broadcasted_iota(jnp.int32, (L, L), 1)
    turn = indicator(row_at + column_at == L - 1)
    d_att = d_resid.astype(bf16)
    r.att_vec_v[...] = jnp.zeros_like(r.att_vec_v)
    loads.out.wait()
    d_context = nt(d_att, r.wo[...]).astype(bf16)
    loads.keep.wait()
    loads.rel.wait()
    for pair in range(PAIRS):
        query = r.keep_v[:, pair_at(pair)]
        key = r.keep_v[:, pair_at(pair, D)]
        value = r.keep_v[:, pair_at(pair, 2 * D)]
        probs = r.keep_v[:, K_P + 2 * pair * L : K_P + 2 * (pair + 1) * L]
        probs_two = jnp.concatenate([probs[:, :L], probs[:, L:]], axis=0)
        rel_q, rel_k = r.rel_v[:, pair_at(pair)], r.rel_v[:, pair_at(pair, D)]
        context_two = stacked(d_context[:, pair_at(pair)], halves)
        probs_f = probs_two.astype(f32)
        weighted = nt(context_two, value) * probs_f
        d_scores = (weighted - probs_f * jnp.sum(weighted, axis=1, keepdims=True)).astype(bf16)
        query_two, key_two = stacked(query, halves), stacked(key, halves)
        d_value = tn(probs_two, context_two)
        d_key = tn(d_scores, query_two)
        d_side = jnp.concatenate([d_scores[:L], d_scores[L:]], axis=1)
        d_query = nn(d_side, key_two)
        d_far = (d_side.astype(f32) * SCALE).astype(bf16)
        query_turned = nn(turn, query).astype(bf16)
        key_turned = nn(turn, key).astype(bf16)
        rows_turned = nn(turn, d_far)
        far_query, far_key = [], []
        for head in range(2):
            columns = slice(head * L, head * L + L)
            far_query.append(unskew(rows_turned[:, columns]).astype(bf16))
            far_key.append(unskew(nt(turn, d_far[:, columns])).astype(bf16))
        d_query_turned = nn(jnp.concatenate(far_query, axis=1), stacked(rel_k, halves))
        d_key_turned = nn(jnp.concatenate(far_key, axis=1), stacked(rel_q, halves))
        r.d_rel_v[:, pair_at(pair)] = tn(jnp.concatenate(far_key, axis=0), stacked(key_turned, halves))
        r.d_rel_v[:, pair_at(pair, D)] = tn(jnp.concatenate(far_query, axis=0), stacked(query_turned, halves))
        d_query = d_query * SCALE + nn(turn, d_query_turned.astype(bf16))
        d_key = d_key * SCALE + nn(turn, d_key_turned.astype(bf16))
        r.att_v[:, pair_at(pair)] = d_query.astype(bf16)
        r.att_v[:, pair_at(pair, D)] = d_key.astype(bf16)
        r.att_v[:, pair_at(pair, 2 * D)] = d_value.astype(bf16)
    stores = store_blocks(row, r, r.att_v, r.att_own, r.att_other, 3)
    loads.w_in.wait()
    d_start = d_resid + nt(r.att_v[:, :D], r.wi[:, :D])
    r.start_v[...] = d_start.astype(bf16)
    stores.append(r.copies.start(r.start_v, r.d_start.at[row]))
    r.grad_out_v[...] = (d_start + nt(r.att_v[:, D : 3 * D], r.wi[:, D:])).astype(bf16)
    stores.append(r.copies.start(r.grad_out_v, r.input_grad.at[row]))
    if section == 1:
        stores.append(r.copies.start(r.grad_out_v, r.sent))
    for part in range(3):
        rows = column_sums(r.att_v[:, block_at(part)].astype(f32))
        if part < 2:
            rows = rows + column_sums(r.d_rel_v[:, block_at(part)])
        r.att_vec_v[part : part + 1] = rows
    stores.append(r.copies.start(r.att_vec_v, r.att_vec.at[row]))
    if row > 0:
        loads.earlier.wait()
        r.d_rel_v[...] = r.d_rel_v[...] + r.d_rel_old[...]
    if row < ROWS - 1:
        stores.append(r.copies.start(r.d_rel_v, r.d_rel))
        return stores
    r.rel_low[...] = r.d_rel_v[...].astype(bf16)
    core = r.ctl[1]
    for block in range(2):
        own_at = pl.multiple_of(block * D + core * HALF, 128)
        other_at = pl.multiple_of(block * D + (1 - core) * HALF, 128)
        rows = pl.ds((3 + block) * ROWS * L, ROWS * L)
        stores.append(r.copies.start(r.rel_low.at[:, pl.ds(own_at, HALF)], r.att_own.at[rows]))
        stores.append(r.copies.start(r.rel_low.at[:, pl.ds(other_at, HALF)], r.att_other.at[rows]))
    if section == 0:
        wait_all(loads.others)
        stores += tail_part(
            r, [r.others_v[...], r.start_v[...]], r.ffn_vec_v[0] + r.ffn_vec_v[1] + r.att_vec_old[...] + r.att_vec_v[...]
        )
    else:
        stores.append(r.copies.start(r.rel_low, r.d_rel_low))
    return stores


def tail_part(r, starts, vectors):
    core = r.ctl[1]

    def put(first, rows, value):
        at = slice(first, first + rows)
        low, high = value[:, :HALF].astype(bf16), value[:, HALF:].astype(bf16)
        r.tail_own_v[at] = jnp.where(core == 0, low, high)
        r.tail_other_v[at] = jnp.where(core == 0, high, low)

    dims = (ABS_ROWS, L)
    place = lax.broadcasted_iota(jnp.int32, dims, 0) - lax.broadcasted_iota(jnp.int32, dims, 1)
    spots = [indicator(place == r.ctl[2 + row]) for row in range(ROWS)]
    put(REL_ROWS, ABS_ROWS, nn(spots[0], starts[0]) + nn(spots[1], starts[1]))
    put(TABLE_ROWS, VECTOR_ROWS, vectors)
    rest = TAIL_ROWS - TABLE_ROWS - VECTOR_ROWS
    put(TABLE_ROWS + VECTOR_ROWS, rest, jnp.zeros((rest, D), f32))
    rows = nt(r.rel_low[...], r.wi[:, : 2 * D]).astype(bf16)
    dims = (REL_ROWS, 2 * L)
    select = lax.broadcasted_iota(jnp.int32, dims, 0) + lax.broadcasted_iota(jnp.int32, dims, 1) == L + SPAN - REL_FROM
    put(0, REL_ROWS, nn(indicator(select), rows))
    rows = pl.ds(ATT_BLOCKS * ROWS * L, TAIL_ROWS)
    return [r.copies.start(r.tail_own_v, r.att_own.at[rows]), r.copies.start(r.tail_other_v, r.att_other.at[rows])]


def backward_body(row, section, parts, r):
    @pl.when(r.ctl[0] == section)
    def _():
        if parts == "ffn":
            d_resid, stores = ffn_part(row, r, ffn_loads(row, section, r))
            r.resid_v[:, :D] = d_resid
            stores.append(r.copies.start(r.resid_v.at[:, pl.ds(0, D)], r.d_resid))
        elif parts == "att":
            load = r.copies.start(r.d_resid, r.d_resid_v)
            loads = att_loads(row, section, r)
            load.wait()
            stores = att_part(row, section, r, loads, r.d_resid_v[...])
        else:
            loads = ffn_loads(row, section, r)
            later = att_loads(row, section, r)
            d_resid, stores = ffn_part(row, r, loads)
            stores = stores + att_part(row, section, r, later, d_resid)
        wait_all(stores)


def backward(row, section, parts, ctl, ins, held):
    outs, scratch, flops, traffic = {}, {}, 0, 0
    if parts == "ffn":
        outs.update(d_resid=shape((L, D), f32))
    if parts != "att":
        outs.update(
            ffn_own=shape((FFN_BLOCKS * ROWS * L, HALF)), ffn_other=shape((FFN_BLOCKS * ROWS * L, HALF)), ffn_vec=shape((ROWS, VECTOR_ROWS, D), f32)
        )
        scratch.update(
            grad_v=shape((L, D)), resid_v=shape((L, 2 * D), f32), gains_v=shape((2, D)), slope_v=shape((L, FF)),
            wu=shape((D, FF)), wd=shape((FF, D)), ffn_v=shape((L, FF + 2 * D)), ffn_vec_v=shape((VECTOR_ROWS, D), f32),
        )
        flops, traffic = flops + 1300000000, traffic + 12000000
    if parts == "att":
        scratch.update(d_resid_v=shape((L, D), f32))
    if parts != "ffn":
        if section == 1:
            outs.update(sent=shape((L, D)))
        outs.update(
            att_own=shape((ATT_ROWS, HALF)), att_other=shape((ATT_ROWS, HALF)), att_vec=shape((ROWS, VECTOR_ROWS, D), f32),
            d_start=shape((ROWS, L, D)), d_rel=shape((2 * L, 2 * D), f32), d_rel_low=shape((2 * L, 2 * D)),
            input_grad=shape((ROWS, L, D)),
        )
        scratch.update(
            wi=shape((D, 3 * D)), wo=shape((D, D)), keep_v=shape((L, K_GP)), rel_v=shape((2 * L, 2 * D)),
            att_v=shape((L, 3 * D)), att_vec_v=shape((VECTOR_ROWS, D), f32), start_v=shape((L, D)), grad_out_v=shape((L, D)),
            d_rel_v=shape((2 * L, 2 * D), f32), d_rel_old=shape((2 * L, 2 * D), f32), rel_low=shape((2 * L, 2 * D)),
        )
        if row == ROWS - 1 and section == 0:
            scratch.update(
                tail_own_v=shape((TAIL_ROWS, HALF)), tail_other_v=shape((TAIL_ROWS, HALF)),
                others_v=shape((L, D)), att_vec_old=shape((VECTOR_ROWS, D), f32), ffn_vec_v=shape((ROWS, VECTOR_ROWS, D), f32),
            )
        flops, traffic = flops + 1100000000, traffic + 8000000
    return run(partial(backward_body, row, section, parts), ctl, ins, outs, held, scratch, 48, flops, traffic)


def tables_body(r):
    @pl.when(r.ctl[0] == 1)
    def _():
        loads = [
            r.copies.start(source, target)
            for source, target in (
                (r.d_start, r.start_v), (r.ffn_vec, r.ffn_vec_v), (r.att_vec, r.att_vec_v), (r.d_rel_low, r.rel_low), (r.w_in, r.wi)
            )
        ]
        wait_all(loads)
        vectors = r.ffn_vec_v[0] + r.ffn_vec_v[1] + r.att_vec_v[0] + r.att_vec_v[1]
        wait_all(tail_part(r, [r.start_v[0], r.start_v[1]], vectors))


def tables(ctl, w_in, held):
    ins = dict(w_in=w_in, **{name: held[name] for name in ("d_start", "ffn_vec", "att_vec", "d_rel_low")})
    outs = dict(att_own=shape((ATT_ROWS, HALF)), att_other=shape((ATT_ROWS, HALF)))
    scratch = dict(
        start_v=shape((ROWS, L, D)), ffn_vec_v=shape((ROWS, VECTOR_ROWS, D), f32), att_vec_v=shape((ROWS, VECTOR_ROWS, D), f32),
        rel_low=shape((2 * L, 2 * D)), wi=shape((D, 3 * D)), tail_own_v=shape((TAIL_ROWS, HALF)), tail_other_v=shape((TAIL_ROWS, HALF)),
    )
    return run(tables_body, ctl, ins, outs, held, scratch, 8, 1000000000, 7000000)


def layout_rows(layout):
    return sum(rows for _, rows, _, _ in layout)


def segments(layout, pieces):
    half_rows = layout_rows(layout) // pieces // 2
    found, at = [], 0
    for target, rows, first, block in layout:
        done = 0
        while done < rows:
            index, inside = divmod(at, half_rows)
            count = min(rows - done, half_rows - inside)
            found.append((index // 2, index % 2, inside, count, target, first + done, block))
            at, done = at + count, done + count
    return found


class Halves:
    def __init__(self, r, first_piece, layout, pieces):
        self.r, self.first_piece, self.pending = r, first_piece, []
        self.cuts = segments(layout, pieces)

    def store(self, source, base, target, first, rows, block):
        for piece, half, inside, count, name, start, at_block in self.cuts:
            if (name, at_block) != (target, block) or not first <= start < first + rows:
                continue
            view = source.at[pl.ds(base + start - first, count)]
            there = pl.ds(inside, count)
            kept = self.r.copies.make(view, getattr(self.r, f"kept{piece}").at[there])
            sem = self.r.copies.sems.at[self.r.copies.used - 1]
            sent = pltpu.make_async_copy(view, getattr(self.r, f"sent{piece}").at[there], sem)
            mine = self.r.ctl[4 + self.first_piece + piece] == half

            @pl.when(mine)
            def _():
                kept.start()

            @pl.when(jnp.logical_not(mine))
            def _():
                sent.start()

            self.pending.append(kept)


def half_outputs(layout, pieces):
    rows = layout_rows(layout) // pieces // 2
    return {f"{kind}{piece}": shape((rows, HALF)) for piece in range(pieces) for kind in ("kept", "sent")}


def both_cores(r, block, acts_at):
    rows = pl.ds(block * ROWS * L, ROWS * L)
    return tn(r.acts_v[:, acts_at], r.rows_v[rows]) + tn(r.acts_sent_v[:, acts_at], r.rows_sent_v[rows])


def load_acts(r, at, size, to):
    return [
        r.copies.start(source.at[row, :, pl.ds(at, size)], target.at[pl.ds(row * L, L), pl.ds(to, size)])
        for row in range(ROWS)
        for source, target in ((r.acts, r.acts_v), (r.acts_sent, r.acts_sent_v))
    ]


def ffn_weights_body(r):
    loads = [r.copies.start(r.rows, r.rows_v), r.copies.start(r.rows_sent, r.rows_sent_v)]
    loads += load_acts(r, A_HID, D, D)
    later = load_acts(r, A_ACT, FF, 2 * D)
    last = load_acts(r, A_CTX, D, 0)
    halves = Halves(r, 0, FFN_LAYOUT, FFN_PIECES)
    wait_all(loads)
    for index, (target, rows, first, block) in enumerate(FFN_LAYOUT):
        if index == 4:
            wait_all(later)
        if index == 8:
            wait_all(last)
        acts_block = 1 if index < 4 else index - 2 if index < 8 else 0
        r.out_v[index] = both_cores(r, min(index, 4) if index < 8 else 5, block_at(acts_block)).astype(bf16)
        halves.store(r.out_v.at[index], 0, target, first, rows, block)
    wait_all(halves.pending)


def ffn_weights(ctl, **ins):
    scratch = dict(
        rows_v=shape((FFN_BLOCKS * ROWS * L, HALF)), rows_sent_v=shape((FFN_BLOCKS * ROWS * L, HALF)),
        acts_v=shape((ROWS * L, FF + 2 * D)), acts_sent_v=shape((ROWS * L, FF + 2 * D)), out_v=shape((len(FFN_LAYOUT), D, HALF)),
    )
    outs = half_outputs(FFN_LAYOUT, FFN_PIECES)
    return run(ffn_weights_body, ctl, ins, outs, {}, scratch, 40, 9 * 2 * 512 * 768 * 384, 14000000)


def att_weights_body(r):
    loads = [r.copies.start(r.rows, r.rows_v), r.copies.start(r.rows_sent, r.rows_sent_v), r.copies.start(r.table, r.table_v)]
    loads += load_acts(r, 0, A_CTX, 0)
    halves = Halves(r, FFN_PIECES, ATT_LAYOUT, ATT_PIECES)
    wait_all(loads)
    for index, (target, rows, first, block) in enumerate(ATT_LAYOUT[:3]):
        total = both_cores(r, index, block_at(min(index, 1)))
        if index < 2:
            at = pl.ds((3 + index) * ROWS * L, ROWS * L)
            far = (r.rows_v[at].astype(f32) + r.rows_sent_v[at].astype(f32)).astype(bf16)
            total = total + tn(r.table_v[...], far)
        r.out_v[index] = total.astype(bf16)
        halves.store(r.out_v.at[index], 0, target, first, rows, block)
    base = ATT_BLOCKS * ROWS * L
    r.rows_v[base:] = r.rows_v[base:] + r.rows_sent_v[base:]
    for target, rows, first, block in ATT_LAYOUT[3:]:
        halves.store(r.rows_v, base, target, first, rows, block)
        base += rows
    wait_all(halves.pending)


def att_weights(ctl, **ins):
    scratch = dict(
        rows_v=shape((ATT_ROWS, HALF)), rows_sent_v=shape((ATT_ROWS, HALF)), table_v=shape((2 * L, D)),
        acts_v=shape((ROWS * L, A_CTX)), acts_sent_v=shape((ROWS * L, A_CTX)), out_v=shape((3, D, HALF)),
    )
    outs = half_outputs(ATT_LAYOUT, ATT_PIECES)
    return run(att_weights_body, ctl, ins, outs, {}, scratch, 32, 4 * 2 * 512 * 768 * 384, 8000000)


def assemble_body(first_piece, layout, pieces, kept, r):
    start_copy = r.copies.start
    core = r.ctl[1]
    half_rows = layout_rows(layout) // pieces // 2
    cuts = segments(layout, pieces)
    loads = []
    for piece in range(pieces):
        loads.append([
            start_copy(array, r.low.at[piece, :, pl.ds(pl.multiple_of(column * HALF, 128), HALF)])
            for array, column in ((getattr(r, f"own{piece}"), core), (getattr(r, f"sent{piece}"), 1 - core))
        ])
    blank = None
    if first_piece > 0 and kept:
        r.blank[...] = jnp.zeros_like(r.blank)
        rest = 2 * SPAN - REL_FROM - REL_ROWS
        blank = [
            start_copy(r.blank, r.g_rel.at[pl.ds(0, REL_FROM)]),
            start_copy(r.blank.at[pl.ds(0, rest)], r.g_rel.at[pl.ds(REL_FROM + REL_ROWS, rest)]),
        ]
    branches = []
    chunk = half_rows // 2
    for piece in range(pieces):
        wait_all(loads[piece])
        for at in range(0, half_rows, chunk):
            r.wide[piece, at : at + chunk] = r.low[piece, at : at + chunk].astype(f32)
            for half in range(2):
                copies = []
                for where, which, inside, count, name, start, block in cuts:
                    low, high = max(inside, at), min(inside + count, at + chunk)
                    if (where, which) != (piece, half) or low >= high or name in ("", "vectors"):
                        continue
                    target = getattr(r, name).at[pl.ds(start + low - inside, high - low), pl.ds(block * D, D)]
                    copies.append(r.copies.make(r.wide.at[piece, pl.ds(low, high - low)], target))
                mine = r.ctl[4 + first_piece + piece] == (half if kept else 1 - half)
                branches.append((mine, copies))

                @pl.when(mine)
                def _():
                    for copy in copies:
                        copy.start()

    for where, which, inside, count, name, _, _ in cuts:
        if name == "vectors":

            @pl.when(r.ctl[4 + first_piece + where] == (which if kept else 1 - which))
            def _():
                vectors = r.wide[where, inside : inside + count, :]
                for part in range(3):
                    r.b_in_v[:, block_at(part)] = vectors[part : part + 1]
                for part in range(4):
                    r.b_up_v[:, block_at(part)] = vectors[3 + part : 4 + part]
                r.gains_v[...] = vectors[7:9]
                r.biases_v[...] = vectors[9:13]
                wait_all([
                    start_copy(r.b_in_v, r.g_b_in), start_copy(r.b_up_v, r.g_b_up),
                    start_copy(r.gains_v, r.g_gains), start_copy(r.biases_v, r.g_biases),
                ])

    wait_all(blank or [])
    for mine, copies in branches:

        @pl.when(mine)
        def _():
            wait_all(copies)


def assemble(first_piece, layout, pieces, kept, ctl, own, sent, shapes, held):
    ins = {f"own{i}": value for i, value in enumerate(own)}
    ins.update({f"sent{i}": value for i, value in enumerate(sent)})
    outs = {name: shape(dims, f32) for name, dims in shapes.items()}
    half_rows = layout_rows(layout) // pieces // 2
    scratch = dict(low=shape((pieces, half_rows, D)), wide=shape((pieces, half_rows, D), f32))
    if first_piece > 0:
        scratch.update(
            blank=shape((REL_FROM, D), f32), b_in_v=shape((1, 3 * D), f32), b_up_v=shape((1, FF), f32),
            gains_v=shape((2, D), f32), biases_v=shape((4, D), f32),
        )
    body = partial(assemble_body, first_piece, layout, pieces, kept)
    return run(body, ctl, ins, outs, held, scratch, 64, 0, pieces * half_rows * D * 6)


FFN_SHAPES = dict(g_up=(D, FF), g_down=(FF, D), g_out=(D, D))
ATT_SHAPES = dict(
    g_in=(D, 3 * D), g_rel=(2 * SPAN, D), g_abs=(ABS_ROWS, D),
    g_b_in=(1, 3 * D), g_b_up=(1, FF), g_gains=(2, D), g_biases=(4, D),
)


SQUARE = ((0, 0), (1, 0), (1, 1), (0, 1))
ROTATION = ("x0", "z0", "x1", "z1", "y")


def dp_place(index):
    return {"core": index % 2, "x": index // 2 % 4, "y": index // 8 % 2, "z": index // 16}


def dp_index(place):
    return ((place["z"] * 2 + place["y"]) * 4 + place["x"]) * 2 + place["core"]


def partner(index, dim):
    place = dp_place(index)
    if len(dim) == 2:
        bits = list(SQUARE[place[dim[0]]])
        bits[int(dim[1])] ^= 1
        place[dim[0]] = SQUARE.index(tuple(bits))
    else:
        place[dim] ^= 1
    return dp_index(place)


def swap(value, dim):
    peers = lax.axis_size("dp")
    return lax.ppermute(value, "dp", [(i, partner(i, dim)) for i in range(peers)])


def side(dim):
    place = dp_place(lax.axis_index("dp"))
    if len(dim) == 1 or dim == "core":
        return place[dim].astype(jnp.int32)
    at = place[dim[0]]
    if dim[1] == "0":
        return ((at == 1) | (at == 2)).astype(jnp.int32)
    return (at >= 2).astype(jnp.int32)


def order_of(piece):
    return [ROTATION[(piece + step) % len(ROTATION)] for step in range(len(ROTATION))]


ORDERS = [order_of(piece) for piece in range(FFN_PIECES + ATT_PIECES)]


SPLIT_STEPS = 3


def next_sum(chunk, dim):
    at, half = side(dim), chunk.shape[0] // 2
    received = swap(lax.dynamic_slice_in_dim(chunk, (1 - at) * half, half, 0), dim)
    return lax.dynamic_slice_in_dim(chunk, at * half, half, 0) + received


def summed_chunk(chunk, order):
    for dim in order[1:SPLIT_STEPS]:
        chunk = next_sum(chunk, dim)
    for dim in order[SPLIT_STEPS:]:
        chunk = chunk + swap(chunk, dim)
    return chunk


def summed_tail_chunk(chunk, order):
    for dim in order[1:SPLIT_STEPS]:
        chunk = next_sum(chunk, dim)
    for dim in order[SPLIT_STEPS:-1]:
        chunk = chunk + swap(chunk, dim)
    peers = lax.axis_size("dp")
    across = [(s * peers + i, (1 - s) * peers + i) for s in range(2) for i in range(peers)]
    aslant = [(s * peers + i, (1 - s) * peers + partner(i, order[-1])) for s in range(2) for i in range(peers)]
    there = lax.ppermute(chunk, ("section", "dp"), across) + lax.ppermute(chunk, ("section", "dp"), aslant)
    chunk = chunk + swap(chunk, order[-1])
    first_row, span = 0, layout_rows(ATT_LAYOUT) // ATT_PIECES
    tail_at = span - TAIL_ROWS
    for dim in order[:SPLIT_STEPS]:
        span //= 2
        first_row = first_row + side(dim) * span
    row_at = first_row + lax.broadcasted_iota(jnp.int32, chunk.shape, 0) - tail_at
    return jnp.where((row_at >= 0) & (row_at < TABLE_ROWS), chunk + there, chunk)


def in_order(at, own, other):
    return jnp.where(
        at == 0,
        jnp.concatenate([own, other], axis=0),
        jnp.concatenate([other, own], axis=0),
    )


def gathered_half(chunk, order):
    for dim in reversed(order[1:SPLIT_STEPS]):
        chunk = in_order(side(dim), chunk, swap(chunk, dim))
    return chunk


def per_device(
    hidden_in,
    cotangent,
    segment_ids,
    positions,
    w_in,
    b_in,
    w_out,
    w_up,
    b_up,
    w_down,
    gains,
    biases,
    rel_table,
    abs_table,
):
    section = lax.axis_index("section").astype(jnp.int32)
    firsts = jnp.where(section == 1, positions[:, 0], 8 * ABS_ROWS)
    ctl = jnp.stack([section, side("core"), firsts[0], firsts[1], *[side(order[0]) for order in ORDERS]])
    weights = dict(w_in=w_in[0], w_out=w_out[0], w_up=w_up[0], w_down=w_down[0], gains=gains[0])
    common = dict(
        weights, hidden_in=hidden_in, segment_ids=segment_ids, biases=biases[0], b_in=b_in, b_up=b_up, abs_table=abs_table
    )

    out = forward(0, 0, ctl, dict(common, rel_table=rel_table), {})
    rel, rel_rows = out["rel"], out["rel_rows"]
    common["rel"] = rel
    received = []
    for row in range(ROWS):
        if row > 0:
            out = forward(row, 0, ctl, common, out)
        received.append(lax.ppermute(out["sent"], "section", [(0, 1)]))
    for row in range(ROWS):
        out = forward(row, 1, ctl, dict(common, received=received[row]), out)
    acts, keep, resid, section_out = out["acts"], out["keep"], out["resid"], out["section_out"]
    acts_sent = swap(acts, "core")

    common = dict(weights, cotangent=cotangent, keep=keep, resid=resid, rel=rel)
    out, received = {}, []
    for row in range(ROWS):
        out = backward(row, 1, "both", ctl, common, out)
        received.append(lax.ppermute(out["sent"], "section", [(1, 0)]))
    out.update(tables(ctl, weights["w_in"], out))
    out = backward(0, 0, "both", ctl, dict(common, received=received[0]), out)
    ffn = backward(1, 0, "ffn", ctl, dict(common, received=received[1]), out)
    ffn_pieces = ffn_weights(
        ctl, acts=acts, acts_sent=acts_sent, rows=ffn["ffn_own"], rows_sent=swap(ffn["ffn_other"], "core")
    )
    d_resid, ffn_pieces = lax.optimization_barrier((ffn["d_resid"], ffn_pieces))
    ffn_orders, att_orders = ORDERS[:FFN_PIECES], ORDERS[FFN_PIECES:]
    ffn_received = [swap(ffn_pieces[f"sent{i}"], order[0]) for i, order in enumerate(ffn_orders)]
    out = backward(1, 0, "att", ctl, dict(common, d_resid=d_resid, ffn_vec=ffn["ffn_vec"]), out)
    att_pieces = att_weights(
        ctl, acts=acts, acts_sent=acts_sent, rows=out["att_own"], rows_sent=swap(out["att_other"], "core"), table=rel_rows
    )
    ffn_received, att_pieces = lax.optimization_barrier((ffn_received, att_pieces))
    att_received = [swap(att_pieces[f"sent{i}"], order[0]) for i, order in enumerate(att_orders)]
    chunks = [
        summed_chunk(ffn_pieces[f"kept{i}"] + received, order)
        for i, (received, order) in enumerate(zip(ffn_received, ffn_orders))
    ]
    for i, (received, order) in enumerate(zip(att_received, att_orders)):
        summed = summed_tail_chunk if i == ATT_PIECES - 1 else summed_chunk
        chunks.append(summed(att_pieces[f"kept{i}"] + received, order))
    mine = [gathered_half(chunk, order) for chunk, order in zip(chunks, ORDERS)]
    partners = [swap(half, order[0]) for half, order in zip(mine, ORDERS)]
    mine_sent = [swap(half, "core") for half in mine]
    ffn = assemble(0, FFN_LAYOUT, FFN_PIECES, True, ctl, mine[:FFN_PIECES], mine_sent[:FFN_PIECES], FFN_SHAPES, {})
    att = assemble(
        FFN_PIECES, ATT_LAYOUT, ATT_PIECES, True, ctl, mine[FFN_PIECES:], mine_sent[FFN_PIECES:], ATT_SHAPES, {}
    )
    partners[:FFN_PIECES], ffn, att = lax.optimization_barrier((partners[:FFN_PIECES], ffn, att))
    partners_sent = [swap(half, "core") for half in partners]
    ffn = assemble(
        0, FFN_LAYOUT, FFN_PIECES, False, ctl, partners[:FFN_PIECES], partners_sent[:FFN_PIECES], FFN_SHAPES, ffn
    )
    att = assemble(
        FFN_PIECES, ATT_LAYOUT, ATT_PIECES, False, ctl, partners[FFN_PIECES:], partners_sent[FFN_PIECES:], ATT_SHAPES, att
    )
    return (
        section_out[None],
        out["input_grad"][None],
        att["g_in"][None],
        att["g_b_in"],
        ffn["g_out"][None],
        ffn["g_up"][None],
        att["g_b_up"],
        ffn["g_down"][None],
        att["g_gains"][None],
        att["g_biases"][None],
        att["g_rel"],
        att["g_abs"],
    )


def solution(mesh):
    in_specs = (
        P("dp", None, None),
        P("dp", None, None),
        P("dp", None),
        P("dp", None),
        P("section", None, None),
        P("section", None),
        P("section", None, None),
        P("section", None, None),
        P("section", None),
        P("section", None, None),
        P("section", None, None),
        P("section", None, None),
        P(),
        P(),
    )
    out_specs = (
        P("section", "dp", None, None),
        P("section", "dp", None, None),
        P("section", None, None),
        P("section", None),
        P("section", None, None),
        P("section", None, None),
        P("section", None),
        P("section", None, None),
        P("section", None, None),
        P("section", None, None),
        P(),
        P(),
    )
    return jax.shard_map(
        per_device, mesh=mesh, in_specs=in_specs, out_specs=out_specs, check_vma=False
    )
```

```python
from functools import partial
import math
from types import SimpleNamespace

import jax
import jax.numpy as jnp
from jax import lax
from jax.experimental import pallas as pl
from jax.experimental.pallas import tpu as pltpu
from jax.sharding import PartitionSpec as P

HEADS = 12
L = 128
D = 768
FF = 3072
HALF = D // 2
PAIRS = HEADS // 2
ROWS = 2
SPAN = 256
EPS = 1e-06
NEG = -1e30
SCALE = 1.0 / math.sqrt(3 * 64)
VMEM_LIMIT = 61 * 1024 * 1024
f32, bf16 = jnp.float32, jnp.bfloat16

A_START, A_X, A_CTX, A_HID, A_ACT, A_ALL = 0, 768, 1536, 2304, 3072, 6144
K_P, K_GP, K_ALL = 2304, 3840, 6912
VECTOR_ROWS = 16
REL_FROM, REL_ROWS, ABS_ROWS, TAIL_ROWS = 128, 272, 512, 896
TABLE_ROWS = REL_ROWS + ABS_ROWS
FFN_LAYOUT = [
    [("g_up", D, 0, 2 * core), ("g_up", D, 0, 2 * core + 1), ("g_down", 2 * D, 2 * D * core, 0), ("g_out", HALF, HALF * core, 0)]
    for core in range(2)
]
ATT_LAYOUT = [
    [("g_in", D, 0, 0), ("g_in", HALF, 0, 1), ("g_rel", REL_ROWS, REL_FROM, 0), ("g_abs", 176, 0, 0)],
    [("g_in", D, 0, 2), ("g_in", HALF, HALF, 1), ("g_abs", 336, 176, 0), ("vectors", VECTOR_ROWS, 0, 0), ("", 96, 0, 0)],
]
FFN_ROWS, ATT_ROWS = 3456, 1600
FFN_PIECES, ATT_PIECES = 2, 1
TAIL_HALF = TAIL_ROWS // 2
TAIL_AT = ATT_ROWS - TAIL_HALF
SWAP_ROWS = 8 * L + TAIL_HALF

VMEM = pl.BlockSpec(memory_space=pltpu.VMEM)
ANY = pl.BlockSpec(memory_space=pl.ANY)
SMEM = pl.BlockSpec(memory_space=pltpu.SMEM)


def nn(a, b):
    return lax.dot_general(a, b, (((1,), (0,)), ((), ())), preferred_element_type=f32)


def nt(a, b):
    return lax.dot_general(a, b, (((1,), (1,)), ((), ())), preferred_element_type=f32)


def tn(a, b):
    return lax.dot_general(a, b, (((0,), (0,)), ((), ())), preferred_element_type=f32)


def norm_parts(value):
    centered = value - jnp.mean(value, axis=1, keepdims=True)
    rstd = lax.rsqrt(jnp.mean(centered * centered, axis=1, keepdims=True) + EPS)
    return centered * rstd, rstd


def norm_backward(normed, rstd, gain, grad):
    scaled = grad * gain
    mean_one = jnp.mean(scaled, axis=1, keepdims=True)
    mean_two = jnp.mean(scaled * normed, axis=1, keepdims=True)
    return (scaled - mean_one - normed * mean_two) * rstd


def column_sums(value):
    return jnp.sum(value, axis=0, keepdims=True)


def indicator(condition):
    return condition.astype(f32).astype(bf16)


def lane_halves():
    lane = lax.broadcasted_iota(jnp.int32, (1, L), 1)
    return indicator(lane < 64), indicator(lane >= 64)


def stacked(value, halves):
    return jnp.concatenate([value * halves[0], value * halves[1]], axis=0)


def skew(table):
    return pltpu.roll(table, L, 1, stride=1, stride_axis=0)[:, :L]


def unskew(turned):
    wide = jnp.concatenate([turned, jnp.zeros_like(turned)], axis=1)
    return pltpu.roll(wide, 1, 1, stride=1, stride_axis=0)


def pair_at(pair, base=0):
    return slice(base + pair * L, base + pair * L + L)


def block_at(block, base=0):
    return slice(base + block * D, base + block * D + D)


def shape(dims, dtype=bf16):
    return jax.ShapeDtypeStruct(dims, dtype)


class Copies:
    def __init__(self, sems):
        self.sems, self.used = sems, 0

    def make(self, source, target):
        self.used += 1
        return pltpu.make_async_copy(source, target, self.sems.at[self.used - 1])

    def start(self, source, target):
        copy = self.make(source, target)
        copy.start()
        return copy


def wait_all(copies):
    for copy in copies:
        copy.wait()


def run(body, ctl, ins, outs, held, scratch, copies, flops, traffic, near=(), limit=VMEM_LIMIT):
    names, out_names, scratch_names = list(ins), list(outs), list(scratch)
    kept = [name for name in out_names if name in held and name != "sent"]

    def kernel(*refs):
        ctl_ref, refs = refs[0], refs[1:]
        r = SimpleNamespace(ctl=ctl_ref, **dict(zip(names, refs)))
        refs = refs[len(names) + len(kept) :]
        for name, ref in zip(out_names + scratch_names, refs):
            setattr(r, name, ref)
        r.copies = Copies(refs[-1])
        body(r)

    results = pl.pallas_call(
        kernel,
        out_shape=tuple(outs.values()),
        in_specs=[SMEM] + [VMEM if name in near else ANY for name in names] + [ANY] * len(kept),
        out_specs=(ANY,) * len(out_names),
        input_output_aliases={1 + len(names) + i: out_names.index(name) for i, name in enumerate(kept)},
        scratch_shapes=[pltpu.VMEM(s.shape, s.dtype) for s in scratch.values()] + [pltpu.SemaphoreType.DMA((copies,))],
        compiler_params=pltpu.CompilerParams(vmem_limit_bytes=limit),
        cost_estimate=pl.CostEstimate(flops=flops, bytes_accessed=traffic, transcendentals=0),
    )(ctl, *ins.values(), *[held[name] for name in kept])
    return dict(zip(out_names, results))


def relative_part(r):
    loads = [r.copies.start(r.rel_table, r.table_v), r.copies.start(r.b_in, r.b_in_v), r.copies.start(r.w_in, r.wi)]
    dims = (2 * L, 2 * SPAN)
    select = indicator(lax.broadcasted_iota(jnp.int32, dims, 0) + lax.broadcasted_iota(jnp.int32, dims, 1) == L + SPAN)
    loads[0].wait()
    rows = nn(select, r.table_v[...]).astype(bf16)
    r.rel_rows_v[...] = rows
    loads[1].wait()
    loads[2].wait()
    r.rel_v[...] = (nn(rows, r.wi[:, : 2 * D]) + r.b_in_v[:, : 2 * D].astype(f32)).astype(bf16)
    return [r.copies.start(r.rel_rows_v, r.rel_rows), r.copies.start(r.rel_v, r.rel)]


def forward_body(row, section, first, r):
    start_copy = r.copies.start
    stores = relative_part(r) if first else []

    @pl.when(r.ctl[0] == section)
    def _():
        x_load = start_copy(r.hidden_in.at[row], r.x_v) if section == 0 else None
        small = [start_copy(r.segment_ids, r.seg_v), start_copy(r.gains, r.gains_v), start_copy(r.biases, r.biases_v)]
        abs_load = start_copy(r.abs_table, r.table_v) if section == 1 else None
        in_loads = [] if first else [start_copy(r.b_in, r.b_in_v), start_copy(r.w_in, r.wi)]
        rel_load = None if first else start_copy(r.rel, r.rel_v)
        loads = [start_copy(r.w_out, r.wo), start_copy(r.b_up, r.b_up_v), start_copy(r.w_up, r.wu), start_copy(r.w_down, r.wd)]
        halves = lane_halves()
        if section == 0:
            x_load.wait()
        x = r.x_v[...] if section == 0 else r.received[...]
        start = x.astype(f32)
        if section == 1:
            abs_load.wait()
            dims = (L, ABS_ROWS)
            place = lax.broadcasted_iota(jnp.int32, dims, 1) - lax.broadcasted_iota(jnp.int32, dims, 0)
            start = start + nn(indicator(place == r.ctl[2 + row]), r.table_v[...])
        query_in = start.astype(bf16)
        r.acts_v[:, block_at(0)] = query_in
        r.acts_v[:, block_at(1)] = x
        wait_all(in_loads)
        b_in = r.b_in_v[...].astype(f32)
        r.keep_v[:, :D] = (nn(query_in, r.wi[:, :D]) + b_in[:, :D]).astype(bf16)
        r.keep_v[:, D : 3 * D] = (nn(x, r.wi[:, D:]) + b_in[:, D:]).astype(bf16)
        wait_all(small)
        if rel_load is not None:
            rel_load.wait()
        seg_rows = jnp.broadcast_to(r.seg_v[row : row + 1, :], (L, L)).astype(f32)
        same = seg_rows == seg_rows.T
        for pair in range(PAIRS):
            query = r.keep_v[:, pair_at(pair)]
            key = r.keep_v[:, pair_at(pair, D)]
            value = r.keep_v[:, pair_at(pair, 2 * D)]
            query_two, key_two = stacked(query, halves), stacked(key, halves)
            content = nt(query_two, key)
            far_query = nt(query_two, r.rel_v[:, pair_at(pair, D)])
            far_key = nt(key_two, r.rel_v[:, pair_at(pair)])
            probs = []
            for head in range(2):
                rows = slice(head * L, head * L + L)
                summed = content[rows] + skew(far_query[rows]) + skew(far_key[rows]).T
                scores = jnp.where(same, summed * SCALE, NEG)
                exponent = jnp.exp(scores - jnp.max(scores, axis=1, keepdims=True))
                total = jnp.sum(exponent, axis=1, keepdims=True)
                probs.append((exponent * (1.0 / total)).astype(bf16))
            probs = jnp.concatenate(probs, axis=1)
            r.keep_v[:, K_P + 2 * pair * L : K_P + 2 * (pair + 1) * L] = probs
            r.acts_v[:, pair_at(pair, A_CTX)] = nn(probs, stacked(value, halves)).astype(bf16)
        loads[0].wait()
        gain = r.gains_v[...].astype(f32)
        shift = r.biases_v[...].astype(f32)
        resid_one = start + nn(r.acts_v[:, A_CTX : A_CTX + D], r.wo[...]) + shift[0:1]
        r.resid_v[:, :D] = resid_one
        hidden = norm_parts(resid_one)[0] * gain[0:1] + shift[1:2]
        hidden_low = hidden.astype(bf16)
        r.acts_v[:, A_HID : A_HID + D] = hidden_low
        early = [
            start_copy(r.acts_v.at[:, pl.ds(0, A_ACT)], r.acts.at[row, :, pl.ds(0, A_ACT)]),
            start_copy(r.keep_v.at[:, pl.ds(0, K_GP)], r.keep.at[row, :, pl.ds(0, K_GP)]),
        ]
        wait_all(loads[1:])
        total = hidden + shift[2:3]
        for part in range(4):
            gate = nn(hidden_low, r.wu[:, block_at(part)]) + r.b_up_v[:, block_at(part)].astype(f32)
            below = 0.5 + 0.5 * lax.erf(gate * (1.0 / math.sqrt(2.0)))
            density = jnp.exp(gate * gate * -0.5) * (1.0 / math.sqrt(2.0 * math.pi))
            active = (gate * below).astype(bf16)
            r.acts_v[:, block_at(part, A_ACT)] = active
            r.keep_v[:, block_at(part, K_GP)] = (below + gate * density).astype(bf16)
            total = total + nn(active, r.wd[block_at(part), :])
        r.resid_v[:, D:] = total
        late = [
            start_copy(r.acts_v.at[:, pl.ds(A_ACT, FF)], r.acts.at[row, :, pl.ds(A_ACT, FF)]),
            start_copy(r.keep_v.at[:, pl.ds(K_GP, FF)], r.keep.at[row, :, pl.ds(K_GP, FF)]),
            start_copy(r.resid_v, r.resid.at[row]),
        ]
        r.x_v[...] = (norm_parts(total)[0] * gain[1:2] + shift[3:4]).astype(bf16)
        late.append(start_copy(r.x_v, r.section_out.at[row]))
        if section == 0:
            late.append(start_copy(r.x_v, r.sent))
        wait_all(early + late)

    wait_all(stores)


def forward(row, section, ctl, ins, held):
    first = not held
    outs = {"sent": shape((L, D))} if section == 0 else {}
    if first:
        outs.update(rel_rows=shape((2 * L, D)), rel=shape((2 * L, 2 * D)))
    outs.update(
        acts=shape((ROWS, L, A_ALL)),
        keep=shape((ROWS, L, K_ALL)),
        resid=shape((ROWS, L, 2 * D), f32),
        section_out=shape((ROWS, L, D)),
    )
    scratch = dict(
        x_v=shape((L, D)), seg_v=shape((ROWS, L), jnp.int32), gains_v=shape((2, D)), biases_v=shape((4, D)),
        b_in_v=shape((1, 3 * D)), b_up_v=shape((1, FF)), table_v=shape((2 * SPAN, D)), rel_v=shape((2 * L, 2 * D)),
        wi=shape((D, 3 * D)), wo=shape((D, D)), wu=shape((D, FF)), wd=shape((FF, D)),
        acts_v=shape((L, A_ALL)), keep_v=shape((L, K_ALL)), resid_v=shape((L, 2 * D), f32),
    )
    if first:
        scratch.update(rel_rows_v=shape((2 * L, D)))
    return run(partial(forward_body, row, section, first), ctl, ins, outs, held, scratch, 24, 1900000000, 18000000, near=("received",))


def ffn_loads(row, section, r):
    return SimpleNamespace(
        grad=[r.copies.start(r.cotangent.at[row], r.grad_v)] if section == 1 else [],
        resid=r.copies.start(r.resid.at[row], r.resid_v),
        gains=r.copies.start(r.gains, r.gains_v),
        down=r.copies.start(r.w_down, r.wd),
        slope=r.copies.start(r.keep.at[row, :, pl.ds(K_GP, FF)], r.slope_v),
        up=r.copies.start(r.w_up, r.wu),
    )


def ffn_part(row, section, r, loads):
    wait_all(loads.grad + [loads.resid, loads.gains])
    gain = r.gains_v[...].astype(f32)
    grad = (r.grad_v if section == 1 else r.received)[...].astype(f32)
    normed, rstd = norm_parts(r.resid_v[:, D:])
    r.ffn_vec_v[...] = jnp.zeros_like(r.ffn_vec_v)
    r.ffn_vec_v[8:9] = column_sums(grad * normed)
    r.ffn_vec_v[12:13] = column_sums(grad)
    d_two = norm_backward(normed, rstd, gain[1:2], grad)
    d_down = d_two.astype(bf16)
    r.ffn_v[:, FF : FF + D] = d_down
    r.ffn_vec_v[11:12] = column_sums(d_down.astype(f32))
    wait_all([loads.down, loads.slope, loads.up])
    d_hidden = d_two
    for part in range(4):
        d_gate = (nt(d_down, r.wd[block_at(part), :]) * r.slope_v[:, block_at(part)].astype(f32)).astype(bf16)
        r.ffn_v[:, block_at(part)] = d_gate
        r.ffn_vec_v[3 + part : 4 + part] = column_sums(d_gate.astype(f32))
        d_hidden = d_hidden + nt(d_gate, r.wu[:, block_at(part)])
    normed, rstd = norm_parts(r.resid_v[:, :D])
    r.ffn_vec_v[7:8] = column_sums(d_hidden * normed)
    r.ffn_vec_v[10:11] = column_sums(d_hidden)
    d_resid = norm_backward(normed, rstd, gain[0:1], d_hidden)
    d_att = d_resid.astype(bf16)
    r.ffn_v[:, FF + D :] = d_att
    r.ffn_vec_v[9:10] = column_sums(d_att.astype(f32))
    stores, rows = [], pl.ds(row * L, L)
    for side_core, target in ((r.ctl[1], r.ffn_own), (1 - r.ctl[1], r.ffn_other)):
        gates = pl.ds(pl.multiple_of(side_core * 2 * D, 128), 2 * D)
        stores.append(r.copies.start(r.ffn_v.at[:, gates], target.at[rows, pl.ds(0, 2 * D)]))
        stores.append(r.copies.start(r.ffn_v.at[:, pl.ds(FF, 2 * D)], target.at[rows, pl.ds(2 * D, 2 * D)]))
    stores.append(r.copies.start(r.ffn_vec_v, r.ffn_vec.at[row]))
    return d_resid, stores


def att_loads(row, section, r):
    return SimpleNamespace(
        out=r.copies.start(r.w_out, r.wo),
        keep=r.copies.start(r.keep.at[row, :, pl.ds(0, K_GP)], r.keep_v),
        rel=r.copies.start(r.rel, r.rel_v),
        earlier=r.copies.start(r.d_rel, r.d_rel_old) if row > 0 else None,
        w_in=r.copies.start(r.w_in, r.wi),
        others=[
            r.copies.start(r.d_start.at[0], r.others_v),
            r.copies.start(r.att_vec.at[0], r.att_vec_old),
            r.copies.start(r.ffn_vec, r.ffn_vec_v),
        ]
        if row == ROWS - 1 and section == 0
        else [],
    )


def att_part(row, section, r, loads, d_resid):
    halves = lane_halves()
    row_at = lax.broadcasted_iota(jnp.int32, (L, L), 0)
    column_at = lax.broadcasted_iota(jnp.int32, (L, L), 1)
    turn = indicator(row_at + column_at == L - 1)
    d_att = d_resid.astype(bf16)
    r.att_vec_v[...] = jnp.zeros_like(r.att_vec_v)
    loads.out.wait()
    d_context = nt(d_att, r.wo[...]).astype(bf16)
    loads.keep.wait()
    loads.rel.wait()
    for pair in range(PAIRS):
        query = r.keep_v[:, pair_at(pair)]
        key = r.keep_v[:, pair_at(pair, D)]
        value = r.keep_v[:, pair_at(pair, 2 * D)]
        probs = r.keep_v[:, K_P + 2 * pair * L : K_P + 2 * (pair + 1) * L]
        probs_two = jnp.concatenate([probs[:, :L], probs[:, L:]], axis=0)
        rel_q, rel_k = r.rel_v[:, pair_at(pair)], r.rel_v[:, pair_at(pair, D)]
        context_two = stacked(d_context[:, pair_at(pair)], halves)
        probs_f = probs_two.astype(f32)
        weighted = nt(context_two, value) * probs_f
        d_scores = (weighted - probs_f * jnp.sum(weighted, axis=1, keepdims=True)).astype(bf16)
        query_two, key_two = stacked(query, halves), stacked(key, halves)
        d_value = tn(probs_two, context_two)
        d_key = tn(d_scores, query_two)
        d_side = jnp.concatenate([d_scores[:L], d_scores[L:]], axis=1)
        d_query = nn(d_side, key_two)
        d_far = (d_side.astype(f32) * SCALE).astype(bf16)
        query_turned = nn(turn, query).astype(bf16)
        key_turned = nn(turn, key).astype(bf16)
        rows_turned = nn(turn, d_far)
        far_query, far_key = [], []
        for head in range(2):
            columns = slice(head * L, head * L + L)
            far_query.append(unskew(rows_turned[:, columns]).astype(bf16))
            far_key.append(unskew(nt(turn, d_far[:, columns])).astype(bf16))
        d_query_turned = nn(jnp.concatenate(far_query, axis=1), stacked(rel_k, halves))
        d_key_turned = nn(jnp.concatenate(far_key, axis=1), stacked(rel_q, halves))
        r.d_rel_v[:, pair_at(pair)] = tn(jnp.concatenate(far_key, axis=0), stacked(key_turned, halves))
        r.d_rel_v[:, pair_at(pair, D)] = tn(jnp.concatenate(far_query, axis=0), stacked(query_turned, halves))
        d_query = d_query * SCALE + nn(turn, d_query_turned.astype(bf16))
        d_key = d_key * SCALE + nn(turn, d_key_turned.astype(bf16))
        r.att_v[:, pair_at(pair)] = d_query.astype(bf16)
        r.att_v[:, pair_at(pair, D)] = d_key.astype(bf16)
        r.att_v[:, pair_at(pair, 2 * D)] = d_value.astype(bf16)
    stores = []
    for side_core, target in ((r.ctl[1], r.att_own), (1 - r.ctl[1], r.att_other)):
        query_or_value = pl.ds(pl.multiple_of(side_core * 2 * D, 128), D)
        stores.append(r.copies.start(r.att_v.at[:, query_or_value], target.at[pl.ds(row * L, L)]))
        stores.append(r.copies.start(r.att_v.at[:, pl.ds(D, D)], target.at[pl.ds((ROWS + row) * L, L)]))
    loads.w_in.wait()
    d_start = d_resid + nt(r.att_v[:, :D], r.wi[:, :D])
    r.start_v[...] = d_start.astype(bf16)
    stores.append(r.copies.start(r.start_v, r.d_start.at[row]))
    r.grad_out_v[...] = (d_start + nt(r.att_v[:, D : 3 * D], r.wi[:, D:])).astype(bf16)
    stores.append(r.copies.start(r.grad_out_v, r.input_grad.at[row]))
    if section == 1:
        stores.append(r.copies.start(r.grad_out_v, r.sent))
    for part in range(3):
        rows = column_sums(r.att_v[:, block_at(part)].astype(f32))
        if part < 2:
            rows = rows + column_sums(r.d_rel_v[:, block_at(part)])
        r.att_vec_v[part : part + 1] = rows
    stores.append(r.copies.start(r.att_vec_v, r.att_vec.at[row]))
    if row > 0:
        loads.earlier.wait()
        r.d_rel_v[...] = r.d_rel_v[...] + r.d_rel_old[...]
    if row < ROWS - 1:
        stores.append(r.copies.start(r.d_rel_v, r.d_rel))
        return stores
    r.rel_low[...] = r.d_rel_v[...].astype(bf16)
    for block in range(2):
        for target in (r.att_own, r.att_other):
            rows = pl.ds((4 + 2 * block) * L, 2 * L)
            stores.append(r.copies.start(r.rel_low.at[:, pl.ds(block * D, D)], target.at[rows]))
    if section == 0:
        wait_all(loads.others)
        stores += tail_part(
            r, [r.others_v[...], r.start_v[...]], r.ffn_vec_v[0] + r.ffn_vec_v[1] + r.att_vec_old[...] + r.att_vec_v[...]
        )
    else:
        stores.append(r.copies.start(r.rel_low, r.d_rel_low))
    return stores


def tail_part(r, starts, vectors):
    def put(first, rows, value):
        r.tail_v[first : first + rows] = value.astype(bf16)

    dims = (ABS_ROWS, L)
    place = lax.broadcasted_iota(jnp.int32, dims, 0) - lax.broadcasted_iota(jnp.int32, dims, 1)
    spots = [indicator(place == r.ctl[2 + row]) for row in range(ROWS)]
    put(REL_ROWS, ABS_ROWS, nn(spots[0], starts[0]) + nn(spots[1], starts[1]))
    put(TABLE_ROWS, VECTOR_ROWS, vectors)
    rest = TAIL_ROWS - TABLE_ROWS - VECTOR_ROWS
    put(TABLE_ROWS + VECTOR_ROWS, rest, jnp.zeros((rest, D), f32))
    rows = nt(r.rel_low[...], r.wi[:, : 2 * D]).astype(bf16)
    dims = (REL_ROWS, 2 * L)
    select = lax.broadcasted_iota(jnp.int32, dims, 0) + lax.broadcasted_iota(jnp.int32, dims, 1) == L + SPAN - REL_FROM
    put(0, REL_ROWS, nn(indicator(select), rows))
    return [
        r.copies.start(
            r.tail_v.at[pl.ds(pl.multiple_of(side_core * TAIL_HALF, 16), TAIL_HALF)], target.at[pl.ds(8 * L, TAIL_HALF)]
        )
        for side_core, target in ((r.ctl[1], r.att_own), (1 - r.ctl[1], r.att_other))
    ]


def backward_body(row, section, parts, r):
    @pl.when(r.ctl[0] == section)
    def _():
        if parts == "ffn":
            d_resid, stores = ffn_part(row, section, r, ffn_loads(row, section, r))
            r.resid_v[:, :D] = d_resid
            stores.append(r.copies.start(r.resid_v.at[:, pl.ds(0, D)], r.d_resid))
        elif parts == "att":
            load = r.copies.start(r.d_resid, r.d_resid_v)
            loads = att_loads(row, section, r)
            load.wait()
            stores = att_part(row, section, r, loads, r.d_resid_v[...])
        else:
            loads = ffn_loads(row, section, r)
            later = att_loads(row, section, r)
            d_resid, stores = ffn_part(row, section, r, loads)
            stores = stores + att_part(row, section, r, later, d_resid)
        wait_all(stores)


def backward(row, section, parts, ctl, ins, held):
    outs, scratch, flops, traffic = {}, {}, 0, 0
    if parts == "ffn":
        outs.update(d_resid=shape((L, D), f32))
    if parts != "att":
        outs.update(
            ffn_own=shape((ROWS * L, 4 * D)), ffn_other=shape((ROWS * L, 4 * D)), ffn_vec=shape((ROWS, VECTOR_ROWS, D), f32)
        )
        scratch.update(
            grad_v=shape((L, D)), resid_v=shape((L, 2 * D), f32), gains_v=shape((2, D)), slope_v=shape((L, FF)),
            wu=shape((D, FF)), wd=shape((FF, D)), ffn_v=shape((L, FF + 2 * D)), ffn_vec_v=shape((VECTOR_ROWS, D), f32),
        )
        flops, traffic = flops + 1300000000, traffic + 12000000
    if parts == "att":
        scratch.update(d_resid_v=shape((L, D), f32))
    if parts != "ffn":
        if section == 1:
            outs.update(sent=shape((L, D)))
        outs.update(
            att_own=shape((SWAP_ROWS, D)), att_other=shape((SWAP_ROWS, D)), att_vec=shape((ROWS, VECTOR_ROWS, D), f32),
            d_start=shape((ROWS, L, D)), d_rel=shape((2 * L, 2 * D), f32), d_rel_low=shape((2 * L, 2 * D)),
            input_grad=shape((ROWS, L, D)),
        )
        scratch.update(
            wi=shape((D, 3 * D)), wo=shape((D, D)), keep_v=shape((L, K_GP)), rel_v=shape((2 * L, 2 * D)),
            att_v=shape((L, 3 * D)), att_vec_v=shape((VECTOR_ROWS, D), f32), start_v=shape((L, D)), grad_out_v=shape((L, D)),
            d_rel_v=shape((2 * L, 2 * D), f32), d_rel_old=shape((2 * L, 2 * D), f32), rel_low=shape((2 * L, 2 * D)),
        )
        if row == ROWS - 1 and section == 0:
            scratch.update(
                tail_v=shape((TAIL_ROWS, D)),
                others_v=shape((L, D)), att_vec_old=shape((VECTOR_ROWS, D), f32), ffn_vec_v=shape((ROWS, VECTOR_ROWS, D), f32),
            )
        flops, traffic = flops + 1100000000, traffic + 8000000
    return run(partial(backward_body, row, section, parts), ctl, ins, outs, held, scratch, 48, flops, traffic, near=("received",))


def tables_body(r):
    @pl.when(r.ctl[0] == 1)
    def _():
        loads = [
            r.copies.start(source, target)
            for source, target in (
                (r.d_start, r.start_v), (r.ffn_vec, r.ffn_vec_v), (r.att_vec, r.att_vec_v), (r.d_rel_low, r.rel_low), (r.w_in, r.wi)
            )
        ]
        wait_all(loads)
        vectors = r.ffn_vec_v[0] + r.ffn_vec_v[1] + r.att_vec_v[0] + r.att_vec_v[1]
        wait_all(tail_part(r, [r.start_v[0], r.start_v[1]], vectors))


def tables(ctl, w_in, held):
    ins = dict(w_in=w_in, **{name: held[name] for name in ("d_start", "ffn_vec", "att_vec", "d_rel_low")})
    outs = dict(att_own=shape((SWAP_ROWS, D)), att_other=shape((SWAP_ROWS, D)))
    scratch = dict(
        start_v=shape((ROWS, L, D)), ffn_vec_v=shape((ROWS, VECTOR_ROWS, D), f32), att_vec_v=shape((ROWS, VECTOR_ROWS, D), f32),
        rel_low=shape((2 * L, 2 * D)), wi=shape((D, 3 * D)), tail_v=shape((TAIL_ROWS, D)),
    )
    return run(tables_body, ctl, ins, outs, held, scratch, 8, 1000000000, 7000000)


class Halves:
    def __init__(self, r, first_piece, half_rows):
        self.r, self.first_piece, self.half_rows, self.pending = r, first_piece, half_rows, []

    def store(self, first, rows):
        while rows > 0:
            index, inside = divmod(first, self.half_rows)
            count = min(rows, self.half_rows - inside)
            piece, half = index // 2, index % 2
            view, there = self.r.out_v.at[pl.ds(first, count)], pl.ds(inside, count)
            kept = self.r.copies.make(view, getattr(self.r, f"kept{piece}").at[there])
            sem = self.r.copies.sems.at[self.r.copies.used - 1]
            sent = pltpu.make_async_copy(view, getattr(self.r, f"sent{piece}").at[there], sem)
            mine = self.r.ctl[bit_at(self.first_piece + piece, False)] == half

            @pl.when(mine)
            def _():
                kept.start()

            @pl.when(jnp.logical_not(mine))
            def _():
                sent.start()

            self.pending.append(kept)
            first, rows = first + count, rows - count


def bit_at(piece, of_other_core):
    return 4 + 2 * piece + int(of_other_core)


def half_outputs(rows, pieces):
    half_rows = rows // pieces // 2
    return {f"{kind}{piece}": shape((half_rows, D)) for piece in range(pieces) for kind in ("kept", "sent")}


def load_acts(r, at, size, to):
    if not isinstance(at, int):
        at = pl.multiple_of(at, 128)
    return [
        r.copies.start(source.at[row, :, pl.ds(at, size)], target.at[pl.ds(row * L, L), pl.ds(to, size)])
        for row in range(ROWS)
        for source, target in ((r.acts, r.acts_v), (r.acts_sent, r.acts_sent_v))
    ]


def ffn_weights_body(r):
    core = r.ctl[1]
    loads = [r.copies.start(r.rows, r.rows_v)] + load_acts(r, A_HID, D, 0)
    later = load_acts(r, A_ACT + core * 2 * D, 2 * D, D)
    last = load_acts(r, A_CTX + core * HALF, HALF, 3 * D)
    halves = Halves(r, 0, FFN_ROWS // FFN_PIECES // 2)

    def product(acts_at, rows_at):
        own = tn(r.acts_v[:, acts_at], r.rows_v[:, rows_at])
        return (own + tn(r.acts_sent_v[:, acts_at], r.rows_sent[:, rows_at])).astype(bf16)

    wait_all(loads)
    for block in range(2):
        r.out_v[block_at(block)] = product(block_at(0), block_at(block))
        halves.store(block * D, D)
    wait_all(later)
    for block in range(2, 4):
        r.out_v[block_at(block)] = product(block_at(block - 1), block_at(2))
        halves.store(block * D, D)
    wait_all(last)
    r.out_v[4 * D :] = product(slice(3 * D, 3 * D + HALF), block_at(3))
    halves.store(4 * D, HALF)
    wait_all(halves.pending)


def ffn_weights(ctl, **ins):
    scratch = dict(
        rows_v=shape((ROWS * L, 4 * D)), acts_v=shape((ROWS * L, 3 * D + HALF)), acts_sent_v=shape((ROWS * L, 3 * D + HALF)),
        out_v=shape((FFN_ROWS, D)),
    )
    outs = half_outputs(FFN_ROWS, FFN_PIECES)
    return run(ffn_weights_body, ctl, ins, outs, {}, scratch, 28, 2 * 512 * 768 * FFN_ROWS, 14000000, ("rows_sent",))


def att_weights_body(r):
    core = r.ctl[1]
    half_at = pl.multiple_of(core * HALF, 128)
    loads = [r.copies.start(r.rows, r.rows_v), r.copies.start(r.table, r.table_v)]
    loads.append(r.copies.start(r.table.at[:, pl.ds(half_at, HALF)], r.table_half_v))
    loads += load_acts(r, core * D, D, 0) + load_acts(r, A_X + core * HALF, HALF, D)
    halves = Halves(r, FFN_PIECES, ATT_ROWS // ATT_PIECES // 2)
    wait_all(loads)

    def product(acts_at, rows_at, table, far_at):
        total = tn(r.acts_v[:, acts_at], r.rows_v[rows_at]) + tn(r.acts_sent_v[:, acts_at], r.rows_sent[rows_at])
        far = (r.rows_v[far_at].astype(f32) + r.rows_sent[far_at].astype(f32)).astype(bf16)
        return total, tn(table, far)

    total, far = product(slice(0, D), slice(0, 2 * L), r.table_v[...], slice(4 * L, 6 * L))
    r.out_v[:D] = (total + far * jnp.where(core == 0, 1.0, 0.0)).astype(bf16)
    halves.store(0, D)
    total, far = product(slice(D, D + HALF), slice(2 * L, 4 * L), r.table_half_v[...], slice(6 * L, 8 * L))
    r.out_v[D : D + HALF] = (total + far).astype(bf16)
    r.out_v[TAIL_AT:] = r.rows_v[8 * L :] + r.rows_sent[8 * L :]
    halves.store(D, ATT_ROWS - D)
    wait_all(halves.pending)


def att_weights(ctl, **ins):
    scratch = dict(
        rows_v=shape((SWAP_ROWS, D)), table_v=shape((2 * L, D)), table_half_v=shape((2 * L, HALF)),
        acts_v=shape((ROWS * L, D + HALF)), acts_sent_v=shape((ROWS * L, D + HALF)), out_v=shape((ATT_ROWS, D)),
    )
    outs = half_outputs(ATT_ROWS, ATT_PIECES)
    return run(att_weights_body, ctl, ins, outs, {}, scratch, 24, 2 * 768 * 768 * 1152, 8000000, ("rows_sent",))


def half_segments(layout, half_rows, piece, half):
    low = (2 * piece + half) * half_rows
    found, at = [], 0
    for target, rows, first, block in layout:
        start, stop = max(at, low), min(at + rows, low + half_rows)
        if start < stop:
            found.append((start - low, stop - start, target, first + start - at, block))
        at += rows
    return found


def assemble_body(first_piece, layouts, half_rows, pieces, kinds, r):
    start_copy = r.copies.start
    core = r.ctl[1]
    blank = None
    if first_piece > 0 and 0 in kinds:
        r.blank[...] = jnp.zeros_like(r.blank)
        rest = 2 * SPAN - REL_FROM - REL_ROWS
        blank = [
            start_copy(r.blank, r.g_rel.at[pl.ds(0, REL_FROM)]),
            start_copy(r.blank.at[pl.ds(0, rest)], r.g_rel.at[pl.ds(REL_FROM + REL_ROWS, rest)]),
        ]
    branches = []
    chunk = half_rows // 2
    items = [(piece, kind, origin) for kind in kinds for piece in range(pieces) for origin in ("own", "sent")]
    for index, (piece, kind, origin) in enumerate(items):
        array = getattr(r, f"{origin}{piece}_{kind}")
        bit = r.ctl[bit_at(first_piece + piece, origin == "sent")]
        maker = core if origin == "own" else 1 - core
        cases = [(made_by, half) for made_by in range(2) for half in range(2)]
        for at in range(0, half_rows, chunk):
            r.wide[index, at : at + chunk] = array[at : at + chunk].astype(f32)
            first_copy = last_copy = r.copies.used
            for made_by, half in cases:
                r.copies.used = first_copy
                copies = []
                for inside, count, name, start, block in half_segments(layouts[made_by], half_rows, piece, half):
                    low, high = max(inside, at), min(inside + count, at + chunk)
                    if low < high and name not in ("", "vectors"):
                        target = getattr(r, name).at[pl.ds(start + low - inside, high - low), pl.ds(block * D, D)]
                        copies.append(r.copies.make(r.wide.at[index, pl.ds(low, high - low)], target))
                last_copy = max(last_copy, r.copies.used)
                here = (maker == made_by) & (bit == (half if kind == 0 else 1 - half))
                branches.append((here, copies))

                @pl.when(here)
                def _():
                    for copy in copies:
                        copy.start()

            r.copies.used = last_copy
        for made_by, half in cases:
            for inside, count, name, _, _ in half_segments(layouts[made_by], half_rows, piece, half):
                if name == "vectors":

                    @pl.when((maker == made_by) & (bit == (half if kind == 0 else 1 - half)))
                    def _():
                        vectors = r.wide[index, inside : inside + count, :]
                        for part in range(3):
                            r.b_in_v[:, block_at(part)] = vectors[part : part + 1]
                        for part in range(4):
                            r.b_up_v[:, block_at(part)] = vectors[3 + part : 4 + part]
                        r.gains_v[...] = vectors[7:9]
                        r.biases_v[...] = vectors[9:13]
                        wait_all([
                            start_copy(r.b_in_v, r.g_b_in), start_copy(r.b_up_v, r.g_b_up),
                            start_copy(r.gains_v, r.g_gains), start_copy(r.biases_v, r.g_biases),
                        ])

    wait_all(blank or [])
    for here, copies in branches:

        @pl.when(here)
        def _():
            wait_all(copies)


def assemble(kinds, first_piece, layouts, rows, pieces, ctl, own, sent, shapes, held):
    ins = {f"own{i}_{kind}": value for kind in kinds for i, value in enumerate(own[kind])}
    ins.update({f"sent{i}_{kind}": value for kind in kinds for i, value in enumerate(sent[kind])})
    outs = {name: shape(dims, f32) for name, dims in shapes.items()}
    half_rows = rows // pieces // 2
    scratch = dict(wide=shape((len(ins), half_rows, D), f32))
    if first_piece > 0:
        scratch.update(
            blank=shape((REL_FROM, D), f32), b_in_v=shape((1, 3 * D), f32), b_up_v=shape((1, FF), f32),
            gains_v=shape((2, D), f32), biases_v=shape((4, D), f32),
        )
    body = partial(assemble_body, first_piece, layouts, half_rows, pieces, kinds)
    return run(body, ctl, ins, outs, held, scratch, 96, 0, len(ins) * half_rows * D * 6, tuple(ins), 44 * 2**20)


FFN_SHAPES = dict(g_up=(D, FF), g_down=(FF, D), g_out=(D, D))
ATT_SHAPES = dict(
    g_in=(D, 3 * D), g_rel=(2 * SPAN, D), g_abs=(ABS_ROWS, D),
    g_b_in=(1, 3 * D), g_b_up=(1, FF), g_gains=(2, D), g_biases=(4, D),
)


SQUARE = ((0, 0), (1, 0), (1, 1), (0, 1))
ROTATION = ("x0", "z0", "x1", "z1", "y")


def dp_place(index):
    return {"core": index % 2, "x": index // 2 % 4, "y": index // 8 % 2, "z": index // 16}


def dp_index(place):
    return ((place["z"] * 2 + place["y"]) * 4 + place["x"]) * 2 + place["core"]


def partner(index, dim):
    place = dp_place(index)
    if len(dim) == 2:
        bits = list(SQUARE[place[dim[0]]])
        bits[int(dim[1])] ^= 1
        place[dim[0]] = SQUARE.index(tuple(bits))
    else:
        place[dim] ^= 1
    return dp_index(place)


def swap(value, dims):
    peers = lax.axis_size("dp")
    return lax.ppermute(value, "dp", [(i, partner(i, dims[i % 2])) for i in range(peers)])


BETWEEN_CORES = ("core", "core")


def side_along(dim):
    place = dp_place(lax.axis_index("dp"))
    if dim == "y":
        return place[dim].astype(jnp.int32)
    at = place[dim[0]]
    if dim[1] == "0":
        return ((at == 1) | (at == 2)).astype(jnp.int32)
    return (at >= 2).astype(jnp.int32)


def this_core():
    return (lax.axis_index("dp") % 2).astype(jnp.int32)


def side(dims):
    return jnp.where(this_core() == 0, side_along(dims[0]), side_along(dims[1]))


def order_of(first, second):
    count = len(ROTATION)
    return [(ROTATION[(first + step) % count], ROTATION[(second + step) % count]) for step in range(count)]


ORDERS = [order_of(0, 2), order_of(1, 3), order_of(0, 4)]
SPLIT_STEPS = 3


def next_sum(chunk, dims):
    at, half = side(dims), chunk.shape[0] // 2
    received = swap(lax.dynamic_slice_in_dim(chunk, (1 - at) * half, half, 0), dims)
    return lax.dynamic_slice_in_dim(chunk, at * half, half, 0) + received


def summed_chunk(chunk, order):
    for dims in order[1:SPLIT_STEPS]:
        chunk = next_sum(chunk, dims)
    for dims in order[SPLIT_STEPS:]:
        chunk = chunk + swap(chunk, dims)
    return chunk


def summed_tail_chunk(chunk, order):
    for dims in order[1:SPLIT_STEPS]:
        chunk = next_sum(chunk, dims)
    for dims in order[SPLIT_STEPS:-1]:
        chunk = chunk + swap(chunk, dims)
    peers = lax.axis_size("dp")
    across = [(s * peers + i, (1 - s) * peers + i) for s in range(2) for i in range(peers)]
    aslant = [(s * peers + i, (1 - s) * peers + partner(i, order[-1][i % 2])) for s in range(2) for i in range(peers)]
    there = lax.ppermute(chunk, ("section", "dp"), across) + lax.ppermute(chunk, ("section", "dp"), aslant)
    chunk = chunk + swap(chunk, order[-1])
    first_row, span = 0, ATT_ROWS
    for dims in order[:SPLIT_STEPS]:
        span //= 2
        first_row = first_row + side(dims) * span
    row_at = first_row + lax.broadcasted_iota(jnp.int32, chunk.shape, 0) - TAIL_AT
    is_table = (row_at >= 0) & (row_at + this_core() * TAIL_HALF < TABLE_ROWS)
    return jnp.where(is_table, chunk + there, chunk)


def in_order(at, own, other):
    return jnp.where(
        at == 0,
        jnp.concatenate([own, other], axis=0),
        jnp.concatenate([other, own], axis=0),
    )


def gathered_half(chunk, order):
    for dims in reversed(order[1:SPLIT_STEPS]):
        chunk = in_order(side(dims), chunk, swap(chunk, dims))
    return chunk


def per_device(
    hidden_in,
    cotangent,
    segment_ids,
    positions,
    w_in,
    b_in,
    w_out,
    w_up,
    b_up,
    w_down,
    gains,
    biases,
    rel_table,
    abs_table,
):
    section = lax.axis_index("section").astype(jnp.int32)
    firsts = jnp.where(section == 1, positions[:, 0], 8 * ABS_ROWS)
    bits = [side(dims) for order in ORDERS for dims in (order[0], order[0][::-1])]
    ctl = jnp.stack([section, this_core(), firsts[0], firsts[1], *bits])
    weights = dict(w_in=w_in[0], w_out=w_out[0], w_up=w_up[0], w_down=w_down[0], gains=gains[0])
    common = dict(
        weights, hidden_in=hidden_in, segment_ids=segment_ids, biases=biases[0], b_in=b_in, b_up=b_up, abs_table=abs_table
    )

    out = forward(0, 0, ctl, dict(common, rel_table=rel_table), {})
    rel, rel_rows = out["rel"], out["rel_rows"]
    common["rel"] = rel
    received = []
    for row in range(ROWS):
        if row > 0:
            out = forward(row, 0, ctl, common, out)
        received.append(lax.ppermute(out["sent"], "section", [(0, 1)]))
    for row in range(ROWS):
        out = forward(row, 1, ctl, dict(common, received=received[row]), out)
    acts, keep, resid, section_out = out["acts"], out["keep"], out["resid"], out["section_out"]
    acts_sent = swap(acts, BETWEEN_CORES)

    common = dict(weights, cotangent=cotangent, keep=keep, resid=resid, rel=rel)
    out, received = {}, []
    for row in range(ROWS):
        out = backward(row, 1, "both", ctl, common, out)
        received.append(lax.ppermute(out["sent"], "section", [(1, 0)]))
    out.update(tables(ctl, weights["w_in"], out))
    out = backward(0, 0, "both", ctl, dict(common, received=received[0]), out)
    ffn = backward(1, 0, "ffn", ctl, dict(common, received=received[1]), out)
    ffn_pieces = ffn_weights(
        ctl, acts=acts, acts_sent=acts_sent, rows=ffn["ffn_own"], rows_sent=swap(ffn["ffn_other"], BETWEEN_CORES)
    )
    d_resid, ffn_pieces = lax.optimization_barrier((ffn["d_resid"], ffn_pieces))
    ffn_orders, att_orders = ORDERS[:FFN_PIECES], ORDERS[FFN_PIECES:]
    ffn_received = [swap(ffn_pieces[f"sent{i}"], order[0]) for i, order in enumerate(ffn_orders)]
    out = backward(1, 0, "att", ctl, dict(common, d_resid=d_resid, ffn_vec=ffn["ffn_vec"]), out)
    att_pieces = att_weights(
        ctl, acts=acts, acts_sent=acts_sent, rows=out["att_own"], rows_sent=swap(out["att_other"], BETWEEN_CORES), table=rel_rows
    )
    ffn_received, _ = lax.optimization_barrier((ffn_received, att_pieces["sent0"]))
    att_received = [swap(att_pieces[f"sent{i}"], order[0]) for i, order in enumerate(att_orders)]
    chunks = [
        summed_chunk(ffn_pieces[f"kept{i}"] + received, order)
        for i, (received, order) in enumerate(zip(ffn_received, ffn_orders))
    ]
    for i, (received, order) in enumerate(zip(att_received, att_orders)):
        summed = summed_tail_chunk if i == ATT_PIECES - 1 else summed_chunk
        chunks.append(summed(att_pieces[f"kept{i}"] + received, order))
    mine = [gathered_half(chunk, order) for chunk, order in zip(chunks, ORDERS)]
    partners = [swap(half, order[0]) for half, order in zip(mine, ORDERS)]
    ffn_halves = mine[:FFN_PIECES], partners[:FFN_PIECES]
    att_halves = mine[FFN_PIECES:], partners[FFN_PIECES:]
    ffn_halves = lax.optimization_barrier(ffn_halves)
    ffn_sent = [[swap(half, BETWEEN_CORES) for half in halves] for halves in ffn_halves]
    att_sent = [[swap(half, BETWEEN_CORES) for half in halves] for halves in att_halves]
    ffn = assemble((0, 1), 0, FFN_LAYOUT, FFN_ROWS, FFN_PIECES, ctl, ffn_halves, ffn_sent, FFN_SHAPES, {})
    att_args = FFN_PIECES, ATT_LAYOUT, ATT_ROWS, ATT_PIECES, ctl, att_halves, att_sent, ATT_SHAPES
    att = assemble((0,), *att_args, {})
    att = assemble((1,), *att_args, att)
    return (
        section_out[None],
        out["input_grad"][None],
        att["g_in"][None],
        att["g_b_in"],
        ffn["g_out"][None],
        ffn["g_up"][None],
        att["g_b_up"],
        ffn["g_down"][None],
        att["g_gains"][None],
        att["g_biases"][None],
        att["g_rel"],
        att["g_abs"],
    )


def solution(mesh):
    in_specs = (
        P("dp", None, None),
        P("dp", None, None),
        P("dp", None),
        P("dp", None),
        P("section", None, None),
        P("section", None),
        P("section", None, None),
        P("section", None, None),
        P("section", None),
        P("section", None, None),
        P("section", None, None),
        P("section", None, None),
        P(),
        P(),
    )
    out_specs = (
        P("section", "dp", None, None),
        P("section", "dp", None, None),
        P("section", None, None),
        P("section", None),
        P("section", None, None),
        P("section", None, None),
        P("section", None),
        P("section", None, None),
        P("section", None, None),
        P("section", None, None),
        P(),
        P(),
    )
    return jax.shard_map(
        per_device, mesh=mesh, in_specs=in_specs, out_specs=out_specs, check_vma=False
    )
```

```python
from functools import partial
import math
from types import SimpleNamespace

import jax
import jax.numpy as jnp
from jax import lax
from jax.experimental import pallas as pl
from jax.experimental.pallas import tpu as pltpu
from jax.sharding import PartitionSpec as P

HEADS = 12
L = 128
D = 768
FF = 3072
HALF = D // 2
PAIRS = HEADS // 2
ROWS = 2
SPAN = 256
EPS = 1e-06
NEG = -1e30
SCALE = 1.0 / math.sqrt(3 * 64)
VMEM_LIMIT = 61 * 1024 * 1024
f32, bf16 = jnp.float32, jnp.bfloat16

A_START, A_X, A_CTX, A_HID, A_ACT, A_ALL = 0, 768, 1536, 2304, 3072, 6144
K_P, K_GP, K_ALL = 2304, 3840, 6912
VECTOR_ROWS = 16
REL_FROM, REL_ROWS, ABS_ROWS, TAIL_ROWS = 128, 272, 512, 896
TABLE_ROWS = REL_ROWS + ABS_ROWS
FFN_LAYOUT = [
    [("g_up", D, 0, 2 * core), ("g_up", D, 0, 2 * core + 1), ("g_down", 2 * D, 2 * D * core, 0), ("g_out", HALF, HALF * core, 0),
     ("g_in", HALF, HALF * core, 2)]
    for core in range(2)
]
ATT_LAYOUT = [
    [("g_in", D, 0, 0), ("g_rel", REL_ROWS, REL_FROM, 0), ("g_abs", 176, 0, 0)],
    [("g_in", D, 0, 1), ("g_abs", 336, 176, 0), ("vectors", VECTOR_ROWS, 0, 0), ("", 96, 0, 0)],
]
FFN_ROWS, ATT_ROWS = 3840, 1216
FFN_PIECES, ATT_PIECES = 2, 1
TAIL_HALF = TAIL_ROWS // 2
TAIL_AT = ATT_ROWS - TAIL_HALF
SWAP_ROWS = 4 * L + TAIL_HALF

VMEM = pl.BlockSpec(memory_space=pltpu.VMEM)
ANY = pl.BlockSpec(memory_space=pl.ANY)
SMEM = pl.BlockSpec(memory_space=pltpu.SMEM)


def nn(a, b):
    return lax.dot_general(a, b, (((1,), (0,)), ((), ())), preferred_element_type=f32)


def nt(a, b):
    return lax.dot_general(a, b, (((1,), (1,)), ((), ())), preferred_element_type=f32)


def tn(a, b):
    return lax.dot_general(a, b, (((0,), (0,)), ((), ())), preferred_element_type=f32)


def norm_parts(value):
    centered = value - jnp.mean(value, axis=1, keepdims=True)
    rstd = lax.rsqrt(jnp.mean(centered * centered, axis=1, keepdims=True) + EPS)
    return centered * rstd, rstd


def norm_backward(normed, rstd, gain, grad):
    scaled = grad * gain
    mean_one = jnp.mean(scaled, axis=1, keepdims=True)
    mean_two = jnp.mean(scaled * normed, axis=1, keepdims=True)
    return (scaled - mean_one - normed * mean_two) * rstd


def column_sums(value):
    return jnp.sum(value, axis=0, keepdims=True)


def indicator(condition):
    return condition.astype(f32).astype(bf16)


def lane_halves():
    lane = lax.broadcasted_iota(jnp.int32, (1, L), 1)
    return indicator(lane < 64), indicator(lane >= 64)


def stacked(value, halves):
    return jnp.concatenate([value * halves[0], value * halves[1]], axis=0)


def skew(table):
    return pltpu.roll(table, L, 1, stride=1, stride_axis=0)[:, :L]


def unskew(turned):
    wide = jnp.concatenate([turned, jnp.zeros_like(turned)], axis=1)
    return pltpu.roll(wide, 1, 1, stride=1, stride_axis=0)


def pair_at(pair, base=0):
    return slice(base + pair * L, base + pair * L + L)


def block_at(block, base=0):
    return slice(base + block * D, base + block * D + D)


def shape(dims, dtype=bf16):
    return jax.ShapeDtypeStruct(dims, dtype)


class Copies:
    def __init__(self, sems):
        self.sems, self.used = sems, 0

    def make(self, source, target):
        self.used += 1
        return pltpu.make_async_copy(source, target, self.sems.at[self.used - 1])

    def start(self, source, target):
        copy = self.make(source, target)
        copy.start()
        return copy


def wait_all(copies):
    for copy in copies:
        copy.wait()


def run(body, ctl, ins, outs, held, scratch, copies, flops, traffic, near=(), limit=VMEM_LIMIT):
    names, out_names, scratch_names = list(ins), list(outs), list(scratch)
    kept = [name for name in out_names if name in held and name != "sent"]

    def kernel(*refs):
        ctl_ref, refs = refs[0], refs[1:]
        r = SimpleNamespace(ctl=ctl_ref, **dict(zip(names, refs)))
        refs = refs[len(names) + len(kept) :]
        for name, ref in zip(out_names + scratch_names, refs):
            setattr(r, name, ref)
        r.copies = Copies(refs[-1])
        body(r)

    results = pl.pallas_call(
        kernel,
        out_shape=tuple(outs.values()),
        in_specs=[SMEM] + [VMEM if name in near else ANY for name in names] + [ANY] * len(kept),
        out_specs=(ANY,) * len(out_names),
        input_output_aliases={1 + len(names) + i: out_names.index(name) for i, name in enumerate(kept)},
        scratch_shapes=[pltpu.VMEM(s.shape, s.dtype) for s in scratch.values()] + [pltpu.SemaphoreType.DMA((copies,))],
        compiler_params=pltpu.CompilerParams(vmem_limit_bytes=limit),
        cost_estimate=pl.CostEstimate(flops=flops, bytes_accessed=traffic, transcendentals=0),
    )(ctl, *ins.values(), *[held[name] for name in kept])
    return dict(zip(out_names, results))


def load_columns(r, source, target, parts):
    return [r.copies.start(source.at[:, block_at(part)], target.at[:, block_at(part)]) for part in range(parts)]


def load_rows(r, source, target, parts):
    return [r.copies.start(source.at[block_at(part)], target.at[block_at(part)]) for part in range(parts)]


def relative_part(r):
    loads = [r.copies.start(r.rel_table, r.table_v), r.copies.start(r.b_in, r.b_in_v), r.copies.start(r.w_in, r.wi)]
    dims = (2 * L, 2 * SPAN)
    select = indicator(lax.broadcasted_iota(jnp.int32, dims, 0) + lax.broadcasted_iota(jnp.int32, dims, 1) == L + SPAN)
    loads[0].wait()
    rows = nn(select, r.table_v[...]).astype(bf16)
    r.rel_rows_v[...] = rows
    loads[1].wait()
    loads[2].wait()
    r.rel_v[...] = (nn(rows, r.wi[:, : 2 * D]) + r.b_in_v[:, : 2 * D].astype(f32)).astype(bf16)
    return [r.copies.start(r.rel_rows_v, r.rel_rows), r.copies.start(r.rel_v, r.rel)]


def forward_body(row, section, first, r):
    start_copy = r.copies.start
    stores = relative_part(r) if first else []

    @pl.when(r.ctl[0] == section)
    def _():
        x_load = start_copy(r.hidden_in.at[row] if section == 0 else r.received, r.x_v)
        small = [start_copy(r.segment_ids, r.seg_v), start_copy(r.gains, r.gains_v), start_copy(r.biases, r.biases_v)]
        abs_load = start_copy(r.abs_table, r.table_v) if section == 1 else None
        in_loads = [] if first else [start_copy(r.b_in, r.b_in_v)] + load_columns(r, r.w_in, r.wi, 3)
        rel_load = None if first else start_copy(r.rel, r.rel_v)
        loads = [start_copy(r.w_out, r.wo), start_copy(r.b_up, r.b_up_v)]
        part_loads = [pair for pair in zip(load_columns(r, r.w_up, r.wu, 4), load_rows(r, r.w_down, r.wd, 4))]
        halves = lane_halves()
        x_load.wait()
        x = r.x_v[...]
        start = x.astype(f32)
        if section == 1:
            abs_load.wait()
            dims = (L, ABS_ROWS)
            place = lax.broadcasted_iota(jnp.int32, dims, 1) - lax.broadcasted_iota(jnp.int32, dims, 0)
            start = start + nn(indicator(place == r.ctl[2 + row]), r.table_v[...])
        query_in = start.astype(bf16)
        r.acts_v[:, block_at(0)] = query_in
        r.acts_v[:, block_at(1)] = x
        wait_all(in_loads[:2])
        b_in = r.b_in_v[...].astype(f32)
        r.keep_v[:, :D] = (nn(query_in, r.wi[:, :D]) + b_in[:, :D]).astype(bf16)
        wait_all(in_loads[2:])
        r.keep_v[:, D : 3 * D] = (nn(x, r.wi[:, D:]) + b_in[:, D:]).astype(bf16)
        wait_all(small)
        if rel_load is not None:
            rel_load.wait()
        seg_rows = jnp.broadcast_to(r.seg_v[row : row + 1, :], (L, L)).astype(f32)
        same = seg_rows == seg_rows.T
        for pair in range(PAIRS):
            query = r.keep_v[:, pair_at(pair)]
            key = r.keep_v[:, pair_at(pair, D)]
            value = r.keep_v[:, pair_at(pair, 2 * D)]
            query_two, key_two = stacked(query, halves), stacked(key, halves)
            content = nt(query_two, key)
            far_query = nt(query_two, r.rel_v[:, pair_at(pair, D)])
            far_key = nt(key_two, r.rel_v[:, pair_at(pair)])
            probs = []
            for head in range(2):
                rows = slice(head * L, head * L + L)
                summed = content[rows] + skew(far_query[rows]) + skew(far_key[rows]).T
                scores = jnp.where(same, summed * SCALE, NEG)
                exponent = jnp.exp(scores - jnp.max(scores, axis=1, keepdims=True))
                total = jnp.sum(exponent, axis=1, keepdims=True)
                probs.append((exponent * (1.0 / total)).astype(bf16))
            probs = jnp.concatenate(probs, axis=1)
            r.keep_v[:, K_P + 2 * pair * L : K_P + 2 * (pair + 1) * L] = probs
            r.acts_v[:, pair_at(pair, A_CTX)] = nn(probs, stacked(value, halves)).astype(bf16)
        wait_all(loads)
        gain = r.gains_v[...].astype(f32)
        shift = r.biases_v[...].astype(f32)
        resid_one = start + nn(r.acts_v[:, A_CTX : A_CTX + D], r.wo[...]) + shift[0:1]
        r.resid_v[:, :D] = resid_one
        hidden = norm_parts(resid_one)[0] * gain[0:1] + shift[1:2]
        hidden_low = hidden.astype(bf16)
        r.acts_v[:, A_HID : A_HID + D] = hidden_low
        early = [
            start_copy(r.acts_v.at[:, pl.ds(0, A_ACT)], r.acts.at[row, :, pl.ds(0, A_ACT)]),
            start_copy(r.keep_v.at[:, pl.ds(0, K_GP)], r.keep.at[row, :, pl.ds(0, K_GP)]),
        ]
        total = hidden + shift[2:3]
        for part in range(4):
            wait_all(part_loads[part])
            gate = nn(hidden_low, r.wu[:, block_at(part)]) + r.b_up_v[:, block_at(part)].astype(f32)
            below = 0.5 + 0.5 * lax.erf(gate * (1.0 / math.sqrt(2.0)))
            density = jnp.exp(gate * gate * -0.5) * (1.0 / math.sqrt(2.0 * math.pi))
            active = (gate * below).astype(bf16)
            r.acts_v[:, block_at(part, A_ACT)] = active
            r.keep_v[:, block_at(part, K_GP)] = (below + gate * density).astype(bf16)
            early.append(start_copy(r.acts_v.at[:, block_at(part, A_ACT)], r.acts.at[row, :, block_at(part, A_ACT)]))
            early.append(start_copy(r.keep_v.at[:, block_at(part, K_GP)], r.keep.at[row, :, block_at(part, K_GP)]))
            total = total + nn(active, r.wd[block_at(part), :])
        r.resid_v[:, D:] = total
        late = [start_copy(r.resid_v, r.resid.at[row])]
        r.x_v[...] = (norm_parts(total)[0] * gain[1:2] + shift[3:4]).astype(bf16)
        late.append(start_copy(r.x_v, r.section_out.at[row]))
        if section == 0:
            late.append(start_copy(r.x_v, r.sent))
        wait_all(early + late)

    wait_all(stores)
    if row == ROWS - 1:

        @pl.when(r.ctl[0] != section)
        def _():
            turn_weights(r)


def turn_weights(r):
    jobs = [(r.w_up, r.wu, r.w_up_t, 0, part) for part in range(4)]
    jobs += [(r.w_down, r.wd, r.w_down_t, part, 0) for part in range(4)]
    loads = [
        r.copies.start(source.at[block_at(row), block_at(column)], near.at[block_at(row), block_at(column)])
        for source, near, _, row, column in jobs
    ]
    stores = []
    for index, (load, (_, near, target, row, column)) in enumerate(zip(loads, jobs)):
        load.wait()
        r.turned_v[index] = near[block_at(row), block_at(column)].T
        stores.append(r.copies.start(r.turned_v.at[index], target.at[block_at(column), block_at(row)]))
    wait_all(stores)


def forward(row, section, ctl, ins, held):
    first = not held
    outs = {"sent": shape((L, D))} if section == 0 else {}
    if first:
        outs.update(rel_rows=shape((2 * L, D)), rel=shape((2 * L, 2 * D)))
    outs.update(
        acts=shape((ROWS, L, A_ALL)),
        keep=shape((ROWS, L, K_ALL)),
        resid=shape((ROWS, L, 2 * D), f32),
        section_out=shape((ROWS, L, D)),
    )
    scratch = dict(
        x_v=shape((L, D)), seg_v=shape((ROWS, L), jnp.int32), gains_v=shape((2, D)), biases_v=shape((4, D)),
        b_in_v=shape((1, 3 * D)), b_up_v=shape((1, FF)), table_v=shape((2 * SPAN, D)), rel_v=shape((2 * L, 2 * D)),
        wi=shape((D, 3 * D)), wo=shape((D, D)), wu=shape((D, FF)), wd=shape((FF, D)),
        acts_v=shape((L, A_ALL)), keep_v=shape((L, K_ALL)), resid_v=shape((L, 2 * D), f32),
    )
    if first:
        scratch.update(rel_rows_v=shape((2 * L, D)))
    if row == ROWS - 1:
        outs.update(w_up_t=shape((FF, D)), w_down_t=shape((D, FF)))
        scratch.update(turned_v=shape((8, D, D)))
    return run(partial(forward_body, row, section, first), ctl, ins, outs, held, scratch, 56, 1900000000, 18000000, near=())


def ffn_loads(row, section, r):
    return SimpleNamespace(
        grad=r.copies.start(r.cotangent.at[row] if section == 1 else r.received, r.grad_v),
        resid=r.copies.start(r.resid.at[row], r.resid_v),
        gains=r.copies.start(r.gains, r.gains_v),
        parts=[
            [
                r.copies.start(r.w_down_t.at[:, block_at(part)], r.wd.at[:, block_at(part)]),
                r.copies.start(r.keep.at[row, :, block_at(part, K_GP)], r.slope_v.at[:, block_at(part)]),
                r.copies.start(r.w_up_t.at[block_at(part)], r.wu.at[block_at(part)]),
            ]
            for part in range(4)
        ],
        out=r.copies.start(r.w_out, r.wo),
        probs=r.copies.start(r.keep.at[row, :, pl.ds(K_P, K_GP - K_P)], r.probs_v),
    )


def ffn_part(row, r, loads):
    wait_all([loads.grad, loads.resid, loads.gains])
    gain = r.gains_v[...].astype(f32)
    grad = r.grad_v[...].astype(f32)
    normed, rstd = norm_parts(r.resid_v[:, D:])
    r.ffn_vec_v[...] = jnp.zeros_like(r.ffn_vec_v)
    r.ffn_vec_v[8:9] = column_sums(grad * normed)
    r.ffn_vec_v[12:13] = column_sums(grad)
    d_two = norm_backward(normed, rstd, gain[1:2], grad)
    d_down = d_two.astype(bf16)
    r.ffn_v[:, FF : FF + D] = d_down
    r.ffn_vec_v[11:12] = column_sums(d_down.astype(f32))
    d_hidden = d_two
    for part in range(4):
        wait_all(loads.parts[part])
        d_gate = (nn(d_down, r.wd[:, block_at(part)]) * r.slope_v[:, block_at(part)].astype(f32)).astype(bf16)
        r.ffn_v[:, block_at(part)] = d_gate
        r.ffn_vec_v[3 + part : 4 + part] = column_sums(d_gate.astype(f32))
        d_hidden = d_hidden + nn(d_gate, r.wu[block_at(part), :])
    normed, rstd = norm_parts(r.resid_v[:, :D])
    r.ffn_vec_v[7:8] = column_sums(d_hidden * normed)
    r.ffn_vec_v[10:11] = column_sums(d_hidden)
    d_resid = norm_backward(normed, rstd, gain[0:1], d_hidden)
    d_att = d_resid.astype(bf16)
    r.ffn_v[:, FF + D : FF + 2 * D] = d_att
    r.ffn_vec_v[9:10] = column_sums(d_att.astype(f32))
    loads.out.wait()
    r.context_v[...] = nt(d_att, r.wo[...]).astype(bf16)
    loads.probs.wait()
    halves = lane_halves()
    for pair in range(PAIRS):
        d_value = tn(two_heads(r.probs_v, pair), stacked(r.context_v[:, pair_at(pair)], halves))
        r.ffn_v[:, pair_at(pair, FF + 2 * D)] = d_value.astype(bf16)
    r.ffn_vec_v[2:3] = column_sums(r.ffn_v[:, FF + 2 * D :].astype(f32))
    stores, rows = [], pl.ds(row * L, L)
    for side_core, target in ((r.ctl[1], r.ffn_own), (1 - r.ctl[1], r.ffn_other)):
        gates = pl.ds(pl.multiple_of(side_core * 2 * D, 128), 2 * D)
        stores.append(r.copies.start(r.ffn_v.at[:, gates], target.at[rows, pl.ds(0, 2 * D)]))
        stores.append(r.copies.start(r.ffn_v.at[:, pl.ds(FF, 3 * D)], target.at[rows, pl.ds(2 * D, 3 * D)]))
    stores.append(r.copies.start(r.ffn_vec_v, r.ffn_vec.at[row]))
    return d_resid, stores


def two_heads(probs, pair):
    columns = probs[:, 2 * pair * L : 2 * (pair + 1) * L]
    return jnp.concatenate([columns[:, :L], columns[:, L:]], axis=0)


def att_loads(row, section, r):
    return SimpleNamespace(
        keep=r.copies.start(r.keep.at[row, :, pl.ds(0, K_P)], r.keep_v),
        rel=r.copies.start(r.rel, r.rel_v),
        earlier=r.copies.start(r.d_rel, r.d_rel_old) if row > 0 else None,
        w_in=r.copies.start(r.w_in, r.wi),
        others=[
            r.copies.start(r.d_start.at[0], r.others_v),
            r.copies.start(r.att_vec.at[0], r.att_vec_old),
            r.copies.start(r.ffn_vec, r.ffn_vec_v),
        ]
        if row == ROWS - 1 and section == 0
        else [],
    )


def att_part(row, section, r, loads, d_resid):
    halves = lane_halves()
    row_at = lax.broadcasted_iota(jnp.int32, (L, L), 0)
    column_at = lax.broadcasted_iota(jnp.int32, (L, L), 1)
    turn = indicator(row_at + column_at == L - 1)
    r.att_vec_v[...] = jnp.zeros_like(r.att_vec_v)
    loads.keep.wait()
    loads.rel.wait()
    for pair in range(PAIRS):
        query = r.keep_v[:, pair_at(pair)]
        key = r.keep_v[:, pair_at(pair, D)]
        value = r.keep_v[:, pair_at(pair, 2 * D)]
        probs_two = two_heads(r.probs_v, pair)
        rel_q, rel_k = r.rel_v[:, pair_at(pair)], r.rel_v[:, pair_at(pair, D)]
        context_two = stacked(r.context_v[:, pair_at(pair)], halves)
        probs_f = probs_two.astype(f32)
        weighted = nt(context_two, value) * probs_f
        d_scores = (weighted - probs_f * jnp.sum(weighted, axis=1, keepdims=True)).astype(bf16)
        query_two, key_two = stacked(query, halves), stacked(key, halves)
        d_key = tn(d_scores, query_two)
        d_side = jnp.concatenate([d_scores[:L], d_scores[L:]], axis=1)
        d_query = nn(d_side, key_two)
        d_far = (d_side.astype(f32) * SCALE).astype(bf16)
        query_turned = nn(turn, query).astype(bf16)
        key_turned = nn(turn, key).astype(bf16)
        rows_turned = nn(turn, d_far)
        far_query, far_key = [], []
        for head in range(2):
            columns = slice(head * L, head * L + L)
            far_query.append(unskew(rows_turned[:, columns]).astype(bf16))
            far_key.append(unskew(nt(turn, d_far[:, columns])).astype(bf16))
        d_query_turned = nn(jnp.concatenate(far_query, axis=1), stacked(rel_k, halves))
        d_key_turned = nn(jnp.concatenate(far_key, axis=1), stacked(rel_q, halves))
        r.d_rel_v[:, pair_at(pair)] = tn(jnp.concatenate(far_key, axis=0), stacked(key_turned, halves))
        r.d_rel_v[:, pair_at(pair, D)] = tn(jnp.concatenate(far_query, axis=0), stacked(query_turned, halves))
        d_query = d_query * SCALE + nn(turn, d_query_turned.astype(bf16))
        d_key = d_key * SCALE + nn(turn, d_key_turned.astype(bf16))
        r.att_v[:, pair_at(pair)] = d_query.astype(bf16)
        r.att_v[:, pair_at(pair, D)] = d_key.astype(bf16)
    stores = []
    for side_core, target in ((r.ctl[1], r.att_own), (1 - r.ctl[1], r.att_other)):
        query_or_key = pl.ds(pl.multiple_of(side_core * D, 128), D)
        stores.append(r.copies.start(r.att_v.at[:, query_or_key], target.at[pl.ds(row * L, L)]))
    loads.w_in.wait()
    d_start = d_resid + nt(r.att_v[:, :D], r.wi[:, :D])
    r.start_v[...] = d_start.astype(bf16)
    stores.append(r.copies.start(r.start_v, r.d_start.at[row]))
    result = d_start + nt(r.att_v[:, D:], r.wi[:, D : 2 * D]) + nt(r.value_v[...], r.wi[:, 2 * D :])
    r.grad_out_v[...] = result.astype(bf16)
    stores.append(r.copies.start(r.grad_out_v, r.input_grad.at[row]))
    if section == 1:
        stores.append(r.copies.start(r.grad_out_v, r.sent))
    for part in range(2):
        rows = column_sums(r.att_v[:, block_at(part)].astype(f32)) + column_sums(r.d_rel_v[:, block_at(part)])
        r.att_vec_v[part : part + 1] = rows
    stores.append(r.copies.start(r.att_vec_v, r.att_vec.at[row]))
    if row > 0:
        loads.earlier.wait()
        r.d_rel_v[...] = r.d_rel_v[...] + r.d_rel_old[...]
    if row < ROWS - 1:
        stores.append(r.copies.start(r.d_rel_v, r.d_rel))
        return stores
    r.rel_low[...] = r.d_rel_v[...].astype(bf16)
    for side_core, target in ((r.ctl[1], r.att_own), (1 - r.ctl[1], r.att_other)):
        query_or_key = pl.ds(pl.multiple_of(side_core * D, 128), D)
        stores.append(r.copies.start(r.rel_low.at[:, query_or_key], target.at[pl.ds(2 * L, 2 * L)]))
    if section == 0:
        wait_all(loads.others)
        stores += tail_part(
            r, [r.others_v[...], r.start_v[...]], r.ffn_vec_v[0] + r.ffn_vec_v[1] + r.att_vec_old[...] + r.att_vec_v[...]
        )
    else:
        stores.append(r.copies.start(r.rel_low, r.d_rel_low))
    return stores


def tail_part(r, starts, vectors):
    def put(first, rows, value):
        r.tail_v[first : first + rows] = value.astype(bf16)

    dims = (ABS_ROWS, L)
    place = lax.broadcasted_iota(jnp.int32, dims, 0) - lax.broadcasted_iota(jnp.int32, dims, 1)
    spots = [indicator(place == r.ctl[2 + row]) for row in range(ROWS)]
    put(REL_ROWS, ABS_ROWS, nn(spots[0], starts[0]) + nn(spots[1], starts[1]))
    put(TABLE_ROWS, VECTOR_ROWS, vectors)
    rest = TAIL_ROWS - TABLE_ROWS - VECTOR_ROWS
    put(TABLE_ROWS + VECTOR_ROWS, rest, jnp.zeros((rest, D), f32))
    rows = nt(r.rel_low[...], r.wi[:, : 2 * D]).astype(bf16)
    dims = (REL_ROWS, 2 * L)
    select = lax.broadcasted_iota(jnp.int32, dims, 0) + lax.broadcasted_iota(jnp.int32, dims, 1) == L + SPAN - REL_FROM
    put(0, REL_ROWS, nn(indicator(select), rows))
    return [
        r.copies.start(
            r.tail_v.at[pl.ds(pl.multiple_of(side_core * TAIL_HALF, 16), TAIL_HALF)], target.at[pl.ds(4 * L, TAIL_HALF)]
        )
        for side_core, target in ((r.ctl[1], r.att_own), (1 - r.ctl[1], r.att_other))
    ]


def backward_body(row, section, parts, r):
    @pl.when(r.ctl[0] == section)
    def _():
        if parts == "ffn":
            d_resid, stores = ffn_part(row, r, ffn_loads(row, section, r))
            r.resid_v[:, :D] = d_resid
            stores.append(r.copies.start(r.resid_v.at[:, pl.ds(0, D)], r.d_resid))
            stores.append(r.copies.start(r.context_v, r.d_context.at[:, pl.ds(0, D)]))
            stores.append(r.copies.start(r.ffn_v.at[:, pl.ds(FF + 2 * D, D)], r.d_context.at[:, pl.ds(D, D)]))
        elif parts == "att":
            first = [
                r.copies.start(r.d_resid, r.d_resid_v),
                r.copies.start(r.d_context.at[:, pl.ds(0, D)], r.context_v),
                r.copies.start(r.keep.at[row, :, pl.ds(K_P, K_GP - K_P)], r.probs_v),
                r.copies.start(r.d_context.at[:, pl.ds(D, D)], r.value_v),
            ]
            loads = att_loads(row, section, r)
            wait_all(first)
            stores = att_part(row, section, r, loads, r.d_resid_v[...])
        else:
            loads = ffn_loads(row, section, r)
            later = att_loads(row, section, r)
            d_resid, stores = ffn_part(row, r, loads)
            r.value_v[...] = r.ffn_v[:, FF + 2 * D :]
            stores = stores + att_part(row, section, r, later, d_resid)
        wait_all(stores)


def backward(row, section, parts, ctl, ins, held):
    outs, scratch, flops, traffic = {}, {}, 0, 0
    if parts == "ffn":
        outs.update(d_resid=shape((L, D), f32), d_context=shape((L, 2 * D)))
    if parts != "att":
        outs.update(
            ffn_own=shape((ROWS * L, 5 * D)), ffn_other=shape((ROWS * L, 5 * D)), ffn_vec=shape((ROWS, VECTOR_ROWS, D), f32)
        )
        scratch.update(
            grad_v=shape((L, D)), resid_v=shape((L, 2 * D), f32), gains_v=shape((2, D)), slope_v=shape((L, FF)),
            wu=shape((FF, D)), wd=shape((D, FF)), ffn_v=shape((L, FF + 3 * D)), wo=shape((D, D)), probs_v=shape((L, 2 * D)), context_v=shape((L, D)), ffn_vec_v=shape((VECTOR_ROWS, D), f32),
        )
        flops, traffic = flops + 1300000000, traffic + 12000000
    if parts == "att":
        scratch.update(d_resid_v=shape((L, D), f32), context_v=shape((L, D)), probs_v=shape((L, 2 * D)))
    if parts != "ffn":
        if section == 1:
            outs.update(sent=shape((L, D)))
        outs.update(
            att_own=shape((SWAP_ROWS, D)), att_other=shape((SWAP_ROWS, D)), att_vec=shape((ROWS, VECTOR_ROWS, D), f32),
            d_start=shape((ROWS, L, D)), d_rel=shape((2 * L, 2 * D), f32), d_rel_low=shape((2 * L, 2 * D)),
            input_grad=shape((ROWS, L, D)),
        )
        scratch.update(
            wi=shape((D, 3 * D)), keep_v=shape((L, K_P)), rel_v=shape((2 * L, 2 * D)),
            att_v=shape((L, 2 * D)), att_vec_v=shape((VECTOR_ROWS, D), f32), start_v=shape((L, D)), grad_out_v=shape((L, D)),
            value_v=shape((L, D)), d_rel_v=shape((2 * L, 2 * D), f32), d_rel_old=shape((2 * L, 2 * D), f32), rel_low=shape((2 * L, 2 * D)),
        )
        if row == ROWS - 1 and section == 0:
            scratch.update(
                tail_v=shape((TAIL_ROWS, D)),
                others_v=shape((L, D)), att_vec_old=shape((VECTOR_ROWS, D), f32), ffn_vec_v=shape((ROWS, VECTOR_ROWS, D), f32),
            )
        flops, traffic = flops + 1100000000, traffic + 8000000
    return run(partial(backward_body, row, section, parts), ctl, ins, outs, held, scratch, 56, flops, traffic, near=())


def tables_body(r):
    @pl.when(r.ctl[0] == 1)
    def _():
        loads = [
            r.copies.start(source, target)
            for source, target in (
                (r.d_start, r.start_v), (r.ffn_vec, r.ffn_vec_v), (r.att_vec, r.att_vec_v), (r.d_rel_low, r.rel_low), (r.w_in, r.wi)
            )
        ]
        wait_all(loads)
        vectors = r.ffn_vec_v[0] + r.ffn_vec_v[1] + r.att_vec_v[0] + r.att_vec_v[1]
        wait_all(tail_part(r, [r.start_v[0], r.start_v[1]], vectors))


def tables(ctl, w_in, held):
    ins = dict(w_in=w_in, **{name: held[name] for name in ("d_start", "ffn_vec", "att_vec", "d_rel_low")})
    outs = dict(att_own=shape((SWAP_ROWS, D)), att_other=shape((SWAP_ROWS, D)))
    scratch = dict(
        start_v=shape((ROWS, L, D)), ffn_vec_v=shape((ROWS, VECTOR_ROWS, D), f32), att_vec_v=shape((ROWS, VECTOR_ROWS, D), f32),
        rel_low=shape((2 * L, 2 * D)), wi=shape((D, 3 * D)), tail_v=shape((TAIL_ROWS, D)),
    )
    return run(tables_body, ctl, ins, outs, held, scratch, 8, 1000000000, 7000000)


class Halves:
    def __init__(self, r, first_piece, half_rows):
        self.r, self.first_piece, self.half_rows, self.pending = r, first_piece, half_rows, []

    def store(self, first, rows):
        while rows > 0:
            index, inside = divmod(first, self.half_rows)
            count = min(rows, self.half_rows - inside)
            piece, half = index // 2, index % 2
            view, there = self.r.out_v.at[pl.ds(first, count)], pl.ds(inside, count)
            kept = self.r.copies.make(view, getattr(self.r, f"kept{piece}").at[there])
            sem = self.r.copies.sems.at[self.r.copies.used - 1]
            sent = pltpu.make_async_copy(view, getattr(self.r, f"sent{piece}").at[there], sem)
            mine = self.r.ctl[bit_at(self.first_piece + piece, False)] == half

            @pl.when(mine)
            def _():
                kept.start()

            @pl.when(jnp.logical_not(mine))
            def _():
                sent.start()

            self.pending.append(kept)
            first, rows = first + count, rows - count


def bit_at(piece, of_other_core):
    return 4 + 2 * piece + int(of_other_core)


def half_outputs(rows, pieces):
    half_rows = rows // pieces // 2
    return {f"{kind}{piece}": shape((half_rows, D)) for piece in range(pieces) for kind in ("kept", "sent")}


def load_acts(r, at, size, to):
    if not isinstance(at, int):
        at = pl.multiple_of(at, 128)
    return [
        r.copies.start(source.at[row, :, pl.ds(at, size)], target.at[pl.ds(row * L, L), pl.ds(to, size)])
        for row in range(ROWS)
        for source, target in ((r.acts, r.acts_v), (r.acts_sent, r.acts_sent_v))
    ]


def ffn_weights_body(r):
    core = r.ctl[1]
    loads = [r.copies.start(r.rows, r.rows_v)] + load_acts(r, A_HID, D, 0)
    later = load_acts(r, A_ACT + core * 2 * D, 2 * D, D)
    last = load_acts(r, A_CTX + core * HALF, HALF, 3 * D) + load_acts(r, A_X + core * HALF, HALF, 3 * D + HALF)
    halves = Halves(r, 0, FFN_ROWS // FFN_PIECES // 2)

    def product(acts_at, rows_at):
        own = tn(r.acts_v[:, acts_at], r.rows_v[:, rows_at])
        return (own + tn(r.acts_sent_v[:, acts_at], r.rows_sent[:, rows_at])).astype(bf16)

    wait_all(loads)
    for block in range(2):
        r.out_v[block_at(block)] = product(block_at(0), block_at(block))
        halves.store(block * D, D)
    wait_all(later)
    for block in range(2, 4):
        r.out_v[block_at(block)] = product(block_at(block - 1), block_at(2))
        halves.store(block * D, D)
    wait_all(last)
    for part in range(2):
        to = slice(4 * D + part * HALF, 4 * D + (part + 1) * HALF)
        r.out_v[to] = product(slice(3 * D + part * HALF, 3 * D + (part + 1) * HALF), block_at(3 + part))
    halves.store(4 * D, D)
    wait_all(halves.pending)


def ffn_weights(ctl, **ins):
    scratch = dict(
        rows_v=shape((ROWS * L, 5 * D)), acts_v=shape((ROWS * L, 4 * D)), acts_sent_v=shape((ROWS * L, 4 * D)),
        out_v=shape((FFN_ROWS, D)),
    )
    outs = half_outputs(FFN_ROWS, FFN_PIECES)
    return run(ffn_weights_body, ctl, ins, outs, {}, scratch, 36, 2 * 512 * 768 * FFN_ROWS, 14000000, ("rows_sent",))


def att_weights_body(r):
    loads = [r.copies.start(r.rows, r.rows_v), r.copies.start(r.table, r.table_v)]
    loads += load_acts(r, r.ctl[1] * D, D, 0)
    halves = Halves(r, FFN_PIECES, ATT_ROWS // ATT_PIECES // 2)
    wait_all(loads)
    total = tn(r.acts_v[...], r.rows_v[: 2 * L]) + tn(r.acts_sent_v[...], r.rows_sent[: 2 * L])
    far = (r.rows_v[2 * L : 4 * L].astype(f32) + r.rows_sent[2 * L : 4 * L].astype(f32)).astype(bf16)
    r.out_v[:D] = (total + tn(r.table_v[...], far)).astype(bf16)
    r.out_v[TAIL_AT:] = r.rows_v[4 * L :] + r.rows_sent[4 * L :]
    halves.store(0, ATT_ROWS)
    wait_all(halves.pending)


def att_weights(ctl, **ins):
    scratch = dict(
        rows_v=shape((SWAP_ROWS, D)), table_v=shape((2 * L, D)),
        acts_v=shape((ROWS * L, D)), acts_sent_v=shape((ROWS * L, D)), out_v=shape((ATT_ROWS, D)),
    )
    outs = half_outputs(ATT_ROWS, ATT_PIECES)
    return run(att_weights_body, ctl, ins, outs, {}, scratch, 16, 2 * 768 * 768 * 768, 6000000, ("rows_sent",))


def half_segments(layout, half_rows, piece, half):
    low = (2 * piece + half) * half_rows
    found, at = [], 0
    for target, rows, first, block in layout:
        start, stop = max(at, low), min(at + rows, low + half_rows)
        if start < stop:
            found.append((start - low, stop - start, target, first + start - at, block))
        at += rows
    return found


def assemble_body(kind, first_piece, layouts, half_rows, pieces, r):
    start_copy = r.copies.start
    core = r.ctl[1]
    blank = None
    if first_piece > 0 and kind == 0:
        r.blank[...] = jnp.zeros_like(r.blank)
        rest = 2 * SPAN - REL_FROM - REL_ROWS
        blank = [
            start_copy(r.blank, r.g_rel.at[pl.ds(0, REL_FROM)]),
            start_copy(r.blank.at[pl.ds(0, rest)], r.g_rel.at[pl.ds(REL_FROM + REL_ROWS, rest)]),
        ]
    branches = []
    chunk = half_rows // 2
    items = [(piece, origin) for piece in range(pieces) for origin in ("own", "sent")]
    for index, (piece, origin) in enumerate(items):
        array = getattr(r, f"{origin}{piece}")
        bit = r.ctl[bit_at(first_piece + piece, origin == "sent")]
        maker = core if origin == "own" else 1 - core
        cases = [(made_by, half) for made_by in range(2) for half in range(2)]
        for at in range(0, half_rows, chunk):
            r.wide[index, at : at + chunk] = array[at : at + chunk].astype(f32)
            first_copy = last_copy = r.copies.used
            for made_by, half in cases:
                r.copies.used = first_copy
                copies = []
                for inside, count, name, start, block in half_segments(layouts[made_by], half_rows, piece, half):
                    low, high = max(inside, at), min(inside + count, at + chunk)
                    if low < high and name not in ("", "vectors"):
                        target = getattr(r, name).at[pl.ds(start + low - inside, high - low), pl.ds(block * D, D)]
                        copies.append(r.copies.make(r.wide.at[index, pl.ds(low, high - low)], target))
                last_copy = max(last_copy, r.copies.used)
                here = (maker == made_by) & (bit == (half if kind == 0 else 1 - half))
                branches.append((here, copies))

                @pl.when(here)
                def _():
                    for copy in copies:
                        copy.start()

            r.copies.used = last_copy
        for made_by, half in cases:
            for inside, count, name, _, _ in half_segments(layouts[made_by], half_rows, piece, half):
                if name == "vectors":

                    @pl.when((maker == made_by) & (bit == (half if kind == 0 else 1 - half)))
                    def _():
                        vectors = r.wide[index, inside : inside + count, :]
                        for part in range(3):
                            r.b_in_v[:, block_at(part)] = vectors[part : part + 1]
                        for part in range(4):
                            r.b_up_v[:, block_at(part)] = vectors[3 + part : 4 + part]
                        r.gains_v[...] = vectors[7:9]
                        r.biases_v[...] = vectors[9:13]
                        wait_all([
                            start_copy(r.b_in_v, r.g_b_in), start_copy(r.b_up_v, r.g_b_up),
                            start_copy(r.gains_v, r.g_gains), start_copy(r.biases_v, r.g_biases),
                        ])

    wait_all(blank or [])
    for here, copies in branches:

        @pl.when(here)
        def _():
            wait_all(copies)


def assemble(kind, first_piece, layouts, rows, pieces, ctl, own, sent, shapes, held):
    ins = {f"own{i}": value for i, value in enumerate(own)}
    ins.update({f"sent{i}": value for i, value in enumerate(sent)})
    outs = {name: shape(dims, f32) for name, dims in shapes.items()}
    half_rows = rows // pieces // 2
    scratch = dict(wide=shape((len(ins), half_rows, D), f32))
    if first_piece > 0:
        scratch.update(
            blank=shape((REL_FROM, D), f32), b_in_v=shape((1, 3 * D), f32), b_up_v=shape((1, FF), f32),
            gains_v=shape((2, D), f32), biases_v=shape((4, D), f32),
        )
    body = partial(assemble_body, kind, first_piece, layouts, half_rows, pieces)
    return run(body, ctl, ins, outs, held, scratch, 96, 0, len(ins) * half_rows * D * 6, tuple(ins), 44 * 2**20)


FFN_SHAPES = dict(g_up=(D, FF), g_down=(FF, D), g_out=(D, D), g_in=(D, 3 * D))
ATT_SHAPES = dict(
    g_in=(D, 3 * D), g_rel=(2 * SPAN, D), g_abs=(ABS_ROWS, D),
    g_b_in=(1, 3 * D), g_b_up=(1, FF), g_gains=(2, D), g_biases=(4, D),
)


SQUARE = ((0, 0), (1, 0), (1, 1), (0, 1))


def dp_place(index):
    return {"core": index % 2, "x": index // 2 % 4, "y": index // 8 % 2, "z": index // 16}


def dp_index(place):
    return ((place["z"] * 2 + place["y"]) * 4 + place["x"]) * 2 + place["core"]


def partner(index, dim):
    place = dp_place(index)
    if len(dim) == 2:
        bits = list(SQUARE[place[dim[0]]])
        bits[int(dim[1])] ^= 1
        place[dim[0]] = SQUARE.index(tuple(bits))
    else:
        place[dim] ^= 1
    return dp_index(place)


def swap(value, dims):
    peers = lax.axis_size("dp")
    return lax.ppermute(value, "dp", [(i, partner(i, dims[i % 2])) for i in range(peers)])


BETWEEN_CORES = ("core", "core")


def side_along(dim):
    place = dp_place(lax.axis_index("dp"))
    if dim == "y":
        return place[dim].astype(jnp.int32)
    at = place[dim[0]]
    if dim[1] == "0":
        return ((at == 1) | (at == 2)).astype(jnp.int32)
    return (at >= 2).astype(jnp.int32)


def this_core():
    return (lax.axis_index("dp") % 2).astype(jnp.int32)


def side(dims):
    return jnp.where(this_core() == 0, side_along(dims[0]), side_along(dims[1]))


ORDERS = [
    [("z1", "z0"), ("z0", "x0"), ("x0", "x1"), ("y", "z1"), ("x1", "y")],
    [("x0", "y"), ("y", "z1"), ("x1", "z0"), ("z0", "x1"), ("z1", "x0")],
    [("x1", "x1"), ("y", "z1"), ("x0", "y"), ("z0", "x0"), ("z1", "z0")],
]
SPLIT_STEPS = 3


def next_sum(chunk, dims):
    at, half = side(dims), chunk.shape[0] // 2
    received = swap(lax.dynamic_slice_in_dim(chunk, (1 - at) * half, half, 0), dims)
    return lax.dynamic_slice_in_dim(chunk, at * half, half, 0) + received


def summed_chunk(chunk, order):
    for dims in order[1:SPLIT_STEPS]:
        chunk = next_sum(chunk, dims)
    for dims in order[SPLIT_STEPS:]:
        chunk = chunk + swap(chunk, dims)
    return chunk


def add_tables_of_both_sections(chunk, order):
    first_row, span = ATT_ROWS - ATT_ROWS // ATT_PIECES, ATT_ROWS // ATT_PIECES
    for dims in order[:SPLIT_STEPS]:
        span //= 2
        first_row = first_row + side(dims) * span
    row_at = first_row + lax.broadcasted_iota(jnp.int32, chunk.shape, 0) - TAIL_AT
    is_table = (row_at >= 0) & (row_at + this_core() * TAIL_HALF < TABLE_ROWS)
    elsewhere = lax.ppermute(chunk, "section", [(0, 1), (1, 0)])
    return jnp.where(is_table, chunk + elsewhere, chunk)


def in_order(at, own, other):
    return jnp.where(
        at == 0,
        jnp.concatenate([own, other], axis=0),
        jnp.concatenate([other, own], axis=0),
    )


def gathered_half(chunk, order):
    for dims in reversed(order[1:SPLIT_STEPS]):
        chunk = in_order(side(dims), chunk, swap(chunk, dims))
    return chunk


def per_device(
    hidden_in,
    cotangent,
    segment_ids,
    positions,
    w_in,
    b_in,
    w_out,
    w_up,
    b_up,
    w_down,
    gains,
    biases,
    rel_table,
    abs_table,
):
    section = lax.axis_index("section").astype(jnp.int32)
    firsts = jnp.where(section == 1, positions[:, 0], 8 * ABS_ROWS)
    bits = [side(dims) for order in ORDERS for dims in (order[0], order[0][::-1])]
    ctl = jnp.stack([section, this_core(), firsts[0], firsts[1], *bits])
    weights = dict(w_in=w_in[0], w_out=w_out[0], w_up=w_up[0], w_down=w_down[0], gains=gains[0])
    common = dict(
        weights, hidden_in=hidden_in, segment_ids=segment_ids, biases=biases[0], b_in=b_in, b_up=b_up, abs_table=abs_table
    )

    out = forward(0, 0, ctl, dict(common, rel_table=rel_table), {})
    rel, rel_rows = out["rel"], out["rel_rows"]
    common["rel"] = rel
    received = []
    for row in range(ROWS):
        if row > 0:
            out = forward(row, 0, ctl, common, out)
        received.append(lax.ppermute(out["sent"], "section", [(0, 1)]))
    for row in range(ROWS):
        out = forward(row, 1, ctl, dict(common, received=received[row]), out)
    acts, keep, resid, section_out = out["acts"], out["keep"], out["resid"], out["section_out"]
    acts_sent = swap(acts, BETWEEN_CORES)

    turned = dict(w_up_t=out["w_up_t"], w_down_t=out["w_down_t"])
    common = dict(weights, **turned, cotangent=cotangent, keep=keep, resid=resid, rel=rel)
    out, received = {}, []
    for row in range(ROWS):
        out = backward(row, 1, "both", ctl, common, out)
        received.append(lax.ppermute(out["sent"], "section", [(1, 0)]))
    out.update(tables(ctl, weights["w_in"], out))
    out = backward(0, 0, "both", ctl, dict(common, received=received[0]), out)
    ffn = backward(1, 0, "ffn", ctl, dict(common, received=received[1]), out)
    ffn_orders, att_orders = ORDERS[:FFN_PIECES], ORDERS[FFN_PIECES:]
    ffn_sent_rows = swap(ffn["ffn_other"], BETWEEN_CORES)
    d_resid = ffn["d_resid"]
    ffn_pieces = ffn_weights(ctl, acts=acts, acts_sent=acts_sent, rows=ffn["ffn_own"], rows_sent=ffn_sent_rows)
    out = backward(1, 0, "att", ctl, dict(common, d_resid=d_resid, d_context=ffn["d_context"], ffn_vec=ffn["ffn_vec"]), out)
    att_other = out["att_other"]
    rows_sent = swap(att_other, BETWEEN_CORES)
    ffn_received = [swap(ffn_pieces[f"sent{i}"], order[0]) for i, order in enumerate(ffn_orders)]
    att_pieces = att_weights(ctl, acts=acts, acts_sent=acts_sent, rows=out["att_own"], rows_sent=rows_sent, table=rel_rows)
    att_received = [swap(att_pieces[f"sent{i}"], order[0]) for i, order in enumerate(att_orders)]
    chunks = [
        summed_chunk(ffn_pieces[f"kept{i}"] + received, order)
        for i, (received, order) in enumerate(zip(ffn_received, ffn_orders))
    ]
    att_chunks = [
        summed_chunk(att_pieces[f"kept{i}"] + received, order)
        for i, (received, order) in enumerate(zip(att_received, att_orders))
    ]
    att_chunks[-1] = add_tables_of_both_sections(att_chunks[-1], ORDERS[-1])
    chunks = chunks + att_chunks
    n = FFN_PIECES
    ffn_args = 0, FFN_LAYOUT, FFN_ROWS, FFN_PIECES, ctl
    att_args = FFN_PIECES, ATT_LAYOUT, ATT_ROWS, ATT_PIECES, ctl
    held = chunks[n:]
    mine = [gathered_half(chunk, order) for chunk, order in zip(chunks[:n], ORDERS)]
    partners = [swap(half, order[0]) for half, order in zip(mine, ORDERS)]
    held = [in_order(side(order[2]), chunk, swap(chunk, order[2])) for chunk, order in zip(held, att_orders)]
    held = [in_order(side(order[1]), chunk, swap(chunk, order[1])) for chunk, order in zip(held, att_orders)]
    held, mine = lax.optimization_barrier((held, mine))
    mine = mine + held
    partners = partners + [swap(half, order[0]) for half, order in zip(held, att_orders)]
    mine_sent = [swap(half, BETWEEN_CORES) for half in mine]
    ffn = assemble(0, *ffn_args, mine[:n], mine_sent[:n], FFN_SHAPES, {})
    partners[:n], ffn = lax.optimization_barrier((partners[:n], ffn))
    partners_sent = [swap(half, BETWEEN_CORES) for half in partners]
    ffn = assemble(1, *ffn_args, partners[:n], partners_sent[:n], FFN_SHAPES, ffn)
    att = assemble(0, *att_args, mine[n:], mine_sent[n:], ATT_SHAPES, dict(g_in=ffn["g_in"]))
    att = assemble(1, *att_args, partners[n:], partners_sent[n:], ATT_SHAPES, att)
    return (
        section_out[None],
        out["input_grad"][None],
        att["g_in"][None],
        att["g_b_in"],
        ffn["g_out"][None],
        ffn["g_up"][None],
        att["g_b_up"],
        ffn["g_down"][None],
        att["g_gains"][None],
        att["g_biases"][None],
        att["g_rel"],
        att["g_abs"],
    )


def solution(mesh):
    in_specs = (
        P("dp", None, None),
        P("dp", None, None),
        P("dp", None),
        P("dp", None),
        P("section", None, None),
        P("section", None),
        P("section", None, None),
        P("section", None, None),
        P("section", None),
        P("section", None, None),
        P("section", None, None),
        P("section", None, None),
        P(),
        P(),
    )
    out_specs = (
        P("section", "dp", None, None),
        P("section", "dp", None, None),
        P("section", None, None),
        P("section", None),
        P("section", None, None),
        P("section", None, None),
        P("section", None),
        P("section", None, None),
        P("section", None, None),
        P("section", None, None),
        P(),
        P(),
    )
    return jax.shard_map(
        per_device, mesh=mesh, in_specs=in_specs, out_specs=out_specs, check_vma=False
    )
```

```python
from functools import partial
import math
from types import SimpleNamespace

import jax
import jax.numpy as jnp
from jax import lax
from jax.experimental import pallas as pl
from jax.experimental.pallas import tpu as pltpu
from jax.sharding import PartitionSpec as P

HEADS = 12
L = 128
D = 768
FF = 3072
HALF = D // 2
PAIRS = HEADS // 2
ROWS = 2
SPAN = 256
EPS = 1e-06
NEG = -1e30
SCALE = 1.0 / math.sqrt(3 * 64)
VMEM_LIMIT = 61 * 1024 * 1024
f32, bf16 = jnp.float32, jnp.bfloat16

A_START, A_X, A_CTX, A_HID, A_ACT, A_ALL = 0, 768, 1536, 2304, 3072, 6144
K_P, K_GP, K_ALL = 2304, 3840, 6912
VECTOR_ROWS = 16
REL_FROM, REL_ROWS, ABS_ROWS, TAIL_ROWS = 128, 272, 512, 896
TABLE_ROWS = REL_ROWS + ABS_ROWS
FFN_LAYOUT = [
    [("g_up", D, 0, 2 * core), ("g_up", D, 0, 2 * core + 1), ("g_down", 2 * D, 2 * D * core, 0), ("g_out", HALF, HALF * core, 0),
     ("g_in", HALF, HALF * core, 2)]
    for core in range(2)
]
ATT_LAYOUT = [
    [("g_in", D, 0, 0), ("g_rel", REL_ROWS, REL_FROM, 0), ("g_abs", 176, 0, 0)],
    [("g_in", D, 0, 1), ("g_abs", 336, 176, 0), ("vectors", VECTOR_ROWS, 0, 0), ("", 96, 0, 0)],
]
FFN_ROWS, ATT_ROWS = 3840, 1216
FFN_PIECES, ATT_PIECES = 2, 1
TAIL_HALF = TAIL_ROWS // 2
TAIL_AT = ATT_ROWS - TAIL_HALF
SWAP_ROWS = 4 * L + TAIL_HALF

VMEM = pl.BlockSpec(memory_space=pltpu.VMEM)
ANY = pl.BlockSpec(memory_space=pl.ANY)
SMEM = pl.BlockSpec(memory_space=pltpu.SMEM)


def nn(a, b):
    return lax.dot_general(a, b, (((1,), (0,)), ((), ())), preferred_element_type=f32)


def nt(a, b):
    return lax.dot_general(a, b, (((1,), (1,)), ((), ())), preferred_element_type=f32)


def tn(a, b):
    return lax.dot_general(a, b, (((0,), (0,)), ((), ())), preferred_element_type=f32)


def norm_parts(value):
    centered = value - jnp.mean(value, axis=1, keepdims=True)
    rstd = lax.rsqrt(jnp.mean(centered * centered, axis=1, keepdims=True) + EPS)
    return centered * rstd, rstd


def norm_backward(normed, rstd, gain, grad):
    scaled = grad * gain
    mean_one = jnp.mean(scaled, axis=1, keepdims=True)
    mean_two = jnp.mean(scaled * normed, axis=1, keepdims=True)
    return (scaled - mean_one - normed * mean_two) * rstd


def column_sums(value):
    return jnp.sum(value, axis=0, keepdims=True)


def indicator(condition):
    return condition.astype(f32).astype(bf16)


def lane_halves():
    lane = lax.broadcasted_iota(jnp.int32, (1, L), 1)
    return indicator(lane < 64), indicator(lane >= 64)


def stacked(value, halves):
    return jnp.concatenate([value * halves[0], value * halves[1]], axis=0)


def skew(table):
    return pltpu.roll(table, L, 1, stride=1, stride_axis=0)[:, :L]


def unskew(turned):
    wide = jnp.concatenate([turned, jnp.zeros_like(turned)], axis=1)
    return pltpu.roll(wide, 1, 1, stride=1, stride_axis=0)


def pair_at(pair, base=0):
    return slice(base + pair * L, base + pair * L + L)


def block_at(block, base=0):
    return slice(base + block * D, base + block * D + D)


def shape(dims, dtype=bf16):
    return jax.ShapeDtypeStruct(dims, dtype)


class Copies:
    def __init__(self, sems):
        self.sems, self.used = sems, 0

    def make(self, source, target):
        self.used += 1
        return pltpu.make_async_copy(source, target, self.sems.at[self.used - 1])

    def start(self, source, target):
        copy = self.make(source, target)
        copy.start()
        return copy


def wait_all(copies):
    for copy in copies:
        copy.wait()


def run(body, ctl, ins, outs, held, scratch, copies, flops, traffic, near=(), limit=VMEM_LIMIT):
    names, out_names, scratch_names = list(ins), list(outs), list(scratch)
    kept = [name for name in out_names if name in held and name != "sent"]

    def kernel(*refs):
        ctl_ref, refs = refs[0], refs[1:]
        r = SimpleNamespace(ctl=ctl_ref, **dict(zip(names, refs)))
        refs = refs[len(names) + len(kept) :]
        for name, ref in zip(out_names + scratch_names, refs):
            setattr(r, name, ref)
        r.copies = Copies(refs[-1])
        body(r)

    results = pl.pallas_call(
        kernel,
        out_shape=tuple(outs.values()),
        in_specs=[SMEM] + [VMEM if name in near else ANY for name in names] + [ANY] * len(kept),
        out_specs=(ANY,) * len(out_names),
        input_output_aliases={1 + len(names) + i: out_names.index(name) for i, name in enumerate(kept)},
        scratch_shapes=[pltpu.VMEM(s.shape, s.dtype) for s in scratch.values()] + [pltpu.SemaphoreType.DMA((copies,))],
        compiler_params=pltpu.CompilerParams(vmem_limit_bytes=limit),
        cost_estimate=pl.CostEstimate(flops=flops, bytes_accessed=traffic, transcendentals=0),
    )(ctl, *ins.values(), *[held[name] for name in kept])
    return dict(zip(out_names, results))


def load_columns(r, source, target, parts):
    return [r.copies.start(source.at[:, block_at(part)], target.at[:, block_at(part)]) for part in range(parts)]


def load_rows(r, source, target, parts):
    return [r.copies.start(source.at[block_at(part)], target.at[block_at(part)]) for part in range(parts)]


def relative_part(r):
    loads = [r.copies.start(r.rel_table, r.table_v), r.copies.start(r.b_in, r.b_in_v), r.copies.start(r.w_in, r.wi)]
    dims = (2 * L, 2 * SPAN)
    select = indicator(lax.broadcasted_iota(jnp.int32, dims, 0) + lax.broadcasted_iota(jnp.int32, dims, 1) == L + SPAN)
    loads[0].wait()
    rows = nn(select, r.table_v[...]).astype(bf16)
    r.rel_rows_v[...] = rows
    loads[1].wait()
    loads[2].wait()
    r.rel_v[...] = (nn(rows, r.wi[:, : 2 * D]) + r.b_in_v[:, : 2 * D].astype(f32)).astype(bf16)
    return [r.copies.start(r.rel_rows_v, r.rel_rows), r.copies.start(r.rel_v, r.rel)]


def forward_body(row, section, first, r):
    start_copy = r.copies.start
    stores = relative_part(r) if first else []

    @pl.when(r.ctl[0] == section)
    def _():
        x_load = start_copy(r.hidden_in.at[row] if section == 0 else r.received, r.x_v)
        small = [start_copy(r.segment_ids, r.seg_v), start_copy(r.gains, r.gains_v), start_copy(r.biases, r.biases_v)]
        abs_load = start_copy(r.abs_table, r.table_v) if section == 1 else None
        in_loads = [] if first else [start_copy(r.b_in, r.b_in_v)] + load_columns(r, r.w_in, r.wi, 3)
        rel_load = None if first else start_copy(r.rel, r.rel_v)
        loads = [start_copy(r.w_out, r.wo), start_copy(r.b_up, r.b_up_v)]
        part_loads = [pair for pair in zip(load_columns(r, r.w_up, r.wu, 4), load_rows(r, r.w_down, r.wd, 4))]
        halves = lane_halves()
        x_load.wait()
        x = r.x_v[...]
        start = x.astype(f32)
        if section == 1:
            abs_load.wait()
            dims = (L, ABS_ROWS)
            place = lax.broadcasted_iota(jnp.int32, dims, 1) - lax.broadcasted_iota(jnp.int32, dims, 0)
            start = start + nn(indicator(place == r.ctl[2 + row]), r.table_v[...])
        query_in = start.astype(bf16)
        r.acts_v[:, block_at(0)] = query_in
        r.acts_v[:, block_at(1)] = x
        wait_all(in_loads[:2])
        b_in = r.b_in_v[...].astype(f32)
        r.keep_v[:, :D] = (nn(query_in, r.wi[:, :D]) + b_in[:, :D]).astype(bf16)
        wait_all(in_loads[2:])
        r.keep_v[:, D : 3 * D] = (nn(x, r.wi[:, D:]) + b_in[:, D:]).astype(bf16)
        wait_all(small)
        if rel_load is not None:
            rel_load.wait()
        seg_rows = jnp.broadcast_to(r.seg_v[row : row + 1, :], (L, L)).astype(f32)
        same = seg_rows == seg_rows.T
        for pair in range(PAIRS):
            query = r.keep_v[:, pair_at(pair)]
            key = r.keep_v[:, pair_at(pair, D)]
            value = r.keep_v[:, pair_at(pair, 2 * D)]
            query_two, key_two = stacked(query, halves), stacked(key, halves)
            content = nt(query_two, key)
            far_query = nt(query_two, r.rel_v[:, pair_at(pair, D)])
            far_key = nt(key_two, r.rel_v[:, pair_at(pair)])
            probs = []
            for head in range(2):
                rows = slice(head * L, head * L + L)
                summed = content[rows] + skew(far_query[rows]) + skew(far_key[rows]).T
                scores = jnp.where(same, summed * SCALE, NEG)
                exponent = jnp.exp(scores - jnp.max(scores, axis=1, keepdims=True))
                total = jnp.sum(exponent, axis=1, keepdims=True)
                probs.append((exponent * (1.0 / total)).astype(bf16))
            probs = jnp.concatenate(probs, axis=1)
            r.keep_v[:, K_P + 2 * pair * L : K_P + 2 * (pair + 1) * L] = probs
            r.acts_v[:, pair_at(pair, A_CTX)] = nn(probs, stacked(value, halves)).astype(bf16)
        wait_all(loads)
        gain = r.gains_v[...].astype(f32)
        shift = r.biases_v[...].astype(f32)
        resid_one = start + nn(r.acts_v[:, A_CTX : A_CTX + D], r.wo[...]) + shift[0:1]
        r.resid_v[:, :D] = resid_one
        hidden = norm_parts(resid_one)[0] * gain[0:1] + shift[1:2]
        hidden_low = hidden.astype(bf16)
        r.acts_v[:, A_HID : A_HID + D] = hidden_low
        early = [
            start_copy(r.acts_v.at[:, pl.ds(0, A_ACT)], r.acts.at[row, :, pl.ds(0, A_ACT)]),
            start_copy(r.keep_v.at[:, pl.ds(0, K_GP)], r.keep.at[row, :, pl.ds(0, K_GP)]),
        ]
        total = hidden + shift[2:3]
        for part in range(4):
            wait_all(part_loads[part])
            gate = nn(hidden_low, r.wu[:, block_at(part)]) + r.b_up_v[:, block_at(part)].astype(f32)
            below = 0.5 + 0.5 * lax.erf(gate * (1.0 / math.sqrt(2.0)))
            density = jnp.exp(gate * gate * -0.5) * (1.0 / math.sqrt(2.0 * math.pi))
            active = (gate * below).astype(bf16)
            r.acts_v[:, block_at(part, A_ACT)] = active
            r.keep_v[:, block_at(part, K_GP)] = (below + gate * density).astype(bf16)
            early.append(start_copy(r.acts_v.at[:, block_at(part, A_ACT)], r.acts.at[row, :, block_at(part, A_ACT)]))
            early.append(start_copy(r.keep_v.at[:, block_at(part, K_GP)], r.keep.at[row, :, block_at(part, K_GP)]))
            total = total + nn(active, r.wd[block_at(part), :])
        r.resid_v[:, D:] = total
        late = [start_copy(r.resid_v, r.resid.at[row])]
        r.x_v[...] = (norm_parts(total)[0] * gain[1:2] + shift[3:4]).astype(bf16)
        late.append(start_copy(r.x_v, r.section_out.at[row]))
        if section == 0:
            late.append(start_copy(r.x_v, r.sent))
        wait_all(early + late)

    wait_all(stores)
    if row == ROWS - 1:

        @pl.when(r.ctl[0] != section)
        def _():
            turn_weights(r)


def turn_weights(r):
    jobs = [(r.w_up, r.wu, r.w_up_t, 0, part) for part in range(4)]
    jobs += [(r.w_down, r.wd, r.w_down_t, part, 0) for part in range(4)]
    loads = [
        r.copies.start(source.at[block_at(row), block_at(column)], near.at[block_at(row), block_at(column)])
        for source, near, _, row, column in jobs
    ]
    stores = []
    for index, (load, (_, near, target, row, column)) in enumerate(zip(loads, jobs)):
        load.wait()
        r.turned_v[index] = near[block_at(row), block_at(column)].T
        stores.append(r.copies.start(r.turned_v.at[index], target.at[block_at(column), block_at(row)]))
    wait_all(stores)


def forward(row, section, ctl, ins, held):
    first = not held
    outs = {"sent": shape((L, D))} if section == 0 else {}
    if first:
        outs.update(rel_rows=shape((2 * L, D)), rel=shape((2 * L, 2 * D)))
    outs.update(
        acts=shape((ROWS, L, A_ALL)),
        keep=shape((ROWS, L, K_ALL)),
        resid=shape((ROWS, L, 2 * D), f32),
        section_out=shape((ROWS, L, D)),
    )
    scratch = dict(
        x_v=shape((L, D)), seg_v=shape((ROWS, L), jnp.int32), gains_v=shape((2, D)), biases_v=shape((4, D)),
        b_in_v=shape((1, 3 * D)), b_up_v=shape((1, FF)), table_v=shape((2 * SPAN, D)), rel_v=shape((2 * L, 2 * D)),
        wi=shape((D, 3 * D)), wo=shape((D, D)), wu=shape((D, FF)), wd=shape((FF, D)),
        acts_v=shape((L, A_ALL)), keep_v=shape((L, K_ALL)), resid_v=shape((L, 2 * D), f32),
    )
    if first:
        scratch.update(rel_rows_v=shape((2 * L, D)))
    if row == ROWS - 1:
        outs.update(w_up_t=shape((FF, D)), w_down_t=shape((D, FF)))
        scratch.update(turned_v=shape((8, D, D)))
    return run(partial(forward_body, row, section, first), ctl, ins, outs, held, scratch, 56, 1900000000, 18000000, near=())


def ffn_loads(row, section, r):
    return SimpleNamespace(
        grad=r.copies.start(r.cotangent.at[row] if section == 1 else r.received, r.grad_v),
        resid=r.copies.start(r.resid.at[row], r.resid_v),
        gains=r.copies.start(r.gains, r.gains_v),
        parts=[
            [
                r.copies.start(r.w_down_t.at[:, block_at(part)], r.wd.at[:, block_at(part)]),
                r.copies.start(r.keep.at[row, :, block_at(part, K_GP)], r.slope_v.at[:, block_at(part)]),
                r.copies.start(r.w_up_t.at[block_at(part)], r.wu.at[block_at(part)]),
            ]
            for part in range(4)
        ],
        out=r.copies.start(r.w_out, r.wo),
        probs=r.copies.start(r.keep.at[row, :, pl.ds(K_P, K_GP - K_P)], r.probs_v),
    )


def ffn_part(row, r, loads):
    wait_all([loads.grad, loads.resid, loads.gains])
    gain = r.gains_v[...].astype(f32)
    grad = r.grad_v[...].astype(f32)
    normed, rstd = norm_parts(r.resid_v[:, D:])
    r.ffn_vec_v[...] = jnp.zeros_like(r.ffn_vec_v)
    r.ffn_vec_v[8:9] = column_sums(grad * normed)
    r.ffn_vec_v[12:13] = column_sums(grad)
    d_two = norm_backward(normed, rstd, gain[1:2], grad)
    d_down = d_two.astype(bf16)
    r.ffn_v[:, FF : FF + D] = d_down
    r.ffn_vec_v[11:12] = column_sums(d_down.astype(f32))
    d_hidden = d_two
    for part in range(4):
        wait_all(loads.parts[part])
        d_gate = (nn(d_down, r.wd[:, block_at(part)]) * r.slope_v[:, block_at(part)].astype(f32)).astype(bf16)
        r.ffn_v[:, block_at(part)] = d_gate
        r.ffn_vec_v[3 + part : 4 + part] = column_sums(d_gate.astype(f32))
        d_hidden = d_hidden + nn(d_gate, r.wu[block_at(part), :])
    normed, rstd = norm_parts(r.resid_v[:, :D])
    r.ffn_vec_v[7:8] = column_sums(d_hidden * normed)
    r.ffn_vec_v[10:11] = column_sums(d_hidden)
    d_resid = norm_backward(normed, rstd, gain[0:1], d_hidden)
    d_att = d_resid.astype(bf16)
    r.ffn_v[:, FF + D : FF + 2 * D] = d_att
    r.ffn_vec_v[9:10] = column_sums(d_att.astype(f32))
    loads.out.wait()
    r.context_v[...] = nt(d_att, r.wo[...]).astype(bf16)
    loads.probs.wait()
    halves = lane_halves()
    for pair in range(PAIRS):
        d_value = tn(two_heads(r.probs_v, pair), stacked(r.context_v[:, pair_at(pair)], halves))
        r.ffn_v[:, pair_at(pair, FF + 2 * D)] = d_value.astype(bf16)
    r.ffn_vec_v[2:3] = column_sums(r.ffn_v[:, FF + 2 * D :].astype(f32))
    stores, rows = [], pl.ds(row * L, L)
    for side_core, target in ((r.ctl[1], r.ffn_own), (1 - r.ctl[1], r.ffn_other)):
        gates = pl.ds(pl.multiple_of(side_core * 2 * D, 128), 2 * D)
        stores.append(r.copies.start(r.ffn_v.at[:, gates], target.at[rows, pl.ds(0, 2 * D)]))
        stores.append(r.copies.start(r.ffn_v.at[:, pl.ds(FF, 3 * D)], target.at[rows, pl.ds(2 * D, 3 * D)]))
    stores.append(r.copies.start(r.ffn_vec_v, r.ffn_vec.at[row]))
    return d_resid, stores


def two_heads(probs, pair):
    columns = probs[:, 2 * pair * L : 2 * (pair + 1) * L]
    return jnp.concatenate([columns[:, :L], columns[:, L:]], axis=0)


def att_loads(row, section, r):
    return SimpleNamespace(
        keep=r.copies.start(r.keep.at[row, :, pl.ds(0, K_P)], r.keep_v),
        rel=r.copies.start(r.rel, r.rel_v),
        earlier=r.copies.start(r.d_rel, r.d_rel_old) if row > 0 else None,
        w_in=r.copies.start(r.w_in, r.wi),
        others=[
            r.copies.start(r.att_vec.at[0], r.att_vec_old),
            r.copies.start(r.ffn_vec, r.ffn_vec_v),
        ]
        if row == ROWS - 1 and section == 0
        else [],
    )


def att_part(row, section, r, loads, d_resid):
    halves = lane_halves()
    row_at = lax.broadcasted_iota(jnp.int32, (L, L), 0)
    column_at = lax.broadcasted_iota(jnp.int32, (L, L), 1)
    turn = indicator(row_at + column_at == L - 1)
    r.att_vec_v[...] = jnp.zeros_like(r.att_vec_v)
    loads.keep.wait()
    loads.rel.wait()
    for pair in range(PAIRS):
        query = r.keep_v[:, pair_at(pair)]
        key = r.keep_v[:, pair_at(pair, D)]
        value = r.keep_v[:, pair_at(pair, 2 * D)]
        probs_two = two_heads(r.probs_v, pair)
        rel_q, rel_k = r.rel_v[:, pair_at(pair)], r.rel_v[:, pair_at(pair, D)]
        context_two = stacked(r.context_v[:, pair_at(pair)], halves)
        probs_f = probs_two.astype(f32)
        weighted = nt(context_two, value) * probs_f
        d_scores = (weighted - probs_f * jnp.sum(weighted, axis=1, keepdims=True)).astype(bf16)
        query_two, key_two = stacked(query, halves), stacked(key, halves)
        d_key = tn(d_scores, query_two)
        d_side = jnp.concatenate([d_scores[:L], d_scores[L:]], axis=1)
        d_query = nn(d_side, key_two)
        d_far = (d_side.astype(f32) * SCALE).astype(bf16)
        query_turned = nn(turn, query).astype(bf16)
        key_turned = nn(turn, key).astype(bf16)
        rows_turned = nn(turn, d_far)
        far_query, far_key = [], []
        for head in range(2):
            columns = slice(head * L, head * L + L)
            far_query.append(unskew(rows_turned[:, columns]).astype(bf16))
            far_key.append(unskew(nt(turn, d_far[:, columns])).astype(bf16))
        d_query_turned = nn(jnp.concatenate(far_query, axis=1), stacked(rel_k, halves))
        d_key_turned = nn(jnp.concatenate(far_key, axis=1), stacked(rel_q, halves))
        r.d_rel_v[:, pair_at(pair)] = tn(jnp.concatenate(far_key, axis=0), stacked(key_turned, halves))
        r.d_rel_v[:, pair_at(pair, D)] = tn(jnp.concatenate(far_query, axis=0), stacked(query_turned, halves))
        d_query = d_query * SCALE + nn(turn, d_query_turned.astype(bf16))
        d_key = d_key * SCALE + nn(turn, d_key_turned.astype(bf16))
        r.att_v[:, pair_at(pair)] = d_query.astype(bf16)
        r.att_v[:, pair_at(pair, D)] = d_key.astype(bf16)
    stores = []
    for side_core, target in ((r.ctl[1], r.att_own), (1 - r.ctl[1], r.att_other)):
        query_or_key = pl.ds(pl.multiple_of(side_core * D, 128), D)
        stores.append(r.copies.start(r.att_v.at[:, query_or_key], target.at[pl.ds(row * L, L)]))
    far_sums = [column_sums(r.d_rel_v[:, block_at(part)]) for part in range(2)]
    if row > 0:
        loads.earlier.wait()
        r.d_rel_v[...] = r.d_rel_v[...] + r.d_rel_old[...]
    last = row == ROWS - 1
    if last:
        r.rel_low[...] = r.d_rel_v[...].astype(bf16)
        for side_core, target in ((r.ctl[1], r.att_own), (1 - r.ctl[1], r.att_other)):
            query_or_key = pl.ds(pl.multiple_of(side_core * D, 128), D)
            stores.append(r.copies.start(r.rel_low.at[:, query_or_key], target.at[pl.ds(2 * L, 2 * L)]))
    else:
        stores.append(r.copies.start(r.d_rel_v, r.d_rel))
    for part in range(2):
        rows = column_sums(r.att_v[:, block_at(part)].astype(f32)) + far_sums[part]
        r.att_vec_v[part : part + 1] = rows
    stores.append(r.copies.start(r.att_vec_v, r.att_vec.at[row]))
    loads.w_in.wait()
    if last and section == 0:
        stores.append(r.copies.start(r.att_v, r.d_rows))
        wait_all(loads.others)
        return stores + tail_part(r, None, r.ffn_vec_v[0] + r.ffn_vec_v[1] + r.att_vec_old[...] + r.att_vec_v[...])
    d_start = d_resid + nt(r.att_v[:, :D], r.wi[:, :D])
    r.start_v[...] = d_start.astype(bf16)
    stores.append(r.copies.start(r.start_v, r.d_start.at[row]))
    result = d_start + nt(r.att_v[:, D:], r.wi[:, D : 2 * D]) + nt(r.value_v[...], r.wi[:, 2 * D :])
    r.grad_out_v[...] = result.astype(bf16)
    stores.append(r.copies.start(r.grad_out_v, r.input_grad.at[row]))
    if section == 1:
        stores.append(r.copies.start(r.grad_out_v, r.sent))
        if last:
            stores.append(r.copies.start(r.rel_low, r.d_rel_low))
    return stores


def finish_body(r):
    @pl.when(r.ctl[0] == 0)
    def _():
        loads = [
            r.copies.start(source, target)
            for source, target in (
                (r.d_resid, r.resid_v), (r.d_rows, r.rows_v), (r.d_context.at[:, pl.ds(D, D)], r.value_v), (r.w_in, r.wi)
            )
        ]
        wait_all(loads)
        result = r.resid_v[...] + nt(r.rows_v[...], r.wi[:, : 2 * D]) + nt(r.value_v[...], r.wi[:, 2 * D :])
        r.grad_v[...] = result.astype(bf16)
        r.copies.start(r.grad_v, r.input_grad.at[ROWS - 1]).wait()


def finish(ctl, held, **ins):
    outs = dict(input_grad=shape((ROWS, L, D)))
    scratch = dict(
        resid_v=shape((L, D), f32), rows_v=shape((L, 2 * D)), value_v=shape((L, D)), wi=shape((D, 3 * D)), grad_v=shape((L, D))
    )
    return run(finish_body, ctl, ins, outs, held, scratch, 5, 500000000, 5000000)["input_grad"]


def tail_part(r, starts, vectors):
    def put(first, rows, value):
        r.tail_v[first : first + rows] = value.astype(bf16)

    if starts is None:
        put(REL_ROWS, ABS_ROWS, jnp.zeros((ABS_ROWS, D), f32))
    else:
        dims = (ABS_ROWS, L)
        place = lax.broadcasted_iota(jnp.int32, dims, 0) - lax.broadcasted_iota(jnp.int32, dims, 1)
        spots = [indicator(place == r.ctl[2 + row]) for row in range(ROWS)]
        put(REL_ROWS, ABS_ROWS, nn(spots[0], starts[0]) + nn(spots[1], starts[1]))
    put(TABLE_ROWS, VECTOR_ROWS, vectors)
    rest = TAIL_ROWS - TABLE_ROWS - VECTOR_ROWS
    put(TABLE_ROWS + VECTOR_ROWS, rest, jnp.zeros((rest, D), f32))
    rows = nt(r.rel_low[...], r.wi[:, : 2 * D]).astype(bf16)
    dims = (REL_ROWS, 2 * L)
    select = lax.broadcasted_iota(jnp.int32, dims, 0) + lax.broadcasted_iota(jnp.int32, dims, 1) == L + SPAN - REL_FROM
    put(0, REL_ROWS, nn(indicator(select), rows))
    return [
        r.copies.start(
            r.tail_v.at[pl.ds(pl.multiple_of(side_core * TAIL_HALF, 16), TAIL_HALF)], target.at[pl.ds(4 * L, TAIL_HALF)]
        )
        for side_core, target in ((r.ctl[1], r.att_own), (1 - r.ctl[1], r.att_other))
    ]


def backward_body(row, section, parts, r):
    @pl.when(r.ctl[0] == section)
    def _():
        if parts == "ffn":
            d_resid, stores = ffn_part(row, r, ffn_loads(row, section, r))
            r.resid_v[:, :D] = d_resid
            stores.append(r.copies.start(r.resid_v.at[:, pl.ds(0, D)], r.d_resid))
            stores.append(r.copies.start(r.context_v, r.d_context.at[:, pl.ds(0, D)]))
            stores.append(r.copies.start(r.ffn_v.at[:, pl.ds(FF + 2 * D, D)], r.d_context.at[:, pl.ds(D, D)]))
        elif parts == "att":
            first = [
                r.copies.start(r.d_resid, r.d_resid_v),
                r.copies.start(r.d_context.at[:, pl.ds(0, D)], r.context_v),
                r.copies.start(r.keep.at[row, :, pl.ds(K_P, K_GP - K_P)], r.probs_v),
                r.copies.start(r.d_context.at[:, pl.ds(D, D)], r.value_v),
            ]
            loads = att_loads(row, section, r)
            wait_all(first)
            stores = att_part(row, section, r, loads, r.d_resid_v[...])
        else:
            loads = ffn_loads(row, section, r)
            later = att_loads(row, section, r)
            d_resid, stores = ffn_part(row, r, loads)
            r.value_v[...] = r.ffn_v[:, FF + 2 * D :]
            stores = stores + att_part(row, section, r, later, d_resid)
        wait_all(stores)


def backward(row, section, parts, ctl, ins, held):
    outs, scratch, flops, traffic = {}, {}, 0, 0
    if parts == "ffn":
        outs.update(d_resid=shape((L, D), f32), d_context=shape((L, 2 * D)))
    if parts != "att":
        outs.update(
            ffn_own=shape((ROWS * L, 5 * D)), ffn_other=shape((ROWS * L, 5 * D)), ffn_vec=shape((ROWS, VECTOR_ROWS, D), f32)
        )
        scratch.update(
            grad_v=shape((L, D)), resid_v=shape((L, 2 * D), f32), gains_v=shape((2, D)), slope_v=shape((L, FF)),
            wu=shape((FF, D)), wd=shape((D, FF)), ffn_v=shape((L, FF + 3 * D)), wo=shape((D, D)), probs_v=shape((L, 2 * D)), context_v=shape((L, D)), ffn_vec_v=shape((VECTOR_ROWS, D), f32),
        )
        flops, traffic = flops + 1300000000, traffic + 12000000
    if parts == "att":
        scratch.update(d_resid_v=shape((L, D), f32), context_v=shape((L, D)), probs_v=shape((L, 2 * D)))
    if parts != "ffn":
        if section == 1:
            outs.update(sent=shape((L, D)))
        outs.update(
            att_own=shape((SWAP_ROWS, D)), att_other=shape((SWAP_ROWS, D)), att_vec=shape((ROWS, VECTOR_ROWS, D), f32),
            d_start=shape((ROWS, L, D)), d_rel=shape((2 * L, 2 * D), f32), d_rel_low=shape((2 * L, 2 * D)),
            input_grad=shape((ROWS, L, D)),
        )
        scratch.update(
            wi=shape((D, 3 * D)), keep_v=shape((L, K_P)), rel_v=shape((2 * L, 2 * D)),
            att_v=shape((L, 2 * D)), att_vec_v=shape((VECTOR_ROWS, D), f32), start_v=shape((L, D)), grad_out_v=shape((L, D)),
            value_v=shape((L, D)), d_rel_v=shape((2 * L, 2 * D), f32), d_rel_old=shape((2 * L, 2 * D), f32), rel_low=shape((2 * L, 2 * D)),
        )
        if row == ROWS - 1 and section == 0:
            outs.update(d_rows=shape((L, 2 * D)))
            del outs["input_grad"], outs["d_start"]
            scratch.update(
                tail_v=shape((TAIL_ROWS, D)),
                att_vec_old=shape((VECTOR_ROWS, D), f32), ffn_vec_v=shape((ROWS, VECTOR_ROWS, D), f32),
            )
        flops, traffic = flops + 1100000000, traffic + 8000000
    return run(partial(backward_body, row, section, parts), ctl, ins, outs, held, scratch, 56, flops, traffic, near=())


def tables_body(r):
    @pl.when(r.ctl[0] == 1)
    def _():
        loads = [
            r.copies.start(source, target)
            for source, target in (
                (r.d_start, r.start_v), (r.ffn_vec, r.ffn_vec_v), (r.att_vec, r.att_vec_v), (r.d_rel_low, r.rel_low), (r.w_in, r.wi)
            )
        ]
        wait_all(loads)
        vectors = r.ffn_vec_v[0] + r.ffn_vec_v[1] + r.att_vec_v[0] + r.att_vec_v[1]
        wait_all(tail_part(r, [r.start_v[0], r.start_v[1]], vectors))


def tables(ctl, w_in, held):
    ins = dict(w_in=w_in, **{name: held[name] for name in ("d_start", "ffn_vec", "att_vec", "d_rel_low")})
    outs = dict(att_own=shape((SWAP_ROWS, D)), att_other=shape((SWAP_ROWS, D)))
    scratch = dict(
        start_v=shape((ROWS, L, D)), ffn_vec_v=shape((ROWS, VECTOR_ROWS, D), f32), att_vec_v=shape((ROWS, VECTOR_ROWS, D), f32),
        rel_low=shape((2 * L, 2 * D)), wi=shape((D, 3 * D)), tail_v=shape((TAIL_ROWS, D)),
    )
    return run(tables_body, ctl, ins, outs, held, scratch, 8, 1000000000, 7000000)


def small_kernel(body, ctl, ins, outs):
    return pl.pallas_call(
        body,
        out_shape=outs,
        in_specs=[SMEM] + [VMEM] * len(ins),
        out_specs=(VMEM,) * len(outs),
        compiler_params=pltpu.CompilerParams(vmem_limit_bytes=16 * 2**20),
        cost_estimate=pl.CostEstimate(flops=0, bytes_accessed=2 * sum(value.size for value in ins) * 2, transcendentals=0),
    )(ctl, *ins)


def added(kept, received):
    return (kept.astype(f32) + received.astype(f32)).astype(bf16)


def split_sum(ctl, bit, kept, received):
    half = kept.shape[0] // 2

    def body(ctl, kept, received, keep, send):
        low, high = (added(kept[at], received[at]) for at in (slice(0, half), slice(half, 2 * half)))
        first = ctl[bit] == 0
        keep[...] = jnp.where(first, low, high)
        send[...] = jnp.where(first, high, low)

    return small_kernel(body, ctl, (kept, received), (shape((half, D)),) * 2)


def in_order(ctl, bit, own, other):
    half = own.shape[0]

    def body(ctl, own, other, out):
        first = ctl[bit] == 0
        out[:half] = jnp.where(first, own[...], other[...])
        out[half:] = jnp.where(first, other[...], own[...])

    return small_kernel(body, ctl, (own, other), (shape((2 * half, D)),))[0]


class Halves:
    def __init__(self, r, first_piece, half_rows):
        self.r, self.first_piece, self.half_rows, self.pending = r, first_piece, half_rows, []

    def store(self, first, rows):
        while rows > 0:
            index, inside = divmod(first, self.half_rows)
            count = min(rows, self.half_rows - inside)
            piece, half = index // 2, index % 2
            view, there = self.r.out_v.at[pl.ds(first, count)], pl.ds(inside, count)
            kept = self.r.copies.make(view, getattr(self.r, f"kept{piece}").at[there])
            sem = self.r.copies.sems.at[self.r.copies.used - 1]
            sent = pltpu.make_async_copy(view, getattr(self.r, f"sent{piece}").at[there], sem)
            mine = self.r.ctl[bit_at(self.first_piece + piece, False)] == half

            @pl.when(mine)
            def _():
                kept.start()

            @pl.when(jnp.logical_not(mine))
            def _():
                sent.start()

            self.pending.append(kept)
            first, rows = first + count, rows - count


def bit_at(piece, of_other_core):
    return 4 + 2 * piece + int(of_other_core)


def half_outputs(rows, pieces):
    half_rows = rows // pieces // 2
    return {f"{kind}{piece}": shape((half_rows, D)) for piece in range(pieces) for kind in ("kept", "sent")}


def load_acts(r, at, size, to):
    if not isinstance(at, int):
        at = pl.multiple_of(at, 128)
    return [
        r.copies.start(source.at[row, :, pl.ds(at, size)], target.at[pl.ds(row * L, L), pl.ds(to, size)])
        for row in range(ROWS)
        for source, target in ((r.acts, r.acts_v), (r.acts_sent, r.acts_sent_v))
    ]


def ffn_weights_body(r):
    core = r.ctl[1]
    loads = [r.copies.start(r.rows, r.rows_v)] + load_acts(r, A_HID, D, 0)
    later = load_acts(r, A_ACT + core * 2 * D, 2 * D, D)
    last = load_acts(r, A_CTX + core * HALF, HALF, 3 * D) + load_acts(r, A_X + core * HALF, HALF, 3 * D + HALF)
    halves = Halves(r, 0, FFN_ROWS // FFN_PIECES // 2)

    def product(acts_at, rows_at):
        own = tn(r.acts_v[:, acts_at], r.rows_v[:, rows_at])
        return (own + tn(r.acts_sent_v[:, acts_at], r.rows_sent[:, rows_at])).astype(bf16)

    wait_all(loads)
    for block in range(2):
        r.out_v[block_at(block)] = product(block_at(0), block_at(block))
        halves.store(block * D, D)
    wait_all(later)
    for block in range(2, 4):
        r.out_v[block_at(block)] = product(block_at(block - 1), block_at(2))
        halves.store(block * D, D)
    wait_all(last)
    for part in range(2):
        to = slice(4 * D + part * HALF, 4 * D + (part + 1) * HALF)
        r.out_v[to] = product(slice(3 * D + part * HALF, 3 * D + (part + 1) * HALF), block_at(3 + part))
    halves.store(4 * D, D)
    wait_all(halves.pending)


def ffn_weights(ctl, **ins):
    scratch = dict(
        rows_v=shape((ROWS * L, 5 * D)), acts_v=shape((ROWS * L, 4 * D)), acts_sent_v=shape((ROWS * L, 4 * D)),
        out_v=shape((FFN_ROWS, D)),
    )
    outs = half_outputs(FFN_ROWS, FFN_PIECES)
    return run(ffn_weights_body, ctl, ins, outs, {}, scratch, 36, 2 * 512 * 768 * FFN_ROWS, 14000000, ("rows_sent",))


def att_weights_body(r):
    loads = [r.copies.start(r.rows, r.rows_v), r.copies.start(r.table, r.table_v)]
    loads += load_acts(r, r.ctl[1] * D, D, 0)
    halves = Halves(r, FFN_PIECES, ATT_ROWS // ATT_PIECES // 2)
    wait_all(loads)
    total = tn(r.acts_v[...], r.rows_v[: 2 * L]) + tn(r.acts_sent_v[...], r.rows_sent[: 2 * L])
    far = (r.rows_v[2 * L : 4 * L].astype(f32) + r.rows_sent[2 * L : 4 * L].astype(f32)).astype(bf16)
    r.out_v[:D] = (total + tn(r.table_v[...], far)).astype(bf16)
    r.out_v[TAIL_AT:] = r.rows_v[4 * L :] + r.rows_sent[4 * L :]
    halves.store(0, ATT_ROWS)
    wait_all(halves.pending)


def att_weights(ctl, **ins):
    scratch = dict(
        rows_v=shape((SWAP_ROWS, D)), table_v=shape((2 * L, D)),
        acts_v=shape((ROWS * L, D)), acts_sent_v=shape((ROWS * L, D)), out_v=shape((ATT_ROWS, D)),
    )
    outs = half_outputs(ATT_ROWS, ATT_PIECES)
    return run(att_weights_body, ctl, ins, outs, {}, scratch, 16, 2 * 768 * 768 * 768, 6000000, ("rows_sent",))


def half_segments(layout, half_rows, piece, half):
    low = (2 * piece + half) * half_rows
    found, at = [], 0
    for target, rows, first, block in layout:
        start, stop = max(at, low), min(at + rows, low + half_rows)
        if start < stop:
            found.append((start - low, stop - start, target, first + start - at, block))
        at += rows
    return found


def assemble_body(kind, first_piece, layouts, half_rows, pieces, r):
    start_copy = r.copies.start
    core = r.ctl[1]
    blank = None
    if first_piece > 0 and kind == 0:
        r.blank[...] = jnp.zeros_like(r.blank)
        rest = 2 * SPAN - REL_FROM - REL_ROWS
        blank = [
            start_copy(r.blank, r.g_rel.at[pl.ds(0, REL_FROM)]),
            start_copy(r.blank.at[pl.ds(0, rest)], r.g_rel.at[pl.ds(REL_FROM + REL_ROWS, rest)]),
        ]
    branches = []
    chunk = half_rows // 2
    items = [(piece, origin) for piece in range(pieces) for origin in ("own", "sent")]
    for index, (piece, origin) in enumerate(items):
        array = getattr(r, f"{origin}{piece}")
        bit = r.ctl[bit_at(first_piece + piece, origin == "sent")]
        maker = core if origin == "own" else 1 - core
        cases = [(made_by, half) for made_by in range(2) for half in range(2)]
        for at in range(0, half_rows, chunk):
            r.wide[index, at : at + chunk] = array[at : at + chunk].astype(f32)
            first_copy = last_copy = r.copies.used
            for made_by, half in cases:
                r.copies.used = first_copy
                copies = []
                for inside, count, name, start, block in half_segments(layouts[made_by], half_rows, piece, half):
                    low, high = max(inside, at), min(inside + count, at + chunk)
                    if low < high and name not in ("", "vectors"):
                        target = getattr(r, name).at[pl.ds(start + low - inside, high - low), pl.ds(block * D, D)]
                        copies.append(r.copies.make(r.wide.at[index, pl.ds(low, high - low)], target))
                last_copy = max(last_copy, r.copies.used)
                here = (maker == made_by) & (bit == (half if kind == 0 else 1 - half))
                branches.append((here, copies))

                @pl.when(here)
                def _():
                    for copy in copies:
                        copy.start()

            r.copies.used = last_copy
        for made_by, half in cases:
            for inside, count, name, _, _ in half_segments(layouts[made_by], half_rows, piece, half):
                if name == "vectors":

                    @pl.when((maker == made_by) & (bit == (half if kind == 0 else 1 - half)))
                    def _():
                        vectors = r.wide[index, inside : inside + count, :]
                        for part in range(3):
                            r.b_in_v[:, block_at(part)] = vectors[part : part + 1]
                        for part in range(4):
                            r.b_up_v[:, block_at(part)] = vectors[3 + part : 4 + part]
                        r.gains_v[...] = vectors[7:9]
                        r.biases_v[...] = vectors[9:13]
                        wait_all([
                            start_copy(r.b_in_v, r.g_b_in), start_copy(r.b_up_v, r.g_b_up),
                            start_copy(r.gains_v, r.g_gains), start_copy(r.biases_v, r.g_biases),
                        ])

    wait_all(blank or [])
    for here, copies in branches:

        @pl.when(here)
        def _():
            wait_all(copies)


def assemble(kind, first_piece, layouts, rows, pieces, ctl, own, sent, shapes, held):
    ins = {f"own{i}": value for i, value in enumerate(own)}
    ins.update({f"sent{i}": value for i, value in enumerate(sent)})
    outs = {name: shape(dims, f32) for name, dims in shapes.items()}
    half_rows = rows // pieces // 2
    scratch = dict(wide=shape((len(ins), half_rows, D), f32))
    if first_piece > 0:
        scratch.update(
            blank=shape((REL_FROM, D), f32), b_in_v=shape((1, 3 * D), f32), b_up_v=shape((1, FF), f32),
            gains_v=shape((2, D), f32), biases_v=shape((4, D), f32),
        )
    body = partial(assemble_body, kind, first_piece, layouts, half_rows, pieces)
    return run(body, ctl, ins, outs, held, scratch, 96, 0, len(ins) * half_rows * D * 6, tuple(ins), 44 * 2**20)


FFN_SHAPES = dict(g_up=(D, FF), g_down=(FF, D), g_out=(D, D), g_in=(D, 3 * D))
ATT_SHAPES = dict(
    g_in=(D, 3 * D), g_rel=(2 * SPAN, D), g_abs=(ABS_ROWS, D),
    g_b_in=(1, 3 * D), g_b_up=(1, FF), g_gains=(2, D), g_biases=(4, D),
)


SQUARE = ((0, 0), (1, 0), (1, 1), (0, 1))


def dp_place(index):
    return {"core": index % 2, "x": index // 2 % 4, "y": index // 8 % 2, "z": index // 16}


def dp_index(place):
    return ((place["z"] * 2 + place["y"]) * 4 + place["x"]) * 2 + place["core"]


def partner(index, dim):
    place = dp_place(index)
    if len(dim) == 2:
        bits = list(SQUARE[place[dim[0]]])
        bits[int(dim[1])] ^= 1
        place[dim[0]] = SQUARE.index(tuple(bits))
    else:
        place[dim] ^= 1
    return dp_index(place)


def swap(value, dims):
    peers = lax.axis_size("dp")
    return lax.ppermute(value, "dp", [(i, partner(i, dims[i % 2])) for i in range(peers)])


BETWEEN_CORES = ("core", "core")


def side_along(dim):
    place = dp_place(lax.axis_index("dp"))
    if dim == "y":
        return place[dim].astype(jnp.int32)
    at = place[dim[0]]
    if dim[1] == "0":
        return ((at == 1) | (at == 2)).astype(jnp.int32)
    return (at >= 2).astype(jnp.int32)


def this_core():
    return (lax.axis_index("dp") % 2).astype(jnp.int32)


def side(dims):
    return jnp.where(this_core() == 0, side_along(dims[0]), side_along(dims[1]))


ORDERS = [
    [("x0", "y"), ("z0", "x1"), ("x1", "z1"), ("y", "z0"), ("z1", "x0")],
    [("x1", "z0"), ("x0", "z1"), ("y", "x0"), ("z1", "x1"), ("z0", "y")],
    [("z1", "y"), ("x1", "z1"), ("y", "z0"), ("x0", "x1"), ("z0", "x0")],
]
BITS_AT = 4 + 2 * (FFN_PIECES + ATT_PIECES)
SPLIT_STEPS = 3


def bit_of(piece, step):
    return BITS_AT + 2 * piece + step - 1


def is_table_row(chunk):
    piece = FFN_PIECES
    first_row, span = 0, ATT_ROWS
    for dims in ORDERS[piece][:SPLIT_STEPS]:
        span //= 2
        first_row = first_row + side(dims) * span
    row_at = first_row + lax.broadcasted_iota(jnp.int32, chunk.shape, 0) - TAIL_AT
    return (row_at >= 0) & (row_at + this_core() * TAIL_HALF < TABLE_ROWS)


class Sequence:
    def __init__(self, last):
        self.last = last

    def after(self, *values):
        values = lax.optimization_barrier((*values, self.last))[:-1]
        return values[0] if len(values) == 1 else values


class Pieces:
    def __init__(self, ctl, seq):
        self.ctl, self.seq = ctl, seq
        self.kept, self.received, self.mine, self.mine_sent, self.partners, self.partners_sent = ({} for _ in range(6))

    def begin(self, piece, kept, sent):
        self.kept[piece], self.received[piece] = kept, swap(sent, ORDERS[piece][0])

    def inputs(self, piece):
        return self.seq.after(self.kept[piece], self.received[piece])

    def hold(self, piece, chunk):
        self.kept[piece] = self.seq.last = chunk

    def land(self, piece):
        self.received[piece] = self.seq.last = self.seq.after(self.received[piece])

    def split(self, piece, step):
        kept, sent = split_sum(self.ctl, bit_of(piece, step), *self.inputs(piece))
        self.hold(piece, kept)
        self.received[piece] = swap(sent, ORDERS[piece][step])

    def add(self, piece, step):
        kept, received = self.inputs(piece)
        self.hold(piece, kept + received)
        self.received[piece] = swap(self.kept[piece], ORDERS[piece][step])

    def add_for_section(self, piece):
        kept, received = self.inputs(piece)
        self.hold(piece, kept + received)
        self.received[piece] = lax.ppermute(self.kept[piece], "section", [(0, 1), (1, 0)])

    def add_tables(self, piece, step):
        kept, received = self.inputs(piece)
        self.hold(piece, jnp.where(is_table_row(kept), kept + received, kept))
        self.received[piece] = swap(self.kept[piece], ORDERS[piece][step])

    def join(self, piece, step):
        self.hold(piece, in_order(self.ctl, bit_of(piece, step), *self.inputs(piece)))
        self.received[piece] = swap(self.kept[piece], ORDERS[piece][step - 1])
        if step == 1:
            self.mine[piece] = self.kept[piece]
            self.mine_sent[piece] = swap(self.mine[piece], BETWEEN_CORES)

    def arrive(self, piece):
        self.partners[piece] = self.seq.last = self.seq.after(self.received[piece])
        self.partners_sent[piece] = swap(self.partners[piece], BETWEEN_CORES)


def per_device(
    hidden_in,
    cotangent,
    segment_ids,
    positions,
    w_in,
    b_in,
    w_out,
    w_up,
    b_up,
    w_down,
    gains,
    biases,
    rel_table,
    abs_table,
):
    section = lax.axis_index("section").astype(jnp.int32)
    firsts = jnp.where(section == 1, positions[:, 0], 8 * ABS_ROWS)
    bits = [side(dims) for order in ORDERS for dims in (order[0], order[0][::-1])]
    bits += [side(order[step]) for order in ORDERS for step in range(1, SPLIT_STEPS)]
    ctl = jnp.stack([section, this_core(), firsts[0], firsts[1], *bits])
    weights = dict(w_in=w_in[0], w_out=w_out[0], w_up=w_up[0], w_down=w_down[0], gains=gains[0])
    common = dict(
        weights, hidden_in=hidden_in, segment_ids=segment_ids, biases=biases[0], b_in=b_in, b_up=b_up, abs_table=abs_table
    )

    out = forward(0, 0, ctl, dict(common, rel_table=rel_table), {})
    rel, rel_rows = out["rel"], out["rel_rows"]
    common["rel"] = rel
    received = []
    for row in range(ROWS):
        if row > 0:
            out = forward(row, 0, ctl, common, out)
        received.append(lax.ppermute(out["sent"], "section", [(0, 1)]))
    grads, back = [], {}
    for row in range(ROWS):
        out = {**out, **forward(row, 1, ctl, dict(common, received=received[row]), out)}
        ready = {name: out[name] for name in ("keep", "resid", "w_up_t", "w_down_t")}
        back = backward(row, 1, "both", ctl, dict(weights, **ready, cotangent=cotangent, rel=rel), back)
        grads.append(lax.ppermute(back["sent"], "section", [(1, 0)]))
        if row < ROWS - 1:
            received[row + 1], _ = lax.optimization_barrier((received[row + 1], back["sent"]))
    acts, section_out = out["acts"], out["section_out"]
    acts_sent = swap(acts, BETWEEN_CORES)
    common = dict(weights, **ready, cotangent=cotangent, rel=rel)
    received, out = grads, back
    out.update(tables(ctl, weights["w_in"], out))
    out = backward(0, 0, "both", ctl, dict(common, received=received[0]), out)
    early = out
    ffn = backward(1, 0, "ffn", ctl, dict(common, received=received[1]), early)
    ffn_sent = swap(ffn["ffn_other"], BETWEEN_CORES)
    seq = Sequence(ffn["ffn_own"])
    pieces = Pieces(ctl, seq)
    grads = {}

    def write(kind, group):
        own, sent = ((pieces.mine, pieces.mine_sent), (pieces.partners, pieces.partners_sent))[kind]
        first, count, layout, rows, shapes = group
        first_own, *own = [own[first + i] for i in range(count)]
        sent = [sent[first + i] for i in range(count)]
        result = assemble(kind, first, layout, rows, count, ctl, [seq.after(first_own), *own], sent, shapes, grads)
        grads.update(result)
        seq.last = result["g_biases"] if first > 0 else result["g_out"]

    ffn_group = 0, FFN_PIECES, FFN_LAYOUT, FFN_ROWS, FFN_SHAPES
    att_group = FFN_PIECES, ATT_PIECES, ATT_LAYOUT, ATT_ROWS, ATT_SHAPES
    ins = dict(common, d_resid=seq.after(ffn["d_resid"]), d_context=ffn["d_context"], ffn_vec=ffn["ffn_vec"])
    out = backward(1, 0, "att", ctl, ins, early)
    att_sent = swap(out["att_other"], BETWEEN_CORES)
    seq.last = out["att_own"]
    halves = ffn_weights(ctl, acts=acts, acts_sent=acts_sent, rows=seq.after(ffn["ffn_own"]), rows_sent=ffn_sent)
    for piece in range(FFN_PIECES):
        pieces.begin(piece, halves[f"kept{piece}"], halves[f"sent{piece}"])
    seq.last = halves["kept0"]
    halves = att_weights(
        ctl, acts=acts, acts_sent=acts_sent, rows=seq.after(out["att_own"]), rows_sent=att_sent, table=rel_rows
    )
    pieces.begin(FFN_PIECES, halves["kept0"], halves["sent0"])
    seq.last = halves["kept0"]
    input_grad = finish(
        ctl, early, d_resid=ffn["d_resid"], d_rows=seq.after(out["d_rows"]), d_context=ffn["d_context"], w_in=weights["w_in"]
    )
    seq.last = input_grad
    pieces.split(0, 1)
    pieces.split(1, 1)
    pieces.land(2)
    pieces.split(0, 2)
    pieces.split(1, 2)
    pieces.split(2, 1)
    pieces.add(0, 3)
    pieces.add(1, 3)
    pieces.split(2, 2)
    pieces.add(0, 4)
    pieces.add(1, 4)
    pieces.add(2, 3)
    pieces.add(0, 2)
    pieces.land(1)
    pieces.add(2, 4)
    pieces.add(1, 2)
    pieces.join(0, 2)
    pieces.add_for_section(2)
    pieces.join(1, 2)
    pieces.add_tables(2, 2)
    pieces.join(0, 1)
    pieces.join(2, 2)
    pieces.join(1, 1)
    pieces.join(2, 1)
    write(0, att_group)
    pieces.arrive(0)
    write(0, ffn_group)
    pieces.arrive(1)
    pieces.arrive(2)
    write(1, ffn_group)
    write(1, att_group)
    return (
        section_out[None],
        input_grad[None],
        grads["g_in"][None],
        grads["g_b_in"],
        grads["g_out"][None],
        grads["g_up"][None],
        grads["g_b_up"],
        grads["g_down"][None],
        grads["g_gains"][None],
        grads["g_biases"][None],
        grads["g_rel"],
        grads["g_abs"],
    )


def solution(mesh):
    in_specs = (
        P("dp", None, None),
        P("dp", None, None),
        P("dp", None),
        P("dp", None),
        P("section", None, None),
        P("section", None),
        P("section", None, None),
        P("section", None, None),
        P("section", None),
        P("section", None, None),
        P("section", None, None),
        P("section", None, None),
        P(),
        P(),
    )
    out_specs = (
        P("section", "dp", None, None),
        P("section", "dp", None, None),
        P("section", None, None),
        P("section", None),
        P("section", None, None),
        P("section", None, None),
        P("section", None),
        P("section", None, None),
        P("section", None, None),
        P("section", None, None),
        P(),
        P(),
    )
    return jax.shard_map(
        per_device, mesh=mesh, in_specs=in_specs, out_specs=out_specs, check_vma=False
    )
```

```python
from functools import partial
import math
from types import SimpleNamespace

import jax
import jax.numpy as jnp
from jax import lax
from jax.experimental import pallas as pl
from jax.experimental.pallas import tpu as pltpu
from jax.sharding import PartitionSpec as P

HEADS = 12
L = 128
D = 768
FF = 3072
HALF = D // 2
PAIRS = HEADS // 2
ROWS = 2
SPAN = 256
EPS = 1e-06
NEG = -1e30
SCALE = 1.0 / math.sqrt(3 * 64)
VMEM_LIMIT = 61 * 1024 * 1024
f32, bf16 = jnp.float32, jnp.bfloat16

A_START, A_X, A_CTX, A_HID, A_ACT, A_ALL = 0, 768, 1536, 2304, 3072, 6144
K_P, K_GP, K_ALL = 2304, 3840, 6912
VECTOR_ROWS = 16
REL_FROM, REL_ROWS, ABS_ROWS, TAIL_ROWS = 128, 272, 512, 896
TABLE_ROWS = REL_ROWS + ABS_ROWS
FFN_LAYOUT = [
    [("g_up", D, 0, 2 * core), ("g_up", D, 0, 2 * core + 1), ("g_down", 2 * D, 2 * D * core, 0), ("g_out", HALF, HALF * core, 0),
     ("g_in", HALF, HALF * core, 2)]
    for core in range(2)
]
ATT_LAYOUT = [
    [("g_in", D, 0, 0), ("g_rel", REL_ROWS, REL_FROM, 0), ("g_abs", 176, 0, 0)],
    [("g_in", D, 0, 1), ("g_abs", 336, 176, 0), ("vectors", VECTOR_ROWS, 0, 0), ("", 96, 0, 0)],
]
FFN_ROWS, ATT_ROWS = 3840, 1216
FFN_PIECES, ATT_PIECES = 2, 1
TAIL_HALF = TAIL_ROWS // 2
TAIL_AT = ATT_ROWS - TAIL_HALF
SWAP_ROWS = 4 * L + TAIL_HALF

VMEM = pl.BlockSpec(memory_space=pltpu.VMEM)
ANY = pl.BlockSpec(memory_space=pl.ANY)
SMEM = pl.BlockSpec(memory_space=pltpu.SMEM)


def nn(a, b):
    return lax.dot_general(a, b, (((1,), (0,)), ((), ())), preferred_element_type=f32)


def nt(a, b):
    return lax.dot_general(a, b, (((1,), (1,)), ((), ())), preferred_element_type=f32)


def tn(a, b):
    return lax.dot_general(a, b, (((0,), (0,)), ((), ())), preferred_element_type=f32)


def norm_parts(value):
    centered = value - jnp.mean(value, axis=1, keepdims=True)
    rstd = lax.rsqrt(jnp.mean(centered * centered, axis=1, keepdims=True) + EPS)
    return centered * rstd, rstd


def norm_backward(normed, rstd, gain, grad):
    scaled = grad * gain
    mean_one = jnp.mean(scaled, axis=1, keepdims=True)
    mean_two = jnp.mean(scaled * normed, axis=1, keepdims=True)
    return (scaled - mean_one - normed * mean_two) * rstd


def column_sums(value):
    return jnp.sum(value, axis=0, keepdims=True)


def indicator(condition):
    return condition.astype(f32).astype(bf16)


def lane_halves():
    lane = lax.broadcasted_iota(jnp.int32, (1, L), 1)
    return indicator(lane < 64), indicator(lane >= 64)


def stacked(value, halves):
    return jnp.concatenate([value * halves[0], value * halves[1]], axis=0)


def skew(table):
    return pltpu.roll(table, L, 1, stride=1, stride_axis=0)[:, :L]


def unskew(turned):
    wide = jnp.concatenate([turned, jnp.zeros_like(turned)], axis=1)
    return pltpu.roll(wide, 1, 1, stride=1, stride_axis=0)


def pair_at(pair, base=0):
    return slice(base + pair * L, base + pair * L + L)


def block_at(block, base=0):
    return slice(base + block * D, base + block * D + D)


def shape(dims, dtype=bf16):
    return jax.ShapeDtypeStruct(dims, dtype)


class Copies:
    def __init__(self, sems):
        self.sems, self.used, self.marks = sems, 0, {}

    def make(self, source, target):
        self.used += 1
        return pltpu.make_async_copy(source, target, self.sems.at[self.used - 1])

    def make_at(self, name):
        again = self.marks.setdefault(name, self.used)
        if again == self.used:
            return self.make
        at = iter(range(again, self.used))
        return lambda source, target: pltpu.make_async_copy(source, target, self.sems.at[next(at)])

    def start(self, source, target):
        copy = self.make(source, target)
        copy.start()
        return copy


def wait_all(copies):
    for copy in copies:
        copy.wait()


def run(body, ctl, ins, outs, held, scratch, copies, flops, traffic, near=("received",), limit=VMEM_LIMIT):
    names, out_names, scratch_names = list(ins), list(outs), list(scratch)
    kept = [name for name in out_names if name in held and name != "sent"]

    def kernel(*refs):
        ctl_ref, refs = refs[0], refs[1:]
        r = SimpleNamespace(ctl=ctl_ref, **dict(zip(names, refs)))
        refs = refs[len(names) + len(kept) :]
        for name, ref in zip(out_names + scratch_names, refs):
            setattr(r, name, ref)
        r.copies = Copies(refs[-1])
        body(r)

    results = pl.pallas_call(
        kernel,
        out_shape=tuple(outs.values()),
        in_specs=[SMEM] + [VMEM if name in near else ANY for name in names] + [ANY] * len(kept),
        out_specs=(ANY,) * len(out_names),
        input_output_aliases={1 + len(names) + i: out_names.index(name) for i, name in enumerate(kept)},
        scratch_shapes=[pltpu.VMEM(s.shape, s.dtype) for s in scratch.values()] + [pltpu.SemaphoreType.DMA((copies,))],
        compiler_params=pltpu.CompilerParams(vmem_limit_bytes=limit),
        cost_estimate=pl.CostEstimate(flops=flops, bytes_accessed=traffic, transcendentals=0),
    )(ctl, *ins.values(), *[held[name] for name in kept])
    return dict(zip(out_names, results))


def relative_loads(r):
    return [r.copies.start(r.rel_table, r.table_v), r.copies.start(r.b_in, r.b_in_v), r.copies.start(r.w_in, r.wi)]


def relative_part(r, loads):
    dims = (2 * L, 2 * SPAN)
    select = indicator(lax.broadcasted_iota(jnp.int32, dims, 0) + lax.broadcasted_iota(jnp.int32, dims, 1) == L + SPAN)
    loads[0].wait()
    rows = nn(select, r.table_v[...]).astype(bf16)
    r.rel_rows_v[...] = rows
    loads[1].wait()
    loads[2].wait()
    r.rel_v[...] = (nn(rows, r.wi[:, : 2 * D]) + r.b_in_v[:, : 2 * D].astype(f32)).astype(bf16)
    return [r.copies.start(r.rel_rows_v, r.rel_rows), r.copies.start(r.rel_v, r.rel)]


def forward_loads(row, section, first, r):
    make = r.copies.make_at("loads")
    loads = SimpleNamespace(
        x=[make(r.hidden_in.at[row], r.x_v)] if section == 0 else [],
        absolute=[make(r.abs_table, r.table_v)] if section == 1 else [],
        w_in=[]
        if first
        else [make(r.b_in, r.b_in_v)] + [make(r.w_in.at[:, block_at(part)], r.wi.at[:, block_at(part)]) for part in range(3)],
        rel=[] if first else [make(r.rel, r.rel_v)],
        small=[make(r.segment_ids, r.seg_v), make(r.gains, r.gains_v), make(r.biases, r.biases_v)],
        out=[make(r.w_out, r.wo), make(r.b_up, r.b_up_v)],
        parts=[
            [
                make(r.w_up.at[:, block_at(part)], r.wu.at[:, block_at(part)]),
                make(r.w_down.at[block_at(part)], r.wd.at[block_at(part)]),
            ]
            for part in range(4)
        ],
    )
    flat = loads.x + loads.absolute + loads.w_in + loads.rel + loads.small + loads.out
    loads.every = flat + [copy for part in loads.parts for copy in part]
    return loads


def forward_body(row, section, first, r):
    start_copy = r.copies.start
    stores = []
    if first:
        rel_loads = relative_loads(r)

        @pl.when(r.ctl[0] == section)
        def _():
            for copy in forward_loads(row, section, first, r).every:
                copy.start()

        stores = relative_part(r, rel_loads)

    @pl.when(r.ctl[0] == section)
    def _():
        loads = forward_loads(row, section, first, r)
        if not first:
            for copy in loads.every:
                copy.start()
        if section == 1:
            back = SimpleNamespace(
                first=[start_copy(r.cotangent.at[row], r.grad_v)],
                parts=[
                    [
                        start_copy(r.w_down_t.at[:, block_at(part)], r.wd_t.at[:, block_at(part)]),
                        start_copy(r.w_up_t.at[block_at(part)], r.wu_t.at[block_at(part)]),
                    ]
                    for part in range(4)
                ],
                last=[],
            )
            earlier = [start_copy(r.d_rel, r.d_rel_old)] if row > 0 else []
            back_att = SimpleNamespace(first=[], earlier=earlier, w_in=[], others=[])
        halves = lane_halves()
        wait_all(loads.x)
        x = r.x_v[...] if section == 0 else r.received[...]
        start = x.astype(f32)
        if section == 1:
            wait_all(loads.absolute)
            dims = (L, ABS_ROWS)
            place = lax.broadcasted_iota(jnp.int32, dims, 1) - lax.broadcasted_iota(jnp.int32, dims, 0)
            start = start + nn(indicator(place == r.ctl[2 + row]), r.table_v[...])
        query_in = start.astype(bf16)
        r.acts_v[:, block_at(0)] = query_in
        r.acts_v[:, block_at(1)] = x
        wait_all(loads.w_in[:2])
        b_in = r.b_in_v[...].astype(f32)
        r.keep_v[:, :D] = (nn(query_in, r.wi[:, :D]) + b_in[:, :D]).astype(bf16)
        wait_all(loads.w_in[2:])
        r.keep_v[:, D : 3 * D] = (nn(x, r.wi[:, D:]) + b_in[:, D:]).astype(bf16)
        wait_all(loads.small + loads.rel)
        seg_rows = jnp.broadcast_to(r.seg_v[row : row + 1, :], (L, L)).astype(f32)
        same = seg_rows == seg_rows.T
        for pair in range(PAIRS):
            query = r.keep_v[:, pair_at(pair)]
            key = r.keep_v[:, pair_at(pair, D)]
            value = r.keep_v[:, pair_at(pair, 2 * D)]
            query_two, key_two = stacked(query, halves), stacked(key, halves)
            content = nt(query_two, key)
            far_query = nt(query_two, r.rel_v[:, pair_at(pair, D)])
            far_key = nt(key_two, r.rel_v[:, pair_at(pair)])
            probs = []
            for head in range(2):
                rows = slice(head * L, head * L + L)
                summed = content[rows] + skew(far_query[rows]) + skew(far_key[rows]).T
                scores = jnp.where(same, summed * SCALE, NEG)
                exponent = jnp.exp(scores - jnp.max(scores, axis=1, keepdims=True))
                total = jnp.sum(exponent, axis=1, keepdims=True)
                probs.append((exponent * (1.0 / total)).astype(bf16))
            probs = jnp.concatenate(probs, axis=1)
            r.keep_v[:, K_P + 2 * pair * L : K_P + 2 * (pair + 1) * L] = probs
            r.acts_v[:, pair_at(pair, A_CTX)] = nn(probs, stacked(value, halves)).astype(bf16)
        wait_all(loads.out)
        gain = r.gains_v[...].astype(f32)
        shift = r.biases_v[...].astype(f32)
        resid_one = start + nn(r.acts_v[:, A_CTX : A_CTX + D], r.wo[...]) + shift[0:1]
        r.resid_v[:, :D] = resid_one
        hidden = norm_parts(resid_one)[0] * gain[0:1] + shift[1:2]
        hidden_low = hidden.astype(bf16)
        r.acts_v[:, A_HID : A_HID + D] = hidden_low
        stored = [start_copy(r.acts_v.at[:, pl.ds(0, A_ACT)], r.acts.at[row, :, pl.ds(0, A_ACT)])]
        if section == 0:
            stored.append(start_copy(r.keep_v.at[:, pl.ds(0, K_GP)], r.keep.at[row, :, pl.ds(0, K_GP)]))
        total = hidden + shift[2:3]
        for part in range(4):
            wait_all(loads.parts[part])
            gate = nn(hidden_low, r.wu[:, block_at(part)]) + r.b_up_v[:, block_at(part)].astype(f32)
            below = 0.5 + 0.5 * lax.erf(gate * (1.0 / math.sqrt(2.0)))
            density = jnp.exp(gate * gate * -0.5) * (1.0 / math.sqrt(2.0 * math.pi))
            active = (gate * below).astype(bf16)
            r.acts_v[:, block_at(part, A_ACT)] = active
            r.keep_v[:, block_at(part, K_GP)] = (below + gate * density).astype(bf16)
            stored.append(start_copy(r.acts_v.at[:, block_at(part, A_ACT)], r.acts.at[row, :, block_at(part, A_ACT)]))
            if section == 0:
                stored.append(start_copy(r.keep_v.at[:, block_at(part, K_GP)], r.keep.at[row, :, block_at(part, K_GP)]))
            total = total + nn(active, r.wd[block_at(part), :])
        r.resid_v[:, D:] = total
        if section == 0:
            stored.append(start_copy(r.resid_v, r.resid.at[row]))
        r.x_v[...] = (norm_parts(total)[0] * gain[1:2] + shift[3:4]).astype(bf16)
        stored.append(start_copy(r.x_v, r.section_out.at[row]))
        if section == 0:
            stored.append(start_copy(r.x_v, r.sent))
        else:
            near = SimpleNamespace(**vars(r))
            near.wu, near.wd = r.wu_t, r.wd_t
            near.probs_v = r.keep_v.at[:, pl.ds(K_P, K_GP - K_P)]
            near.slope_v = r.keep_v.at[:, pl.ds(K_GP, FF)]
            d_resid, out_copies = ffn_part(row, section, near, back)
            r.value_v[...] = r.ffn_v[:, FF + 2 * D :]
            stored += out_copies + att_part(row, section, near, back_att, d_resid)
        wait_all(stored)

    wait_all(stores)
    if row == ROWS - 1:

        @pl.when(r.ctl[0] != section)
        def _():
            turn_weights(r)


def turn_weights(r):
    jobs = [(r.w_up, r.wu, r.w_up_t, 0, part) for part in range(4)]
    jobs += [(r.w_down, r.wd, r.w_down_t, part, 0) for part in range(4)]
    loads = [
        r.copies.start(source.at[block_at(row), block_at(column)], near.at[block_at(row), block_at(column)])
        for source, near, _, row, column in jobs
    ]
    stores = []
    for load, (source, near, target, row, column) in zip(loads, jobs):
        load.wait()
        turned = r.wu_t if near is r.wu else r.wd_t
        turned[block_at(column), block_at(row)] = near[block_at(row), block_at(column)].T
        stores.append(
            r.copies.start(turned.at[block_at(column), block_at(row)], target.at[block_at(column), block_at(row)])
        )
    wait_all(stores)


def forward(row, section, ctl, ins, held):
    first = not held
    outs = {"sent": shape((L, D))}
    if first:
        outs.update(rel_rows=shape((2 * L, D)), rel=shape((2 * L, 2 * D)))
    outs.update(acts=shape((ROWS, L, A_ALL)), section_out=shape((ROWS, L, D)))
    scratch = dict(
        x_v=shape((L, D)), seg_v=shape((ROWS, L), jnp.int32), gains_v=shape((2, D)), biases_v=shape((4, D)),
        b_in_v=shape((1, 3 * D)), b_up_v=shape((1, FF)), table_v=shape((2 * SPAN, D)), rel_v=shape((2 * L, 2 * D)),
        wi=shape((D, 3 * D)), wo=shape((D, D)), wu=shape((D, FF)), wd=shape((FF, D)),
        acts_v=shape((L, A_ALL)), keep_v=shape((L, K_ALL)), resid_v=shape((L, 2 * D), f32),
    )
    if section == 0:
        outs.update(keep=shape((ROWS, L, K_ALL)), resid=shape((ROWS, L, 2 * D), f32))
    else:
        outs.update(backward_results(row, section))
        scratch.update(
            grad_v=shape((L, D)), ffn_v=shape((L, FF + 3 * D)), context_v=shape((L, D)), ffn_vec_v=shape((VECTOR_ROWS, D), f32),
            att_v=shape((L, 2 * D)), att_vec_v=shape((VECTOR_ROWS, D), f32), start_v=shape((L, D)), grad_out_v=shape((L, D)),
            value_v=shape((L, D)), d_rel_v=shape((2 * L, 2 * D), f32), d_rel_old=shape((2 * L, 2 * D), f32),
            rel_low=shape((2 * L, 2 * D)),
        )
    if first:
        scratch.update(rel_rows_v=shape((2 * L, D)))
    if row == ROWS - 1:
        outs.update(w_up_t=shape((FF, D)), w_down_t=shape((D, FF)))
    if row == ROWS - 1 or section == 1:
        scratch.update(wu_t=shape((FF, D)), wd_t=shape((D, FF)))
    return run(partial(forward_body, row, section, first), ctl, ins, outs, held, scratch, 84, 1900000000, 18000000, ("received",))


def backward_results(row, section):
    results = dict(
        ffn_own=shape((ROWS * L, 5 * D)), ffn_other=shape((ROWS * L, 5 * D)), ffn_vec=shape((ROWS, VECTOR_ROWS, D), f32),
        att_own=shape((SWAP_ROWS, D)), att_other=shape((SWAP_ROWS, D)), att_vec=shape((ROWS, VECTOR_ROWS, D), f32),
        d_start=shape((ROWS, L, D)), d_rel=shape((2 * L, 2 * D), f32), d_rel_low=shape((2 * L, 2 * D)),
        input_grad=shape((ROWS, L, D)),
    )
    return results


def ffn_loads(row, section, r):
    return SimpleNamespace(
        first=[r.copies.start(r.resid.at[row], r.resid_v), r.copies.start(r.gains, r.gains_v)],
        parts=[
            [
                r.copies.start(r.w_down_t.at[:, block_at(part)], r.wd.at[:, block_at(part)]),
                r.copies.start(r.keep.at[row, :, block_at(part, K_GP)], r.slope_v.at[:, block_at(part)]),
                r.copies.start(r.w_up_t.at[block_at(part)], r.wu.at[block_at(part)]),
            ]
            for part in range(4)
        ],
        last=[r.copies.start(r.w_out, r.wo), r.copies.start(r.keep.at[row, :, pl.ds(K_P, K_GP - K_P)], r.probs_v)],
    )


def ffn_part(row, section, r, loads):
    wait_all(loads.first)
    gain = r.gains_v[...].astype(f32)
    grad = (r.grad_v if section == 1 else r.received)[...].astype(f32)
    normed, rstd = norm_parts(r.resid_v[:, D:])
    r.ffn_vec_v[...] = jnp.zeros_like(r.ffn_vec_v)
    r.ffn_vec_v[8:9] = column_sums(grad * normed)
    r.ffn_vec_v[12:13] = column_sums(grad)
    d_two = norm_backward(normed, rstd, gain[1:2], grad)
    d_down = d_two.astype(bf16)
    r.ffn_v[:, FF : FF + D] = d_down
    r.ffn_vec_v[11:12] = column_sums(d_down.astype(f32))
    d_hidden = d_two
    for part in range(4):
        wait_all(loads.parts[part])
        d_gate = (nn(d_down, r.wd[:, block_at(part)]) * r.slope_v[:, block_at(part)].astype(f32)).astype(bf16)
        r.ffn_v[:, block_at(part)] = d_gate
        r.ffn_vec_v[3 + part : 4 + part] = column_sums(d_gate.astype(f32))
        d_hidden = d_hidden + nn(d_gate, r.wu[block_at(part), :])
    normed, rstd = norm_parts(r.resid_v[:, :D])
    r.ffn_vec_v[7:8] = column_sums(d_hidden * normed)
    r.ffn_vec_v[10:11] = column_sums(d_hidden)
    d_resid = norm_backward(normed, rstd, gain[0:1], d_hidden)
    d_att = d_resid.astype(bf16)
    r.ffn_v[:, FF + D : FF + 2 * D] = d_att
    r.ffn_vec_v[9:10] = column_sums(d_att.astype(f32))
    wait_all(loads.last)
    r.context_v[...] = nt(d_att, r.wo[...]).astype(bf16)
    halves = lane_halves()
    for pair in range(PAIRS):
        d_value = tn(two_heads(r.probs_v, pair), stacked(r.context_v[:, pair_at(pair)], halves))
        r.ffn_v[:, pair_at(pair, FF + 2 * D)] = d_value.astype(bf16)
    r.ffn_vec_v[2:3] = column_sums(r.ffn_v[:, FF + 2 * D :].astype(f32))
    stores, rows = [], pl.ds(row * L, L)
    for side_core, target in ((r.ctl[1], r.ffn_own), (1 - r.ctl[1], r.ffn_other)):
        gates = pl.ds(pl.multiple_of(side_core * 2 * D, 128), 2 * D)
        stores.append(r.copies.start(r.ffn_v.at[:, gates], target.at[rows, pl.ds(0, 2 * D)]))
        stores.append(r.copies.start(r.ffn_v.at[:, pl.ds(FF, 3 * D)], target.at[rows, pl.ds(2 * D, 3 * D)]))
    stores.append(r.copies.start(r.ffn_vec_v, r.ffn_vec.at[row]))
    return d_resid, stores


def two_heads(probs, pair):
    columns = probs[:, 2 * pair * L : 2 * (pair + 1) * L]
    return jnp.concatenate([columns[:, :L], columns[:, L:]], axis=0)


def att_loads(row, section, r):
    return SimpleNamespace(
        first=[r.copies.start(r.keep.at[row, :, pl.ds(0, K_P)], r.keep_v), r.copies.start(r.rel, r.rel_v)],
        earlier=[r.copies.start(r.d_rel, r.d_rel_old)] if row > 0 else [],
        w_in=[r.copies.start(r.w_in, r.wi)],
        others=[
            r.copies.start(r.att_vec.at[0], r.att_vec_old),
            r.copies.start(r.ffn_vec, r.ffn_vec_v),
        ]
        if row == ROWS - 1 and section == 0
        else [],
    )


def att_part(row, section, r, loads, d_resid):
    halves = lane_halves()
    row_at = lax.broadcasted_iota(jnp.int32, (L, L), 0)
    column_at = lax.broadcasted_iota(jnp.int32, (L, L), 1)
    turn = indicator(row_at + column_at == L - 1)
    r.att_vec_v[...] = jnp.zeros_like(r.att_vec_v)
    wait_all(loads.first)
    for pair in range(PAIRS):
        query = r.keep_v[:, pair_at(pair)]
        key = r.keep_v[:, pair_at(pair, D)]
        value = r.keep_v[:, pair_at(pair, 2 * D)]
        probs_two = two_heads(r.probs_v, pair)
        rel_q, rel_k = r.rel_v[:, pair_at(pair)], r.rel_v[:, pair_at(pair, D)]
        context_two = stacked(r.context_v[:, pair_at(pair)], halves)
        probs_f = probs_two.astype(f32)
        weighted = nt(context_two, value) * probs_f
        d_scores = (weighted - probs_f * jnp.sum(weighted, axis=1, keepdims=True)).astype(bf16)
        query_two, key_two = stacked(query, halves), stacked(key, halves)
        d_key = tn(d_scores, query_two)
        d_side = jnp.concatenate([d_scores[:L], d_scores[L:]], axis=1)
        d_query = nn(d_side, key_two)
        d_far = (d_side.astype(f32) * SCALE).astype(bf16)
        query_turned = nn(turn, query).astype(bf16)
        key_turned = nn(turn, key).astype(bf16)
        rows_turned = nn(turn, d_far)
        far_query, far_key = [], []
        for head in range(2):
            columns = slice(head * L, head * L + L)
            far_query.append(unskew(rows_turned[:, columns]).astype(bf16))
            far_key.append(unskew(nt(turn, d_far[:, columns])).astype(bf16))
        d_query_turned = nn(jnp.concatenate(far_query, axis=1), stacked(rel_k, halves))
        d_key_turned = nn(jnp.concatenate(far_key, axis=1), stacked(rel_q, halves))
        r.d_rel_v[:, pair_at(pair)] = tn(jnp.concatenate(far_key, axis=0), stacked(key_turned, halves))
        r.d_rel_v[:, pair_at(pair, D)] = tn(jnp.concatenate(far_query, axis=0), stacked(query_turned, halves))
        d_query = d_query * SCALE + nn(turn, d_query_turned.astype(bf16))
        d_key = d_key * SCALE + nn(turn, d_key_turned.astype(bf16))
        r.att_v[:, pair_at(pair)] = d_query.astype(bf16)
        r.att_v[:, pair_at(pair, D)] = d_key.astype(bf16)
    stores = []
    for side_core, target in ((r.ctl[1], r.att_own), (1 - r.ctl[1], r.att_other)):
        query_or_key = pl.ds(pl.multiple_of(side_core * D, 128), D)
        stores.append(r.copies.start(r.att_v.at[:, query_or_key], target.at[pl.ds(row * L, L)]))
    far_sums = [column_sums(r.d_rel_v[:, block_at(part)]) for part in range(2)]
    if row > 0:
        wait_all(loads.earlier)
        r.d_rel_v[...] = r.d_rel_v[...] + r.d_rel_old[...]
    last = row == ROWS - 1
    if last:
        r.rel_low[...] = r.d_rel_v[...].astype(bf16)
        for side_core, target in ((r.ctl[1], r.att_own), (1 - r.ctl[1], r.att_other)):
            query_or_key = pl.ds(pl.multiple_of(side_core * D, 128), D)
            stores.append(r.copies.start(r.rel_low.at[:, query_or_key], target.at[pl.ds(2 * L, 2 * L)]))
    else:
        stores.append(r.copies.start(r.d_rel_v, r.d_rel))
    for part in range(2):
        rows = column_sums(r.att_v[:, block_at(part)].astype(f32)) + far_sums[part]
        r.att_vec_v[part : part + 1] = rows
    stores.append(r.copies.start(r.att_vec_v, r.att_vec.at[row]))
    wait_all(loads.w_in)
    if last and section == 0:
        stores.append(r.copies.start(r.att_v, r.d_rows))
        wait_all(loads.others)
        return stores + tail_part(r, None, r.ffn_vec_v[0] + r.ffn_vec_v[1] + r.att_vec_old[...] + r.att_vec_v[...])
    d_start = d_resid + nt(r.att_v[:, :D], r.wi[:, :D])
    r.start_v[...] = d_start.astype(bf16)
    stores.append(r.copies.start(r.start_v, r.d_start.at[row]))
    result = d_start + nt(r.att_v[:, D:], r.wi[:, D : 2 * D]) + nt(r.value_v[...], r.wi[:, 2 * D :])
    r.grad_out_v[...] = result.astype(bf16)
    stores.append(r.copies.start(r.grad_out_v, r.input_grad.at[row]))
    if section == 1:
        stores.append(r.copies.start(r.grad_out_v, r.sent))
        if last:
            stores.append(r.copies.start(r.rel_low, r.d_rel_low))
    return stores


def finish_body(r):
    @pl.when(r.ctl[0] == 0)
    def _():
        loads = [
            r.copies.start(source, target)
            for source, target in (
                (r.d_resid, r.resid_v), (r.d_rows, r.rows_v), (r.d_context.at[:, pl.ds(D, D)], r.value_v), (r.w_in, r.wi)
            )
        ]
        wait_all(loads)
        result = r.resid_v[...] + nt(r.rows_v[...], r.wi[:, : 2 * D]) + nt(r.value_v[...], r.wi[:, 2 * D :])
        r.grad_v[...] = result.astype(bf16)
        r.copies.start(r.grad_v, r.input_grad.at[ROWS - 1]).wait()


def finish(ctl, held, **ins):
    outs = dict(input_grad=shape((ROWS, L, D)))
    scratch = dict(
        resid_v=shape((L, D), f32), rows_v=shape((L, 2 * D)), value_v=shape((L, D)), wi=shape((D, 3 * D)), grad_v=shape((L, D))
    )
    return run(finish_body, ctl, ins, outs, held, scratch, 5, 500000000, 5000000)["input_grad"]


def tail_part(r, starts, vectors):
    def put(first, rows, value):
        r.tail_v[first : first + rows] = value.astype(bf16)

    if starts is None:
        put(REL_ROWS, ABS_ROWS, jnp.zeros((ABS_ROWS, D), f32))
    else:
        dims = (ABS_ROWS, L)
        place = lax.broadcasted_iota(jnp.int32, dims, 0) - lax.broadcasted_iota(jnp.int32, dims, 1)
        spots = [indicator(place == r.ctl[2 + row]) for row in range(ROWS)]
        put(REL_ROWS, ABS_ROWS, nn(spots[0], starts[0]) + nn(spots[1], starts[1]))
    put(TABLE_ROWS, VECTOR_ROWS, vectors)
    rest = TAIL_ROWS - TABLE_ROWS - VECTOR_ROWS
    put(TABLE_ROWS + VECTOR_ROWS, rest, jnp.zeros((rest, D), f32))
    rows = nt(r.rel_low[...], r.wi[:, : 2 * D]).astype(bf16)
    dims = (REL_ROWS, 2 * L)
    select = lax.broadcasted_iota(jnp.int32, dims, 0) + lax.broadcasted_iota(jnp.int32, dims, 1) == L + SPAN - REL_FROM
    put(0, REL_ROWS, nn(indicator(select), rows))
    return [
        r.copies.start(
            r.tail_v.at[pl.ds(pl.multiple_of(side_core * TAIL_HALF, 16), TAIL_HALF)], target.at[pl.ds(4 * L, TAIL_HALF)]
        )
        for side_core, target in ((r.ctl[1], r.att_own), (1 - r.ctl[1], r.att_other))
    ]


def backward_body(row, section, parts, r):
    @pl.when(r.ctl[0] == section)
    def _():
        if parts == "ffn":
            d_resid, stores = ffn_part(row, section, r, ffn_loads(row, section, r))
            r.resid_v[:, :D] = d_resid
            stores.append(r.copies.start(r.resid_v.at[:, pl.ds(0, D)], r.d_resid))
            stores.append(r.copies.start(r.context_v, r.d_context.at[:, pl.ds(0, D)]))
            stores.append(r.copies.start(r.ffn_v.at[:, pl.ds(FF + 2 * D, D)], r.d_context.at[:, pl.ds(D, D)]))
        elif parts == "att":
            first = [
                r.copies.start(r.d_resid, r.d_resid_v),
                r.copies.start(r.d_context.at[:, pl.ds(0, D)], r.context_v),
                r.copies.start(r.keep.at[row, :, pl.ds(K_P, K_GP - K_P)], r.probs_v),
                r.copies.start(r.d_context.at[:, pl.ds(D, D)], r.value_v),
            ]
            loads = att_loads(row, section, r)
            wait_all(first)
            stores = att_part(row, section, r, loads, r.d_resid_v[...])
        else:
            loads = ffn_loads(row, section, r)
            later = att_loads(row, section, r)
            d_resid, stores = ffn_part(row, section, r, loads)
            r.value_v[...] = r.ffn_v[:, FF + 2 * D :]
            stores = stores + att_part(row, section, r, later, d_resid)
        wait_all(stores)


def backward(row, section, parts, ctl, ins, held):
    outs, scratch, flops, traffic = {}, {}, 0, 0
    if parts == "ffn":
        outs.update(d_resid=shape((L, D), f32), d_context=shape((L, 2 * D)))
    if parts != "att":
        outs.update(
            ffn_own=shape((ROWS * L, 5 * D)), ffn_other=shape((ROWS * L, 5 * D)), ffn_vec=shape((ROWS, VECTOR_ROWS, D), f32)
        )
        scratch.update(
            grad_v=shape((L, D)), resid_v=shape((L, 2 * D), f32), gains_v=shape((2, D)), slope_v=shape((L, FF)),
            wu=shape((FF, D)), wd=shape((D, FF)), ffn_v=shape((L, FF + 3 * D)), wo=shape((D, D)), probs_v=shape((L, 2 * D)), context_v=shape((L, D)), ffn_vec_v=shape((VECTOR_ROWS, D), f32),
        )
        flops, traffic = flops + 1300000000, traffic + 12000000
    if parts == "att":
        scratch.update(d_resid_v=shape((L, D), f32), context_v=shape((L, D)), probs_v=shape((L, 2 * D)))
    if parts != "ffn":
        if section == 1:
            outs.update(sent=shape((L, D)))
        outs.update(
            att_own=shape((SWAP_ROWS, D)), att_other=shape((SWAP_ROWS, D)), att_vec=shape((ROWS, VECTOR_ROWS, D), f32),
            d_start=shape((ROWS, L, D)), d_rel=shape((2 * L, 2 * D), f32), d_rel_low=shape((2 * L, 2 * D)),
            input_grad=shape((ROWS, L, D)),
        )
        scratch.update(
            wi=shape((D, 3 * D)), keep_v=shape((L, K_P)), rel_v=shape((2 * L, 2 * D)),
            att_v=shape((L, 2 * D)), att_vec_v=shape((VECTOR_ROWS, D), f32), start_v=shape((L, D)), grad_out_v=shape((L, D)),
            value_v=shape((L, D)), d_rel_v=shape((2 * L, 2 * D), f32), d_rel_old=shape((2 * L, 2 * D), f32), rel_low=shape((2 * L, 2 * D)),
        )
        if row == ROWS - 1 and section == 0:
            outs.update(d_rows=shape((L, 2 * D)))
            del outs["input_grad"], outs["d_start"]
            scratch.update(
                tail_v=shape((TAIL_ROWS, D)),
                att_vec_old=shape((VECTOR_ROWS, D), f32), ffn_vec_v=shape((ROWS, VECTOR_ROWS, D), f32),
            )
        flops, traffic = flops + 1100000000, traffic + 8000000
    return run(partial(backward_body, row, section, parts), ctl, ins, outs, held, scratch, 56, flops, traffic, near=("received",))


def tables_body(r):
    @pl.when(r.ctl[0] == 1)
    def _():
        loads = [
            r.copies.start(source, target)
            for source, target in (
                (r.d_start, r.start_v), (r.ffn_vec, r.ffn_vec_v), (r.att_vec, r.att_vec_v), (r.d_rel_low, r.rel_low), (r.w_in, r.wi)
            )
        ]
        wait_all(loads)
        vectors = r.ffn_vec_v[0] + r.ffn_vec_v[1] + r.att_vec_v[0] + r.att_vec_v[1]
        wait_all(tail_part(r, [r.start_v[0], r.start_v[1]], vectors))


def tables(ctl, w_in, held):
    ins = dict(w_in=w_in, **{name: held[name] for name in ("d_start", "ffn_vec", "att_vec", "d_rel_low")})
    outs = dict(att_own=shape((SWAP_ROWS, D)), att_other=shape((SWAP_ROWS, D)))
    scratch = dict(
        start_v=shape((ROWS, L, D)), ffn_vec_v=shape((ROWS, VECTOR_ROWS, D), f32), att_vec_v=shape((ROWS, VECTOR_ROWS, D), f32),
        rel_low=shape((2 * L, 2 * D)), wi=shape((D, 3 * D)), tail_v=shape((TAIL_ROWS, D)),
    )
    return run(tables_body, ctl, ins, outs, held, scratch, 8, 1000000000, 7000000)


def small_kernel(body, ctl, ins, outs):
    return pl.pallas_call(
        body,
        out_shape=outs,
        in_specs=[SMEM] + [VMEM] * len(ins),
        out_specs=(VMEM,) * len(outs),
        compiler_params=pltpu.CompilerParams(vmem_limit_bytes=16 * 2**20),
        cost_estimate=pl.CostEstimate(flops=0, bytes_accessed=2 * sum(value.size for value in ins) * 2, transcendentals=0),
    )(ctl, *ins)


def added(kept, received):
    return (kept.astype(f32) + received.astype(f32)).astype(bf16)


def split_sum(ctl, bit, kept, received):
    half = kept.shape[0] // 2

    def body(ctl, kept, received, keep, send):
        low, high = (added(kept[at], received[at]) for at in (slice(0, half), slice(half, 2 * half)))
        first = ctl[bit] == 0
        keep[...] = jnp.where(first, low, high)
        send[...] = jnp.where(first, high, low)

    return small_kernel(body, ctl, (kept, received), (shape((half, D)),) * 2)


def in_order(ctl, bit, own, other):
    half = own.shape[0]

    def body(ctl, own, other, out):
        first = ctl[bit] == 0
        out[:half] = jnp.where(first, own[...], other[...])
        out[half:] = jnp.where(first, other[...], own[...])

    return small_kernel(body, ctl, (own, other), (shape((2 * half, D)),))[0]


class Halves:
    def __init__(self, r, first_piece, half_rows):
        self.r, self.first_piece, self.half_rows, self.pending = r, first_piece, half_rows, []

    def store(self, first, rows):
        while rows > 0:
            index, inside = divmod(first, self.half_rows)
            count = min(rows, self.half_rows - inside)
            piece, half = index // 2, index % 2
            view, there = self.r.out_v.at[pl.ds(first, count)], pl.ds(inside, count)
            kept = self.r.copies.make(view, getattr(self.r, f"kept{piece}").at[there])
            sem = self.r.copies.sems.at[self.r.copies.used - 1]
            sent = pltpu.make_async_copy(view, getattr(self.r, f"sent{piece}").at[there], sem)
            mine = self.r.ctl[bit_at(self.first_piece + piece, False)] == half

            @pl.when(mine)
            def _():
                kept.start()

            @pl.when(jnp.logical_not(mine))
            def _():
                sent.start()

            self.pending.append(kept)
            first, rows = first + count, rows - count


def bit_at(piece, of_other_core):
    return 4 + 2 * piece + int(of_other_core)


def half_outputs(rows, pieces):
    half_rows = rows // pieces // 2
    return {f"{kind}{piece}": shape((half_rows, D)) for piece in range(pieces) for kind in ("kept", "sent")}


def load_acts(r, at, size, to):
    if not isinstance(at, int):
        at = pl.multiple_of(at, 128)
    return [
        r.copies.start(source.at[row, :, pl.ds(at, size)], target.at[pl.ds(row * L, L), pl.ds(to, size)])
        for row in range(ROWS)
        for source, target in ((r.acts, r.acts_v), (r.acts_sent, r.acts_sent_v))
    ]


def ffn_weights_body(r):
    core = r.ctl[1]
    loads = [r.copies.start(r.rows, r.rows_v)] + load_acts(r, A_HID, D, 0)
    later = load_acts(r, A_ACT + core * 2 * D, 2 * D, D)
    last = load_acts(r, A_CTX + core * HALF, HALF, 3 * D) + load_acts(r, A_X + core * HALF, HALF, 3 * D + HALF)
    halves = Halves(r, 0, FFN_ROWS // FFN_PIECES // 2)

    def product(acts_at, rows_at):
        own = tn(r.acts_v[:, acts_at], r.rows_v[:, rows_at])
        return (own + tn(r.acts_sent_v[:, acts_at], r.rows_sent[:, rows_at])).astype(bf16)

    wait_all(loads)
    for block in range(2):
        r.out_v[block_at(block)] = product(block_at(0), block_at(block))
        halves.store(block * D, D)
    wait_all(later)
    for block in range(2, 4):
        r.out_v[block_at(block)] = product(block_at(block - 1), block_at(2))
        halves.store(block * D, D)
    wait_all(last)
    for part in range(2):
        to = slice(4 * D + part * HALF, 4 * D + (part + 1) * HALF)
        r.out_v[to] = product(slice(3 * D + part * HALF, 3 * D + (part + 1) * HALF), block_at(3 + part))
    halves.store(4 * D, D)
    wait_all(halves.pending)


def ffn_weights(ctl, **ins):
    scratch = dict(
        rows_v=shape((ROWS * L, 5 * D)), acts_v=shape((ROWS * L, 4 * D)), acts_sent_v=shape((ROWS * L, 4 * D)),
        out_v=shape((FFN_ROWS, D)),
    )
    outs = half_outputs(FFN_ROWS, FFN_PIECES)
    return run(ffn_weights_body, ctl, ins, outs, {}, scratch, 36, 2 * 512 * 768 * FFN_ROWS, 14000000, ("rows_sent",))


def att_weights_body(r):
    loads = [r.copies.start(r.rows, r.rows_v), r.copies.start(r.table, r.table_v)]
    loads += load_acts(r, r.ctl[1] * D, D, 0)
    halves = Halves(r, FFN_PIECES, ATT_ROWS // ATT_PIECES // 2)
    wait_all(loads)
    total = tn(r.acts_v[...], r.rows_v[: 2 * L]) + tn(r.acts_sent_v[...], r.rows_sent[: 2 * L])
    far = (r.rows_v[2 * L : 4 * L].astype(f32) + r.rows_sent[2 * L : 4 * L].astype(f32)).astype(bf16)
    r.out_v[:D] = (total + tn(r.table_v[...], far)).astype(bf16)
    r.out_v[TAIL_AT:] = r.rows_v[4 * L :] + r.rows_sent[4 * L :]
    halves.store(0, ATT_ROWS)
    wait_all(halves.pending)


def att_weights(ctl, **ins):
    scratch = dict(
        rows_v=shape((SWAP_ROWS, D)), table_v=shape((2 * L, D)),
        acts_v=shape((ROWS * L, D)), acts_sent_v=shape((ROWS * L, D)), out_v=shape((ATT_ROWS, D)),
    )
    outs = half_outputs(ATT_ROWS, ATT_PIECES)
    return run(att_weights_body, ctl, ins, outs, {}, scratch, 16, 2 * 768 * 768 * 768, 6000000, ("rows_sent",))


def half_segments(layout, half_rows, piece, half):
    low = (2 * piece + half) * half_rows
    found, at = [], 0
    for target, rows, first, block in layout:
        start, stop = max(at, low), min(at + rows, low + half_rows)
        if start < stop:
            found.append((start - low, stop - start, target, first + start - at, block))
        at += rows
    return found


def assemble_body(kind, first_piece, layouts, half_rows, chosen, r):
    start_copy = r.copies.start
    core = r.ctl[1]
    blank = None
    if first_piece > 0 and kind == 0:
        r.blank[...] = jnp.zeros_like(r.blank)
        rest = 2 * SPAN - REL_FROM - REL_ROWS
        blank = [
            start_copy(r.blank, r.g_rel.at[pl.ds(0, REL_FROM)]),
            start_copy(r.blank.at[pl.ds(0, rest)], r.g_rel.at[pl.ds(REL_FROM + REL_ROWS, rest)]),
        ]
    branches = []
    chunk = half_rows // 2
    items = [(piece, origin) for piece in chosen for origin in ("own", "sent")]
    for index, (piece, origin) in enumerate(items):
        array = getattr(r, f"{origin}{piece}")
        bit = r.ctl[bit_at(first_piece + piece, origin == "sent")]
        maker = core if origin == "own" else 1 - core
        cases = [(made_by, half) for made_by in range(2) for half in range(2)]
        for at in range(0, half_rows, chunk):
            r.wide[index, at : at + chunk] = array[at : at + chunk].astype(f32)
            first_copy = last_copy = r.copies.used
            for made_by, half in cases:
                r.copies.used = first_copy
                copies = []
                for inside, count, name, start, block in half_segments(layouts[made_by], half_rows, piece, half):
                    low, high = max(inside, at), min(inside + count, at + chunk)
                    if low < high and name not in ("", "vectors"):
                        target = getattr(r, name).at[pl.ds(start + low - inside, high - low), pl.ds(block * D, D)]
                        copies.append(r.copies.make(r.wide.at[index, pl.ds(low, high - low)], target))
                last_copy = max(last_copy, r.copies.used)
                here = (maker == made_by) & (bit == (half if kind == 0 else 1 - half))
                branches.append((here, copies))

                @pl.when(here)
                def _():
                    for copy in copies:
                        copy.start()

            r.copies.used = last_copy
        for made_by, half in cases:
            for inside, count, name, _, _ in half_segments(layouts[made_by], half_rows, piece, half):
                if name == "vectors":

                    @pl.when((maker == made_by) & (bit == (half if kind == 0 else 1 - half)))
                    def _():
                        vectors = r.wide[index, inside : inside + count, :]
                        for part in range(3):
                            r.b_in_v[:, block_at(part)] = vectors[part : part + 1]
                        for part in range(4):
                            r.b_up_v[:, block_at(part)] = vectors[3 + part : 4 + part]
                        r.gains_v[...] = vectors[7:9]
                        r.biases_v[...] = vectors[9:13]
                        wait_all([
                            start_copy(r.b_in_v, r.g_b_in), start_copy(r.b_up_v, r.g_b_up),
                            start_copy(r.gains_v, r.g_gains), start_copy(r.biases_v, r.g_biases),
                        ])

    wait_all(blank or [])
    for here, copies in branches:

        @pl.when(here)
        def _():
            wait_all(copies)


def assemble(kind, first_piece, layouts, rows, pieces, chosen, ctl, own, sent, shapes, held):
    ins = {f"own{i}": value for i, value in zip(chosen, own)}
    ins.update({f"sent{i}": value for i, value in zip(chosen, sent)})
    outs = {name: shape(dims, f32) for name, dims in shapes.items()}
    half_rows = rows // pieces // 2
    scratch = dict(wide=shape((len(ins), half_rows, D), f32))
    if first_piece > 0:
        scratch.update(
            blank=shape((REL_FROM, D), f32), b_in_v=shape((1, 3 * D), f32), b_up_v=shape((1, FF), f32),
            gains_v=shape((2, D), f32), biases_v=shape((4, D), f32),
        )
    body = partial(assemble_body, kind, first_piece, layouts, half_rows, chosen)
    return run(body, ctl, ins, outs, held, scratch, 96, 0, len(ins) * half_rows * D * 6, tuple(ins), 44 * 2**20)


FFN_SHAPES = dict(g_up=(D, FF), g_down=(FF, D), g_out=(D, D), g_in=(D, 3 * D))
ATT_SHAPES = dict(
    g_in=(D, 3 * D), g_rel=(2 * SPAN, D), g_abs=(ABS_ROWS, D),
    g_b_in=(1, 3 * D), g_b_up=(1, FF), g_gains=(2, D), g_biases=(4, D),
)


SQUARE = ((0, 0), (1, 0), (1, 1), (0, 1))


def dp_place(index):
    return {"core": index % 2, "x": index // 2 % 4, "y": index // 8 % 2, "z": index // 16}


def dp_index(place):
    return ((place["z"] * 2 + place["y"]) * 4 + place["x"]) * 2 + place["core"]


def partner(index, dim):
    place = dp_place(index)
    if len(dim) == 2:
        bits = list(SQUARE[place[dim[0]]])
        bits[int(dim[1])] ^= 1
        place[dim[0]] = SQUARE.index(tuple(bits))
    else:
        place[dim] ^= 1
    return dp_index(place)


def swap(value, dims):
    peers = lax.axis_size("dp")
    return lax.ppermute(value, "dp", [(i, partner(i, dims[i % 2])) for i in range(peers)])


BETWEEN_CORES = ("core", "core")


def side_along(dim):
    place = dp_place(lax.axis_index("dp"))
    if dim == "y":
        return place[dim].astype(jnp.int32)
    at = place[dim[0]]
    if dim[1] == "0":
        return ((at == 1) | (at == 2)).astype(jnp.int32)
    return (at >= 2).astype(jnp.int32)


def this_core():
    return (lax.axis_index("dp") % 2).astype(jnp.int32)


def side(dims):
    return jnp.where(this_core() == 0, side_along(dims[0]), side_along(dims[1]))


ORDERS = [
    [("x0", "y"), ("z0", "x1"), ("x1", "z1"), ("y", "z0"), ("z1", "x0")],
    [("x1", "z0"), ("x0", "z1"), ("y", "x0"), ("z1", "x1"), ("z0", "y")],
    [("z1", "y"), ("x1", "z1"), ("y", "z0"), ("x0", "x1"), ("z0", "x0")],
]
BITS_AT = 4 + 2 * (FFN_PIECES + ATT_PIECES)
SPLIT_STEPS = 3


def bit_of(piece, step):
    return BITS_AT + 2 * piece + step - 1


def is_table_row(chunk):
    piece = FFN_PIECES
    first_row, span = 0, ATT_ROWS
    for dims in ORDERS[piece][:SPLIT_STEPS]:
        span //= 2
        first_row = first_row + side(dims) * span
    row_at = first_row + lax.broadcasted_iota(jnp.int32, chunk.shape, 0) - TAIL_AT
    return (row_at >= 0) & (row_at + this_core() * TAIL_HALF < TABLE_ROWS)


class Sequence:
    def __init__(self, last):
        self.last = last

    def after(self, *values):
        values = lax.optimization_barrier((*values, self.last))[:-1]
        return values[0] if len(values) == 1 else values


class Pieces:
    def __init__(self, ctl, seq):
        self.ctl, self.seq = ctl, seq
        self.kept, self.received, self.mine, self.mine_sent, self.partners, self.partners_sent = ({} for _ in range(6))

    def begin(self, piece, kept, sent):
        self.kept[piece], self.received[piece] = kept, swap(sent, ORDERS[piece][0])

    def inputs(self, piece):
        return self.seq.after(self.kept[piece], self.received[piece])

    def hold(self, piece, chunk):
        self.kept[piece] = self.seq.last = chunk

    def land(self, piece):
        self.received[piece] = self.seq.last = self.seq.after(self.received[piece])

    def split(self, piece, step):
        kept, sent = split_sum(self.ctl, bit_of(piece, step), *self.inputs(piece))
        self.hold(piece, kept)
        self.received[piece] = swap(sent, ORDERS[piece][step])

    def add(self, piece, step):
        kept, received = self.inputs(piece)
        self.hold(piece, kept + received)
        self.received[piece] = swap(self.kept[piece], ORDERS[piece][step])

    def add_for_section(self, piece):
        kept, received = self.inputs(piece)
        self.hold(piece, kept + received)
        self.received[piece] = lax.ppermute(self.kept[piece], "section", [(0, 1), (1, 0)])

    def add_tables(self, piece, step):
        kept, received = self.inputs(piece)
        self.hold(piece, jnp.where(is_table_row(kept), kept + received, kept))
        self.received[piece] = swap(self.kept[piece], ORDERS[piece][step])

    def join(self, piece, step):
        self.hold(piece, in_order(self.ctl, bit_of(piece, step), *self.inputs(piece)))
        self.received[piece] = swap(self.kept[piece], ORDERS[piece][step - 1])

    def cross(self, piece):
        self.mine[piece] = self.seq.last = self.seq.after(self.kept[piece])
        self.mine_sent[piece] = swap(self.mine[piece], BETWEEN_CORES)

    def arrive(self, piece):
        self.partners[piece] = self.seq.last = self.seq.after(self.received[piece])
        self.partners_sent[piece] = swap(self.partners[piece], BETWEEN_CORES)


def per_device(
    hidden_in,
    cotangent,
    segment_ids,
    positions,
    w_in,
    b_in,
    w_out,
    w_up,
    b_up,
    w_down,
    gains,
    biases,
    rel_table,
    abs_table,
):
    section = lax.axis_index("section").astype(jnp.int32)
    firsts = jnp.where(section == 1, positions[:, 0], 8 * ABS_ROWS)
    bits = [side(dims) for order in ORDERS for dims in (order[0], order[0][::-1])]
    bits += [side(order[step]) for order in ORDERS for step in range(1, SPLIT_STEPS)]
    ctl = jnp.stack([section, this_core(), firsts[0], firsts[1], *bits])
    weights = dict(w_in=w_in[0], w_out=w_out[0], w_up=w_up[0], w_down=w_down[0], gains=gains[0])
    common = dict(
        weights, hidden_in=hidden_in, segment_ids=segment_ids, biases=biases[0], b_in=b_in, b_up=b_up, abs_table=abs_table
    )

    out = forward(0, 0, ctl, dict(common, rel_table=rel_table), {})
    rel, rel_rows = out["rel"], out["rel_rows"]
    common["rel"] = rel
    received = []
    for row in range(ROWS):
        if row > 0:
            out = forward(row, 0, ctl, common, out)
        received.append(lax.ppermute(out["sent"], "section", [(0, 1)]))
    ready = {name: out[name] for name in ("keep", "resid")}
    back_ins = dict(common, cotangent=cotangent)
    grads = []
    for row in range(ROWS):
        turned = {name: out[name] for name in ("w_up_t", "w_down_t")} if row < ROWS - 1 else {}
        out = {**out, **forward(row, 1, ctl, dict(back_ins, **turned, received=received[row]), out)}
        grads.append(lax.ppermute(out["sent"], "section", [(1, 0)]))
    acts, section_out = out["acts"], out["section_out"]
    acts_sent = swap(acts, BETWEEN_CORES)
    turned = {name: out[name] for name in ("w_up_t", "w_down_t")}
    common = dict(weights, **ready, **turned, rel=rel)
    received = grads
    out.update(tables(ctl, weights["w_in"], out))
    out = backward(0, 0, "both", ctl, dict(common, received=received[0]), out)
    early = out
    ffn = backward(1, 0, "ffn", ctl, dict(common, received=received[1]), early)
    ffn_sent = swap(ffn["ffn_other"], BETWEEN_CORES)
    seq = Sequence(ffn["ffn_own"])
    pieces = Pieces(ctl, seq)
    grads = {}

    def write(kind, group, *chosen):
        own, sent = ((pieces.mine, pieces.mine_sent), (pieces.partners, pieces.partners_sent))[kind]
        first, count, layout, rows, shapes = group
        first_own, *own = [own[first + i] for i in chosen]
        sent = [sent[first + i] for i in chosen]
        result = assemble(kind, first, layout, rows, count, chosen, ctl, [seq.after(first_own), *own], sent, shapes, grads)
        grads.update(result)
        seq.last = result["g_biases"] if first > 0 else result["g_out"]

    ffn_group = 0, FFN_PIECES, FFN_LAYOUT, FFN_ROWS, FFN_SHAPES
    att_group = FFN_PIECES, ATT_PIECES, ATT_LAYOUT, ATT_ROWS, ATT_SHAPES
    ins = dict(common, d_resid=seq.after(ffn["d_resid"]), d_context=ffn["d_context"], ffn_vec=ffn["ffn_vec"])
    out = backward(1, 0, "att", ctl, ins, early)
    att_sent = swap(out["att_other"], BETWEEN_CORES)
    seq.last = out["att_own"]
    halves = ffn_weights(ctl, acts=acts, acts_sent=acts_sent, rows=seq.after(ffn["ffn_own"]), rows_sent=ffn_sent)
    for piece in range(FFN_PIECES):
        pieces.begin(piece, halves[f"kept{piece}"], halves[f"sent{piece}"])
    seq.last = halves["kept0"]
    halves = att_weights(
        ctl, acts=acts, acts_sent=acts_sent, rows=seq.after(out["att_own"]), rows_sent=att_sent, table=rel_rows
    )
    pieces.begin(FFN_PIECES, halves["kept0"], halves["sent0"])
    seq.last = halves["kept0"]
    input_grad = finish(
        ctl, early, d_resid=ffn["d_resid"], d_rows=seq.after(out["d_rows"]), d_context=ffn["d_context"], w_in=weights["w_in"]
    )
    seq.last = input_grad
    pieces.split(0, 1)
    pieces.split(1, 1)
    pieces.land(2)
    pieces.split(0, 2)
    pieces.split(1, 2)
    pieces.split(2, 1)
    pieces.add(0, 3)
    pieces.add(1, 3)
    pieces.split(2, 2)
    pieces.add(0, 4)
    pieces.add(1, 4)
    pieces.add(2, 3)
    pieces.add(0, 2)
    pieces.land(1)
    pieces.add(2, 4)
    pieces.add(1, 2)
    pieces.join(0, 2)
    pieces.add_for_section(2)
    pieces.join(1, 2)
    pieces.add_tables(2, 2)
    pieces.join(0, 1)
    pieces.cross(0)
    pieces.join(2, 2)
    pieces.join(1, 1)
    pieces.cross(1)
    pieces.join(2, 1)
    pieces.cross(2)
    write(0, att_group, 0)
    pieces.arrive(0)
    write(0, ffn_group, 0, 1)
    pieces.arrive(1)
    pieces.arrive(2)
    write(1, ffn_group, 0, 1)
    write(1, att_group, 0)
    return (
        section_out[None],
        input_grad[None],
        grads["g_in"][None],
        grads["g_b_in"],
        grads["g_out"][None],
        grads["g_up"][None],
        grads["g_b_up"],
        grads["g_down"][None],
        grads["g_gains"][None],
        grads["g_biases"][None],
        grads["g_rel"],
        grads["g_abs"],
    )


def solution(mesh):
    in_specs = (
        P("dp", None, None),
        P("dp", None, None),
        P("dp", None),
        P("dp", None),
        P("section", None, None),
        P("section", None),
        P("section", None, None),
        P("section", None, None),
        P("section", None),
        P("section", None, None),
        P("section", None, None),
        P("section", None, None),
        P(),
        P(),
    )
    out_specs = (
        P("section", "dp", None, None),
        P("section", "dp", None, None),
        P("section", None, None),
        P("section", None),
        P("section", None, None),
        P("section", None, None),
        P("section", None),
        P("section", None, None),
        P("section", None, None),
        P("section", None, None),
        P(),
        P(),
    )
    return jax.shard_map(
        per_device, mesh=mesh, in_specs=in_specs, out_specs=out_specs, check_vma=False
    )
```

```python
from functools import partial
import math
from types import SimpleNamespace

import jax
import jax.numpy as jnp
from jax import lax
from jax.experimental import pallas as pl
from jax.experimental.pallas import tpu as pltpu
from jax.sharding import PartitionSpec as P

HEADS = 12
L = 128
D = 768
FF = 3072
HALF = D // 2
PAIRS = HEADS // 2
ROWS = 2
SPAN = 256
EPS = 1e-06
NEG = -1e30
SCALE = 1.0 / math.sqrt(3 * 64)
VMEM_LIMIT = 61 * 1024 * 1024
f32, bf16 = jnp.float32, jnp.bfloat16

A_START, A_X, A_CTX, A_HID, A_ACT, A_ALL = 0, 768, 1536, 2304, 3072, 6144
K_P, K_GP, K_ALL = 2304, 3840, 6912
VECTOR_ROWS = 16
REL_FROM, REL_ROWS, ABS_ROWS, TAIL_ROWS = 128, 272, 512, 896
TABLE_ROWS = REL_ROWS + ABS_ROWS
FFN_LAYOUT = [
    [("g_up", D, 0, 2 * core), ("g_up", D, 0, 2 * core + 1), ("g_down", 2 * D, 2 * D * core, 0), ("g_out", HALF, HALF * core, 0),
     ("g_in", HALF, HALF * core, 2)]
    for core in range(2)
]
ATT_LAYOUT = [
    [("g_in", D, 0, 0), ("g_rel", REL_ROWS, REL_FROM, 0), ("g_abs", 176, 0, 0)],
    [("g_in", D, 0, 1), ("g_abs", 336, 176, 0), ("vectors", VECTOR_ROWS, 0, 0), ("", 96, 0, 0)],
]
FFN_ROWS, ATT_ROWS = 3840, 1216
FFN_PIECES, ATT_PIECES = 2, 1
TAIL_HALF = TAIL_ROWS // 2
TAIL_AT = ATT_ROWS - TAIL_HALF
SWAP_ROWS = 4 * L + TAIL_HALF

VMEM = pl.BlockSpec(memory_space=pltpu.VMEM)
ANY = pl.BlockSpec(memory_space=pl.ANY)
SMEM = pl.BlockSpec(memory_space=pltpu.SMEM)


def nn(a, b):
    return lax.dot_general(a, b, (((1,), (0,)), ((), ())), preferred_element_type=f32)


def nt(a, b):
    return lax.dot_general(a, b, (((1,), (1,)), ((), ())), preferred_element_type=f32)


def tn(a, b):
    return lax.dot_general(a, b, (((0,), (0,)), ((), ())), preferred_element_type=f32)


def norm_parts(value):
    centered = value - jnp.mean(value, axis=1, keepdims=True)
    rstd = lax.rsqrt(jnp.mean(centered * centered, axis=1, keepdims=True) + EPS)
    return centered * rstd, rstd


def norm_backward(normed, rstd, gain, grad):
    scaled = grad * gain
    mean_one = jnp.mean(scaled, axis=1, keepdims=True)
    mean_two = jnp.mean(scaled * normed, axis=1, keepdims=True)
    return (scaled - mean_one - normed * mean_two) * rstd


def column_sums(value):
    return jnp.sum(value, axis=0, keepdims=True)


def indicator(condition):
    return condition.astype(f32).astype(bf16)


def lane_halves():
    lane = lax.broadcasted_iota(jnp.int32, (1, L), 1)
    return indicator(lane < 64), indicator(lane >= 64)


def stacked(value, halves):
    return jnp.concatenate([value * halves[0], value * halves[1]], axis=0)


def skew(table):
    return pltpu.roll(table, L, 1, stride=1, stride_axis=0)[:, :L]


def unskew(turned):
    wide = jnp.concatenate([turned, jnp.zeros_like(turned)], axis=1)
    return pltpu.roll(wide, 1, 1, stride=1, stride_axis=0)


def pair_at(pair, base=0, width=L):
    return pl.ds(pl.multiple_of(base + pair * width, L), width)


def block_at(block, base=0):
    return slice(base + block * D, base + block * D + D)


def shape(dims, dtype=bf16):
    return jax.ShapeDtypeStruct(dims, dtype)


class Copies:
    def __init__(self, sems):
        self.sems, self.used, self.marks = sems, 0, {}

    def make(self, source, target):
        self.used += 1
        return pltpu.make_async_copy(source, target, self.sems.at[self.used - 1])

    def make_at(self, name):
        again = self.marks.setdefault(name, self.used)
        if again == self.used:
            return self.make
        at = iter(range(again, self.used))
        return lambda source, target: pltpu.make_async_copy(source, target, self.sems.at[next(at)])

    def start(self, source, target):
        copy = self.make(source, target)
        copy.start()
        return copy


def wait_all(copies):
    for copy in copies:
        copy.wait()


def run(body, ctl, ins, outs, held, scratch, copies, flops, traffic, near=(), limit=VMEM_LIMIT):
    names, out_names, scratch_names = list(ins), list(outs), list(scratch)
    kept = [name for name in out_names if name in held and name != "sent"]

    def kernel(*refs):
        ctl_ref, refs = refs[0], refs[1:]
        r = SimpleNamespace(ctl=ctl_ref, **dict(zip(names, refs)))
        refs = refs[len(names) + len(kept) :]
        for name, ref in zip(out_names + scratch_names, refs):
            setattr(r, name, ref)
        r.copies = Copies(refs[-1])
        body(r)

    results = pl.pallas_call(
        kernel,
        out_shape=tuple(outs.values()),
        in_specs=[SMEM] + [VMEM if name in near else ANY for name in names] + [ANY] * len(kept),
        out_specs=(ANY,) * len(out_names),
        input_output_aliases={1 + len(names) + i: out_names.index(name) for i, name in enumerate(kept)},
        scratch_shapes=[pltpu.VMEM(s.shape, s.dtype) for s in scratch.values()] + [pltpu.SemaphoreType.DMA((copies,))],
        compiler_params=pltpu.CompilerParams(vmem_limit_bytes=limit),
        cost_estimate=pl.CostEstimate(flops=flops, bytes_accessed=traffic, transcendentals=0),
    )(ctl, *ins.values(), *[held[name] for name in kept])
    return dict(zip(out_names, results))


def relative_loads(r):
    return [r.copies.start(r.rel_table, r.table_v), r.copies.start(r.b_in, r.b_in_v), r.copies.start(r.w_in, r.wi)]


def relative_part(r, loads):
    dims = (2 * L, 2 * SPAN)
    select = indicator(lax.broadcasted_iota(jnp.int32, dims, 0) + lax.broadcasted_iota(jnp.int32, dims, 1) == L + SPAN)
    loads[0].wait()
    rows = nn(select, r.table_v[...]).astype(bf16)
    r.rel_rows_v[...] = rows
    loads[1].wait()
    loads[2].wait()
    r.rel_v[...] = (nn(rows, r.wi[:, : 2 * D]) + r.b_in_v[:, : 2 * D].astype(f32)).astype(bf16)
    return [r.copies.start(r.rel_rows_v, r.rel_rows), r.copies.start(r.rel_v, r.rel)]


def forward_loads(row, section, first, r):
    make = r.copies.make_at("loads")
    loads = SimpleNamespace(
        x=[make(r.hidden_in.at[row] if section == 0 else r.received, r.x_v)],
        absolute=[make(r.abs_table, r.table_v)] if section == 1 else [],
        w_in=[]
        if first
        else [make(r.b_in, r.b_in_v)] + [make(r.w_in.at[:, block_at(part)], r.wi.at[:, block_at(part)]) for part in range(3)],
        rel=[] if first else [make(r.rel, r.rel_v)],
        small=[make(r.segment_ids, r.seg_v), make(r.gains, r.gains_v), make(r.biases, r.biases_v)],
        out=[make(r.w_out, r.wo), make(r.b_up, r.b_up_v)],
        parts=[
            [
                make(r.w_up.at[:, block_at(part)], r.wu.at[:, block_at(part)]),
                make(r.w_down.at[block_at(part)], r.wd.at[block_at(part)]),
            ]
            for part in range(4)
        ],
    )
    flat = loads.x + loads.absolute + loads.w_in + loads.rel + loads.small + loads.out
    loads.every = flat + [copy for part in loads.parts for copy in part]
    return loads


def forward_body(row, section, first, r):
    start_copy = r.copies.start
    stores = []
    if first:
        rel_loads = relative_loads(r)

        @pl.when(r.ctl[0] == section)
        def _():
            for copy in forward_loads(row, section, first, r).every:
                copy.start()

        stores = relative_part(r, rel_loads)

    @pl.when(r.ctl[0] == section)
    def _():
        loads = forward_loads(row, section, first, r)
        if not first:
            for copy in loads.every:
                copy.start()
        if section == 1:
            back = SimpleNamespace(
                first=[start_copy(r.cotangent.at[row], r.grad_v)],
                parts=[
                    [
                        start_copy(r.w_down_t.at[:, block_at(part)], r.wd_t.at[:, block_at(part)]),
                        start_copy(r.w_up_t.at[block_at(part)], r.wu_t.at[block_at(part)]),
                    ]
                    for part in range(4)
                ],
                last=[],
            )
            earlier = [start_copy(r.d_rel, r.d_rel_old)] if row > 0 else []
            back_att = SimpleNamespace(first=[], earlier=earlier, w_in=[], others=[])
        halves = lane_halves()
        wait_all(loads.x)
        x = r.x_v[...]
        start = x.astype(f32)
        if section == 1:
            wait_all(loads.absolute)
            dims = (L, ABS_ROWS)
            place = lax.broadcasted_iota(jnp.int32, dims, 1) - lax.broadcasted_iota(jnp.int32, dims, 0)
            start = start + nn(indicator(place == r.ctl[2 + row]), r.table_v[...])
        query_in = start.astype(bf16)
        r.acts_v[:, block_at(0)] = query_in
        r.acts_v[:, block_at(1)] = x
        wait_all(loads.w_in[:2])
        b_in = r.b_in_v[...].astype(f32)
        r.keep_v[:, :D] = (nn(query_in, r.wi[:, :D]) + b_in[:, :D]).astype(bf16)
        wait_all(loads.w_in[2:])
        r.keep_v[:, D : 3 * D] = (nn(x, r.wi[:, D:]) + b_in[:, D:]).astype(bf16)
        wait_all(loads.small + loads.rel)
        seg_rows = jnp.broadcast_to(r.seg_v[row : row + 1, :], (L, L)).astype(f32)
        same = seg_rows == seg_rows.T
        def attend(pair):
            query = r.keep_v[:, pair_at(pair)]
            key = r.keep_v[:, pair_at(pair, D)]
            value = r.keep_v[:, pair_at(pair, 2 * D)]
            query_two, key_two = stacked(query, halves), stacked(key, halves)
            content = nt(query_two, key)
            far_query = nt(query_two, r.rel_v[:, pair_at(pair, D)])
            far_key = nt(key_two, r.rel_v[:, pair_at(pair)])
            probs = []
            for head in range(2):
                rows = slice(head * L, head * L + L)
                summed = content[rows] + skew(far_query[rows]) + skew(far_key[rows]).T
                scores = jnp.where(same, summed * SCALE, NEG)
                exponent = jnp.exp(scores - jnp.max(scores, axis=1, keepdims=True))
                total = jnp.sum(exponent, axis=1, keepdims=True)
                probs.append((exponent * (1.0 / total)).astype(bf16))
            probs = jnp.concatenate(probs, axis=1)
            r.keep_v[:, pair_at(pair, K_P, 2 * L)] = probs
            r.acts_v[:, pair_at(pair, A_CTX)] = nn(probs, stacked(value, halves)).astype(bf16)

        if section == 0:
            for pair in range(PAIRS):
                attend(pair)
        else:
            pl.loop(0, PAIRS, unroll=3)(attend)
        wait_all(loads.out)
        gain = r.gains_v[...].astype(f32)
        shift = r.biases_v[...].astype(f32)
        resid_one = start + nn(r.acts_v[:, A_CTX : A_CTX + D], r.wo[...]) + shift[0:1]
        r.resid_v[:, :D] = resid_one
        hidden = norm_parts(resid_one)[0] * gain[0:1] + shift[1:2]
        hidden_low = hidden.astype(bf16)
        r.acts_v[:, A_HID : A_HID + D] = hidden_low
        stored = [start_copy(r.acts_v.at[:, pl.ds(0, A_ACT)], r.acts.at[row, :, pl.ds(0, A_ACT)])]
        if section == 0:
            stored.append(start_copy(r.keep_v.at[:, pl.ds(0, K_GP)], r.keep.at[row, :, pl.ds(0, K_GP)]))
        total = hidden + shift[2:3]
        for part in range(4):
            wait_all(loads.parts[part])
            gate = nn(hidden_low, r.wu[:, block_at(part)]) + r.b_up_v[:, block_at(part)].astype(f32)
            below = 0.5 + 0.5 * lax.erf(gate * (1.0 / math.sqrt(2.0)))
            density = jnp.exp(gate * gate * -0.5) * (1.0 / math.sqrt(2.0 * math.pi))
            active = (gate * below).astype(bf16)
            r.acts_v[:, block_at(part, A_ACT)] = active
            r.keep_v[:, block_at(part, K_GP)] = (below + gate * density).astype(bf16)
            stored.append(start_copy(r.acts_v.at[:, block_at(part, A_ACT)], r.acts.at[row, :, block_at(part, A_ACT)]))
            if section == 0:
                stored.append(start_copy(r.keep_v.at[:, block_at(part, K_GP)], r.keep.at[row, :, block_at(part, K_GP)]))
            total = total + nn(active, r.wd[block_at(part), :])
        r.resid_v[:, D:] = total
        if section == 0:
            stored.append(start_copy(r.resid_v, r.resid.at[row]))
        r.x_v[...] = (norm_parts(total)[0] * gain[1:2] + shift[3:4]).astype(bf16)
        stored.append(start_copy(r.x_v, r.section_out.at[row]))
        if section == 0:
            stored.append(start_copy(r.x_v, r.sent))
        else:
            near = SimpleNamespace(**vars(r))
            near.wu, near.wd = r.wu_t, r.wd_t
            near.probs_v = r.keep_v.at[:, pl.ds(K_P, K_GP - K_P)]
            near.slope_v = r.keep_v.at[:, pl.ds(K_GP, FF)]
            d_resid, out_copies = ffn_part(row, section, near, back)
            r.value_v[...] = r.ffn_v[:, FF + 2 * D :]
            stored += out_copies + att_part(row, section, near, back_att, d_resid)
        wait_all(stored)

    wait_all(stores)
    if row == ROWS - 1:

        @pl.when(r.ctl[0] != section)
        def _():
            turn_weights(r)


def turn_weights(r):
    jobs = [(r.w_up, r.wu, r.w_up_t, 0, part) for part in range(4)]
    jobs += [(r.w_down, r.wd, r.w_down_t, part, 0) for part in range(4)]
    loads = [
        r.copies.start(source.at[block_at(row), block_at(column)], near.at[block_at(row), block_at(column)])
        for source, near, _, row, column in jobs
    ]
    stores = []
    for load, (source, near, target, row, column) in zip(loads, jobs):
        load.wait()
        turned = r.wu_t if near is r.wu else r.wd_t
        turned[block_at(column), block_at(row)] = near[block_at(row), block_at(column)].T
        stores.append(
            r.copies.start(turned.at[block_at(column), block_at(row)], target.at[block_at(column), block_at(row)])
        )
    wait_all(stores)


def forward(row, section, ctl, ins, held):
    first = not held
    outs = {"sent": shape((L, D))}
    if first:
        outs.update(rel_rows=shape((2 * L, D)), rel=shape((2 * L, 2 * D)))
    outs.update(acts=shape((ROWS, L, A_ALL)), section_out=shape((ROWS, L, D)))
    scratch = dict(
        x_v=shape((L, D)), seg_v=shape((ROWS, L), jnp.int32), gains_v=shape((2, D)), biases_v=shape((4, D)),
        b_in_v=shape((1, 3 * D)), b_up_v=shape((1, FF)), table_v=shape((2 * SPAN, D)), rel_v=shape((2 * L, 2 * D)),
        wi=shape((D, 3 * D)), wo=shape((D, D)), wu=shape((D, FF)), wd=shape((FF, D)),
        acts_v=shape((L, A_ALL)), keep_v=shape((L, K_ALL)), resid_v=shape((L, 2 * D), f32),
    )
    if section == 0:
        outs.update(keep=shape((ROWS, L, K_ALL)), resid=shape((ROWS, L, 2 * D), f32))
    else:
        outs.update(backward_results(row, section))
        scratch.update(
            grad_v=shape((L, D)), ffn_v=shape((L, FF + 3 * D)), context_v=shape((L, D)), ffn_vec_v=shape((VECTOR_ROWS, D), f32),
            att_v=shape((L, 2 * D)), att_vec_v=shape((VECTOR_ROWS, D), f32), start_v=shape((L, D)), grad_out_v=shape((L, D)),
            value_v=shape((L, D)), d_rel_v=shape((2 * L, 2 * D), f32), d_rel_old=shape((2 * L, 2 * D), f32),
            rel_low=shape((2 * L, 2 * D)),
        )
    if first:
        scratch.update(rel_rows_v=shape((2 * L, D)))
    if row == ROWS - 1:
        outs.update(w_up_t=shape((FF, D)), w_down_t=shape((D, FF)))
    if row == ROWS - 1 or section == 1:
        scratch.update(wu_t=shape((FF, D)), wd_t=shape((D, FF)))
    return run(partial(forward_body, row, section, first), ctl, ins, outs, held, scratch, 84, 1900000000, 18000000)


def backward_results(row, section):
    results = dict(
        ffn_own=shape((ROWS * L, 5 * D)), ffn_other=shape((ROWS * L, 5 * D)), ffn_vec=shape((ROWS, VECTOR_ROWS, D), f32),
        att_own=shape((SWAP_ROWS, D)), att_other=shape((SWAP_ROWS, D)), att_vec=shape((ROWS, VECTOR_ROWS, D), f32),
        d_start=shape((ROWS, L, D)), d_rel=shape((2 * L, 2 * D), f32), d_rel_low=shape((2 * L, 2 * D)),
        input_grad=shape((ROWS, L, D)),
    )
    return results


def ffn_loads(row, section, r):
    return SimpleNamespace(
        first=[r.copies.start(source, near) for source, near in ((r.received, r.grad_v), (r.resid.at[row], r.resid_v), (r.gains, r.gains_v))],
        parts=[
            [
                r.copies.start(r.w_down_t.at[:, block_at(part)], r.wd.at[:, block_at(part)]),
                r.copies.start(r.keep.at[row, :, block_at(part, K_GP)], r.slope_v.at[:, block_at(part)]),
                r.copies.start(r.w_up_t.at[block_at(part)], r.wu.at[block_at(part)]),
            ]
            for part in range(4)
        ],
        last=[r.copies.start(r.w_out, r.wo), r.copies.start(r.keep.at[row, :, pl.ds(K_P, K_GP - K_P)], r.probs_v)],
    )


def ffn_part(row, section, r, loads):
    wait_all(loads.first)
    gain = r.gains_v[...].astype(f32)
    grad = r.grad_v[...].astype(f32)
    normed, rstd = norm_parts(r.resid_v[:, D:])
    r.ffn_vec_v[...] = jnp.zeros_like(r.ffn_vec_v)
    r.ffn_vec_v[8:9] = column_sums(grad * normed)
    r.ffn_vec_v[12:13] = column_sums(grad)
    d_two = norm_backward(normed, rstd, gain[1:2], grad)
    d_down = d_two.astype(bf16)
    r.ffn_v[:, FF : FF + D] = d_down
    r.ffn_vec_v[11:12] = column_sums(d_down.astype(f32))
    d_hidden = d_two
    for part in range(4):
        wait_all(loads.parts[part])
        d_gate = (nn(d_down, r.wd[:, block_at(part)]) * r.slope_v[:, block_at(part)].astype(f32)).astype(bf16)
        r.ffn_v[:, block_at(part)] = d_gate
        r.ffn_vec_v[3 + part : 4 + part] = column_sums(d_gate.astype(f32))
        d_hidden = d_hidden + nn(d_gate, r.wu[block_at(part), :])
    normed, rstd = norm_parts(r.resid_v[:, :D])
    r.ffn_vec_v[7:8] = column_sums(d_hidden * normed)
    r.ffn_vec_v[10:11] = column_sums(d_hidden)
    d_resid = norm_backward(normed, rstd, gain[0:1], d_hidden)
    d_att = d_resid.astype(bf16)
    r.ffn_v[:, FF + D : FF + 2 * D] = d_att
    r.ffn_vec_v[9:10] = column_sums(d_att.astype(f32))
    wait_all(loads.last)
    r.context_v[...] = nt(d_att, r.wo[...]).astype(bf16)
    halves = lane_halves()
    for pair in range(PAIRS):
        d_value = tn(two_heads(r.probs_v, pair), stacked(r.context_v[:, pair_at(pair)], halves))
        r.ffn_v[:, pair_at(pair, FF + 2 * D)] = d_value.astype(bf16)
    r.ffn_vec_v[2:3] = column_sums(r.ffn_v[:, FF + 2 * D :].astype(f32))
    stores, rows = [], pl.ds(row * L, L)
    for side_core, target in ((r.ctl[1], r.ffn_own), (1 - r.ctl[1], r.ffn_other)):
        gates = pl.ds(pl.multiple_of(side_core * 2 * D, 128), 2 * D)
        stores.append(r.copies.start(r.ffn_v.at[:, gates], target.at[rows, pl.ds(0, 2 * D)]))
        stores.append(r.copies.start(r.ffn_v.at[:, pl.ds(FF, 3 * D)], target.at[rows, pl.ds(2 * D, 3 * D)]))
    stores.append(r.copies.start(r.ffn_vec_v, r.ffn_vec.at[row]))
    return d_resid, stores


def two_heads(probs, pair):
    columns = probs[:, pair_at(pair, 0, 2 * L)]
    return jnp.concatenate([columns[:, :L], columns[:, L:]], axis=0)


def att_loads(row, section, r):
    return SimpleNamespace(
        first=[r.copies.start(r.keep.at[row, :, pl.ds(0, K_P)], r.keep_v), r.copies.start(r.rel, r.rel_v)],
        earlier=[r.copies.start(r.d_rel, r.d_rel_old)] if row > 0 else [],
        w_in=[r.copies.start(r.w_in, r.wi)],
        others=[
            r.copies.start(r.att_vec.at[0], r.att_vec_old),
            r.copies.start(r.ffn_vec, r.ffn_vec_v),
        ]
        if row == ROWS - 1 and section == 0
        else [],
    )


def att_part(row, section, r, loads, d_resid):
    halves = lane_halves()
    row_at = lax.broadcasted_iota(jnp.int32, (L, L), 0)
    column_at = lax.broadcasted_iota(jnp.int32, (L, L), 1)
    turn = indicator(row_at + column_at == L - 1)
    r.att_vec_v[...] = jnp.zeros_like(r.att_vec_v)
    wait_all(loads.first)
    for pair in range(PAIRS):
        query = r.keep_v[:, pair_at(pair)]
        key = r.keep_v[:, pair_at(pair, D)]
        value = r.keep_v[:, pair_at(pair, 2 * D)]
        probs_two = two_heads(r.probs_v, pair)
        rel_q, rel_k = r.rel_v[:, pair_at(pair)], r.rel_v[:, pair_at(pair, D)]
        context_two = stacked(r.context_v[:, pair_at(pair)], halves)
        probs_f = probs_two.astype(f32)
        weighted = nt(context_two, value) * probs_f
        d_scores = (weighted - probs_f * jnp.sum(weighted, axis=1, keepdims=True)).astype(bf16)
        query_two, key_two = stacked(query, halves), stacked(key, halves)
        d_key = tn(d_scores, query_two)
        d_side = jnp.concatenate([d_scores[:L], d_scores[L:]], axis=1)
        d_query = nn(d_side, key_two)
        d_far = (d_side.astype(f32) * SCALE).astype(bf16)
        query_turned = nn(turn, query).astype(bf16)
        key_turned = nn(turn, key).astype(bf16)
        rows_turned = nn(turn, d_far)
        far_query, far_key = [], []
        for head in range(2):
            columns = slice(head * L, head * L + L)
            far_query.append(unskew(rows_turned[:, columns]).astype(bf16))
            far_key.append(unskew(nt(turn, d_far[:, columns])).astype(bf16))
        d_query_turned = nn(jnp.concatenate(far_query, axis=1), stacked(rel_k, halves))
        d_key_turned = nn(jnp.concatenate(far_key, axis=1), stacked(rel_q, halves))
        r.d_rel_v[:, pair_at(pair)] = tn(jnp.concatenate(far_key, axis=0), stacked(key_turned, halves))
        r.d_rel_v[:, pair_at(pair, D)] = tn(jnp.concatenate(far_query, axis=0), stacked(query_turned, halves))
        d_query = d_query * SCALE + nn(turn, d_query_turned.astype(bf16))
        d_key = d_key * SCALE + nn(turn, d_key_turned.astype(bf16))
        r.att_v[:, pair_at(pair)] = d_query.astype(bf16)
        r.att_v[:, pair_at(pair, D)] = d_key.astype(bf16)
    stores = []
    for side_core, target in ((r.ctl[1], r.att_own), (1 - r.ctl[1], r.att_other)):
        query_or_key = pl.ds(pl.multiple_of(side_core * D, 128), D)
        stores.append(r.copies.start(r.att_v.at[:, query_or_key], target.at[pl.ds(row * L, L)]))
    far_sums = [column_sums(r.d_rel_v[:, block_at(part)]) for part in range(2)]
    if row > 0:
        wait_all(loads.earlier)
        r.d_rel_v[...] = r.d_rel_v[...] + r.d_rel_old[...]
    last = row == ROWS - 1
    if last:
        r.rel_low[...] = r.d_rel_v[...].astype(bf16)
        for side_core, target in ((r.ctl[1], r.att_own), (1 - r.ctl[1], r.att_other)):
            query_or_key = pl.ds(pl.multiple_of(side_core * D, 128), D)
            stores.append(r.copies.start(r.rel_low.at[:, query_or_key], target.at[pl.ds(2 * L, 2 * L)]))
    else:
        stores.append(r.copies.start(r.d_rel_v, r.d_rel))
    for part in range(2):
        rows = column_sums(r.att_v[:, block_at(part)].astype(f32)) + far_sums[part]
        r.att_vec_v[part : part + 1] = rows
    stores.append(r.copies.start(r.att_vec_v, r.att_vec.at[row]))
    wait_all(loads.w_in)
    if last and section == 0:
        stores.append(r.copies.start(r.att_v, r.d_rows))
        wait_all(loads.others)
        return stores + tail_part(r, None, r.ffn_vec_v[0] + r.ffn_vec_v[1] + r.att_vec_old[...] + r.att_vec_v[...])
    d_start = d_resid + nt(r.att_v[:, :D], r.wi[:, :D])
    r.start_v[...] = d_start.astype(bf16)
    stores.append(r.copies.start(r.start_v, r.d_start.at[row]))
    result = d_start + nt(r.att_v[:, D:], r.wi[:, D : 2 * D]) + nt(r.value_v[...], r.wi[:, 2 * D :])
    r.grad_out_v[...] = result.astype(bf16)
    stores.append(r.copies.start(r.grad_out_v, r.input_grad.at[row]))
    if section == 1:
        stores.append(r.copies.start(r.grad_out_v, r.sent))
        if last:
            stores.append(r.copies.start(r.rel_low, r.d_rel_low))
    return stores


def finish_body(r):
    @pl.when(r.ctl[0] == 0)
    def _():
        loads = [
            r.copies.start(source, target)
            for source, target in (
                (r.d_resid, r.resid_v), (r.d_rows, r.rows_v), (r.d_context.at[:, pl.ds(D, D)], r.value_v), (r.w_in, r.wi)
            )
        ]
        wait_all(loads)
        result = r.resid_v[...] + nt(r.rows_v[...], r.wi[:, : 2 * D]) + nt(r.value_v[...], r.wi[:, 2 * D :])
        r.grad_v[...] = result.astype(bf16)
        r.copies.start(r.grad_v, r.input_grad.at[ROWS - 1]).wait()


def finish(ctl, held, **ins):
    outs = dict(input_grad=shape((ROWS, L, D)))
    scratch = dict(
        resid_v=shape((L, D), f32), rows_v=shape((L, 2 * D)), value_v=shape((L, D)), wi=shape((D, 3 * D)), grad_v=shape((L, D))
    )
    return run(finish_body, ctl, ins, outs, held, scratch, 5, 500000000, 5000000)["input_grad"]


def tail_part(r, starts, vectors):
    def put(first, rows, value):
        r.tail_v[first : first + rows] = value.astype(bf16)

    if starts is None:
        put(REL_ROWS, ABS_ROWS, jnp.zeros((ABS_ROWS, D), f32))
    else:
        dims = (ABS_ROWS, L)
        place = lax.broadcasted_iota(jnp.int32, dims, 0) - lax.broadcasted_iota(jnp.int32, dims, 1)
        spots = [indicator(place == r.ctl[2 + row]) for row in range(ROWS)]
        put(REL_ROWS, ABS_ROWS, nn(spots[0], starts[0]) + nn(spots[1], starts[1]))
    put(TABLE_ROWS, VECTOR_ROWS, vectors)
    rest = TAIL_ROWS - TABLE_ROWS - VECTOR_ROWS
    put(TABLE_ROWS + VECTOR_ROWS, rest, jnp.zeros((rest, D), f32))
    rows = nt(r.rel_low[...], r.wi[:, : 2 * D]).astype(bf16)
    dims = (REL_ROWS, 2 * L)
    select = lax.broadcasted_iota(jnp.int32, dims, 0) + lax.broadcasted_iota(jnp.int32, dims, 1) == L + SPAN - REL_FROM
    put(0, REL_ROWS, nn(indicator(select), rows))
    return [
        r.copies.start(
            r.tail_v.at[pl.ds(pl.multiple_of(side_core * TAIL_HALF, 16), TAIL_HALF)], target.at[pl.ds(4 * L, TAIL_HALF)]
        )
        for side_core, target in ((r.ctl[1], r.att_own), (1 - r.ctl[1], r.att_other))
    ]


def backward_body(row, section, parts, r):
    @pl.when(r.ctl[0] == section)
    def _():
        if parts == "ffn":
            d_resid, stores = ffn_part(row, section, r, ffn_loads(row, section, r))
            r.resid_v[:, :D] = d_resid
            stores.append(r.copies.start(r.resid_v.at[:, pl.ds(0, D)], r.d_resid))
            stores.append(r.copies.start(r.context_v, r.d_context.at[:, pl.ds(0, D)]))
            stores.append(r.copies.start(r.ffn_v.at[:, pl.ds(FF + 2 * D, D)], r.d_context.at[:, pl.ds(D, D)]))
        elif parts == "att":
            first = [
                r.copies.start(r.d_resid, r.d_resid_v),
                r.copies.start(r.d_context.at[:, pl.ds(0, D)], r.context_v),
                r.copies.start(r.keep.at[row, :, pl.ds(K_P, K_GP - K_P)], r.probs_v),
                r.copies.start(r.d_context.at[:, pl.ds(D, D)], r.value_v),
            ]
            loads = att_loads(row, section, r)
            wait_all(first)
            stores = att_part(row, section, r, loads, r.d_resid_v[...])
        else:
            loads = ffn_loads(row, section, r)
            later = att_loads(row, section, r)
            d_resid, stores = ffn_part(row, section, r, loads)
            r.value_v[...] = r.ffn_v[:, FF + 2 * D :]
            stores = stores + att_part(row, section, r, later, d_resid)
        wait_all(stores)


def backward(row, section, parts, ctl, ins, held):
    outs, scratch, flops, traffic = {}, {}, 0, 0
    if parts == "ffn":
        outs.update(d_resid=shape((L, D), f32), d_context=shape((L, 2 * D)))
    if parts != "att":
        outs.update(
            ffn_own=shape((ROWS * L, 5 * D)), ffn_other=shape((ROWS * L, 5 * D)), ffn_vec=shape((ROWS, VECTOR_ROWS, D), f32)
        )
        scratch.update(
            grad_v=shape((L, D)), resid_v=shape((L, 2 * D), f32), gains_v=shape((2, D)), slope_v=shape((L, FF)),
            wu=shape((FF, D)), wd=shape((D, FF)), ffn_v=shape((L, FF + 3 * D)), wo=shape((D, D)), probs_v=shape((L, 2 * D)), context_v=shape((L, D)), ffn_vec_v=shape((VECTOR_ROWS, D), f32),
        )
        flops, traffic = flops + 1300000000, traffic + 12000000
    if parts == "att":
        scratch.update(d_resid_v=shape((L, D), f32), context_v=shape((L, D)), probs_v=shape((L, 2 * D)))
    if parts != "ffn":
        if section == 1:
            outs.update(sent=shape((L, D)))
        outs.update(
            att_own=shape((SWAP_ROWS, D)), att_other=shape((SWAP_ROWS, D)), att_vec=shape((ROWS, VECTOR_ROWS, D), f32),
            d_start=shape((ROWS, L, D)), d_rel=shape((2 * L, 2 * D), f32), d_rel_low=shape((2 * L, 2 * D)),
            input_grad=shape((ROWS, L, D)),
        )
        scratch.update(
            wi=shape((D, 3 * D)), keep_v=shape((L, K_P)), rel_v=shape((2 * L, 2 * D)),
            att_v=shape((L, 2 * D)), att_vec_v=shape((VECTOR_ROWS, D), f32), start_v=shape((L, D)), grad_out_v=shape((L, D)),
            value_v=shape((L, D)), d_rel_v=shape((2 * L, 2 * D), f32), d_rel_old=shape((2 * L, 2 * D), f32), rel_low=shape((2 * L, 2 * D)),
        )
        if row == ROWS - 1 and section == 0:
            outs.update(d_rows=shape((L, 2 * D)))
            del outs["input_grad"], outs["d_start"]
            scratch.update(
                tail_v=shape((TAIL_ROWS, D)),
                att_vec_old=shape((VECTOR_ROWS, D), f32), ffn_vec_v=shape((ROWS, VECTOR_ROWS, D), f32),
            )
        flops, traffic = flops + 1100000000, traffic + 8000000
    return run(partial(backward_body, row, section, parts), ctl, ins, outs, held, scratch, 56, flops, traffic, near=())


def tables_body(r):
    @pl.when(r.ctl[0] == 1)
    def _():
        loads = [
            r.copies.start(source, target)
            for source, target in (
                (r.d_start, r.start_v), (r.ffn_vec, r.ffn_vec_v), (r.att_vec, r.att_vec_v), (r.d_rel_low, r.rel_low), (r.w_in, r.wi)
            )
        ]
        wait_all(loads)
        vectors = r.ffn_vec_v[0] + r.ffn_vec_v[1] + r.att_vec_v[0] + r.att_vec_v[1]
        wait_all(tail_part(r, [r.start_v[0], r.start_v[1]], vectors))


def tables(ctl, w_in, held):
    ins = dict(w_in=w_in, **{name: held[name] for name in ("d_start", "ffn_vec", "att_vec", "d_rel_low")})
    outs = dict(att_own=shape((SWAP_ROWS, D)), att_other=shape((SWAP_ROWS, D)))
    scratch = dict(
        start_v=shape((ROWS, L, D)), ffn_vec_v=shape((ROWS, VECTOR_ROWS, D), f32), att_vec_v=shape((ROWS, VECTOR_ROWS, D), f32),
        rel_low=shape((2 * L, 2 * D)), wi=shape((D, 3 * D)), tail_v=shape((TAIL_ROWS, D)),
    )
    return run(tables_body, ctl, ins, outs, held, scratch, 8, 1000000000, 7000000)


def small_kernel(body, ctl, ins, outs):
    return pl.pallas_call(
        body,
        out_shape=outs,
        in_specs=[SMEM] + [VMEM] * len(ins),
        out_specs=(VMEM,) * len(outs),
        compiler_params=pltpu.CompilerParams(vmem_limit_bytes=16 * 2**20),
        cost_estimate=pl.CostEstimate(flops=0, bytes_accessed=2 * sum(value.size for value in ins) * 2, transcendentals=0),
    )(ctl, *ins)


def added(kept, received):
    return (kept.astype(f32) + received.astype(f32)).astype(bf16)


def split_sum(ctl, bit, kept, received):
    half = kept.shape[0] // 2

    def body(ctl, kept, received, keep, send):
        low, high = (added(kept[at], received[at]) for at in (slice(0, half), slice(half, 2 * half)))
        first = ctl[bit] == 0
        keep[...] = jnp.where(first, low, high)
        send[...] = jnp.where(first, high, low)

    return small_kernel(body, ctl, (kept, received), (shape((half, D)),) * 2)


def in_order(ctl, bit, own, other):
    half = own.shape[0]

    def body(ctl, own, other, out):
        first = ctl[bit] == 0
        out[:half] = jnp.where(first, own[...], other[...])
        out[half:] = jnp.where(first, other[...], own[...])

    return small_kernel(body, ctl, (own, other), (shape((2 * half, D)),))[0]


class Halves:
    def __init__(self, r, first_piece, half_rows):
        self.r, self.first_piece, self.half_rows, self.pending = r, first_piece, half_rows, []

    def store(self, first, rows):
        while rows > 0:
            index, inside = divmod(first, self.half_rows)
            count = min(rows, self.half_rows - inside)
            piece, half = index // 2, index % 2
            view, there = self.r.out_v.at[pl.ds(first, count)], pl.ds(inside, count)
            kept = self.r.copies.make(view, getattr(self.r, f"kept{piece}").at[there])
            sem = self.r.copies.sems.at[self.r.copies.used - 1]
            sent = pltpu.make_async_copy(view, getattr(self.r, f"sent{piece}").at[there], sem)
            mine = self.r.ctl[bit_at(self.first_piece + piece, False)] == half

            @pl.when(mine)
            def _():
                kept.start()

            @pl.when(jnp.logical_not(mine))
            def _():
                sent.start()

            self.pending.append(kept)
            first, rows = first + count, rows - count


def bit_at(piece, of_other_core):
    return 4 + 2 * piece + int(of_other_core)


def half_outputs(rows, pieces):
    half_rows = rows // pieces // 2
    return {f"{kind}{piece}": shape((half_rows, D)) for piece in range(pieces) for kind in ("kept", "sent")}


def load_acts(r, at, size, to):
    if not isinstance(at, int):
        at = pl.multiple_of(at, 128)
    return [
        r.copies.start(source.at[row, :, pl.ds(at, size)], target.at[pl.ds(row * L, L), pl.ds(to, size)])
        for row in range(ROWS)
        for source, target in ((r.acts, r.acts_v), (r.acts_sent, r.acts_sent_v))
    ]


def ffn_weights_body(r):
    core = r.ctl[1]
    loads = [r.copies.start(r.rows, r.rows_v)] + load_acts(r, A_HID, D, 0)
    later = load_acts(r, A_ACT + core * 2 * D, 2 * D, D)
    last = load_acts(r, A_CTX + core * HALF, HALF, 3 * D) + load_acts(r, A_X + core * HALF, HALF, 3 * D + HALF)
    halves = Halves(r, 0, FFN_ROWS // FFN_PIECES // 2)

    def product(acts_at, rows_at):
        own = tn(r.acts_v[:, acts_at], r.rows_v[:, rows_at])
        return (own + tn(r.acts_sent_v[:, acts_at], r.rows_sent[:, rows_at])).astype(bf16)

    wait_all(loads)
    for block in range(2):
        r.out_v[block_at(block)] = product(block_at(0), block_at(block))
        halves.store(block * D, D)
    wait_all(later)
    for block in range(2, 4):
        r.out_v[block_at(block)] = product(block_at(block - 1), block_at(2))
        halves.store(block * D, D)
    wait_all(last)
    for part in range(2):
        to = slice(4 * D + part * HALF, 4 * D + (part + 1) * HALF)
        r.out_v[to] = product(slice(3 * D + part * HALF, 3 * D + (part + 1) * HALF), block_at(3 + part))
    halves.store(4 * D, D)
    wait_all(halves.pending)


def ffn_weights(ctl, **ins):
    scratch = dict(
        rows_v=shape((ROWS * L, 5 * D)), acts_v=shape((ROWS * L, 4 * D)), acts_sent_v=shape((ROWS * L, 4 * D)),
        out_v=shape((FFN_ROWS, D)),
    )
    outs = half_outputs(FFN_ROWS, FFN_PIECES)
    return run(ffn_weights_body, ctl, ins, outs, {}, scratch, 36, 2 * 512 * 768 * FFN_ROWS, 14000000, ("rows_sent",))


def att_weights_body(r):
    loads = [r.copies.start(r.rows, r.rows_v), r.copies.start(r.table, r.table_v)]
    loads += load_acts(r, r.ctl[1] * D, D, 0)
    halves = Halves(r, FFN_PIECES, ATT_ROWS // ATT_PIECES // 2)
    wait_all(loads)
    total = tn(r.acts_v[...], r.rows_v[: 2 * L]) + tn(r.acts_sent_v[...], r.rows_sent[: 2 * L])
    far = (r.rows_v[2 * L : 4 * L].astype(f32) + r.rows_sent[2 * L : 4 * L].astype(f32)).astype(bf16)
    r.out_v[:D] = (total + tn(r.table_v[...], far)).astype(bf16)
    r.out_v[TAIL_AT:] = r.rows_v[4 * L :] + r.rows_sent[4 * L :]
    halves.store(0, ATT_ROWS)
    wait_all(halves.pending)


def att_weights(ctl, **ins):
    scratch = dict(
        rows_v=shape((SWAP_ROWS, D)), table_v=shape((2 * L, D)),
        acts_v=shape((ROWS * L, D)), acts_sent_v=shape((ROWS * L, D)), out_v=shape((ATT_ROWS, D)),
    )
    outs = half_outputs(ATT_ROWS, ATT_PIECES)
    return run(att_weights_body, ctl, ins, outs, {}, scratch, 16, 2 * 768 * 768 * 768, 6000000, ("rows_sent",))


def half_segments(layout, half_rows, piece, half):
    low = (2 * piece + half) * half_rows
    found, at = [], 0
    for target, rows, first, block in layout:
        start, stop = max(at, low), min(at + rows, low + half_rows)
        if start < stop:
            found.append((start - low, stop - start, target, first + start - at, block))
        at += rows
    return found


def assemble_body(kind, first_piece, layouts, half_rows, chosen, r):
    start_copy = r.copies.start
    core = r.ctl[1]
    blank = None
    if first_piece > 0 and kind == 0:
        r.blank[...] = jnp.zeros_like(r.blank)
        rest = 2 * SPAN - REL_FROM - REL_ROWS
        blank = [
            start_copy(r.blank, r.g_rel.at[pl.ds(0, REL_FROM)]),
            start_copy(r.blank.at[pl.ds(0, rest)], r.g_rel.at[pl.ds(REL_FROM + REL_ROWS, rest)]),
        ]
    branches = []
    chunk = half_rows // 2
    items = [(piece, origin) for piece in chosen for origin in ("own", "sent")]
    for index, (piece, origin) in enumerate(items):
        array = getattr(r, f"{origin}{piece}")
        bit = r.ctl[bit_at(first_piece + piece, origin == "sent")]
        maker = core if origin == "own" else 1 - core
        cases = [(made_by, half) for made_by in range(2) for half in range(2)]
        for at in range(0, half_rows, chunk):
            r.wide[index, at : at + chunk] = array[at : at + chunk].astype(f32)
            first_copy = last_copy = r.copies.used
            for made_by, half in cases:
                r.copies.used = first_copy
                copies = []
                for inside, count, name, start, block in half_segments(layouts[made_by], half_rows, piece, half):
                    low, high = max(inside, at), min(inside + count, at + chunk)
                    if low < high and name not in ("", "vectors"):
                        target = getattr(r, name).at[pl.ds(start + low - inside, high - low), pl.ds(block * D, D)]
                        copies.append(r.copies.make(r.wide.at[index, pl.ds(low, high - low)], target))
                last_copy = max(last_copy, r.copies.used)
                here = (maker == made_by) & (bit == (half if kind == 0 else 1 - half))
                branches.append((here, copies))

                @pl.when(here)
                def _():
                    for copy in copies:
                        copy.start()

            r.copies.used = last_copy
        for made_by, half in cases:
            for inside, count, name, _, _ in half_segments(layouts[made_by], half_rows, piece, half):
                if name == "vectors":

                    @pl.when((maker == made_by) & (bit == (half if kind == 0 else 1 - half)))
                    def _():
                        vectors = r.wide[index, inside : inside + count, :]
                        for part in range(3):
                            r.b_in_v[:, block_at(part)] = vectors[part : part + 1]
                        for part in range(4):
                            r.b_up_v[:, block_at(part)] = vectors[3 + part : 4 + part]
                        r.gains_v[...] = vectors[7:9]
                        r.biases_v[...] = vectors[9:13]
                        wait_all([
                            start_copy(r.b_in_v, r.g_b_in), start_copy(r.b_up_v, r.g_b_up),
                            start_copy(r.gains_v, r.g_gains), start_copy(r.biases_v, r.g_biases),
                        ])

    wait_all(blank or [])
    for here, copies in branches:

        @pl.when(here)
        def _():
            wait_all(copies)


def assemble(kind, first_piece, layouts, rows, pieces, chosen, ctl, own, sent, shapes, held):
    ins = {f"own{i}": value for i, value in zip(chosen, own)}
    ins.update({f"sent{i}": value for i, value in zip(chosen, sent)})
    outs = {name: shape(dims, f32) for name, dims in shapes.items()}
    half_rows = rows // pieces // 2
    scratch = dict(wide=shape((len(ins), half_rows, D), f32))
    if first_piece > 0:
        scratch.update(
            blank=shape((REL_FROM, D), f32), b_in_v=shape((1, 3 * D), f32), b_up_v=shape((1, FF), f32),
            gains_v=shape((2, D), f32), biases_v=shape((4, D), f32),
        )
    body = partial(assemble_body, kind, first_piece, layouts, half_rows, chosen)
    return run(body, ctl, ins, outs, held, scratch, 96, 0, len(ins) * half_rows * D * 6, tuple(ins), 44 * 2**20)


FFN_SHAPES = dict(g_up=(D, FF), g_down=(FF, D), g_out=(D, D), g_in=(D, 3 * D))
ATT_SHAPES = dict(
    g_in=(D, 3 * D), g_rel=(2 * SPAN, D), g_abs=(ABS_ROWS, D),
    g_b_in=(1, 3 * D), g_b_up=(1, FF), g_gains=(2, D), g_biases=(4, D),
)


SQUARE = ((0, 0), (1, 0), (1, 1), (0, 1))


def dp_place(index):
    return {"core": index % 2, "x": index // 2 % 4, "y": index // 8 % 2, "z": index // 16}


def dp_index(place):
    return ((place["z"] * 2 + place["y"]) * 4 + place["x"]) * 2 + place["core"]


def partner(index, dim):
    place = dp_place(index)
    if len(dim) == 2:
        bits = list(SQUARE[place[dim[0]]])
        bits[int(dim[1])] ^= 1
        place[dim[0]] = SQUARE.index(tuple(bits))
    else:
        place[dim] ^= 1
    return dp_index(place)


def swap(value, dims):
    peers = lax.axis_size("dp")
    return lax.ppermute(value, "dp", [(i, partner(i, dims[i % 2])) for i in range(peers)])


BETWEEN_CORES = ("core", "core")


def side_along(dim):
    place = dp_place(lax.axis_index("dp"))
    if dim == "y":
        return place[dim].astype(jnp.int32)
    at = place[dim[0]]
    if dim[1] == "0":
        return ((at == 1) | (at == 2)).astype(jnp.int32)
    return (at >= 2).astype(jnp.int32)


def this_core():
    return (lax.axis_index("dp") % 2).astype(jnp.int32)


def side(dims):
    return jnp.where(this_core() == 0, side_along(dims[0]), side_along(dims[1]))


ORDERS = [
    [("x0", "y"), ("z0", "x1"), ("x1", "z1"), ("y", "z0"), ("z1", "x0")],
    [("x1", "z0"), ("x0", "z1"), ("y", "x0"), ("z1", "x1"), ("z0", "y")],
    [("z1", "y"), ("x1", "z1"), ("y", "z0"), ("x0", "x1"), ("z0", "x0")],
]
BITS_AT = 4 + 2 * (FFN_PIECES + ATT_PIECES)
SPLIT_STEPS = 3


def bit_of(piece, step):
    return BITS_AT + 2 * piece + step - 1


def is_table_row(chunk):
    piece = FFN_PIECES
    first_row, span = 0, ATT_ROWS
    for dims in ORDERS[piece][:SPLIT_STEPS]:
        span //= 2
        first_row = first_row + side(dims) * span
    row_at = first_row + lax.broadcasted_iota(jnp.int32, chunk.shape, 0) - TAIL_AT
    return (row_at >= 0) & (row_at + this_core() * TAIL_HALF < TABLE_ROWS)


class Sequence:
    def __init__(self, last):
        self.last = last

    def after(self, *values):
        values = lax.optimization_barrier((*values, self.last))[:-1]
        return values[0] if len(values) == 1 else values


class Pieces:
    def __init__(self, ctl, seq):
        self.ctl, self.seq = ctl, seq
        self.kept, self.received, self.mine, self.mine_sent, self.partners, self.partners_sent = ({} for _ in range(6))

    def begin(self, piece, kept, sent):
        self.kept[piece], self.received[piece] = kept, swap(sent, ORDERS[piece][0])

    def inputs(self, piece):
        return self.seq.after(self.kept[piece], self.received[piece])

    def hold(self, piece, chunk):
        self.kept[piece] = self.seq.last = chunk

    def land(self, piece):
        self.received[piece] = self.seq.last = self.seq.after(self.received[piece])

    def split(self, piece, step):
        kept, sent = split_sum(self.ctl, bit_of(piece, step), *self.inputs(piece))
        self.hold(piece, kept)
        self.received[piece] = swap(sent, ORDERS[piece][step])

    def add(self, piece, step):
        kept, received = self.inputs(piece)
        self.hold(piece, kept + received)
        self.received[piece] = swap(self.kept[piece], ORDERS[piece][step])

    def add_for_section(self, piece):
        kept, received = self.inputs(piece)
        self.hold(piece, kept + received)
        self.received[piece] = lax.ppermute(self.kept[piece], "section", [(0, 1), (1, 0)])

    def add_tables(self, piece, step):
        kept, received = self.inputs(piece)
        self.hold(piece, jnp.where(is_table_row(kept), kept + received, kept))
        self.received[piece] = swap(self.kept[piece], ORDERS[piece][step])

    def join(self, piece, step):
        self.hold(piece, in_order(self.ctl, bit_of(piece, step), *self.inputs(piece)))
        self.received[piece] = swap(self.kept[piece], ORDERS[piece][step - 1])

    def cross(self, piece):
        self.mine[piece] = self.seq.last = self.seq.after(self.kept[piece])
        self.mine_sent[piece] = swap(self.mine[piece], BETWEEN_CORES)

    def arrive(self, piece):
        self.partners[piece] = self.seq.last = self.seq.after(self.received[piece])
        self.partners_sent[piece] = swap(self.partners[piece], BETWEEN_CORES)


def per_device(
    hidden_in,
    cotangent,
    segment_ids,
    positions,
    w_in,
    b_in,
    w_out,
    w_up,
    b_up,
    w_down,
    gains,
    biases,
    rel_table,
    abs_table,
):
    section = lax.axis_index("section").astype(jnp.int32)
    firsts = jnp.where(section == 1, positions[:, 0], 8 * ABS_ROWS)
    bits = [side(dims) for order in ORDERS for dims in (order[0], order[0][::-1])]
    bits += [side(order[step]) for order in ORDERS for step in range(1, SPLIT_STEPS)]
    ctl = jnp.stack([section, this_core(), firsts[0], firsts[1], *bits])
    weights = dict(w_in=w_in[0], w_out=w_out[0], w_up=w_up[0], w_down=w_down[0], gains=gains[0])
    common = dict(
        weights, hidden_in=hidden_in, segment_ids=segment_ids, biases=biases[0], b_in=b_in, b_up=b_up, abs_table=abs_table
    )

    out = forward(0, 0, ctl, dict(common, rel_table=rel_table), {})
    rel, rel_rows = out["rel"], out["rel_rows"]
    common["rel"] = rel
    received = []
    for row in range(ROWS):
        if row > 0:
            out = forward(row, 0, ctl, common, out)
        received.append(lax.ppermute(out["sent"], "section", [(0, 1)]))
    ready = {name: out[name] for name in ("keep", "resid")}
    back_ins = dict(common, cotangent=cotangent)
    grads = []
    for row in range(ROWS):
        turned = {name: out[name] for name in ("w_up_t", "w_down_t")} if row < ROWS - 1 else {}
        out = {**out, **forward(row, 1, ctl, dict(back_ins, **turned, received=received[row]), out)}
        grads.append(lax.ppermute(out["sent"], "section", [(1, 0)]))
    acts, section_out = out["acts"], out["section_out"]
    acts_sent = swap(acts, BETWEEN_CORES)
    turned = {name: out[name] for name in ("w_up_t", "w_down_t")}
    common = dict(weights, **ready, **turned, rel=rel)
    received = grads
    out.update(tables(ctl, weights["w_in"], out))
    out = backward(0, 0, "both", ctl, dict(common, received=received[0]), out)
    early = out
    ffn = backward(1, 0, "ffn", ctl, dict(common, received=received[1]), early)
    ffn_sent = swap(ffn["ffn_other"], BETWEEN_CORES)
    seq = Sequence(ffn["ffn_own"])
    pieces = Pieces(ctl, seq)
    grads = {}

    def write(kind, group, *chosen):
        own, sent = ((pieces.mine, pieces.mine_sent), (pieces.partners, pieces.partners_sent))[kind]
        first, count, layout, rows, shapes = group
        first_own, *own = [own[first + i] for i in chosen]
        sent = [sent[first + i] for i in chosen]
        result = assemble(kind, first, layout, rows, count, chosen, ctl, [seq.after(first_own), *own], sent, shapes, grads)
        grads.update(result)
        seq.last = result["g_biases"] if first > 0 else result["g_out"]

    ffn_group = 0, FFN_PIECES, FFN_LAYOUT, FFN_ROWS, FFN_SHAPES
    att_group = FFN_PIECES, ATT_PIECES, ATT_LAYOUT, ATT_ROWS, ATT_SHAPES
    ins = dict(common, d_resid=seq.after(ffn["d_resid"]), d_context=ffn["d_context"], ffn_vec=ffn["ffn_vec"])
    out = backward(1, 0, "att", ctl, ins, early)
    att_sent = swap(out["att_other"], BETWEEN_CORES)
    seq.last = out["att_own"]
    halves = ffn_weights(ctl, acts=acts, acts_sent=acts_sent, rows=seq.after(ffn["ffn_own"]), rows_sent=ffn_sent)
    for piece in range(FFN_PIECES):
        pieces.begin(piece, halves[f"kept{piece}"], halves[f"sent{piece}"])
    seq.last = halves["kept0"]
    halves = att_weights(
        ctl, acts=acts, acts_sent=acts_sent, rows=seq.after(out["att_own"]), rows_sent=att_sent, table=rel_rows
    )
    pieces.begin(FFN_PIECES, halves["kept0"], halves["sent0"])
    seq.last = halves["kept0"]
    input_grad = finish(
        ctl, early, d_resid=ffn["d_resid"], d_rows=seq.after(out["d_rows"]), d_context=ffn["d_context"], w_in=weights["w_in"]
    )
    seq.last = input_grad
    pieces.split(0, 1)
    pieces.split(1, 1)
    pieces.land(2)
    pieces.split(0, 2)
    pieces.split(1, 2)
    pieces.split(2, 1)
    pieces.add(0, 3)
    pieces.add(1, 3)
    pieces.split(2, 2)
    pieces.add(0, 4)
    pieces.add(1, 4)
    pieces.add(2, 3)
    pieces.add(0, 2)
    pieces.land(1)
    pieces.add(2, 4)
    pieces.add(1, 2)
    pieces.join(0, 2)
    pieces.add_for_section(2)
    pieces.join(1, 2)
    pieces.add_tables(2, 2)
    pieces.join(0, 1)
    pieces.cross(0)
    pieces.join(2, 2)
    pieces.join(1, 1)
    pieces.cross(1)
    pieces.join(2, 1)
    pieces.cross(2)
    write(0, att_group, 0)
    pieces.arrive(0)
    write(0, ffn_group, 0, 1)
    pieces.arrive(1)
    pieces.arrive(2)
    write(1, ffn_group, 0, 1)
    write(1, att_group, 0)
    return (
        section_out[None],
        input_grad[None],
        grads["g_in"][None],
        grads["g_b_in"],
        grads["g_out"][None],
        grads["g_up"][None],
        grads["g_b_up"],
        grads["g_down"][None],
        grads["g_gains"][None],
        grads["g_biases"][None],
        grads["g_rel"],
        grads["g_abs"],
    )


def solution(mesh):
    in_specs = (
        P("dp", None, None),
        P("dp", None, None),
        P("dp", None),
        P("dp", None),
        P("section", None, None),
        P("section", None),
        P("section", None, None),
        P("section", None, None),
        P("section", None),
        P("section", None, None),
        P("section", None, None),
        P("section", None, None),
        P(),
        P(),
    )
    out_specs = (
        P("section", "dp", None, None),
        P("section", "dp", None, None),
        P("section", None, None),
        P("section", None),
        P("section", None, None),
        P("section", None, None),
        P("section", None),
        P("section", None, None),
        P("section", None, None),
        P("section", None, None),
        P(),
        P(),
    )
    return jax.shard_map(
        per_device, mesh=mesh, in_specs=in_specs, out_specs=out_specs, check_vma=False
    )
```

```python
from functools import partial
import math
from types import SimpleNamespace

import jax
import jax.numpy as jnp
from jax import lax
from jax.experimental import pallas as pl
from jax.experimental.pallas import tpu as pltpu
from jax.sharding import PartitionSpec as P

HEADS = 12
L = 128
D = 768
FF = 3072
HALF = D // 2
PAIRS = HEADS // 2
ROWS = 2
SPAN = 256
EPS = 1e-06
NEG = -1e30
SCALE = 1.0 / math.sqrt(3 * 64)
VMEM_LIMIT = 61 * 1024 * 1024
f32, bf16 = jnp.float32, jnp.bfloat16

A_START, A_X, A_CTX, A_HID, A_ACT, A_ALL = 0, 768, 1536, 2304, 3072, 6144
K_P, K_GP, K_ALL = 2304, 3840, 6912
VECTOR_ROWS = 16
REL_FROM, REL_ROWS, ABS_ROWS, TAIL_ROWS = 128, 272, 512, 896
TABLE_ROWS = REL_ROWS + ABS_ROWS
FFN_LAYOUT = [
    [("g_up", D, 0, 2 * core), ("g_up", D, 0, 2 * core + 1), ("g_down", 2 * D, 2 * D * core, 0), ("g_out", HALF, HALF * core, 0),
     ("g_in", HALF, HALF * core, 2)]
    for core in range(2)
]
ATT_LAYOUT = [
    [("g_in", D, 0, 0), ("g_rel", REL_ROWS, REL_FROM, 0), ("g_abs", 176, 0, 0)],
    [("g_in", D, 0, 1), ("g_abs", 336, 176, 0), ("vectors", VECTOR_ROWS, 0, 0), ("", 96, 0, 0)],
]
FFN_ROWS, ATT_ROWS = 3840, 1216
FFN_PIECES, ATT_PIECES = 2, 1
TAIL_HALF = TAIL_ROWS // 2
TAIL_AT = ATT_ROWS - TAIL_HALF
SWAP_ROWS = 4 * L + TAIL_HALF

VMEM = pl.BlockSpec(memory_space=pltpu.VMEM)
ANY = pl.BlockSpec(memory_space=pl.ANY)
SMEM = pl.BlockSpec(memory_space=pltpu.SMEM)


def nn(a, b):
    return lax.dot_general(a, b, (((1,), (0,)), ((), ())), preferred_element_type=f32)


def nt(a, b):
    return lax.dot_general(a, b, (((1,), (1,)), ((), ())), preferred_element_type=f32)


def tn(a, b):
    return lax.dot_general(a, b, (((0,), (0,)), ((), ())), preferred_element_type=f32)


def norm_parts(value):
    centered = value - jnp.mean(value, axis=1, keepdims=True)
    rstd = lax.rsqrt(jnp.mean(centered * centered, axis=1, keepdims=True) + EPS)
    return centered * rstd, rstd


def norm_backward(normed, rstd, gain, grad):
    scaled = grad * gain
    mean_one = jnp.mean(scaled, axis=1, keepdims=True)
    mean_two = jnp.mean(scaled * normed, axis=1, keepdims=True)
    return (scaled - mean_one - normed * mean_two) * rstd


def column_sums(value):
    return jnp.sum(value, axis=0, keepdims=True)


def indicator(condition):
    return condition.astype(f32).astype(bf16)


def lane_halves():
    lane = lax.broadcasted_iota(jnp.int32, (1, L), 1)
    return indicator(lane < 64), indicator(lane >= 64)


def stacked(value, halves):
    return jnp.concatenate([value * halves[0], value * halves[1]], axis=0)


def skew(table):
    return pltpu.roll(table, L, 1, stride=1, stride_axis=0)[:, :L]


def unskew(turned):
    wide = jnp.concatenate([turned, jnp.zeros_like(turned)], axis=1)
    return pltpu.roll(wide, 1, 1, stride=1, stride_axis=0)


def pair_at(pair, base=0, width=L):
    return pl.ds(pl.multiple_of(base + pair * width, L), width)


def block_at(block, base=0):
    return slice(base + block * D, base + block * D + D)


def shape(dims, dtype=bf16):
    return jax.ShapeDtypeStruct(dims, dtype)


class Copies:
    def __init__(self, sems):
        self.sems, self.used, self.marks = sems, 0, {}

    def make(self, source, target):
        self.used += 1
        return pltpu.make_async_copy(source, target, self.sems.at[self.used - 1])

    def make_at(self, name):
        again = self.marks.setdefault(name, self.used)
        if again == self.used:
            return self.make
        at = iter(range(again, self.used))
        return lambda source, target: pltpu.make_async_copy(source, target, self.sems.at[next(at)])

    def start(self, source, target):
        copy = self.make(source, target)
        copy.start()
        return copy


def wait_all(copies):
    for copy in copies:
        copy.wait()


def run(body, ctl, ins, outs, held, scratch, copies, flops, traffic, near=(), limit=VMEM_LIMIT):
    names, out_names, scratch_names = list(ins), list(outs), list(scratch)
    kept = [name for name in out_names if name in held and name != "sent"]

    def kernel(*refs):
        ctl_ref, refs = refs[0], refs[1:]
        r = SimpleNamespace(ctl=ctl_ref, **dict(zip(names, refs)))
        refs = refs[len(names) + len(kept) :]
        for name, ref in zip(out_names + scratch_names, refs):
            setattr(r, name, ref)
        r.copies = Copies(refs[-1])
        body(r)

    results = pl.pallas_call(
        kernel,
        out_shape=tuple(outs.values()),
        in_specs=[SMEM] + [VMEM if name in near else ANY for name in names] + [ANY] * len(kept),
        out_specs=(ANY,) * len(out_names),
        input_output_aliases={1 + len(names) + i: out_names.index(name) for i, name in enumerate(kept)},
        scratch_shapes=[pltpu.VMEM(s.shape, s.dtype) for s in scratch.values()] + [pltpu.SemaphoreType.DMA((copies,))],
        compiler_params=pltpu.CompilerParams(vmem_limit_bytes=limit),
        cost_estimate=pl.CostEstimate(flops=flops, bytes_accessed=traffic, transcendentals=0),
    )(ctl, *ins.values(), *[held[name] for name in kept])
    return dict(zip(out_names, results))


def relative_loads(r):
    return [r.copies.start(r.rel_table, r.table_v), r.copies.start(r.b_in, r.b_in_v), r.copies.start(r.w_in, r.wi)]


def relative_part(r, loads):
    dims = (2 * L, 2 * SPAN)
    select = indicator(lax.broadcasted_iota(jnp.int32, dims, 0) + lax.broadcasted_iota(jnp.int32, dims, 1) == L + SPAN)
    loads[0].wait()
    rows = nn(select, r.table_v[...]).astype(bf16)
    r.rel_rows_v[...] = rows
    loads[1].wait()
    loads[2].wait()
    r.rel_v[...] = (nn(rows, r.wi[:, : 2 * D]) + r.b_in_v[:, : 2 * D].astype(f32)).astype(bf16)
    return [r.copies.start(r.rel_rows_v, r.rel_rows), r.copies.start(r.rel_v, r.rel)]


def forward_loads(row, section, first, r):
    make = r.copies.make_at("loads")
    loads = SimpleNamespace(
        x=[make(r.hidden_in.at[row] if section == 0 else r.received, r.x_v)],
        absolute=[make(r.abs_table, r.table_v)] if section == 1 else [],
        w_in=[]
        if first
        else [make(r.b_in, r.b_in_v)] + [make(r.w_in.at[:, block_at(part)], r.wi.at[:, block_at(part)]) for part in range(3)],
        rel=[] if first else [make(r.rel, r.rel_v)],
        small=[make(r.segment_ids, r.seg_v), make(r.gains, r.gains_v), make(r.biases, r.biases_v)],
        out=[make(r.w_out, r.wo), make(r.b_up, r.b_up_v)],
        parts=[
            [
                make(r.w_up.at[:, block_at(part)], r.wu.at[:, block_at(part)]),
                make(r.w_down.at[block_at(part)], r.wd.at[block_at(part)]),
            ]
            for part in range(4)
        ],
    )
    flat = loads.x + loads.absolute + loads.w_in + loads.rel + loads.small + loads.out
    loads.every = flat + [copy for part in loads.parts for copy in part]
    return loads


def forward_body(row, section, first, r):
    start_copy = r.copies.start
    stores = []
    if first:
        rel_loads = relative_loads(r)

        @pl.when(r.ctl[0] == section)
        def _():
            for copy in forward_loads(row, section, first, r).every:
                copy.start()

        stores = relative_part(r, rel_loads)

    @pl.when(r.ctl[0] == section)
    def _():
        loads = forward_loads(row, section, first, r)
        if not first:
            for copy in loads.every:
                copy.start()
        if section == 1:
            back = SimpleNamespace(
                first=[start_copy(r.cotangent.at[row], r.grad_v)],
                parts=[
                    [
                        start_copy(r.w_down_t.at[:, block_at(part)], r.wd_t.at[:, block_at(part)]),
                        start_copy(r.w_up_t.at[block_at(part)], r.wu_t.at[block_at(part)]),
                    ]
                    for part in range(4)
                ],
                last=[],
            )
            earlier = [start_copy(r.d_rel, r.d_rel_old)] if row > 0 else []
            back_att = SimpleNamespace(first=[], earlier=earlier, w_in=[], others=[])
        halves = lane_halves()
        wait_all(loads.x)
        x = r.x_v[...]
        start = x.astype(f32)
        if section == 1:
            wait_all(loads.absolute)
            dims = (L, ABS_ROWS)
            place = lax.broadcasted_iota(jnp.int32, dims, 1) - lax.broadcasted_iota(jnp.int32, dims, 0)
            start = start + nn(indicator(place == r.ctl[2 + row]), r.table_v[...])
        query_in = start.astype(bf16)
        r.acts_v[:, block_at(0)] = query_in
        r.acts_v[:, block_at(1)] = x
        wait_all(loads.w_in[:2])
        b_in = r.b_in_v[...].astype(f32)
        r.keep_v[:, :D] = (nn(query_in, r.wi[:, :D]) + b_in[:, :D]).astype(bf16)
        wait_all(loads.w_in[2:])
        r.keep_v[:, D : 3 * D] = (nn(x, r.wi[:, D:]) + b_in[:, D:]).astype(bf16)
        wait_all(loads.small + loads.rel)
        seg_rows = jnp.broadcast_to(r.seg_v[row : row + 1, :], (L, L)).astype(f32)
        same = seg_rows == seg_rows.T
        def attend(pair):
            query = r.keep_v[:, pair_at(pair)]
            key = r.keep_v[:, pair_at(pair, D)]
            value = r.keep_v[:, pair_at(pair, 2 * D)]
            query_two, key_two = stacked(query, halves), stacked(key, halves)
            content = nt(query_two, key)
            far_query = nt(query_two, r.rel_v[:, pair_at(pair, D)])
            far_key = nt(key_two, r.rel_v[:, pair_at(pair)])
            probs = []
            for head in range(2):
                rows = slice(head * L, head * L + L)
                summed = content[rows] + skew(far_query[rows]) + skew(far_key[rows]).T
                scores = jnp.where(same, summed * SCALE, NEG)
                exponent = jnp.exp(scores - jnp.max(scores, axis=1, keepdims=True))
                total = jnp.sum(exponent, axis=1, keepdims=True)
                probs.append((exponent * (1.0 / total)).astype(bf16))
            probs = jnp.concatenate(probs, axis=1)
            r.keep_v[:, pair_at(pair, K_P, 2 * L)] = probs
            r.acts_v[:, pair_at(pair, A_CTX)] = nn(probs, stacked(value, halves)).astype(bf16)

        if section == 0:
            for pair in range(PAIRS):
                attend(pair)
        else:
            pl.loop(0, PAIRS, unroll=3)(attend)
        wait_all(loads.out)
        gain = r.gains_v[...].astype(f32)
        shift = r.biases_v[...].astype(f32)
        resid_one = start + nn(r.acts_v[:, A_CTX : A_CTX + D], r.wo[...]) + shift[0:1]
        r.resid_v[:, :D] = resid_one
        hidden = norm_parts(resid_one)[0] * gain[0:1] + shift[1:2]
        hidden_low = hidden.astype(bf16)
        r.acts_v[:, A_HID : A_HID + D] = hidden_low
        stored = [start_copy(r.acts_v.at[:, pl.ds(0, A_ACT)], r.acts.at[row, :, pl.ds(0, A_ACT)])]
        if section == 0:
            stored.append(start_copy(r.keep_v.at[:, pl.ds(0, K_GP)], r.keep.at[row, :, pl.ds(0, K_GP)]))
        total = hidden + shift[2:3]
        for part in range(4):
            wait_all(loads.parts[part])
            gate = nn(hidden_low, r.wu[:, block_at(part)]) + r.b_up_v[:, block_at(part)].astype(f32)
            below = 0.5 + 0.5 * lax.erf(gate * (1.0 / math.sqrt(2.0)))
            density = jnp.exp(gate * gate * -0.5) * (1.0 / math.sqrt(2.0 * math.pi))
            active = (gate * below).astype(bf16)
            r.acts_v[:, block_at(part, A_ACT)] = active
            r.keep_v[:, block_at(part, K_GP)] = (below + gate * density).astype(bf16)
            stored.append(start_copy(r.acts_v.at[:, block_at(part, A_ACT)], r.acts.at[row, :, block_at(part, A_ACT)]))
            if section == 0:
                stored.append(start_copy(r.keep_v.at[:, block_at(part, K_GP)], r.keep.at[row, :, block_at(part, K_GP)]))
            total = total + nn(active, r.wd[block_at(part), :])
        r.resid_v[:, D:] = total
        if section == 0:
            stored.append(start_copy(r.resid_v, r.resid.at[row]))
        r.x_v[...] = (norm_parts(total)[0] * gain[1:2] + shift[3:4]).astype(bf16)
        stored.append(start_copy(r.x_v, r.section_out.at[row]))
        if section == 0:
            stored.append(start_copy(r.x_v, r.sent))
        else:
            near = SimpleNamespace(**vars(r))
            near.wu, near.wd = r.wu_t, r.wd_t
            near.probs_v = r.keep_v.at[:, pl.ds(K_P, K_GP - K_P)]
            near.slope_v = r.keep_v.at[:, pl.ds(K_GP, FF)]
            d_resid, out_copies = ffn_part(row, section, near, back)
            r.value_v[...] = r.ffn_v[:, FF + 2 * D :]
            stored += out_copies + att_part(row, section, near, back_att, d_resid)
        wait_all(stored)

    wait_all(stores)
    if turns_weights(row, section):

        @pl.when(r.ctl[0] != section)
        def _():
            turn_weights(r)


def turns_weights(row, section):
    return row == (ROWS - 1 if section == 0 else 0)


def turn_weights(r):
    jobs = [(r.w_up, r.wu, r.w_up_t, 0, part) for part in range(4)]
    jobs += [(r.w_down, r.wd, r.w_down_t, part, 0) for part in range(4)]
    loads = [
        r.copies.start(source.at[block_at(row), block_at(column)], near.at[block_at(row), block_at(column)])
        for source, near, _, row, column in jobs
    ]
    stores = []
    for load, (source, near, target, row, column) in zip(loads, jobs):
        load.wait()
        turned = r.wu_t if near is r.wu else r.wd_t
        turned[block_at(column), block_at(row)] = near[block_at(row), block_at(column)].T
        stores.append(
            r.copies.start(turned.at[block_at(column), block_at(row)], target.at[block_at(column), block_at(row)])
        )
    wait_all(stores)


def forward(row, section, ctl, ins, held):
    first = not held
    outs = {"sent": shape((L, D))}
    if first:
        outs.update(rel_rows=shape((2 * L, D)), rel=shape((2 * L, 2 * D)))
    outs.update(acts=shape((ROWS, L, A_ALL)), section_out=shape((ROWS, L, D)))
    scratch = dict(
        x_v=shape((L, D)), seg_v=shape((ROWS, L), jnp.int32), gains_v=shape((2, D)), biases_v=shape((4, D)),
        b_in_v=shape((1, 3 * D)), b_up_v=shape((1, FF)), table_v=shape((2 * SPAN, D)), rel_v=shape((2 * L, 2 * D)),
        wi=shape((D, 3 * D)), wo=shape((D, D)), wu=shape((D, FF)), wd=shape((FF, D)),
        acts_v=shape((L, A_ALL)), keep_v=shape((L, K_ALL)), resid_v=shape((L, 2 * D), f32),
    )
    if section == 0:
        outs.update(keep=shape((ROWS, L, K_ALL)), resid=shape((ROWS, L, 2 * D), f32))
    else:
        outs.update(backward_results(row, section))
        scratch.update(
            grad_v=shape((L, D)), ffn_v=shape((L, FF + 3 * D)), context_v=shape((L, D)), ffn_vec_v=shape((VECTOR_ROWS, D), f32),
            att_v=shape((L, 2 * D)), att_vec_v=shape((VECTOR_ROWS, D), f32), start_v=shape((L, D)), grad_out_v=shape((L, D)),
            value_v=shape((L, D)), d_rel_v=shape((2 * L, 2 * D), f32), d_rel_old=shape((2 * L, 2 * D), f32),
            rel_low=shape((2 * L, 2 * D)),
        )
    if first:
        scratch.update(rel_rows_v=shape((2 * L, D)))
    if turns_weights(row, section):
        outs.update(w_up_t=shape((FF, D)), w_down_t=shape((D, FF)))
    if row == ROWS - 1 or section == 1:
        scratch.update(wu_t=shape((FF, D)), wd_t=shape((D, FF)))
    return run(partial(forward_body, row, section, first), ctl, ins, outs, held, scratch, 84, 1900000000, 18000000)


def backward_results(row, section):
    results = dict(
        ffn_own=shape((ROWS * L, 5 * D)), ffn_other=shape((ROWS * L, 5 * D)), ffn_vec=shape((ROWS, VECTOR_ROWS, D), f32),
        att_own=shape((SWAP_ROWS, D)), att_other=shape((SWAP_ROWS, D)), att_vec=shape((ROWS, VECTOR_ROWS, D), f32),
        d_start=shape((ROWS, L, D)), d_rel=shape((2 * L, 2 * D), f32), d_rel_low=shape((2 * L, 2 * D)),
        input_grad=shape((ROWS, L, D)),
    )
    return results


def ffn_loads(row, section, r):
    return SimpleNamespace(
        first=[r.copies.start(source, near) for source, near in ((r.received, r.grad_v), (r.resid.at[row], r.resid_v), (r.gains, r.gains_v))],
        parts=[
            [
                r.copies.start(r.w_down_t.at[:, block_at(part)], r.wd.at[:, block_at(part)]),
                r.copies.start(r.keep.at[row, :, block_at(part, K_GP)], r.slope_v.at[:, block_at(part)]),
                r.copies.start(r.w_up_t.at[block_at(part)], r.wu.at[block_at(part)]),
            ]
            for part in range(4)
        ],
        last=[r.copies.start(r.w_out, r.wo), r.copies.start(r.keep.at[row, :, pl.ds(K_P, K_GP - K_P)], r.probs_v)],
    )


def ffn_part(row, section, r, loads):
    wait_all(loads.first)
    gain = r.gains_v[...].astype(f32)
    grad = r.grad_v[...].astype(f32)
    normed, rstd = norm_parts(r.resid_v[:, D:])
    r.ffn_vec_v[...] = jnp.zeros_like(r.ffn_vec_v)
    r.ffn_vec_v[8:9] = column_sums(grad * normed)
    r.ffn_vec_v[12:13] = column_sums(grad)
    d_two = norm_backward(normed, rstd, gain[1:2], grad)
    d_down = d_two.astype(bf16)
    r.ffn_v[:, FF : FF + D] = d_down
    r.ffn_vec_v[11:12] = column_sums(d_down.astype(f32))
    d_hidden = d_two
    for part in range(4):
        wait_all(loads.parts[part])
        d_gate = (nn(d_down, r.wd[:, block_at(part)]) * r.slope_v[:, block_at(part)].astype(f32)).astype(bf16)
        r.ffn_v[:, block_at(part)] = d_gate
        r.ffn_vec_v[3 + part : 4 + part] = column_sums(d_gate.astype(f32))
        d_hidden = d_hidden + nn(d_gate, r.wu[block_at(part), :])
    normed, rstd = norm_parts(r.resid_v[:, :D])
    r.ffn_vec_v[7:8] = column_sums(d_hidden * normed)
    r.ffn_vec_v[10:11] = column_sums(d_hidden)
    d_resid = norm_backward(normed, rstd, gain[0:1], d_hidden)
    d_att = d_resid.astype(bf16)
    r.ffn_v[:, FF + D : FF + 2 * D] = d_att
    r.ffn_vec_v[9:10] = column_sums(d_att.astype(f32))
    wait_all(loads.last)
    r.context_v[...] = nt(d_att, r.wo[...]).astype(bf16)
    halves = lane_halves()
    for pair in range(PAIRS):
        d_value = tn(two_heads(r.probs_v, pair), stacked(r.context_v[:, pair_at(pair)], halves))
        r.ffn_v[:, pair_at(pair, FF + 2 * D)] = d_value.astype(bf16)
    r.ffn_vec_v[2:3] = column_sums(r.ffn_v[:, FF + 2 * D :].astype(f32))
    stores, rows = [], pl.ds(row * L, L)
    for side_core, target in ((r.ctl[1], r.ffn_own), (1 - r.ctl[1], r.ffn_other)):
        gates = pl.ds(pl.multiple_of(side_core * 2 * D, 128), 2 * D)
        stores.append(r.copies.start(r.ffn_v.at[:, gates], target.at[rows, pl.ds(0, 2 * D)]))
        stores.append(r.copies.start(r.ffn_v.at[:, pl.ds(FF, 3 * D)], target.at[rows, pl.ds(2 * D, 3 * D)]))
    stores.append(r.copies.start(r.ffn_vec_v, r.ffn_vec.at[row]))
    return d_resid, stores


def two_heads(probs, pair):
    columns = probs[:, pair_at(pair, 0, 2 * L)]
    return jnp.concatenate([columns[:, :L], columns[:, L:]], axis=0)


def att_loads(row, section, r):
    return SimpleNamespace(
        first=[r.copies.start(r.keep.at[row, :, pl.ds(0, K_P)], r.keep_v), r.copies.start(r.rel, r.rel_v)],
        earlier=[r.copies.start(r.d_rel, r.d_rel_old)] if row > 0 else [],
        w_in=[r.copies.start(r.w_in, r.wi)],
        others=[
            r.copies.start(r.att_vec.at[0], r.att_vec_old),
            r.copies.start(r.ffn_vec, r.ffn_vec_v),
        ]
        if row == ROWS - 1 and section == 0
        else [],
    )


def att_part(row, section, r, loads, d_resid):
    halves = lane_halves()
    row_at = lax.broadcasted_iota(jnp.int32, (L, L), 0)
    column_at = lax.broadcasted_iota(jnp.int32, (L, L), 1)
    turn = indicator(row_at + column_at == L - 1)
    r.att_vec_v[...] = jnp.zeros_like(r.att_vec_v)
    wait_all(loads.first)
    for pair in range(PAIRS):
        query = r.keep_v[:, pair_at(pair)]
        key = r.keep_v[:, pair_at(pair, D)]
        value = r.keep_v[:, pair_at(pair, 2 * D)]
        probs_two = two_heads(r.probs_v, pair)
        rel_q, rel_k = r.rel_v[:, pair_at(pair)], r.rel_v[:, pair_at(pair, D)]
        context_two = stacked(r.context_v[:, pair_at(pair)], halves)
        probs_f = probs_two.astype(f32)
        weighted = nt(context_two, value) * probs_f
        d_scores = (weighted - probs_f * jnp.sum(weighted, axis=1, keepdims=True)).astype(bf16)
        query_two, key_two = stacked(query, halves), stacked(key, halves)
        d_key = tn(d_scores, query_two)
        d_side = jnp.concatenate([d_scores[:L], d_scores[L:]], axis=1)
        d_query = nn(d_side, key_two)
        d_far = (d_side.astype(f32) * SCALE).astype(bf16)
        query_turned = nn(turn, query).astype(bf16)
        key_turned = nn(turn, key).astype(bf16)
        rows_turned = nn(turn, d_far)
        far_query, far_key = [], []
        for head in range(2):
            columns = slice(head * L, head * L + L)
            far_query.append(unskew(rows_turned[:, columns]).astype(bf16))
            far_key.append(unskew(nt(turn, d_far[:, columns])).astype(bf16))
        d_query_turned = nn(jnp.concatenate(far_query, axis=1), stacked(rel_k, halves))
        d_key_turned = nn(jnp.concatenate(far_key, axis=1), stacked(rel_q, halves))
        r.d_rel_v[:, pair_at(pair)] = tn(jnp.concatenate(far_key, axis=0), stacked(key_turned, halves))
        r.d_rel_v[:, pair_at(pair, D)] = tn(jnp.concatenate(far_query, axis=0), stacked(query_turned, halves))
        d_query = d_query * SCALE + nn(turn, d_query_turned.astype(bf16))
        d_key = d_key * SCALE + nn(turn, d_key_turned.astype(bf16))
        r.att_v[:, pair_at(pair)] = d_query.astype(bf16)
        r.att_v[:, pair_at(pair, D)] = d_key.astype(bf16)
    stores = []
    for side_core, target in ((r.ctl[1], r.att_own), (1 - r.ctl[1], r.att_other)):
        query_or_key = pl.ds(pl.multiple_of(side_core * D, 128), D)
        stores.append(r.copies.start(r.att_v.at[:, query_or_key], target.at[pl.ds(row * L, L)]))
    far_sums = [column_sums(r.d_rel_v[:, block_at(part)]) for part in range(2)]
    if row > 0:
        wait_all(loads.earlier)
        r.d_rel_v[...] = r.d_rel_v[...] + r.d_rel_old[...]
    last = row == ROWS - 1
    if last:
        r.rel_low[...] = r.d_rel_v[...].astype(bf16)
        for side_core, target in ((r.ctl[1], r.att_own), (1 - r.ctl[1], r.att_other)):
            query_or_key = pl.ds(pl.multiple_of(side_core * D, 128), D)
            stores.append(r.copies.start(r.rel_low.at[:, query_or_key], target.at[pl.ds(2 * L, 2 * L)]))
    else:
        stores.append(r.copies.start(r.d_rel_v, r.d_rel))
    for part in range(2):
        rows = column_sums(r.att_v[:, block_at(part)].astype(f32)) + far_sums[part]
        r.att_vec_v[part : part + 1] = rows
    stores.append(r.copies.start(r.att_vec_v, r.att_vec.at[row]))
    wait_all(loads.w_in)
    if last and section == 0:
        stores.append(r.copies.start(r.att_v, r.d_rows))
        wait_all(loads.others)
        return stores + tail_part(r, None, r.ffn_vec_v[0] + r.ffn_vec_v[1] + r.att_vec_old[...] + r.att_vec_v[...])
    d_start = d_resid + nt(r.att_v[:, :D], r.wi[:, :D])
    r.start_v[...] = d_start.astype(bf16)
    stores.append(r.copies.start(r.start_v, r.d_start.at[row]))
    result = d_start + nt(r.att_v[:, D:], r.wi[:, D : 2 * D]) + nt(r.value_v[...], r.wi[:, 2 * D :])
    r.grad_out_v[...] = result.astype(bf16)
    stores.append(r.copies.start(r.grad_out_v, r.input_grad.at[row]))
    if section == 1:
        stores.append(r.copies.start(r.grad_out_v, r.sent))
        if last:
            stores.append(r.copies.start(r.rel_low, r.d_rel_low))
    return stores


def finish_body(r):
    @pl.when(r.ctl[0] == 0)
    def _():
        loads = [
            r.copies.start(source, target)
            for source, target in (
                (r.d_resid, r.resid_v), (r.d_rows, r.rows_v), (r.d_context.at[:, pl.ds(D, D)], r.value_v), (r.w_in, r.wi)
            )
        ]
        wait_all(loads)
        result = r.resid_v[...] + nt(r.rows_v[...], r.wi[:, : 2 * D]) + nt(r.value_v[...], r.wi[:, 2 * D :])
        r.grad_v[...] = result.astype(bf16)
        r.copies.start(r.grad_v, r.input_grad.at[ROWS - 1]).wait()


def finish(ctl, held, **ins):
    outs = dict(input_grad=shape((ROWS, L, D)))
    scratch = dict(
        resid_v=shape((L, D), f32), rows_v=shape((L, 2 * D)), value_v=shape((L, D)), wi=shape((D, 3 * D)), grad_v=shape((L, D))
    )
    return run(finish_body, ctl, ins, outs, held, scratch, 5, 500000000, 5000000)["input_grad"]


def tail_part(r, starts, vectors):
    def put(first, rows, value):
        r.tail_v[first : first + rows] = value.astype(bf16)

    if starts is None:
        put(REL_ROWS, ABS_ROWS, jnp.zeros((ABS_ROWS, D), f32))
    else:
        dims = (ABS_ROWS, L)
        place = lax.broadcasted_iota(jnp.int32, dims, 0) - lax.broadcasted_iota(jnp.int32, dims, 1)
        spots = [indicator(place == r.ctl[2 + row]) for row in range(ROWS)]
        put(REL_ROWS, ABS_ROWS, nn(spots[0], starts[0]) + nn(spots[1], starts[1]))
    put(TABLE_ROWS, VECTOR_ROWS, vectors)
    rest = TAIL_ROWS - TABLE_ROWS - VECTOR_ROWS
    put(TABLE_ROWS + VECTOR_ROWS, rest, jnp.zeros((rest, D), f32))
    rows = nt(r.rel_low[...], r.wi[:, : 2 * D]).astype(bf16)
    dims = (REL_ROWS, 2 * L)
    select = lax.broadcasted_iota(jnp.int32, dims, 0) + lax.broadcasted_iota(jnp.int32, dims, 1) == L + SPAN - REL_FROM
    put(0, REL_ROWS, nn(indicator(select), rows))
    return [
        r.copies.start(
            r.tail_v.at[pl.ds(pl.multiple_of(side_core * TAIL_HALF, 16), TAIL_HALF)], target.at[pl.ds(4 * L, TAIL_HALF)]
        )
        for side_core, target in ((r.ctl[1], r.att_own), (1 - r.ctl[1], r.att_other))
    ]


def backward_body(row, section, parts, r):
    @pl.when(r.ctl[0] == section)
    def _():
        if parts == "ffn":
            d_resid, stores = ffn_part(row, section, r, ffn_loads(row, section, r))
            r.resid_v[:, :D] = d_resid
            stores.append(r.copies.start(r.resid_v.at[:, pl.ds(0, D)], r.d_resid))
            stores.append(r.copies.start(r.context_v, r.d_context.at[:, pl.ds(0, D)]))
            stores.append(r.copies.start(r.ffn_v.at[:, pl.ds(FF + 2 * D, D)], r.d_context.at[:, pl.ds(D, D)]))
        elif parts == "att":
            first = [
                r.copies.start(r.d_resid, r.d_resid_v),
                r.copies.start(r.d_context.at[:, pl.ds(0, D)], r.context_v),
                r.copies.start(r.keep.at[row, :, pl.ds(K_P, K_GP - K_P)], r.probs_v),
                r.copies.start(r.d_context.at[:, pl.ds(D, D)], r.value_v),
            ]
            loads = att_loads(row, section, r)
            wait_all(first)
            stores = att_part(row, section, r, loads, r.d_resid_v[...])
        else:
            loads = ffn_loads(row, section, r)
            later = att_loads(row, section, r)
            d_resid, stores = ffn_part(row, section, r, loads)
            r.value_v[...] = r.ffn_v[:, FF + 2 * D :]
            stores = stores + att_part(row, section, r, later, d_resid)
        wait_all(stores)


def backward(row, section, parts, ctl, ins, held):
    outs, scratch, flops, traffic = {}, {}, 0, 0
    if parts == "ffn":
        outs.update(d_resid=shape((L, D), f32), d_context=shape((L, 2 * D)))
    if parts != "att":
        outs.update(
            ffn_own=shape((ROWS * L, 5 * D)), ffn_other=shape((ROWS * L, 5 * D)), ffn_vec=shape((ROWS, VECTOR_ROWS, D), f32)
        )
        scratch.update(
            grad_v=shape((L, D)), resid_v=shape((L, 2 * D), f32), gains_v=shape((2, D)), slope_v=shape((L, FF)),
            wu=shape((FF, D)), wd=shape((D, FF)), ffn_v=shape((L, FF + 3 * D)), wo=shape((D, D)), probs_v=shape((L, 2 * D)), context_v=shape((L, D)), ffn_vec_v=shape((VECTOR_ROWS, D), f32),
        )
        flops, traffic = flops + 1300000000, traffic + 12000000
    if parts == "att":
        scratch.update(d_resid_v=shape((L, D), f32), context_v=shape((L, D)), probs_v=shape((L, 2 * D)))
    if parts != "ffn":
        if section == 1:
            outs.update(sent=shape((L, D)))
        outs.update(
            att_own=shape((SWAP_ROWS, D)), att_other=shape((SWAP_ROWS, D)), att_vec=shape((ROWS, VECTOR_ROWS, D), f32),
            d_start=shape((ROWS, L, D)), d_rel=shape((2 * L, 2 * D), f32), d_rel_low=shape((2 * L, 2 * D)),
            input_grad=shape((ROWS, L, D)),
        )
        scratch.update(
            wi=shape((D, 3 * D)), keep_v=shape((L, K_P)), rel_v=shape((2 * L, 2 * D)),
            att_v=shape((L, 2 * D)), att_vec_v=shape((VECTOR_ROWS, D), f32), start_v=shape((L, D)), grad_out_v=shape((L, D)),
            value_v=shape((L, D)), d_rel_v=shape((2 * L, 2 * D), f32), d_rel_old=shape((2 * L, 2 * D), f32), rel_low=shape((2 * L, 2 * D)),
        )
        if row == ROWS - 1 and section == 0:
            outs.update(d_rows=shape((L, 2 * D)))
            del outs["input_grad"], outs["d_start"]
            scratch.update(
                tail_v=shape((TAIL_ROWS, D)),
                att_vec_old=shape((VECTOR_ROWS, D), f32), ffn_vec_v=shape((ROWS, VECTOR_ROWS, D), f32),
            )
        flops, traffic = flops + 1100000000, traffic + 8000000
    return run(partial(backward_body, row, section, parts), ctl, ins, outs, held, scratch, 56, flops, traffic, near=())


def tables_body(r):
    @pl.when(r.ctl[0] == 1)
    def _():
        loads = [
            r.copies.start(source, target)
            for source, target in (
                (r.d_start, r.start_v), (r.ffn_vec, r.ffn_vec_v), (r.att_vec, r.att_vec_v), (r.d_rel_low, r.rel_low), (r.w_in, r.wi)
            )
        ]
        wait_all(loads)
        vectors = r.ffn_vec_v[0] + r.ffn_vec_v[1] + r.att_vec_v[0] + r.att_vec_v[1]
        wait_all(tail_part(r, [r.start_v[0], r.start_v[1]], vectors))


def tables(ctl, w_in, held):
    ins = dict(w_in=w_in, **{name: held[name] for name in ("d_start", "ffn_vec", "att_vec", "d_rel_low")})
    outs = dict(att_own=shape((SWAP_ROWS, D)), att_other=shape((SWAP_ROWS, D)))
    scratch = dict(
        start_v=shape((ROWS, L, D)), ffn_vec_v=shape((ROWS, VECTOR_ROWS, D), f32), att_vec_v=shape((ROWS, VECTOR_ROWS, D), f32),
        rel_low=shape((2 * L, 2 * D)), wi=shape((D, 3 * D)), tail_v=shape((TAIL_ROWS, D)),
    )
    return run(tables_body, ctl, ins, outs, held, scratch, 8, 1000000000, 7000000)


def small_kernel(body, ctl, ins, outs):
    return pl.pallas_call(
        body,
        out_shape=outs,
        in_specs=[SMEM] + [VMEM] * len(ins),
        out_specs=(VMEM,) * len(outs),
        compiler_params=pltpu.CompilerParams(vmem_limit_bytes=16 * 2**20),
        cost_estimate=pl.CostEstimate(flops=0, bytes_accessed=2 * sum(value.size for value in ins) * 2, transcendentals=0),
    )(ctl, *ins)


def added(kept, received):
    return (kept.astype(f32) + received.astype(f32)).astype(bf16)


def split_sum(ctl, bit, kept, received):
    half = kept.shape[0] // 2

    def body(ctl, kept, received, keep, send):
        low, high = (added(kept[at], received[at]) for at in (slice(0, half), slice(half, 2 * half)))
        first = ctl[bit] == 0
        keep[...] = jnp.where(first, low, high)
        send[...] = jnp.where(first, high, low)

    return small_kernel(body, ctl, (kept, received), (shape((half, D)),) * 2)


def in_order(ctl, bit, own, other):
    half = own.shape[0]

    def body(ctl, own, other, out):
        first = ctl[bit] == 0
        out[:half] = jnp.where(first, own[...], other[...])
        out[half:] = jnp.where(first, other[...], own[...])

    return small_kernel(body, ctl, (own, other), (shape((2 * half, D)),))[0]


class Halves:
    def __init__(self, r, first_piece, half_rows):
        self.r, self.first_piece, self.half_rows, self.pending = r, first_piece, half_rows, []

    def store(self, first, rows):
        while rows > 0:
            index, inside = divmod(first, self.half_rows)
            count = min(rows, self.half_rows - inside)
            piece, half = index // 2, index % 2
            view, there = self.r.out_v.at[pl.ds(first, count)], pl.ds(inside, count)
            kept = self.r.copies.make(view, getattr(self.r, f"kept{piece}").at[there])
            sem = self.r.copies.sems.at[self.r.copies.used - 1]
            sent = pltpu.make_async_copy(view, getattr(self.r, f"sent{piece}").at[there], sem)
            mine = self.r.ctl[bit_at(self.first_piece + piece, False)] == half

            @pl.when(mine)
            def _():
                kept.start()

            @pl.when(jnp.logical_not(mine))
            def _():
                sent.start()

            self.pending.append(kept)
            first, rows = first + count, rows - count


def bit_at(piece, of_other_core):
    return 4 + 2 * piece + int(of_other_core)


def half_outputs(rows, pieces):
    half_rows = rows // pieces // 2
    return {f"{kind}{piece}": shape((half_rows, D)) for piece in range(pieces) for kind in ("kept", "sent")}


def load_acts(r, at, size, to):
    if not isinstance(at, int):
        at = pl.multiple_of(at, 128)
    return [
        r.copies.start(source.at[row, :, pl.ds(at, size)], target.at[pl.ds(row * L, L), pl.ds(to, size)])
        for row in range(ROWS)
        for source, target in ((r.acts, r.acts_v), (r.acts_sent, r.acts_sent_v))
    ]


def ffn_weights_body(r):
    core = r.ctl[1]
    loads = [r.copies.start(r.rows, r.rows_v)] + load_acts(r, A_HID, D, 0)
    later = load_acts(r, A_ACT + core * 2 * D, 2 * D, D)
    last = load_acts(r, A_CTX + core * HALF, HALF, 3 * D) + load_acts(r, A_X + core * HALF, HALF, 3 * D + HALF)
    halves = Halves(r, 0, FFN_ROWS // FFN_PIECES // 2)

    def product(acts_at, rows_at):
        own = tn(r.acts_v[:, acts_at], r.rows_v[:, rows_at])
        return (own + tn(r.acts_sent_v[:, acts_at], r.rows_sent[:, rows_at])).astype(bf16)

    wait_all(loads)
    for block in range(2):
        r.out_v[block_at(block)] = product(block_at(0), block_at(block))
        halves.store(block * D, D)
    wait_all(later)
    for block in range(2, 4):
        r.out_v[block_at(block)] = product(block_at(block - 1), block_at(2))
        halves.store(block * D, D)
    wait_all(last)
    for part in range(2):
        to = slice(4 * D + part * HALF, 4 * D + (part + 1) * HALF)
        r.out_v[to] = product(slice(3 * D + part * HALF, 3 * D + (part + 1) * HALF), block_at(3 + part))
    halves.store(4 * D, D)
    wait_all(halves.pending)


def ffn_weights(ctl, **ins):
    scratch = dict(
        rows_v=shape((ROWS * L, 5 * D)), acts_v=shape((ROWS * L, 4 * D)), acts_sent_v=shape((ROWS * L, 4 * D)),
        out_v=shape((FFN_ROWS, D)),
    )
    outs = half_outputs(FFN_ROWS, FFN_PIECES)
    return run(ffn_weights_body, ctl, ins, outs, {}, scratch, 36, 2 * 512 * 768 * FFN_ROWS, 14000000, ("rows_sent",))


def att_weights_body(r):
    loads = [r.copies.start(r.rows, r.rows_v), r.copies.start(r.table, r.table_v)]
    loads += load_acts(r, r.ctl[1] * D, D, 0)
    halves = Halves(r, FFN_PIECES, ATT_ROWS // ATT_PIECES // 2)
    wait_all(loads)
    total = tn(r.acts_v[...], r.rows_v[: 2 * L]) + tn(r.acts_sent_v[...], r.rows_sent[: 2 * L])
    far = (r.rows_v[2 * L : 4 * L].astype(f32) + r.rows_sent[2 * L : 4 * L].astype(f32)).astype(bf16)
    r.out_v[:D] = (total + tn(r.table_v[...], far)).astype(bf16)
    r.out_v[TAIL_AT:] = r.rows_v[4 * L :] + r.rows_sent[4 * L :]
    halves.store(0, ATT_ROWS)
    wait_all(halves.pending)


def att_weights(ctl, **ins):
    scratch = dict(
        rows_v=shape((SWAP_ROWS, D)), table_v=shape((2 * L, D)),
        acts_v=shape((ROWS * L, D)), acts_sent_v=shape((ROWS * L, D)), out_v=shape((ATT_ROWS, D)),
    )
    outs = half_outputs(ATT_ROWS, ATT_PIECES)
    return run(att_weights_body, ctl, ins, outs, {}, scratch, 16, 2 * 768 * 768 * 768, 6000000, ("rows_sent",))


def half_segments(layout, half_rows, piece, half):
    low = (2 * piece + half) * half_rows
    found, at = [], 0
    for target, rows, first, block in layout:
        start, stop = max(at, low), min(at + rows, low + half_rows)
        if start < stop:
            found.append((start - low, stop - start, target, first + start - at, block))
        at += rows
    return found


def assemble_body(kind, first_piece, layouts, half_rows, chosen, r):
    start_copy = r.copies.start
    core = r.ctl[1]
    blank = None
    if first_piece > 0 and kind == 0:
        r.blank[...] = jnp.zeros_like(r.blank)
        rest = 2 * SPAN - REL_FROM - REL_ROWS
        blank = [
            start_copy(r.blank, r.g_rel.at[pl.ds(0, REL_FROM)]),
            start_copy(r.blank.at[pl.ds(0, rest)], r.g_rel.at[pl.ds(REL_FROM + REL_ROWS, rest)]),
        ]
    branches = []
    chunk = half_rows // 2
    items = [(piece, origin) for piece in chosen for origin in ("own", "sent")]
    for index, (piece, origin) in enumerate(items):
        array = getattr(r, f"{origin}{piece}")
        bit = r.ctl[bit_at(first_piece + piece, origin == "sent")]
        maker = core if origin == "own" else 1 - core
        cases = [(made_by, half) for made_by in range(2) for half in range(2)]
        for at in range(0, half_rows, chunk):
            r.wide[index, at : at + chunk] = array[at : at + chunk].astype(f32)
            first_copy = last_copy = r.copies.used
            for made_by, half in cases:
                r.copies.used = first_copy
                copies = []
                for inside, count, name, start, block in half_segments(layouts[made_by], half_rows, piece, half):
                    low, high = max(inside, at), min(inside + count, at + chunk)
                    if low < high and name not in ("", "vectors"):
                        target = getattr(r, name).at[pl.ds(start + low - inside, high - low), pl.ds(block * D, D)]
                        copies.append(r.copies.make(r.wide.at[index, pl.ds(low, high - low)], target))
                last_copy = max(last_copy, r.copies.used)
                here = (maker == made_by) & (bit == (half if kind == 0 else 1 - half))
                branches.append((here, copies))

                @pl.when(here)
                def _():
                    for copy in copies:
                        copy.start()

            r.copies.used = last_copy
        for made_by, half in cases:
            for inside, count, name, _, _ in half_segments(layouts[made_by], half_rows, piece, half):
                if name == "vectors":

                    @pl.when((maker == made_by) & (bit == (half if kind == 0 else 1 - half)))
                    def _():
                        vectors = r.wide[index, inside : inside + count, :]
                        for part in range(3):
                            r.b_in_v[:, block_at(part)] = vectors[part : part + 1]
                        for part in range(4):
                            r.b_up_v[:, block_at(part)] = vectors[3 + part : 4 + part]
                        r.gains_v[...] = vectors[7:9]
                        r.biases_v[...] = vectors[9:13]
                        wait_all([
                            start_copy(r.b_in_v, r.g_b_in), start_copy(r.b_up_v, r.g_b_up),
                            start_copy(r.gains_v, r.g_gains), start_copy(r.biases_v, r.g_biases),
                        ])

    wait_all(blank or [])
    for here, copies in branches:

        @pl.when(here)
        def _():
            wait_all(copies)


def assemble(kind, first_piece, layouts, rows, pieces, chosen, ctl, own, sent, shapes, held):
    ins = {f"own{i}": value for i, value in zip(chosen, own)}
    ins.update({f"sent{i}": value for i, value in zip(chosen, sent)})
    outs = {name: shape(dims, f32) for name, dims in shapes.items()}
    half_rows = rows // pieces // 2
    scratch = dict(wide=shape((len(ins), half_rows, D), f32))
    if first_piece > 0:
        scratch.update(
            blank=shape((REL_FROM, D), f32), b_in_v=shape((1, 3 * D), f32), b_up_v=shape((1, FF), f32),
            gains_v=shape((2, D), f32), biases_v=shape((4, D), f32),
        )
    body = partial(assemble_body, kind, first_piece, layouts, half_rows, chosen)
    return run(body, ctl, ins, outs, held, scratch, 96, 0, len(ins) * half_rows * D * 6, tuple(ins), 44 * 2**20)


FFN_SHAPES = dict(g_up=(D, FF), g_down=(FF, D), g_out=(D, D), g_in=(D, 3 * D))
ATT_SHAPES = dict(
    g_in=(D, 3 * D), g_rel=(2 * SPAN, D), g_abs=(ABS_ROWS, D),
    g_b_in=(1, 3 * D), g_b_up=(1, FF), g_gains=(2, D), g_biases=(4, D),
)


SQUARE = ((0, 0), (1, 0), (1, 1), (0, 1))


def dp_place(index):
    return {"core": index % 2, "x": index // 2 % 4, "y": index // 8 % 2, "z": index // 16}


def dp_index(place):
    return ((place["z"] * 2 + place["y"]) * 4 + place["x"]) * 2 + place["core"]


def partner(index, dim):
    place = dp_place(index)
    if len(dim) == 2:
        bits = list(SQUARE[place[dim[0]]])
        bits[int(dim[1])] ^= 1
        place[dim[0]] = SQUARE.index(tuple(bits))
    else:
        place[dim] ^= 1
    return dp_index(place)


def swap(value, dims):
    peers = lax.axis_size("dp")
    return lax.ppermute(value, "dp", [(i, partner(i, dims[i % 2])) for i in range(peers)])


BETWEEN_CORES = ("core", "core")


def side_along(dim):
    place = dp_place(lax.axis_index("dp"))
    if dim == "y":
        return place[dim].astype(jnp.int32)
    at = place[dim[0]]
    if dim[1] == "0":
        return ((at == 1) | (at == 2)).astype(jnp.int32)
    return (at >= 2).astype(jnp.int32)


def this_core():
    return (lax.axis_index("dp") % 2).astype(jnp.int32)


def side(dims):
    return jnp.where(this_core() == 0, side_along(dims[0]), side_along(dims[1]))


ORDERS = [
    [("x0", "y"), ("z0", "x1"), ("x1", "z1"), ("y", "z0"), ("z1", "x0")],
    [("x1", "z0"), ("x0", "z1"), ("y", "x0"), ("z1", "x1"), ("z0", "y")],
    [("z1", "y"), ("x1", "z1"), ("y", "z0"), ("x0", "x1"), ("z0", "x0")],
]
BITS_AT = 4 + 2 * (FFN_PIECES + ATT_PIECES)
SPLIT_STEPS = 3


def bit_of(piece, step):
    return BITS_AT + 2 * piece + step - 1


def is_table_row(chunk):
    piece = FFN_PIECES
    first_row, span = 0, ATT_ROWS
    for dims in ORDERS[piece][:SPLIT_STEPS]:
        span //= 2
        first_row = first_row + side(dims) * span
    row_at = first_row + lax.broadcasted_iota(jnp.int32, chunk.shape, 0) - TAIL_AT
    return (row_at >= 0) & (row_at + this_core() * TAIL_HALF < TABLE_ROWS)


class Sequence:
    def __init__(self, last):
        self.last = last

    def after(self, *values):
        values = lax.optimization_barrier((*values, self.last))[:-1]
        return values[0] if len(values) == 1 else values


class Pieces:
    def __init__(self, ctl, seq):
        self.ctl, self.seq = ctl, seq
        self.kept, self.received, self.mine, self.mine_sent, self.partners, self.partners_sent = ({} for _ in range(6))

    def begin(self, piece, kept, sent):
        self.kept[piece], self.received[piece] = kept, swap(sent, ORDERS[piece][0])

    def inputs(self, piece):
        return self.seq.after(self.kept[piece], self.received[piece])

    def hold(self, piece, chunk):
        self.kept[piece] = self.seq.last = chunk

    def land(self, piece):
        self.received[piece] = self.seq.last = self.seq.after(self.received[piece])

    def split(self, piece, step):
        kept, sent = split_sum(self.ctl, bit_of(piece, step), *self.inputs(piece))
        self.hold(piece, kept)
        self.received[piece] = swap(sent, ORDERS[piece][step])

    def add(self, piece, step):
        kept, received = self.inputs(piece)
        self.hold(piece, kept + received)
        self.received[piece] = swap(self.kept[piece], ORDERS[piece][step])

    def add_for_section(self, piece):
        kept, received = self.inputs(piece)
        self.hold(piece, kept + received)
        self.received[piece] = lax.ppermute(self.kept[piece], "section", [(0, 1), (1, 0)])

    def add_tables(self, piece, step):
        kept, received = self.inputs(piece)
        self.hold(piece, jnp.where(is_table_row(kept), kept + received, kept))
        self.received[piece] = swap(self.kept[piece], ORDERS[piece][step])

    def join(self, piece, step):
        self.hold(piece, in_order(self.ctl, bit_of(piece, step), *self.inputs(piece)))
        self.received[piece] = swap(self.kept[piece], ORDERS[piece][step - 1])

    def cross(self, piece):
        self.mine[piece] = self.seq.last = self.seq.after(self.kept[piece])
        self.mine_sent[piece] = swap(self.mine[piece], BETWEEN_CORES)

    def arrive(self, piece):
        self.partners[piece] = self.seq.last = self.seq.after(self.received[piece])
        self.partners_sent[piece] = swap(self.partners[piece], BETWEEN_CORES)


def per_device(
    hidden_in,
    cotangent,
    segment_ids,
    positions,
    w_in,
    b_in,
    w_out,
    w_up,
    b_up,
    w_down,
    gains,
    biases,
    rel_table,
    abs_table,
):
    section = lax.axis_index("section").astype(jnp.int32)
    firsts = jnp.where(section == 1, positions[:, 0], 8 * ABS_ROWS)
    bits = [side(dims) for order in ORDERS for dims in (order[0], order[0][::-1])]
    bits += [side(order[step]) for order in ORDERS for step in range(1, SPLIT_STEPS)]
    ctl = jnp.stack([section, this_core(), firsts[0], firsts[1], *bits])
    weights = dict(w_in=w_in[0], w_out=w_out[0], w_up=w_up[0], w_down=w_down[0], gains=gains[0])
    common = dict(
        weights, hidden_in=hidden_in, segment_ids=segment_ids, biases=biases[0], b_in=b_in, b_up=b_up, abs_table=abs_table
    )

    out = forward(0, 0, ctl, dict(common, rel_table=rel_table), {})
    rel, rel_rows = out["rel"], out["rel_rows"]
    common["rel"] = rel
    received = []
    for row in range(ROWS):
        if row > 0:
            out = forward(row, 0, ctl, common, out)
        received.append(lax.ppermute(out["sent"], "section", [(0, 1)]))
    ready = {name: out[name] for name in ("keep", "resid")}
    back_ins = dict(common, cotangent=cotangent)
    grads = []
    for row in range(ROWS):
        turned = {name: out[name] for name in ("w_up_t", "w_down_t")} if row > 0 else {}
        out = {**out, **forward(row, 1, ctl, dict(back_ins, **turned, received=received[row]), out)}
        grads.append(lax.ppermute(out["sent"], "section", [(1, 0)]))
        if row < ROWS - 1:
            received[row + 1], grads[row] = lax.optimization_barrier((received[row + 1], grads[row]))
    acts, section_out = out["acts"], out["section_out"]
    acts_sent = swap(acts, BETWEEN_CORES)
    turned = {name: out[name] for name in ("w_up_t", "w_down_t")}
    common = dict(weights, **ready, **turned, rel=rel)
    received = grads
    out.update(tables(ctl, weights["w_in"], out))
    out = backward(0, 0, "both", ctl, dict(common, received=received[0]), out)
    early = out
    ffn = backward(1, 0, "ffn", ctl, dict(common, received=received[1]), early)
    ffn_sent = swap(ffn["ffn_other"], BETWEEN_CORES)
    seq = Sequence(ffn["ffn_own"])
    pieces = Pieces(ctl, seq)
    grads = {}

    def write(kind, group, *chosen):
        own, sent = ((pieces.mine, pieces.mine_sent), (pieces.partners, pieces.partners_sent))[kind]
        first, count, layout, rows, shapes = group
        first_own, *own = [own[first + i] for i in chosen]
        sent = [sent[first + i] for i in chosen]
        result = assemble(kind, first, layout, rows, count, chosen, ctl, [seq.after(first_own), *own], sent, shapes, grads)
        grads.update(result)
        seq.last = result["g_biases"] if first > 0 else result["g_out"]

    ffn_group = 0, FFN_PIECES, FFN_LAYOUT, FFN_ROWS, FFN_SHAPES
    att_group = FFN_PIECES, ATT_PIECES, ATT_LAYOUT, ATT_ROWS, ATT_SHAPES
    ins = dict(common, d_resid=seq.after(ffn["d_resid"]), d_context=ffn["d_context"], ffn_vec=ffn["ffn_vec"])
    out = backward(1, 0, "att", ctl, ins, early)
    att_sent = swap(out["att_other"], BETWEEN_CORES)
    seq.last = out["att_own"]
    halves = ffn_weights(ctl, acts=acts, acts_sent=acts_sent, rows=seq.after(ffn["ffn_own"]), rows_sent=ffn_sent)
    for piece in range(FFN_PIECES):
        pieces.begin(piece, halves[f"kept{piece}"], halves[f"sent{piece}"])
    seq.last = halves["kept0"]
    halves = att_weights(
        ctl, acts=acts, acts_sent=acts_sent, rows=seq.after(out["att_own"]), rows_sent=att_sent, table=rel_rows
    )
    pieces.begin(FFN_PIECES, halves["kept0"], halves["sent0"])
    seq.last = halves["kept0"]
    input_grad = finish(
        ctl, early, d_resid=ffn["d_resid"], d_rows=seq.after(out["d_rows"]), d_context=ffn["d_context"], w_in=weights["w_in"]
    )
    seq.last = input_grad
    pieces.split(0, 1)
    pieces.split(1, 1)
    pieces.land(2)
    pieces.split(0, 2)
    pieces.split(1, 2)
    pieces.split(2, 1)
    pieces.add(0, 3)
    pieces.add(1, 3)
    pieces.split(2, 2)
    pieces.add(0, 4)
    pieces.add(1, 4)
    pieces.add(2, 3)
    pieces.add(0, 2)
    pieces.land(1)
    pieces.add(2, 4)
    pieces.add(1, 2)
    pieces.join(0, 2)
    pieces.add_for_section(2)
    pieces.join(1, 2)
    pieces.add_tables(2, 2)
    pieces.join(0, 1)
    pieces.cross(0)
    pieces.join(2, 2)
    pieces.join(1, 1)
    pieces.cross(1)
    pieces.join(2, 1)
    pieces.cross(2)
    write(0, att_group, 0)
    pieces.arrive(0)
    write(0, ffn_group, 0, 1)
    pieces.arrive(1)
    pieces.arrive(2)
    write(1, ffn_group, 0, 1)
    write(1, att_group, 0)
    return (
        section_out[None],
        input_grad[None],
        grads["g_in"][None],
        grads["g_b_in"],
        grads["g_out"][None],
        grads["g_up"][None],
        grads["g_b_up"],
        grads["g_down"][None],
        grads["g_gains"][None],
        grads["g_biases"][None],
        grads["g_rel"],
        grads["g_abs"],
    )


def solution(mesh):
    in_specs = (
        P("dp", None, None),
        P("dp", None, None),
        P("dp", None),
        P("dp", None),
        P("section", None, None),
        P("section", None),
        P("section", None, None),
        P("section", None, None),
        P("section", None),
        P("section", None, None),
        P("section", None, None),
        P("section", None, None),
        P(),
        P(),
    )
    out_specs = (
        P("section", "dp", None, None),
        P("section", "dp", None, None),
        P("section", None, None),
        P("section", None),
        P("section", None, None),
        P("section", None, None),
        P("section", None),
        P("section", None, None),
        P("section", None, None),
        P("section", None, None),
        P(),
        P(),
    )
    return jax.shard_map(
        per_device, mesh=mesh, in_specs=in_specs, out_specs=out_specs, check_vma=False
    )
```

```python
from functools import partial
import math
from types import SimpleNamespace

import jax
import jax.numpy as jnp
from jax import lax
from jax.experimental import pallas as pl
from jax.experimental.pallas import tpu as pltpu
from jax.sharding import PartitionSpec as P

HEADS = 12
L = 128
D = 768
FF = 3072
HALF = D // 2
PAIRS = HEADS // 2
ROWS = 2
SPAN = 256
EPS = 1e-06
NEG = -1e30
SCALE = 1.0 / math.sqrt(3 * 64)
VMEM_LIMIT = 61 * 1024 * 1024
f32, bf16 = jnp.float32, jnp.bfloat16

A_START, A_X, A_CTX, A_HID, A_ACT, A_ALL = 0, 768, 1536, 2304, 3072, 6144
K_P, K_GP, K_ALL = 2304, 3840, 6912
VECTOR_ROWS = 16
REL_FROM, REL_ROWS, ABS_ROWS, TAIL_ROWS = 128, 272, 512, 896
TABLE_ROWS = REL_ROWS + ABS_ROWS
FFN_LAYOUT = [
    [("g_up", D, 0, 2 * core), ("g_up", D, 0, 2 * core + 1), ("g_down", 2 * D, 2 * D * core, 0), ("g_out", HALF, HALF * core, 0),
     ("g_in", HALF, HALF * core, 2)]
    for core in range(2)
]
ATT_LAYOUT = [
    [("g_in", D, 0, 0), ("g_rel", REL_ROWS, REL_FROM, 0), ("g_abs", 176, 0, 0)],
    [("g_in", D, 0, 1), ("g_abs", 336, 176, 0), ("vectors", VECTOR_ROWS, 0, 0), ("", 96, 0, 0)],
]
FFN_ROWS, ATT_ROWS = 3840, 1216
FFN_PIECES, ATT_PIECES = 2, 1
TAIL_HALF = TAIL_ROWS // 2
TAIL_AT = ATT_ROWS - TAIL_HALF
SWAP_ROWS = 4 * L + TAIL_HALF

VMEM = pl.BlockSpec(memory_space=pltpu.VMEM)
ANY = pl.BlockSpec(memory_space=pl.ANY)
SMEM = pl.BlockSpec(memory_space=pltpu.SMEM)


def nn(a, b):
    return lax.dot_general(a, b, (((1,), (0,)), ((), ())), preferred_element_type=f32)


def nt(a, b):
    return lax.dot_general(a, b, (((1,), (1,)), ((), ())), preferred_element_type=f32)


def tn(a, b):
    return lax.dot_general(a, b, (((0,), (0,)), ((), ())), preferred_element_type=f32)


def norm_parts(value):
    centered = value - jnp.mean(value, axis=1, keepdims=True)
    rstd = lax.rsqrt(jnp.mean(centered * centered, axis=1, keepdims=True) + EPS)
    return centered * rstd, rstd


def norm_backward(normed, rstd, gain, grad):
    scaled = grad * gain
    mean_one = jnp.mean(scaled, axis=1, keepdims=True)
    mean_two = jnp.mean(scaled * normed, axis=1, keepdims=True)
    return (scaled - mean_one - normed * mean_two) * rstd


def column_sums(value):
    return jnp.sum(value, axis=0, keepdims=True)


def indicator(condition):
    return condition.astype(f32).astype(bf16)


def lane_halves():
    lane = lax.broadcasted_iota(jnp.int32, (1, L), 1)
    return indicator(lane < 64), indicator(lane >= 64)


def stacked(value, halves):
    return jnp.concatenate([value * halves[0], value * halves[1]], axis=0)


def skew(table):
    return pltpu.roll(table, L, 1, stride=1, stride_axis=0)[:, :L]


def unskew(turned):
    wide = jnp.concatenate([turned, jnp.zeros_like(turned)], axis=1)
    return pltpu.roll(wide, 1, 1, stride=1, stride_axis=0)


def pair_at(pair, base=0, width=L):
    return pl.ds(pl.multiple_of(base + pair * width, L), width)


def block_at(block, base=0):
    return slice(base + block * D, base + block * D + D)


def shape(dims, dtype=bf16):
    return jax.ShapeDtypeStruct(dims, dtype)


class Copies:
    def __init__(self, sems):
        self.sems, self.used, self.marks = sems, 0, {}

    def make(self, source, target):
        self.used += 1
        return pltpu.make_async_copy(source, target, self.sems.at[self.used - 1])

    def make_at(self, name):
        again = self.marks.setdefault(name, self.used)
        if again == self.used:
            return self.make
        at = iter(range(again, self.used))
        return lambda source, target: pltpu.make_async_copy(source, target, self.sems.at[next(at)])

    def start(self, source, target):
        copy = self.make(source, target)
        copy.start()
        return copy


def wait_all(copies):
    for copy in copies:
        copy.wait()


def run(body, ctl, ins, outs, held, scratch, copies, flops, traffic, near=(), limit=VMEM_LIMIT):
    names, out_names, scratch_names = list(ins), list(outs), list(scratch)
    kept = [name for name in out_names if name in held and name != "sent"]

    def kernel(*refs):
        ctl_ref, refs = refs[0], refs[1:]
        r = SimpleNamespace(ctl=ctl_ref, **dict(zip(names, refs)))
        refs = refs[len(names) + len(kept) :]
        for name, ref in zip(out_names + scratch_names, refs):
            setattr(r, name, ref)
        r.copies = Copies(refs[-1])
        body(r)

    results = pl.pallas_call(
        kernel,
        out_shape=tuple(outs.values()),
        in_specs=[SMEM] + [VMEM if name in near else ANY for name in names] + [ANY] * len(kept),
        out_specs=(ANY,) * len(out_names),
        input_output_aliases={1 + len(names) + i: out_names.index(name) for i, name in enumerate(kept)},
        scratch_shapes=[pltpu.VMEM(s.shape, s.dtype) for s in scratch.values()] + [pltpu.SemaphoreType.DMA((copies,))],
        compiler_params=pltpu.CompilerParams(vmem_limit_bytes=limit),
        cost_estimate=pl.CostEstimate(flops=flops, bytes_accessed=traffic, transcendentals=0),
    )(ctl, *ins.values(), *[held[name] for name in kept])
    return dict(zip(out_names, results))


def relative_loads(r):
    return [r.copies.start(r.rel_table, r.table_v), r.copies.start(r.b_in, r.b_in_v), r.copies.start(r.w_in, r.wi)]


def relative_part(r, loads):
    dims = (2 * L, 2 * SPAN)
    select = indicator(lax.broadcasted_iota(jnp.int32, dims, 0) + lax.broadcasted_iota(jnp.int32, dims, 1) == L + SPAN)
    loads[0].wait()
    rows = nn(select, r.table_v[...]).astype(bf16)
    r.rel_rows_v[...] = rows
    loads[1].wait()
    loads[2].wait()
    r.rel_v[...] = (nn(rows, r.wi[:, : 2 * D]) + r.b_in_v[:, : 2 * D].astype(f32)).astype(bf16)
    return [r.copies.start(r.rel_rows_v, r.rel_rows), r.copies.start(r.rel_v, r.rel)]


def forward_loads(row, section, first, r):
    make = r.copies.make_at("loads")
    loads = SimpleNamespace(
        x=[make(r.hidden_in.at[row] if section == 0 else r.received, r.x_v)],
        absolute=[make(r.abs_table, r.table_v)] if section == 1 else [],
        w_in=[]
        if first
        else [make(r.b_in, r.b_in_v)] + [make(r.w_in.at[:, block_at(part)], r.wi.at[:, block_at(part)]) for part in range(3)],
        rel=[] if first else [make(r.rel, r.rel_v)],
        small=[make(r.segment_ids, r.seg_v), make(r.gains, r.gains_v), make(r.biases, r.biases_v)],
        out=[make(r.w_out, r.wo), make(r.b_up, r.b_up_v)],
        parts=[
            [
                make(r.w_up.at[:, block_at(part)], r.wu.at[:, block_at(part)]),
                make(r.w_down.at[block_at(part)], r.wd.at[block_at(part)]),
            ]
            for part in range(4)
        ],
    )
    flat = loads.x + loads.absolute + loads.w_in + loads.rel + loads.small + loads.out
    loads.every = flat + [copy for part in loads.parts for copy in part]
    return loads


def forward_body(row, section, first, r):
    start_copy = r.copies.start
    stores = []
    if first:
        rel_loads = relative_loads(r)

        @pl.when(r.ctl[0] == section)
        def _():
            for copy in forward_loads(row, section, first, r).every:
                copy.start()

        stores = relative_part(r, rel_loads)

    @pl.when(r.ctl[0] == section)
    def _():
        loads = forward_loads(row, section, first, r)
        if not first:
            for copy in loads.every:
                copy.start()
        if section == 1:
            back = SimpleNamespace(
                first=[start_copy(r.cotangent.at[row], r.grad_v)],
                parts=[
                    [
                        start_copy(r.w_down_t.at[:, block_at(part)], r.wd_t.at[:, block_at(part)]),
                        start_copy(r.w_up_t.at[block_at(part)], r.wu_t.at[block_at(part)]),
                    ]
                    for part in range(4)
                ],
                last=[],
            )
            earlier = [start_copy(r.d_rel, r.d_rel_old)] if row > 0 else []
            back_att = SimpleNamespace(first=[], earlier=earlier, w_in=[], others=[])
        halves = lane_halves()
        wait_all(loads.x)
        x = r.x_v[...]
        start = x.astype(f32)
        if section == 1:
            wait_all(loads.absolute)
            dims = (L, ABS_ROWS)
            place = lax.broadcasted_iota(jnp.int32, dims, 1) - lax.broadcasted_iota(jnp.int32, dims, 0)
            start = start + nn(indicator(place == r.ctl[2 + row]), r.table_v[...])
        query_in = start.astype(bf16)
        r.acts_v[:, block_at(0)] = query_in
        r.acts_v[:, block_at(1)] = x
        wait_all(loads.w_in[:2])
        b_in = r.b_in_v[...].astype(f32)
        r.keep_v[:, :D] = (nn(query_in, r.wi[:, :D]) + b_in[:, :D]).astype(bf16)
        wait_all(loads.w_in[2:])
        r.keep_v[:, D : 3 * D] = (nn(x, r.wi[:, D:]) + b_in[:, D:]).astype(bf16)
        wait_all(loads.small + loads.rel)
        seg_rows = jnp.broadcast_to(r.seg_v[row : row + 1, :], (L, L)).astype(f32)
        same = seg_rows == seg_rows.T
        def attend(pair):
            query = r.keep_v[:, pair_at(pair)]
            key = r.keep_v[:, pair_at(pair, D)]
            value = r.keep_v[:, pair_at(pair, 2 * D)]
            query_two, key_two = stacked(query, halves), stacked(key, halves)
            content = nt(query_two, key)
            far_query = nt(query_two, r.rel_v[:, pair_at(pair, D)])
            far_key = nt(key_two, r.rel_v[:, pair_at(pair)])
            probs = []
            for head in range(2):
                rows = slice(head * L, head * L + L)
                summed = content[rows] + skew(far_query[rows]) + skew(far_key[rows]).T
                scores = jnp.where(same, summed * SCALE, NEG)
                exponent = jnp.exp(scores - jnp.max(scores, axis=1, keepdims=True))
                total = jnp.sum(exponent, axis=1, keepdims=True)
                probs.append((exponent * (1.0 / total)).astype(bf16))
            probs = jnp.concatenate(probs, axis=1)
            r.keep_v[:, pair_at(pair, K_P, 2 * L)] = probs
            r.acts_v[:, pair_at(pair, A_CTX)] = nn(probs, stacked(value, halves)).astype(bf16)

        if section == 0:
            for pair in range(PAIRS):
                attend(pair)
        else:
            pl.loop(0, PAIRS, unroll=3)(attend)
        wait_all(loads.out)
        gain = r.gains_v[...].astype(f32)
        shift = r.biases_v[...].astype(f32)
        resid_one = start + nn(r.acts_v[:, A_CTX : A_CTX + D], r.wo[...]) + shift[0:1]
        r.resid_v[:, :D] = resid_one
        hidden = norm_parts(resid_one)[0] * gain[0:1] + shift[1:2]
        hidden_low = hidden.astype(bf16)
        r.acts_v[:, A_HID : A_HID + D] = hidden_low
        stored = [start_copy(r.acts_v.at[:, pl.ds(0, A_ACT)], r.acts.at[row, :, pl.ds(0, A_ACT)])]
        if section == 0:
            stored.append(start_copy(r.keep_v.at[:, pl.ds(0, K_GP)], r.keep.at[row, :, pl.ds(0, K_GP)]))
        total = hidden + shift[2:3]
        for part in range(4):
            wait_all(loads.parts[part])
            gate = nn(hidden_low, r.wu[:, block_at(part)]) + r.b_up_v[:, block_at(part)].astype(f32)
            below = 0.5 + 0.5 * lax.erf(gate * (1.0 / math.sqrt(2.0)))
            density = jnp.exp(gate * gate * -0.5) * (1.0 / math.sqrt(2.0 * math.pi))
            active = (gate * below).astype(bf16)
            r.acts_v[:, block_at(part, A_ACT)] = active
            r.keep_v[:, block_at(part, K_GP)] = (below + gate * density).astype(bf16)
            stored.append(start_copy(r.acts_v.at[:, block_at(part, A_ACT)], r.acts.at[row, :, block_at(part, A_ACT)]))
            if section == 0:
                stored.append(start_copy(r.keep_v.at[:, block_at(part, K_GP)], r.keep.at[row, :, block_at(part, K_GP)]))
            total = total + nn(active, r.wd[block_at(part), :])
        r.resid_v[:, D:] = total
        if section == 0:
            stored.append(start_copy(r.resid_v, r.resid.at[row]))
        r.x_v[...] = (norm_parts(total)[0] * gain[1:2] + shift[3:4]).astype(bf16)
        stored.append(start_copy(r.x_v, r.section_out.at[row]))
        if section == 0:
            stored.append(start_copy(r.x_v, r.sent))
        else:
            near = SimpleNamespace(**vars(r))
            near.wu, near.wd = r.wu_t, r.wd_t
            near.probs_v = r.keep_v.at[:, pl.ds(K_P, K_GP - K_P)]
            near.slope_v = r.keep_v.at[:, pl.ds(K_GP, FF)]
            d_resid, out_copies = ffn_part(row, section, near, back)
            r.value_v[...] = r.ffn_v[:, FF + 2 * D :]
            stored += out_copies + att_part(row, section, near, back_att, d_resid)
        wait_all(stored)

    wait_all(stores)
    if turns_weights(row, section):

        @pl.when(r.ctl[0] != section)
        def _():
            turn_weights(r)


def turns_weights(row, section):
    return row == (ROWS - 1 if section == 0 else 0)


def turn_weights(r):
    jobs = [(r.w_up, r.wu, r.w_up_t, 0, part) for part in range(4)]
    jobs += [(r.w_down, r.wd, r.w_down_t, part, 0) for part in range(4)]
    loads = [
        r.copies.start(source.at[block_at(row), block_at(column)], near.at[block_at(row), block_at(column)])
        for source, near, _, row, column in jobs
    ]
    stores = []
    for load, (source, near, target, row, column) in zip(loads, jobs):
        load.wait()
        turned = r.wu_t if near is r.wu else r.wd_t
        turned[block_at(column), block_at(row)] = near[block_at(row), block_at(column)].T
        stores.append(
            r.copies.start(turned.at[block_at(column), block_at(row)], target.at[block_at(column), block_at(row)])
        )
    wait_all(stores)


def forward(row, section, ctl, ins, held):
    first = not held
    outs = {"sent": shape((L, D))}
    if first:
        outs.update(rel_rows=shape((2 * L, D)), rel=shape((2 * L, 2 * D)))
    outs.update(acts=shape((ROWS, L, A_ALL)), section_out=shape((ROWS, L, D)))
    scratch = dict(
        x_v=shape((L, D)), seg_v=shape((ROWS, L), jnp.int32), gains_v=shape((2, D)), biases_v=shape((4, D)),
        b_in_v=shape((1, 3 * D)), b_up_v=shape((1, FF)), table_v=shape((2 * SPAN, D)), rel_v=shape((2 * L, 2 * D)),
        wi=shape((D, 3 * D)), wo=shape((D, D)), wu=shape((D, FF)), wd=shape((FF, D)),
        acts_v=shape((L, A_ALL)), keep_v=shape((L, K_ALL)), resid_v=shape((L, 2 * D), f32),
    )
    if section == 0:
        outs.update(keep=shape((ROWS, L, K_ALL)), resid=shape((ROWS, L, 2 * D), f32))
    else:
        outs.update(backward_results(row, section))
        scratch.update(
            grad_v=shape((L, D)), ffn_v=shape((L, FF + 3 * D)), context_v=shape((L, D)), ffn_vec_v=shape((VECTOR_ROWS, D), f32),
            att_v=shape((L, 2 * D)), att_vec_v=shape((VECTOR_ROWS, D), f32), start_v=shape((L, D)), grad_out_v=shape((L, D)),
            value_v=shape((L, D)), d_rel_v=shape((2 * L, 2 * D), f32), d_rel_old=shape((2 * L, 2 * D), f32),
            rel_low=shape((2 * L, 2 * D)),
        )
    if first:
        scratch.update(rel_rows_v=shape((2 * L, D)))
    if turns_weights(row, section):
        outs.update(w_up_t=shape((FF, D)), w_down_t=shape((D, FF)))
    if row == ROWS - 1 or section == 1:
        scratch.update(wu_t=shape((FF, D)), wd_t=shape((D, FF)))
    return run(partial(forward_body, row, section, first), ctl, ins, outs, held, scratch, 84, 1900000000, 18000000)


def backward_results(row, section):
    results = dict(
        ffn_own=shape((ROWS * L, 5 * D)), ffn_other=shape((ROWS * L, 5 * D)), ffn_vec=shape((ROWS, VECTOR_ROWS, D), f32),
        att_own=shape((SWAP_ROWS, D)), att_other=shape((SWAP_ROWS, D)), att_vec=shape((ROWS, VECTOR_ROWS, D), f32),
        d_start=shape((ROWS, L, D)), d_rel=shape((2 * L, 2 * D), f32), d_rel_low=shape((2 * L, 2 * D)),
        input_grad=shape((ROWS, L, D)),
    )
    return results


def ffn_loads(row, section, r):
    return SimpleNamespace(
        first=[r.copies.start(source, near) for source, near in ((r.received, r.grad_v), (r.resid.at[row], r.resid_v), (r.gains, r.gains_v))],
        parts=[
            [
                r.copies.start(r.w_down_t.at[:, block_at(part)], r.wd.at[:, block_at(part)]),
                r.copies.start(r.keep.at[row, :, block_at(part, K_GP)], r.slope_v.at[:, block_at(part)]),
                r.copies.start(r.w_up_t.at[block_at(part)], r.wu.at[block_at(part)]),
            ]
            for part in range(4)
        ],
        last=[r.copies.start(r.w_out, r.wo), r.copies.start(r.keep.at[row, :, pl.ds(K_P, K_GP - K_P)], r.probs_v)],
    )


def ffn_part(row, section, r, loads):
    wait_all(loads.first)
    gain = r.gains_v[...].astype(f32)
    grad = r.grad_v[...].astype(f32)
    normed, rstd = norm_parts(r.resid_v[:, D:])
    r.ffn_vec_v[...] = jnp.zeros_like(r.ffn_vec_v)
    r.ffn_vec_v[8:9] = column_sums(grad * normed)
    r.ffn_vec_v[12:13] = column_sums(grad)
    d_two = norm_backward(normed, rstd, gain[1:2], grad)
    d_down = d_two.astype(bf16)
    r.ffn_v[:, FF : FF + D] = d_down
    r.ffn_vec_v[11:12] = column_sums(d_down.astype(f32))
    d_hidden = d_two
    for part in range(4):
        wait_all(loads.parts[part])
        d_gate = (nn(d_down, r.wd[:, block_at(part)]) * r.slope_v[:, block_at(part)].astype(f32)).astype(bf16)
        r.ffn_v[:, block_at(part)] = d_gate
        r.ffn_vec_v[3 + part : 4 + part] = column_sums(d_gate.astype(f32))
        d_hidden = d_hidden + nn(d_gate, r.wu[block_at(part), :])
    normed, rstd = norm_parts(r.resid_v[:, :D])
    r.ffn_vec_v[7:8] = column_sums(d_hidden * normed)
    r.ffn_vec_v[10:11] = column_sums(d_hidden)
    d_resid = norm_backward(normed, rstd, gain[0:1], d_hidden)
    d_att = d_resid.astype(bf16)
    r.ffn_v[:, FF + D : FF + 2 * D] = d_att
    r.ffn_vec_v[9:10] = column_sums(d_att.astype(f32))
    wait_all(loads.last)
    r.context_v[...] = nt(d_att, r.wo[...]).astype(bf16)
    halves = lane_halves()
    for pair in range(PAIRS):
        d_value = tn(two_heads(r.probs_v, pair), stacked(r.context_v[:, pair_at(pair)], halves))
        r.ffn_v[:, pair_at(pair, FF + 2 * D)] = d_value.astype(bf16)
    r.ffn_vec_v[2:3] = column_sums(r.ffn_v[:, FF + 2 * D :].astype(f32))
    stores, rows = [], pl.ds(row * L, L)
    for side_core, target in ((r.ctl[1], r.ffn_own), (1 - r.ctl[1], r.ffn_other)):
        gates = pl.ds(pl.multiple_of(side_core * 2 * D, 128), 2 * D)
        stores.append(r.copies.start(r.ffn_v.at[:, gates], target.at[rows, pl.ds(0, 2 * D)]))
        stores.append(r.copies.start(r.ffn_v.at[:, pl.ds(FF, 3 * D)], target.at[rows, pl.ds(2 * D, 3 * D)]))
    stores.append(r.copies.start(r.ffn_vec_v, r.ffn_vec.at[row]))
    return d_resid, stores


def two_heads(probs, pair):
    columns = probs[:, pair_at(pair, 0, 2 * L)]
    return jnp.concatenate([columns[:, :L], columns[:, L:]], axis=0)


def att_loads(row, section, r):
    return SimpleNamespace(
        first=[r.copies.start(r.keep.at[row, :, pl.ds(0, K_P)], r.keep_v), r.copies.start(r.rel, r.rel_v)],
        earlier=[r.copies.start(r.d_rel, r.d_rel_old)] if row > 0 else [],
        w_in=[r.copies.start(r.w_in, r.wi)],
        others=[
            r.copies.start(r.att_vec.at[0], r.att_vec_old),
            r.copies.start(r.ffn_vec, r.ffn_vec_v),
        ]
        if row == ROWS - 1 and section == 0
        else [],
    )


def att_part(row, section, r, loads, d_resid):
    halves = lane_halves()
    row_at = lax.broadcasted_iota(jnp.int32, (L, L), 0)
    column_at = lax.broadcasted_iota(jnp.int32, (L, L), 1)
    turn = indicator(row_at + column_at == L - 1)
    r.att_vec_v[...] = jnp.zeros_like(r.att_vec_v)
    wait_all(loads.first)
    for pair in range(PAIRS):
        query = r.keep_v[:, pair_at(pair)]
        key = r.keep_v[:, pair_at(pair, D)]
        value = r.keep_v[:, pair_at(pair, 2 * D)]
        probs_two = two_heads(r.probs_v, pair)
        rel_q, rel_k = r.rel_v[:, pair_at(pair)], r.rel_v[:, pair_at(pair, D)]
        context_two = stacked(r.context_v[:, pair_at(pair)], halves)
        probs_f = probs_two.astype(f32)
        weighted = nt(context_two, value) * probs_f
        d_scores = (weighted - probs_f * jnp.sum(weighted, axis=1, keepdims=True)).astype(bf16)
        query_two, key_two = stacked(query, halves), stacked(key, halves)
        d_key = tn(d_scores, query_two)
        d_side = jnp.concatenate([d_scores[:L], d_scores[L:]], axis=1)
        d_query = nn(d_side, key_two)
        d_far = (d_side.astype(f32) * SCALE).astype(bf16)
        query_turned = nn(turn, query).astype(bf16)
        key_turned = nn(turn, key).astype(bf16)
        rows_turned = nn(turn, d_far)
        far_query, far_key = [], []
        for head in range(2):
            columns = slice(head * L, head * L + L)
            far_query.append(unskew(rows_turned[:, columns]).astype(bf16))
            far_key.append(unskew(nt(turn, d_far[:, columns])).astype(bf16))
        d_query_turned = nn(jnp.concatenate(far_query, axis=1), stacked(rel_k, halves))
        d_key_turned = nn(jnp.concatenate(far_key, axis=1), stacked(rel_q, halves))
        r.d_rel_v[:, pair_at(pair)] = tn(jnp.concatenate(far_key, axis=0), stacked(key_turned, halves))
        r.d_rel_v[:, pair_at(pair, D)] = tn(jnp.concatenate(far_query, axis=0), stacked(query_turned, halves))
        d_query = d_query * SCALE + nn(turn, d_query_turned.astype(bf16))
        d_key = d_key * SCALE + nn(turn, d_key_turned.astype(bf16))
        r.att_v[:, pair_at(pair)] = d_query.astype(bf16)
        r.att_v[:, pair_at(pair, D)] = d_key.astype(bf16)
    stores = []
    for side_core, target in ((r.ctl[1], r.att_own), (1 - r.ctl[1], r.att_other)):
        query_or_key = pl.ds(pl.multiple_of(side_core * D, 128), D)
        stores.append(r.copies.start(r.att_v.at[:, query_or_key], target.at[pl.ds(row * L, L)]))
    far_sums = [column_sums(r.d_rel_v[:, block_at(part)]) for part in range(2)]
    if row > 0:
        wait_all(loads.earlier)
        r.d_rel_v[...] = r.d_rel_v[...] + r.d_rel_old[...]
    last = row == ROWS - 1
    if last:
        r.rel_low[...] = r.d_rel_v[...].astype(bf16)
        for side_core, target in ((r.ctl[1], r.att_own), (1 - r.ctl[1], r.att_other)):
            query_or_key = pl.ds(pl.multiple_of(side_core * D, 128), D)
            stores.append(r.copies.start(r.rel_low.at[:, query_or_key], target.at[pl.ds(2 * L, 2 * L)]))
    else:
        stores.append(r.copies.start(r.d_rel_v, r.d_rel))
    for part in range(2):
        rows = column_sums(r.att_v[:, block_at(part)].astype(f32)) + far_sums[part]
        r.att_vec_v[part : part + 1] = rows
    stores.append(r.copies.start(r.att_vec_v, r.att_vec.at[row]))
    wait_all(loads.w_in)
    if last and section == 0:
        stores.append(r.copies.start(r.att_v, r.d_rows))
        wait_all(loads.others)
        return stores + tail_part(r, None, r.ffn_vec_v[0] + r.ffn_vec_v[1] + r.att_vec_old[...] + r.att_vec_v[...])
    d_start = d_resid + nt(r.att_v[:, :D], r.wi[:, :D])
    r.start_v[...] = d_start.astype(bf16)
    stores.append(r.copies.start(r.start_v, r.d_start.at[row]))
    result = d_start + nt(r.att_v[:, D:], r.wi[:, D : 2 * D]) + nt(r.value_v[...], r.wi[:, 2 * D :])
    r.grad_out_v[...] = result.astype(bf16)
    stores.append(r.copies.start(r.grad_out_v, r.input_grad.at[row]))
    if section == 1:
        stores.append(r.copies.start(r.grad_out_v, r.sent))
        if last:
            stores.append(r.copies.start(r.rel_low, r.d_rel_low))
    return stores


def finish_body(r):
    @pl.when(r.ctl[0] == 0)
    def _():
        loads = [
            r.copies.start(source, target)
            for source, target in (
                (r.d_resid, r.resid_v), (r.d_rows, r.rows_v), (r.d_context.at[:, pl.ds(D, D)], r.value_v), (r.w_in, r.wi)
            )
        ]
        wait_all(loads)
        result = r.resid_v[...] + nt(r.rows_v[...], r.wi[:, : 2 * D]) + nt(r.value_v[...], r.wi[:, 2 * D :])
        r.grad_v[...] = result.astype(bf16)
        r.copies.start(r.grad_v, r.input_grad.at[ROWS - 1]).wait()


def finish(ctl, held, **ins):
    outs = dict(input_grad=shape((ROWS, L, D)))
    scratch = dict(
        resid_v=shape((L, D), f32), rows_v=shape((L, 2 * D)), value_v=shape((L, D)), wi=shape((D, 3 * D)), grad_v=shape((L, D))
    )
    return run(finish_body, ctl, ins, outs, held, scratch, 5, 500000000, 5000000)["input_grad"]


def tail_part(r, starts, vectors):
    def put(first, rows, value):
        r.tail_v[first : first + rows] = value.astype(bf16)

    if starts is None:
        put(REL_ROWS, ABS_ROWS, jnp.zeros((ABS_ROWS, D), f32))
    else:
        dims = (ABS_ROWS, L)
        place = lax.broadcasted_iota(jnp.int32, dims, 0) - lax.broadcasted_iota(jnp.int32, dims, 1)
        spots = [indicator(place == r.ctl[2 + row]) for row in range(ROWS)]
        put(REL_ROWS, ABS_ROWS, nn(spots[0], starts[0]) + nn(spots[1], starts[1]))
    put(TABLE_ROWS, VECTOR_ROWS, vectors)
    rest = TAIL_ROWS - TABLE_ROWS - VECTOR_ROWS
    put(TABLE_ROWS + VECTOR_ROWS, rest, jnp.zeros((rest, D), f32))
    rows = nt(r.rel_low[...], r.wi[:, : 2 * D]).astype(bf16)
    dims = (REL_ROWS, 2 * L)
    select = lax.broadcasted_iota(jnp.int32, dims, 0) + lax.broadcasted_iota(jnp.int32, dims, 1) == L + SPAN - REL_FROM
    put(0, REL_ROWS, nn(indicator(select), rows))
    return [
        r.copies.start(
            r.tail_v.at[pl.ds(pl.multiple_of(side_core * TAIL_HALF, 16), TAIL_HALF)], target.at[pl.ds(4 * L, TAIL_HALF)]
        )
        for side_core, target in ((r.ctl[1], r.att_own), (1 - r.ctl[1], r.att_other))
    ]


def backward_body(row, section, parts, r):
    @pl.when(r.ctl[0] == section)
    def _():
        if parts == "ffn":
            d_resid, stores = ffn_part(row, section, r, ffn_loads(row, section, r))
            r.resid_v[:, :D] = d_resid
            stores.append(r.copies.start(r.resid_v.at[:, pl.ds(0, D)], r.d_resid))
            stores.append(r.copies.start(r.context_v, r.d_context.at[:, pl.ds(0, D)]))
            stores.append(r.copies.start(r.ffn_v.at[:, pl.ds(FF + 2 * D, D)], r.d_context.at[:, pl.ds(D, D)]))
        elif parts == "att":
            first = [
                r.copies.start(r.d_resid, r.d_resid_v),
                r.copies.start(r.d_context.at[:, pl.ds(0, D)], r.context_v),
                r.copies.start(r.keep.at[row, :, pl.ds(K_P, K_GP - K_P)], r.probs_v),
                r.copies.start(r.d_context.at[:, pl.ds(D, D)], r.value_v),
            ]
            loads = att_loads(row, section, r)
            wait_all(first)
            stores = att_part(row, section, r, loads, r.d_resid_v[...])
        else:
            loads = ffn_loads(row, section, r)
            later = att_loads(row, section, r)
            d_resid, stores = ffn_part(row, section, r, loads)
            r.value_v[...] = r.ffn_v[:, FF + 2 * D :]
            stores = stores + att_part(row, section, r, later, d_resid)
        wait_all(stores)


def backward(row, section, parts, ctl, ins, held):
    outs, scratch, flops, traffic = {}, {}, 0, 0
    if parts == "ffn":
        outs.update(d_resid=shape((L, D), f32), d_context=shape((L, 2 * D)))
    if parts != "att":
        outs.update(
            ffn_own=shape((ROWS * L, 5 * D)), ffn_other=shape((ROWS * L, 5 * D)), ffn_vec=shape((ROWS, VECTOR_ROWS, D), f32)
        )
        scratch.update(
            grad_v=shape((L, D)), resid_v=shape((L, 2 * D), f32), gains_v=shape((2, D)), slope_v=shape((L, FF)),
            wu=shape((FF, D)), wd=shape((D, FF)), ffn_v=shape((L, FF + 3 * D)), wo=shape((D, D)), probs_v=shape((L, 2 * D)), context_v=shape((L, D)), ffn_vec_v=shape((VECTOR_ROWS, D), f32),
        )
        flops, traffic = flops + 1300000000, traffic + 12000000
    if parts == "att":
        scratch.update(d_resid_v=shape((L, D), f32), context_v=shape((L, D)), probs_v=shape((L, 2 * D)))
    if parts != "ffn":
        if section == 1:
            outs.update(sent=shape((L, D)))
        outs.update(
            att_own=shape((SWAP_ROWS, D)), att_other=shape((SWAP_ROWS, D)), att_vec=shape((ROWS, VECTOR_ROWS, D), f32),
            d_start=shape((ROWS, L, D)), d_rel=shape((2 * L, 2 * D), f32), d_rel_low=shape((2 * L, 2 * D)),
            input_grad=shape((ROWS, L, D)),
        )
        scratch.update(
            wi=shape((D, 3 * D)), keep_v=shape((L, K_P)), rel_v=shape((2 * L, 2 * D)),
            att_v=shape((L, 2 * D)), att_vec_v=shape((VECTOR_ROWS, D), f32), start_v=shape((L, D)), grad_out_v=shape((L, D)),
            value_v=shape((L, D)), d_rel_v=shape((2 * L, 2 * D), f32), d_rel_old=shape((2 * L, 2 * D), f32), rel_low=shape((2 * L, 2 * D)),
        )
        if row == ROWS - 1 and section == 0:
            outs.update(d_rows=shape((L, 2 * D)))
            del outs["input_grad"], outs["d_start"]
            scratch.update(
                tail_v=shape((TAIL_ROWS, D)),
                att_vec_old=shape((VECTOR_ROWS, D), f32), ffn_vec_v=shape((ROWS, VECTOR_ROWS, D), f32),
            )
        flops, traffic = flops + 1100000000, traffic + 8000000
    return run(partial(backward_body, row, section, parts), ctl, ins, outs, held, scratch, 56, flops, traffic, near=())


def tables_body(r):
    @pl.when(r.ctl[0] == 1)
    def _():
        loads = [
            r.copies.start(source, target)
            for source, target in (
                (r.d_start, r.start_v), (r.ffn_vec, r.ffn_vec_v), (r.att_vec, r.att_vec_v), (r.d_rel_low, r.rel_low), (r.w_in, r.wi)
            )
        ]
        wait_all(loads)
        vectors = r.ffn_vec_v[0] + r.ffn_vec_v[1] + r.att_vec_v[0] + r.att_vec_v[1]
        wait_all(tail_part(r, [r.start_v[0], r.start_v[1]], vectors))


def tables(ctl, w_in, held):
    ins = dict(w_in=w_in, **{name: held[name] for name in ("d_start", "ffn_vec", "att_vec", "d_rel_low")})
    outs = dict(att_own=shape((SWAP_ROWS, D)), att_other=shape((SWAP_ROWS, D)))
    scratch = dict(
        start_v=shape((ROWS, L, D)), ffn_vec_v=shape((ROWS, VECTOR_ROWS, D), f32), att_vec_v=shape((ROWS, VECTOR_ROWS, D), f32),
        rel_low=shape((2 * L, 2 * D)), wi=shape((D, 3 * D)), tail_v=shape((TAIL_ROWS, D)),
    )
    return run(tables_body, ctl, ins, outs, held, scratch, 8, 1000000000, 7000000)


def small_kernel(body, ctl, ins, outs):
    return pl.pallas_call(
        body,
        out_shape=outs,
        in_specs=[SMEM] + [VMEM] * len(ins),
        out_specs=(VMEM,) * len(outs),
        compiler_params=pltpu.CompilerParams(vmem_limit_bytes=16 * 2**20),
        cost_estimate=pl.CostEstimate(flops=0, bytes_accessed=2 * sum(value.size for value in ins) * 2, transcendentals=0),
    )(ctl, *ins)


def added(kept, received):
    return (kept.astype(f32) + received.astype(f32)).astype(bf16)


def split_sum(ctl, bit, kept, received):
    half = kept.shape[0] // 2
    if half % 16 != 0:
        total, at = kept + received, ctl[bit]
        return (lax.dynamic_slice_in_dim(total, part * half, half, 0) for part in (at, 1 - at))

    def body(ctl, kept, received, keep, send):
        low, high = (added(kept[at], received[at]) for at in (slice(0, half), slice(half, 2 * half)))
        first = ctl[bit] == 0
        keep[...] = jnp.where(first, low, high)
        send[...] = jnp.where(first, high, low)

    return small_kernel(body, ctl, (kept, received), (shape((half, D)),) * 2)


def in_order(ctl, bit, own, other):
    half = own.shape[0]
    if half % 16 != 0:
        pairs = jnp.concatenate([own, other], axis=0), jnp.concatenate([other, own], axis=0)
        return jnp.where(ctl[bit] == 0, *pairs)

    def body(ctl, own, other, out):
        first = ctl[bit] == 0
        out[:half] = jnp.where(first, own[...], other[...])
        out[half:] = jnp.where(first, other[...], own[...])

    return small_kernel(body, ctl, (own, other), (shape((2 * half, D)),))[0]


class Halves:
    def __init__(self, r, first_piece, half_rows):
        self.r, self.first_piece, self.half_rows, self.pending = r, first_piece, half_rows, []

    def store(self, first, rows):
        while rows > 0:
            index, inside = divmod(first, self.half_rows)
            count = min(rows, self.half_rows - inside)
            piece, half = index // 2, index % 2
            view, there = self.r.out_v.at[pl.ds(first, count)], pl.ds(inside, count)
            kept = self.r.copies.make(view, getattr(self.r, f"kept{piece}").at[there])
            sem = self.r.copies.sems.at[self.r.copies.used - 1]
            sent = pltpu.make_async_copy(view, getattr(self.r, f"sent{piece}").at[there], sem)
            mine = self.r.ctl[bit_at(self.first_piece + piece, False)] == half

            @pl.when(mine)
            def _():
                kept.start()

            @pl.when(jnp.logical_not(mine))
            def _():
                sent.start()

            self.pending.append(kept)
            first, rows = first + count, rows - count


def bit_at(piece, of_other_core):
    return 4 + 2 * piece + int(of_other_core)


def half_outputs(rows, pieces):
    half_rows = rows // pieces // 2
    return {f"{kind}{piece}": shape((half_rows, D)) for piece in range(pieces) for kind in ("kept", "sent")}


def load_acts(r, at, size, to):
    if not isinstance(at, int):
        at = pl.multiple_of(at, 128)
    return [
        r.copies.start(source.at[row, :, pl.ds(at, size)], target.at[pl.ds(row * L, L), pl.ds(to, size)])
        for row in range(ROWS)
        for source, target in ((r.acts, r.acts_v), (r.acts_sent, r.acts_sent_v))
    ]


def ffn_weights_body(r):
    core = r.ctl[1]
    loads = [r.copies.start(r.rows, r.rows_v)] + load_acts(r, A_HID, D, 0)
    later = load_acts(r, A_ACT + core * 2 * D, 2 * D, D)
    last = load_acts(r, A_CTX + core * HALF, HALF, 3 * D) + load_acts(r, A_X + core * HALF, HALF, 3 * D + HALF)
    halves = Halves(r, 0, FFN_ROWS // FFN_PIECES // 2)

    def product(acts_at, rows_at):
        own = tn(r.acts_v[:, acts_at], r.rows_v[:, rows_at])
        return (own + tn(r.acts_sent_v[:, acts_at], r.rows_sent[:, rows_at])).astype(bf16)

    wait_all(loads)
    for block in range(2):
        r.out_v[block_at(block)] = product(block_at(0), block_at(block))
        halves.store(block * D, D)
    wait_all(later)
    for block in range(2, 4):
        r.out_v[block_at(block)] = product(block_at(block - 1), block_at(2))
        halves.store(block * D, D)
    wait_all(last)
    for part in range(2):
        to = slice(4 * D + part * HALF, 4 * D + (part + 1) * HALF)
        r.out_v[to] = product(slice(3 * D + part * HALF, 3 * D + (part + 1) * HALF), block_at(3 + part))
    halves.store(4 * D, D)
    wait_all(halves.pending)


def ffn_weights(ctl, **ins):
    scratch = dict(
        rows_v=shape((ROWS * L, 5 * D)), acts_v=shape((ROWS * L, 4 * D)), acts_sent_v=shape((ROWS * L, 4 * D)),
        out_v=shape((FFN_ROWS, D)),
    )
    outs = half_outputs(FFN_ROWS, FFN_PIECES)
    return run(ffn_weights_body, ctl, ins, outs, {}, scratch, 36, 2 * 512 * 768 * FFN_ROWS, 14000000, ("rows_sent",))


def att_weights_body(r):
    loads = [r.copies.start(r.rows, r.rows_v), r.copies.start(r.table, r.table_v)]
    loads += load_acts(r, r.ctl[1] * D, D, 0)
    halves = Halves(r, FFN_PIECES, ATT_ROWS // ATT_PIECES // 2)
    wait_all(loads)
    total = tn(r.acts_v[...], r.rows_v[: 2 * L]) + tn(r.acts_sent_v[...], r.rows_sent[: 2 * L])
    far = (r.rows_v[2 * L : 4 * L].astype(f32) + r.rows_sent[2 * L : 4 * L].astype(f32)).astype(bf16)
    r.out_v[:D] = (total + tn(r.table_v[...], far)).astype(bf16)
    r.out_v[TAIL_AT:] = r.rows_v[4 * L :] + r.rows_sent[4 * L :]
    halves.store(0, ATT_ROWS)
    wait_all(halves.pending)


def att_weights(ctl, **ins):
    scratch = dict(
        rows_v=shape((SWAP_ROWS, D)), table_v=shape((2 * L, D)),
        acts_v=shape((ROWS * L, D)), acts_sent_v=shape((ROWS * L, D)), out_v=shape((ATT_ROWS, D)),
    )
    outs = half_outputs(ATT_ROWS, ATT_PIECES)
    return run(att_weights_body, ctl, ins, outs, {}, scratch, 16, 2 * 768 * 768 * 768, 6000000, ("rows_sent",))


def half_segments(layout, half_rows, piece, half):
    low = (2 * piece + half) * half_rows
    found, at = [], 0
    for target, rows, first, block in layout:
        start, stop = max(at, low), min(at + rows, low + half_rows)
        if start < stop:
            found.append((start - low, stop - start, target, first + start - at, block))
        at += rows
    return found


def assemble_body(kind, first_piece, layouts, half_rows, chosen, r):
    start_copy = r.copies.start
    core = r.ctl[1]
    blank = None
    if first_piece > 0 and kind == 0:
        r.blank[...] = jnp.zeros_like(r.blank)
        rest = 2 * SPAN - REL_FROM - REL_ROWS
        blank = [
            start_copy(r.blank, r.g_rel.at[pl.ds(0, REL_FROM)]),
            start_copy(r.blank.at[pl.ds(0, rest)], r.g_rel.at[pl.ds(REL_FROM + REL_ROWS, rest)]),
        ]
    branches = []
    chunk = half_rows // 2
    items = [(piece, origin) for piece in chosen for origin in ("own", "sent")]
    for index, (piece, origin) in enumerate(items):
        array = getattr(r, f"{origin}{piece}")
        bit = r.ctl[bit_at(first_piece + piece, origin == "sent")]
        maker = core if origin == "own" else 1 - core
        cases = [(made_by, half) for made_by in range(2) for half in range(2)]
        for at in range(0, half_rows, chunk):
            r.wide[index, at : at + chunk] = array[at : at + chunk].astype(f32)
            first_copy = last_copy = r.copies.used
            for made_by, half in cases:
                r.copies.used = first_copy
                copies = []
                for inside, count, name, start, block in half_segments(layouts[made_by], half_rows, piece, half):
                    low, high = max(inside, at), min(inside + count, at + chunk)
                    if low < high and name not in ("", "vectors"):
                        target = getattr(r, name).at[pl.ds(start + low - inside, high - low), pl.ds(block * D, D)]
                        copies.append(r.copies.make(r.wide.at[index, pl.ds(low, high - low)], target))
                last_copy = max(last_copy, r.copies.used)
                here = (maker == made_by) & (bit == (half if kind == 0 else 1 - half))
                branches.append((here, copies))

                @pl.when(here)
                def _():
                    for copy in copies:
                        copy.start()

            r.copies.used = last_copy
        for made_by, half in cases:
            for inside, count, name, _, _ in half_segments(layouts[made_by], half_rows, piece, half):
                if name == "vectors":

                    @pl.when((maker == made_by) & (bit == (half if kind == 0 else 1 - half)))
                    def _():
                        vectors = r.wide[index, inside : inside + count, :]
                        for part in range(3):
                            r.b_in_v[:, block_at(part)] = vectors[part : part + 1]
                        for part in range(4):
                            r.b_up_v[:, block_at(part)] = vectors[3 + part : 4 + part]
                        r.gains_v[...] = vectors[7:9]
                        r.biases_v[...] = vectors[9:13]
                        wait_all([
                            start_copy(r.b_in_v, r.g_b_in), start_copy(r.b_up_v, r.g_b_up),
                            start_copy(r.gains_v, r.g_gains), start_copy(r.biases_v, r.g_biases),
                        ])

    wait_all(blank or [])
    for here, copies in branches:

        @pl.when(here)
        def _():
            wait_all(copies)


def assemble(kind, first_piece, layouts, rows, pieces, chosen, ctl, own, sent, shapes, held):
    ins = {f"own{i}": value for i, value in zip(chosen, own)}
    ins.update({f"sent{i}": value for i, value in zip(chosen, sent)})
    outs = {name: shape(dims, f32) for name, dims in shapes.items()}
    half_rows = rows // pieces // 2
    scratch = dict(wide=shape((len(ins), half_rows, D), f32))
    if first_piece > 0:
        scratch.update(
            blank=shape((REL_FROM, D), f32), b_in_v=shape((1, 3 * D), f32), b_up_v=shape((1, FF), f32),
            gains_v=shape((2, D), f32), biases_v=shape((4, D), f32),
        )
    body = partial(assemble_body, kind, first_piece, layouts, half_rows, chosen)
    return run(body, ctl, ins, outs, held, scratch, 96, 0, len(ins) * half_rows * D * 6, tuple(ins), 44 * 2**20)


FFN_SHAPES = dict(g_up=(D, FF), g_down=(FF, D), g_out=(D, D), g_in=(D, 3 * D))
ATT_SHAPES = dict(
    g_in=(D, 3 * D), g_rel=(2 * SPAN, D), g_abs=(ABS_ROWS, D),
    g_b_in=(1, 3 * D), g_b_up=(1, FF), g_gains=(2, D), g_biases=(4, D),
)


SQUARE = ((0, 0), (1, 0), (1, 1), (0, 1))


def dp_place(index):
    return {"core": index % 2, "x": index // 2 % 4, "y": index // 8 % 2, "z": index // 16}


def dp_index(place):
    return ((place["z"] * 2 + place["y"]) * 4 + place["x"]) * 2 + place["core"]


def partner(index, dim):
    place = dp_place(index)
    if len(dim) == 2:
        bits = list(SQUARE[place[dim[0]]])
        bits[int(dim[1])] ^= 1
        place[dim[0]] = SQUARE.index(tuple(bits))
    else:
        place[dim] ^= 1
    return dp_index(place)


def swap(value, dims):
    peers = lax.axis_size("dp")
    return lax.ppermute(value, "dp", [(i, partner(i, dims[i % 2])) for i in range(peers)])


BETWEEN_CORES = ("core", "core")


def side_along(dim):
    place = dp_place(lax.axis_index("dp"))
    if dim == "y":
        return place[dim].astype(jnp.int32)
    at = place[dim[0]]
    if dim[1] == "0":
        return ((at == 1) | (at == 2)).astype(jnp.int32)
    return (at >= 2).astype(jnp.int32)


def this_core():
    return (lax.axis_index("dp") % 2).astype(jnp.int32)


def side(dims):
    return jnp.where(this_core() == 0, side_along(dims[0]), side_along(dims[1]))


ORDERS = [
    [("x0", "y"), ("z0", "x1"), ("x1", "z1"), ("y", "z0"), ("z1", "x0")],
    [("x1", "z0"), ("x0", "z1"), ("y", "x0"), ("z1", "x1"), ("z0", "y")],
    [("z1", "y"), ("x1", "z1"), ("y", "z0"), ("x0", "x1"), ("z0", "x0")],
]
BITS_AT = 4 + 2 * (FFN_PIECES + ATT_PIECES)
SPLIT_STEPS = 3


def bit_of(piece, step):
    return BITS_AT + 2 * piece + step - 1


def is_table_row(chunk):
    piece = FFN_PIECES
    first_row, span = 0, ATT_ROWS
    for dims in ORDERS[piece][:SPLIT_STEPS]:
        span //= 2
        first_row = first_row + side(dims) * span
    row_at = first_row + lax.broadcasted_iota(jnp.int32, chunk.shape, 0) - TAIL_AT
    return (row_at >= 0) & (row_at + this_core() * TAIL_HALF < TABLE_ROWS)


class Sequence:
    def __init__(self, last):
        self.last = last

    def after(self, *values):
        values = lax.optimization_barrier((*values, self.last))[:-1]
        return values[0] if len(values) == 1 else values


class Pieces:
    def __init__(self, ctl, seq):
        self.ctl, self.seq = ctl, seq
        self.kept, self.received, self.mine, self.mine_sent, self.partners, self.partners_sent = ({} for _ in range(6))

    def begin(self, piece, kept, sent):
        self.kept[piece], self.received[piece] = kept, swap(sent, ORDERS[piece][0])

    def inputs(self, piece):
        return self.seq.after(self.kept[piece], self.received[piece])

    def hold(self, piece, chunk):
        self.kept[piece] = self.seq.last = chunk

    def land(self, piece):
        self.received[piece] = self.seq.last = self.seq.after(self.received[piece])

    def split(self, piece, step):
        kept, sent = split_sum(self.ctl, bit_of(piece, step), *self.inputs(piece))
        self.hold(piece, kept)
        self.received[piece] = swap(sent, ORDERS[piece][step])

    def add(self, piece, step):
        kept, received = self.inputs(piece)
        self.hold(piece, kept + received)
        self.received[piece] = swap(self.kept[piece], ORDERS[piece][step])

    def add_for_section(self, piece):
        kept, received = self.inputs(piece)
        self.hold(piece, kept + received)
        self.received[piece] = lax.ppermute(self.kept[piece], "section", [(0, 1), (1, 0)])

    def add_tables(self, piece, step):
        kept, received = self.inputs(piece)
        self.hold(piece, jnp.where(is_table_row(kept), kept + received, kept))
        self.received[piece] = swap(self.kept[piece], ORDERS[piece][step])

    def join(self, piece, step):
        self.hold(piece, in_order(self.ctl, bit_of(piece, step), *self.inputs(piece)))
        self.received[piece] = swap(self.kept[piece], ORDERS[piece][step - 1])

    def cross(self, piece):
        self.mine[piece] = self.seq.last = self.seq.after(self.kept[piece])
        self.mine_sent[piece] = swap(self.mine[piece], BETWEEN_CORES)

    def arrive(self, piece):
        self.partners[piece] = self.seq.last = self.seq.after(self.received[piece])
        self.partners_sent[piece] = swap(self.partners[piece], BETWEEN_CORES)


def per_device(
    hidden_in,
    cotangent,
    segment_ids,
    positions,
    w_in,
    b_in,
    w_out,
    w_up,
    b_up,
    w_down,
    gains,
    biases,
    rel_table,
    abs_table,
):
    section = lax.axis_index("section").astype(jnp.int32)
    firsts = jnp.where(section == 1, positions[:, 0], 8 * ABS_ROWS)
    bits = [side(dims) for order in ORDERS for dims in (order[0], order[0][::-1])]
    bits += [side(order[step]) for order in ORDERS for step in range(1, SPLIT_STEPS)]
    ctl = jnp.stack([section, this_core(), firsts[0], firsts[1], *bits])
    weights = dict(w_in=w_in[0], w_out=w_out[0], w_up=w_up[0], w_down=w_down[0], gains=gains[0])
    common = dict(
        weights, hidden_in=hidden_in, segment_ids=segment_ids, biases=biases[0], b_in=b_in, b_up=b_up, abs_table=abs_table
    )

    out = forward(0, 0, ctl, dict(common, rel_table=rel_table), {})
    rel, rel_rows = out["rel"], out["rel_rows"]
    common["rel"] = rel
    received = []
    for row in range(ROWS):
        if row > 0:
            out = forward(row, 0, ctl, common, out)
        received.append(lax.ppermute(out["sent"], "section", [(0, 1)]))
    ready = {name: out[name] for name in ("keep", "resid")}
    back_ins = dict(common, cotangent=cotangent)
    grads = []
    for row in range(ROWS):
        turned = {name: out[name] for name in ("w_up_t", "w_down_t")} if row > 0 else {}
        out = {**out, **forward(row, 1, ctl, dict(back_ins, **turned, received=received[row]), out)}
        grads.append(lax.ppermute(out["sent"], "section", [(1, 0)]))
        if row < ROWS - 1:
            received[row + 1], grads[row] = lax.optimization_barrier((received[row + 1], grads[row]))
    acts, section_out = out["acts"], out["section_out"]
    acts_sent = swap(acts, BETWEEN_CORES)
    turned = {name: out[name] for name in ("w_up_t", "w_down_t")}
    common = dict(weights, **ready, **turned, rel=rel)
    received = grads
    out.update(tables(ctl, weights["w_in"], out))
    out = backward(0, 0, "both", ctl, dict(common, received=received[0]), out)
    early = out
    ffn = backward(1, 0, "ffn", ctl, dict(common, received=received[1]), early)
    ffn_sent = swap(ffn["ffn_other"], BETWEEN_CORES)
    seq = Sequence(ffn["ffn_own"])
    pieces = Pieces(ctl, seq)
    grads = {}

    def write(kind, group, *chosen):
        own, sent = ((pieces.mine, pieces.mine_sent), (pieces.partners, pieces.partners_sent))[kind]
        first, count, layout, rows, shapes = group
        first_own, *own = [own[first + i] for i in chosen]
        sent = [sent[first + i] for i in chosen]
        result = assemble(kind, first, layout, rows, count, chosen, ctl, [seq.after(first_own), *own], sent, shapes, grads)
        grads.update(result)
        seq.last = result["g_biases"] if first > 0 else result["g_out"]

    ffn_group = 0, FFN_PIECES, FFN_LAYOUT, FFN_ROWS, FFN_SHAPES
    att_group = FFN_PIECES, ATT_PIECES, ATT_LAYOUT, ATT_ROWS, ATT_SHAPES
    ins = dict(common, d_resid=seq.after(ffn["d_resid"]), d_context=ffn["d_context"], ffn_vec=ffn["ffn_vec"])
    out = backward(1, 0, "att", ctl, ins, early)
    att_sent = swap(out["att_other"], BETWEEN_CORES)
    seq.last = out["att_own"]
    halves = ffn_weights(ctl, acts=acts, acts_sent=acts_sent, rows=seq.after(ffn["ffn_own"]), rows_sent=ffn_sent)
    for piece in range(FFN_PIECES):
        pieces.begin(piece, halves[f"kept{piece}"], halves[f"sent{piece}"])
    seq.last = halves["kept0"]
    halves = att_weights(
        ctl, acts=acts, acts_sent=acts_sent, rows=seq.after(out["att_own"]), rows_sent=att_sent, table=rel_rows
    )
    pieces.begin(FFN_PIECES, halves["kept0"], halves["sent0"])
    seq.last = halves["kept0"]
    input_grad = finish(
        ctl, early, d_resid=ffn["d_resid"], d_rows=seq.after(out["d_rows"]), d_context=ffn["d_context"], w_in=weights["w_in"]
    )
    seq.last = input_grad
    pieces.split(0, 1)
    pieces.split(1, 1)
    pieces.land(2)
    pieces.split(0, 2)
    pieces.split(1, 2)
    pieces.split(2, 1)
    pieces.add(0, 3)
    pieces.add(1, 3)
    pieces.split(2, 2)
    pieces.add(0, 4)
    pieces.add(1, 4)
    pieces.add(2, 3)
    pieces.add(0, 2)
    pieces.land(1)
    pieces.add(2, 4)
    pieces.add(1, 2)
    pieces.join(0, 2)
    pieces.add_for_section(2)
    pieces.join(1, 2)
    pieces.add_tables(2, 2)
    pieces.join(0, 1)
    pieces.cross(0)
    pieces.join(2, 2)
    pieces.join(1, 1)
    pieces.cross(1)
    pieces.join(2, 1)
    pieces.cross(2)
    write(0, att_group, 0)
    pieces.arrive(0)
    write(0, ffn_group, 0, 1)
    pieces.arrive(1)
    pieces.arrive(2)
    write(1, ffn_group, 0, 1)
    write(1, att_group, 0)
    return (
        section_out[None],
        input_grad[None],
        grads["g_in"][None],
        grads["g_b_in"],
        grads["g_out"][None],
        grads["g_up"][None],
        grads["g_b_up"],
        grads["g_down"][None],
        grads["g_gains"][None],
        grads["g_biases"][None],
        grads["g_rel"],
        grads["g_abs"],
    )


def solution(mesh):
    in_specs = (
        P("dp", None, None),
        P("dp", None, None),
        P("dp", None),
        P("dp", None),
        P("section", None, None),
        P("section", None),
        P("section", None, None),
        P("section", None, None),
        P("section", None),
        P("section", None, None),
        P("section", None, None),
        P("section", None, None),
        P(),
        P(),
    )
    out_specs = (
        P("section", "dp", None, None),
        P("section", "dp", None, None),
        P("section", None, None),
        P("section", None),
        P("section", None, None),
        P("section", None, None),
        P("section", None),
        P("section", None, None),
        P("section", None, None),
        P("section", None, None),
        P(),
        P(),
    )
    return jax.shard_map(
        per_device, mesh=mesh, in_specs=in_specs, out_specs=out_specs, check_vma=False
    )
```

```python
from functools import partial
import math
from types import SimpleNamespace

import jax
import jax.numpy as jnp
from jax import lax
from jax.experimental import pallas as pl
from jax.experimental.pallas import tpu as pltpu
from jax.sharding import PartitionSpec as P

HEADS = 12
L = 128
D = 768
FF = 3072
HALF = D // 2
PAIRS = HEADS // 2
ROWS = 2
SPAN = 256
EPS = 1e-06
NEG = -1e30
SCALE = 1.0 / math.sqrt(3 * 64)
VMEM_LIMIT = 61 * 1024 * 1024
f32, bf16 = jnp.float32, jnp.bfloat16

A_START, A_X, A_CTX, A_HID, A_ACT, A_ALL = 0, 768, 1536, 2304, 3072, 6144
K_P, K_GP, K_ALL = 2304, 3840, 6912
VECTOR_ROWS = 16
REL_FROM, REL_ROWS, ABS_ROWS, TAIL_ROWS = 128, 272, 512, 896
TABLE_ROWS = REL_ROWS + ABS_ROWS
FFN_LAYOUT = [
    [("g_up", D, 0, 2 * core), ("g_up", D, 0, 2 * core + 1), ("g_down", 2 * D, 2 * D * core, 0), ("g_out", HALF, HALF * core, 0),
     ("g_in", HALF, HALF * core, 2)]
    for core in range(2)
]
ATT_LAYOUT = [
    [("g_in", D, 0, 0), ("g_rel", REL_ROWS, REL_FROM, 0), ("g_abs", 176, 0, 0)],
    [("g_in", D, 0, 1), ("g_abs", 336, 176, 0), ("vectors", VECTOR_ROWS, 0, 0), ("", 96, 0, 0)],
]
FFN_ROWS, ATT_ROWS = 3840, 1216
FFN_PIECES, ATT_PIECES = 2, 1
TAIL_HALF = TAIL_ROWS // 2
TAIL_AT = ATT_ROWS - TAIL_HALF
SWAP_ROWS = 4 * L + TAIL_HALF

VMEM = pl.BlockSpec(memory_space=pltpu.VMEM)
ANY = pl.BlockSpec(memory_space=pl.ANY)
SMEM = pl.BlockSpec(memory_space=pltpu.SMEM)


def nn(a, b):
    return lax.dot_general(a, b, (((1,), (0,)), ((), ())), preferred_element_type=f32)


def nt(a, b):
    return lax.dot_general(a, b, (((1,), (1,)), ((), ())), preferred_element_type=f32)


def tn(a, b):
    return lax.dot_general(a, b, (((0,), (0,)), ((), ())), preferred_element_type=f32)


def norm_parts(value):
    centered = value - jnp.mean(value, axis=1, keepdims=True)
    rstd = lax.rsqrt(jnp.mean(centered * centered, axis=1, keepdims=True) + EPS)
    return centered * rstd, rstd


def norm_backward(normed, rstd, gain, grad):
    scaled = grad * gain
    mean_one = jnp.mean(scaled, axis=1, keepdims=True)
    mean_two = jnp.mean(scaled * normed, axis=1, keepdims=True)
    return (scaled - mean_one - normed * mean_two) * rstd


def column_sums(value):
    return jnp.sum(value, axis=0, keepdims=True)


def indicator(condition):
    return condition.astype(f32).astype(bf16)


def lane_halves():
    lane = lax.broadcasted_iota(jnp.int32, (1, L), 1)
    return indicator(lane < 64), indicator(lane >= 64)


def stacked(value, halves):
    return jnp.concatenate([value * halves[0], value * halves[1]], axis=0)


def skew(table):
    return pltpu.roll(table, L, 1, stride=1, stride_axis=0)[:, :L]


def unskew(turned):
    wide = jnp.concatenate([turned, jnp.zeros_like(turned)], axis=1)
    return pltpu.roll(wide, 1, 1, stride=1, stride_axis=0)


def pair_at(pair, base=0, width=L):
    return pl.ds(pl.multiple_of(base + pair * width, L), width)


def block_at(block, base=0):
    return slice(base + block * D, base + block * D + D)


def shape(dims, dtype=bf16):
    return jax.ShapeDtypeStruct(dims, dtype)


class Copies:
    def __init__(self, sems):
        self.sems, self.used, self.marks = sems, 0, {}

    def make(self, source, target):
        self.used += 1
        return pltpu.make_async_copy(source, target, self.sems.at[self.used - 1])

    def make_at(self, name):
        again = self.marks.setdefault(name, self.used)
        if again == self.used:
            return self.make
        at = iter(range(again, self.used))
        return lambda source, target: pltpu.make_async_copy(source, target, self.sems.at[next(at)])

    def start(self, source, target):
        copy = self.make(source, target)
        copy.start()
        return copy


def wait_all(copies):
    for copy in copies:
        copy.wait()


def run(body, ctl, ins, outs, held, scratch, copies, flops, traffic, near=(), limit=VMEM_LIMIT):
    names, out_names, scratch_names = list(ins), list(outs), list(scratch)
    kept = [name for name in out_names if name in held and name != "sent"]

    def kernel(*refs):
        ctl_ref, refs = refs[0], refs[1:]
        r = SimpleNamespace(ctl=ctl_ref, **dict(zip(names, refs)))
        refs = refs[len(names) + len(kept) :]
        for name, ref in zip(out_names + scratch_names, refs):
            setattr(r, name, ref)
        r.copies = Copies(refs[-1])
        body(r)

    results = pl.pallas_call(
        kernel,
        out_shape=tuple(outs.values()),
        in_specs=[SMEM] + [VMEM if name in near else ANY for name in names] + [ANY] * len(kept),
        out_specs=(ANY,) * len(out_names),
        input_output_aliases={1 + len(names) + i: out_names.index(name) for i, name in enumerate(kept)},
        scratch_shapes=[pltpu.VMEM(s.shape, s.dtype) for s in scratch.values()] + [pltpu.SemaphoreType.DMA((copies,))],
        compiler_params=pltpu.CompilerParams(vmem_limit_bytes=limit),
        cost_estimate=pl.CostEstimate(flops=flops, bytes_accessed=traffic, transcendentals=0),
    )(ctl, *ins.values(), *[held[name] for name in kept])
    return dict(zip(out_names, results))


def relative_loads(r):
    return [r.copies.start(r.rel_table, r.table_v), r.copies.start(r.b_in, r.b_in_v), r.copies.start(r.w_in, r.wi)]


def relative_part(r, loads):
    dims = (2 * L, 2 * SPAN)
    select = indicator(lax.broadcasted_iota(jnp.int32, dims, 0) + lax.broadcasted_iota(jnp.int32, dims, 1) == L + SPAN)
    loads[0].wait()
    rows = nn(select, r.table_v[...]).astype(bf16)
    r.rel_rows_v[...] = rows
    loads[1].wait()
    loads[2].wait()
    r.rel_v[...] = (nn(rows, r.wi[:, : 2 * D]) + r.b_in_v[:, : 2 * D].astype(f32)).astype(bf16)
    return [r.copies.start(r.rel_rows_v, r.rel_rows), r.copies.start(r.rel_v, r.rel)]


def forward_loads(row, section, first, r):
    make = r.copies.make_at("loads")
    loads = SimpleNamespace(
        x=[make(r.hidden_in.at[row] if section == 0 else r.received, r.x_v)],
        absolute=[make(r.abs_table, r.table_v)] if section == 1 else [],
        w_in=[]
        if first
        else [make(r.b_in, r.b_in_v)] + [make(r.w_in.at[:, block_at(part)], r.wi.at[:, block_at(part)]) for part in range(3)],
        rel=[] if first else [make(r.rel, r.rel_v)],
        small=[make(r.segment_ids, r.seg_v), make(r.gains, r.gains_v), make(r.biases, r.biases_v)],
        out=[make(r.w_out, r.wo), make(r.b_up, r.b_up_v)],
        parts=[
            [
                make(r.w_up.at[:, block_at(part)], r.wu.at[:, block_at(part)]),
                make(r.w_down.at[block_at(part)], r.wd.at[block_at(part)]),
            ]
            for part in range(4)
        ],
    )
    flat = loads.x + loads.absolute + loads.w_in + loads.rel + loads.small + loads.out
    loads.every = flat + [copy for part in loads.parts for copy in part]
    return loads


def forward_body(row, section, first, r):
    start_copy = r.copies.start
    stores = []
    if first:
        rel_loads = relative_loads(r)

        @pl.when(r.ctl[0] == section)
        def _():
            for copy in forward_loads(row, section, first, r).every:
                copy.start()

        stores = relative_part(r, rel_loads)

    @pl.when(r.ctl[0] == section)
    def _():
        loads = forward_loads(row, section, first, r)
        if not first:
            for copy in loads.every:
                copy.start()
        if section == 1:
            back = SimpleNamespace(
                first=[start_copy(r.cotangent.at[row], r.grad_v)],
                parts=[
                    [
                        start_copy(r.w_down_t.at[:, block_at(part)], r.wd_t.at[:, block_at(part)]),
                        start_copy(r.w_up_t.at[block_at(part)], r.wu_t.at[block_at(part)]),
                    ]
                    for part in range(4)
                ],
                last=[],
            )
            earlier = [start_copy(r.d_rel, r.d_rel_old)] if row > 0 else []
            back_att = SimpleNamespace(first=[], earlier=earlier, w_in=[], others=[])
        halves = lane_halves()
        wait_all(loads.x)
        x = r.x_v[...]
        start = x.astype(f32)
        if section == 1:
            wait_all(loads.absolute)
            dims = (L, ABS_ROWS)
            place = lax.broadcasted_iota(jnp.int32, dims, 1) - lax.broadcasted_iota(jnp.int32, dims, 0)
            start = start + nn(indicator(place == r.ctl[2 + row]), r.table_v[...])
        query_in = start.astype(bf16)
        r.acts_v[:, block_at(0)] = query_in
        r.acts_v[:, block_at(1)] = x
        wait_all(loads.w_in[:2])
        b_in = r.b_in_v[...].astype(f32)
        r.keep_v[:, :D] = (nn(query_in, r.wi[:, :D]) + b_in[:, :D]).astype(bf16)
        wait_all(loads.w_in[2:])
        r.keep_v[:, D : 3 * D] = (nn(x, r.wi[:, D:]) + b_in[:, D:]).astype(bf16)
        wait_all(loads.small + loads.rel)
        seg_rows = jnp.broadcast_to(r.seg_v[row : row + 1, :], (L, L)).astype(f32)
        same = seg_rows == seg_rows.T
        def attend(pair):
            query = r.keep_v[:, pair_at(pair)]
            key = r.keep_v[:, pair_at(pair, D)]
            value = r.keep_v[:, pair_at(pair, 2 * D)]
            query_two, key_two = stacked(query, halves), stacked(key, halves)
            content = nt(query_two, key)
            far_query = nt(query_two, r.rel_v[:, pair_at(pair, D)])
            far_key = nt(key_two, r.rel_v[:, pair_at(pair)])
            probs = []
            for head in range(2):
                rows = slice(head * L, head * L + L)
                summed = content[rows] + skew(far_query[rows]) + skew(far_key[rows]).T
                scores = jnp.where(same, summed * SCALE, NEG)
                exponent = jnp.exp(scores - jnp.max(scores, axis=1, keepdims=True))
                total = jnp.sum(exponent, axis=1, keepdims=True)
                probs.append((exponent * (1.0 / total)).astype(bf16))
            probs = jnp.concatenate(probs, axis=1)
            r.keep_v[:, pair_at(pair, K_P, 2 * L)] = probs
            r.acts_v[:, pair_at(pair, A_CTX)] = nn(probs, stacked(value, halves)).astype(bf16)

        if section == 0:
            for pair in range(PAIRS):
                attend(pair)
        else:
            pl.loop(0, PAIRS, unroll=3)(attend)
        wait_all(loads.out)
        gain = r.gains_v[...].astype(f32)
        shift = r.biases_v[...].astype(f32)
        resid_one = start + nn(r.acts_v[:, A_CTX : A_CTX + D], r.wo[...]) + shift[0:1]
        r.resid_v[:, :D] = resid_one
        hidden = norm_parts(resid_one)[0] * gain[0:1] + shift[1:2]
        hidden_low = hidden.astype(bf16)
        r.acts_v[:, A_HID : A_HID + D] = hidden_low
        stored = [start_copy(r.acts_v.at[:, pl.ds(0, A_ACT)], r.acts.at[row, :, pl.ds(0, A_ACT)])]
        if section == 0:
            stored.append(start_copy(r.keep_v.at[:, pl.ds(0, K_GP)], r.keep.at[row, :, pl.ds(0, K_GP)]))
        total = hidden + shift[2:3]
        for part in range(4):
            wait_all(loads.parts[part])
            gate = nn(hidden_low, r.wu[:, block_at(part)]) + r.b_up_v[:, block_at(part)].astype(f32)
            below = 0.5 + 0.5 * lax.erf(gate * (1.0 / math.sqrt(2.0)))
            density = jnp.exp(gate * gate * -0.5) * (1.0 / math.sqrt(2.0 * math.pi))
            active = (gate * below).astype(bf16)
            r.acts_v[:, block_at(part, A_ACT)] = active
            r.keep_v[:, block_at(part, K_GP)] = (below + gate * density).astype(bf16)
            stored.append(start_copy(r.acts_v.at[:, block_at(part, A_ACT)], r.acts.at[row, :, block_at(part, A_ACT)]))
            if section == 0:
                stored.append(start_copy(r.keep_v.at[:, block_at(part, K_GP)], r.keep.at[row, :, block_at(part, K_GP)]))
            total = total + nn(active, r.wd[block_at(part), :])
        r.resid_v[:, D:] = total
        if section == 0:
            stored.append(start_copy(r.resid_v, r.resid.at[row]))
        r.x_v[...] = (norm_parts(total)[0] * gain[1:2] + shift[3:4]).astype(bf16)
        stored.append(start_copy(r.x_v, r.section_out.at[row]))
        if section == 0:
            stored.append(start_copy(r.x_v, r.sent))
        else:
            near = SimpleNamespace(**vars(r))
            near.wu, near.wd = r.wu_t, r.wd_t
            near.probs_v = r.keep_v.at[:, pl.ds(K_P, K_GP - K_P)]
            near.slope_v = r.keep_v.at[:, pl.ds(K_GP, FF)]
            d_resid, out_copies = ffn_part(row, section, near, back)
            r.value_v[...] = r.ffn_v[:, FF + 2 * D :]
            stored += out_copies + att_part(row, section, near, back_att, d_resid)
        wait_all(stored)

    wait_all(stores)
    if turns_weights(row, section):

        @pl.when(r.ctl[0] != section)
        def _():
            turn_weights(r)


def turns_weights(row, section):
    return row == (ROWS - 1 if section == 0 else 0)


def turn_weights(r):
    jobs = [(r.w_up, r.wu, r.w_up_t, 0, part) for part in range(4)]
    jobs += [(r.w_down, r.wd, r.w_down_t, part, 0) for part in range(4)]
    loads = [
        r.copies.start(source.at[block_at(row), block_at(column)], near.at[block_at(row), block_at(column)])
        for source, near, _, row, column in jobs
    ]
    stores = []
    for load, (source, near, target, row, column) in zip(loads, jobs):
        load.wait()
        turned = r.wu_t if near is r.wu else r.wd_t
        turned[block_at(column), block_at(row)] = near[block_at(row), block_at(column)].T
        stores.append(
            r.copies.start(turned.at[block_at(column), block_at(row)], target.at[block_at(column), block_at(row)])
        )
    wait_all(stores)


def forward(row, section, ctl, ins, held):
    first = not held
    outs = {"sent": shape((L, D))}
    if first:
        outs.update(rel_rows=shape((2 * L, D)), rel=shape((2 * L, 2 * D)))
    outs.update(acts=shape((ROWS, L, A_ALL)), section_out=shape((ROWS, L, D)))
    scratch = dict(
        x_v=shape((L, D)), seg_v=shape((ROWS, L), jnp.int32), gains_v=shape((2, D)), biases_v=shape((4, D)),
        b_in_v=shape((1, 3 * D)), b_up_v=shape((1, FF)), table_v=shape((2 * SPAN, D)), rel_v=shape((2 * L, 2 * D)),
        wi=shape((D, 3 * D)), wo=shape((D, D)), wu=shape((D, FF)), wd=shape((FF, D)),
        acts_v=shape((L, A_ALL)), keep_v=shape((L, K_ALL)), resid_v=shape((L, 2 * D), f32),
    )
    if section == 0:
        outs.update(keep=shape((ROWS, L, K_ALL)), resid=shape((ROWS, L, 2 * D), f32))
    else:
        outs.update(backward_results(row, section))
        scratch.update(
            grad_v=shape((L, D)), ffn_v=shape((L, FF + 3 * D)), context_v=shape((L, D)), ffn_vec_v=shape((VECTOR_ROWS, D), f32),
            att_v=shape((L, 2 * D)), att_vec_v=shape((VECTOR_ROWS, D), f32), start_v=shape((L, D)), grad_out_v=shape((L, D)),
            value_v=shape((L, D)), d_rel_v=shape((2 * L, 2 * D), f32), d_rel_old=shape((2 * L, 2 * D), f32),
            rel_low=shape((2 * L, 2 * D)),
        )
    if first:
        scratch.update(rel_rows_v=shape((2 * L, D)))
    if turns_weights(row, section):
        outs.update(w_up_t=shape((FF, D)), w_down_t=shape((D, FF)))
    if row == ROWS - 1 or section == 1:
        scratch.update(wu_t=shape((FF, D)), wd_t=shape((D, FF)))
    return run(partial(forward_body, row, section, first), ctl, ins, outs, held, scratch, 84, 1900000000, 18000000)


def backward_results(row, section):
    results = dict(
        ffn_own=shape((ROWS * L, 5 * D)), ffn_other=shape((ROWS * L, 5 * D)), ffn_vec=shape((ROWS, VECTOR_ROWS, D), f32),
        att_own=shape((SWAP_ROWS, D)), att_other=shape((SWAP_ROWS, D)), att_vec=shape((ROWS, VECTOR_ROWS, D), f32),
        d_start=shape((ROWS, L, D)), d_rel=shape((2 * L, 2 * D), f32), d_rel_low=shape((2 * L, 2 * D)),
        input_grad=shape((ROWS, L, D)),
    )
    return results


def ffn_loads(row, section, r):
    return SimpleNamespace(
        first=[r.copies.start(source, near) for source, near in ((r.received, r.grad_v), (r.resid.at[row], r.resid_v), (r.gains, r.gains_v))],
        parts=[
            [
                r.copies.start(r.w_down_t.at[:, block_at(part)], r.wd.at[:, block_at(part)]),
                r.copies.start(r.keep.at[row, :, block_at(part, K_GP)], r.slope_v.at[:, block_at(part)]),
                r.copies.start(r.w_up_t.at[block_at(part)], r.wu.at[block_at(part)]),
            ]
            for part in range(4)
        ],
        last=[r.copies.start(r.w_out, r.wo), r.copies.start(r.keep.at[row, :, pl.ds(K_P, K_GP - K_P)], r.probs_v)],
    )


def ffn_part(row, section, r, loads):
    wait_all(loads.first)
    gain = r.gains_v[...].astype(f32)
    grad = r.grad_v[...].astype(f32)
    normed, rstd = norm_parts(r.resid_v[:, D:])
    r.ffn_vec_v[...] = jnp.zeros_like(r.ffn_vec_v)
    r.ffn_vec_v[8:9] = column_sums(grad * normed)
    r.ffn_vec_v[12:13] = column_sums(grad)
    d_two = norm_backward(normed, rstd, gain[1:2], grad)
    d_down = d_two.astype(bf16)
    r.ffn_v[:, FF : FF + D] = d_down
    r.ffn_vec_v[11:12] = column_sums(d_down.astype(f32))
    d_hidden = d_two
    for part in range(4):
        wait_all(loads.parts[part])
        d_gate = (nn(d_down, r.wd[:, block_at(part)]) * r.slope_v[:, block_at(part)].astype(f32)).astype(bf16)
        r.ffn_v[:, block_at(part)] = d_gate
        r.ffn_vec_v[3 + part : 4 + part] = column_sums(d_gate.astype(f32))
        d_hidden = d_hidden + nn(d_gate, r.wu[block_at(part), :])
    normed, rstd = norm_parts(r.resid_v[:, :D])
    r.ffn_vec_v[7:8] = column_sums(d_hidden * normed)
    r.ffn_vec_v[10:11] = column_sums(d_hidden)
    d_resid = norm_backward(normed, rstd, gain[0:1], d_hidden)
    d_att = d_resid.astype(bf16)
    r.ffn_v[:, FF + D : FF + 2 * D] = d_att
    r.ffn_vec_v[9:10] = column_sums(d_att.astype(f32))
    wait_all(loads.last)
    r.context_v[...] = nt(d_att, r.wo[...]).astype(bf16)
    halves = lane_halves()
    for pair in range(PAIRS):
        d_value = tn(two_heads(r.probs_v, pair), stacked(r.context_v[:, pair_at(pair)], halves))
        r.ffn_v[:, pair_at(pair, FF + 2 * D)] = d_value.astype(bf16)
    r.ffn_vec_v[2:3] = column_sums(r.ffn_v[:, FF + 2 * D :].astype(f32))
    stores, rows = [], pl.ds(row * L, L)
    for side_core, target in ((r.ctl[1], r.ffn_own), (1 - r.ctl[1], r.ffn_other)):
        gates = pl.ds(pl.multiple_of(side_core * 2 * D, 128), 2 * D)
        stores.append(r.copies.start(r.ffn_v.at[:, gates], target.at[rows, pl.ds(0, 2 * D)]))
        stores.append(r.copies.start(r.ffn_v.at[:, pl.ds(FF, 3 * D)], target.at[rows, pl.ds(2 * D, 3 * D)]))
    stores.append(r.copies.start(r.ffn_vec_v, r.ffn_vec.at[row]))
    return d_resid, stores


def two_heads(probs, pair):
    columns = probs[:, pair_at(pair, 0, 2 * L)]
    return jnp.concatenate([columns[:, :L], columns[:, L:]], axis=0)


def att_loads(row, section, r):
    return SimpleNamespace(
        first=[r.copies.start(r.keep.at[row, :, pl.ds(0, K_P)], r.keep_v), r.copies.start(r.rel, r.rel_v)],
        earlier=[r.copies.start(r.d_rel, r.d_rel_old)] if row > 0 else [],
        w_in=[r.copies.start(r.w_in, r.wi)],
        others=[
            r.copies.start(r.att_vec.at[0], r.att_vec_old),
            r.copies.start(r.ffn_vec, r.ffn_vec_v),
        ]
        if row == ROWS - 1 and section == 0
        else [],
    )


def att_part(row, section, r, loads, d_resid):
    halves = lane_halves()
    row_at = lax.broadcasted_iota(jnp.int32, (L, L), 0)
    column_at = lax.broadcasted_iota(jnp.int32, (L, L), 1)
    turn = indicator(row_at + column_at == L - 1)
    r.att_vec_v[...] = jnp.zeros_like(r.att_vec_v)
    wait_all(loads.first)
    for pair in range(PAIRS):
        query = r.keep_v[:, pair_at(pair)]
        key = r.keep_v[:, pair_at(pair, D)]
        value = r.keep_v[:, pair_at(pair, 2 * D)]
        probs_two = two_heads(r.probs_v, pair)
        rel_q, rel_k = r.rel_v[:, pair_at(pair)], r.rel_v[:, pair_at(pair, D)]
        context_two = stacked(r.context_v[:, pair_at(pair)], halves)
        probs_f = probs_two.astype(f32)
        weighted = nt(context_two, value) * probs_f
        d_scores = (weighted - probs_f * jnp.sum(weighted, axis=1, keepdims=True)).astype(bf16)
        query_two, key_two = stacked(query, halves), stacked(key, halves)
        d_key = tn(d_scores, query_two)
        d_side = jnp.concatenate([d_scores[:L], d_scores[L:]], axis=1)
        d_query = nn(d_side, key_two)
        d_far = (d_side.astype(f32) * SCALE).astype(bf16)
        query_turned = nn(turn, query).astype(bf16)
        key_turned = nn(turn, key).astype(bf16)
        rows_turned = nn(turn, d_far)
        far_query, far_key = [], []
        for head in range(2):
            columns = slice(head * L, head * L + L)
            far_query.append(unskew(rows_turned[:, columns]).astype(bf16))
            far_key.append(unskew(nt(turn, d_far[:, columns])).astype(bf16))
        d_query_turned = nn(jnp.concatenate(far_query, axis=1), stacked(rel_k, halves))
        d_key_turned = nn(jnp.concatenate(far_key, axis=1), stacked(rel_q, halves))
        r.d_rel_v[:, pair_at(pair)] = tn(jnp.concatenate(far_key, axis=0), stacked(key_turned, halves))
        r.d_rel_v[:, pair_at(pair, D)] = tn(jnp.concatenate(far_query, axis=0), stacked(query_turned, halves))
        d_query = d_query * SCALE + nn(turn, d_query_turned.astype(bf16))
        d_key = d_key * SCALE + nn(turn, d_key_turned.astype(bf16))
        r.att_v[:, pair_at(pair)] = d_query.astype(bf16)
        r.att_v[:, pair_at(pair, D)] = d_key.astype(bf16)
    stores = []
    for side_core, target in ((r.ctl[1], r.att_own), (1 - r.ctl[1], r.att_other)):
        query_or_key = pl.ds(pl.multiple_of(side_core * D, 128), D)
        stores.append(r.copies.start(r.att_v.at[:, query_or_key], target.at[pl.ds(row * L, L)]))
    far_sums = [column_sums(r.d_rel_v[:, block_at(part)]) for part in range(2)]
    if row > 0:
        wait_all(loads.earlier)
        r.d_rel_v[...] = r.d_rel_v[...] + r.d_rel_old[...]
    last = row == ROWS - 1
    if last:
        r.rel_low[...] = r.d_rel_v[...].astype(bf16)
        for side_core, target in ((r.ctl[1], r.att_own), (1 - r.ctl[1], r.att_other)):
            query_or_key = pl.ds(pl.multiple_of(side_core * D, 128), D)
            stores.append(r.copies.start(r.rel_low.at[:, query_or_key], target.at[pl.ds(2 * L, 2 * L)]))
    else:
        stores.append(r.copies.start(r.d_rel_v, r.d_rel))
    for part in range(2):
        rows = column_sums(r.att_v[:, block_at(part)].astype(f32)) + far_sums[part]
        r.att_vec_v[part : part + 1] = rows
    stores.append(r.copies.start(r.att_vec_v, r.att_vec.at[row]))
    wait_all(loads.w_in)
    if last and section == 0:
        stores.append(r.copies.start(r.att_v, r.d_rows))
        wait_all(loads.others)
        return stores + tail_part(r, None, r.ffn_vec_v[0] + r.ffn_vec_v[1] + r.att_vec_old[...] + r.att_vec_v[...])
    d_start = d_resid + nt(r.att_v[:, :D], r.wi[:, :D])
    r.start_v[...] = d_start.astype(bf16)
    stores.append(r.copies.start(r.start_v, r.d_start.at[row]))
    result = d_start + nt(r.att_v[:, D:], r.wi[:, D : 2 * D]) + nt(r.value_v[...], r.wi[:, 2 * D :])
    r.grad_out_v[...] = result.astype(bf16)
    stores.append(r.copies.start(r.grad_out_v, r.input_grad.at[row]))
    if section == 1:
        stores.append(r.copies.start(r.grad_out_v, r.sent))
        if last:
            stores.append(r.copies.start(r.rel_low, r.d_rel_low))
    return stores


def finish_body(r):
    @pl.when(r.ctl[0] == 0)
    def _():
        loads = [
            r.copies.start(source, target)
            for source, target in (
                (r.d_resid, r.resid_v), (r.d_rows, r.rows_v), (r.d_context.at[:, pl.ds(D, D)], r.value_v), (r.w_in, r.wi)
            )
        ]
        wait_all(loads)
        result = r.resid_v[...] + nt(r.rows_v[...], r.wi[:, : 2 * D]) + nt(r.value_v[...], r.wi[:, 2 * D :])
        r.grad_v[...] = result.astype(bf16)
        r.copies.start(r.grad_v, r.input_grad.at[ROWS - 1]).wait()


def finish(ctl, held, **ins):
    outs = dict(input_grad=shape((ROWS, L, D)))
    scratch = dict(
        resid_v=shape((L, D), f32), rows_v=shape((L, 2 * D)), value_v=shape((L, D)), wi=shape((D, 3 * D)), grad_v=shape((L, D))
    )
    return run(finish_body, ctl, ins, outs, held, scratch, 5, 500000000, 5000000)["input_grad"]


def tail_part(r, starts, vectors):
    def put(first, rows, value):
        r.tail_v[first : first + rows] = value.astype(bf16)

    if starts is None:
        put(REL_ROWS, ABS_ROWS, jnp.zeros((ABS_ROWS, D), f32))
    else:
        dims = (ABS_ROWS, L)
        place = lax.broadcasted_iota(jnp.int32, dims, 0) - lax.broadcasted_iota(jnp.int32, dims, 1)
        spots = [indicator(place == r.ctl[2 + row]) for row in range(ROWS)]
        put(REL_ROWS, ABS_ROWS, nn(spots[0], starts[0]) + nn(spots[1], starts[1]))
    put(TABLE_ROWS, VECTOR_ROWS, vectors)
    rest = TAIL_ROWS - TABLE_ROWS - VECTOR_ROWS
    put(TABLE_ROWS + VECTOR_ROWS, rest, jnp.zeros((rest, D), f32))
    rows = nt(r.rel_low[...], r.wi[:, : 2 * D]).astype(bf16)
    dims = (REL_ROWS, 2 * L)
    select = lax.broadcasted_iota(jnp.int32, dims, 0) + lax.broadcasted_iota(jnp.int32, dims, 1) == L + SPAN - REL_FROM
    put(0, REL_ROWS, nn(indicator(select), rows))
    return [
        r.copies.start(
            r.tail_v.at[pl.ds(pl.multiple_of(side_core * TAIL_HALF, 16), TAIL_HALF)], target.at[pl.ds(4 * L, TAIL_HALF)]
        )
        for side_core, target in ((r.ctl[1], r.att_own), (1 - r.ctl[1], r.att_other))
    ]


def backward_body(row, section, parts, r):
    @pl.when(r.ctl[0] == section)
    def _():
        if parts == "ffn":
            d_resid, stores = ffn_part(row, section, r, ffn_loads(row, section, r))
            r.resid_v[:, :D] = d_resid
            stores.append(r.copies.start(r.resid_v.at[:, pl.ds(0, D)], r.d_resid))
            stores.append(r.copies.start(r.context_v, r.d_context.at[:, pl.ds(0, D)]))
            stores.append(r.copies.start(r.ffn_v.at[:, pl.ds(FF + 2 * D, D)], r.d_context.at[:, pl.ds(D, D)]))
        elif parts == "att":
            first = [
                r.copies.start(r.d_resid, r.d_resid_v),
                r.copies.start(r.d_context.at[:, pl.ds(0, D)], r.context_v),
                r.copies.start(r.keep.at[row, :, pl.ds(K_P, K_GP - K_P)], r.probs_v),
                r.copies.start(r.d_context.at[:, pl.ds(D, D)], r.value_v),
            ]
            loads = att_loads(row, section, r)
            wait_all(first)
            stores = att_part(row, section, r, loads, r.d_resid_v[...])
        else:
            loads = ffn_loads(row, section, r)
            later = att_loads(row, section, r)
            d_resid, stores = ffn_part(row, section, r, loads)
            r.value_v[...] = r.ffn_v[:, FF + 2 * D :]
            stores = stores + att_part(row, section, r, later, d_resid)
        wait_all(stores)


def backward(row, section, parts, ctl, ins, held):
    outs, scratch, flops, traffic = {}, {}, 0, 0
    if parts == "ffn":
        outs.update(d_resid=shape((L, D), f32), d_context=shape((L, 2 * D)))
    if parts != "att":
        outs.update(
            ffn_own=shape((ROWS * L, 5 * D)), ffn_other=shape((ROWS * L, 5 * D)), ffn_vec=shape((ROWS, VECTOR_ROWS, D), f32)
        )
        scratch.update(
            grad_v=shape((L, D)), resid_v=shape((L, 2 * D), f32), gains_v=shape((2, D)), slope_v=shape((L, FF)),
            wu=shape((FF, D)), wd=shape((D, FF)), ffn_v=shape((L, FF + 3 * D)), wo=shape((D, D)), probs_v=shape((L, 2 * D)), context_v=shape((L, D)), ffn_vec_v=shape((VECTOR_ROWS, D), f32),
        )
        flops, traffic = flops + 1300000000, traffic + 12000000
    if parts == "att":
        scratch.update(d_resid_v=shape((L, D), f32), context_v=shape((L, D)), probs_v=shape((L, 2 * D)))
    if parts != "ffn":
        if section == 1:
            outs.update(sent=shape((L, D)))
        outs.update(
            att_own=shape((SWAP_ROWS, D)), att_other=shape((SWAP_ROWS, D)), att_vec=shape((ROWS, VECTOR_ROWS, D), f32),
            d_start=shape((ROWS, L, D)), d_rel=shape((2 * L, 2 * D), f32), d_rel_low=shape((2 * L, 2 * D)),
            input_grad=shape((ROWS, L, D)),
        )
        scratch.update(
            wi=shape((D, 3 * D)), keep_v=shape((L, K_P)), rel_v=shape((2 * L, 2 * D)),
            att_v=shape((L, 2 * D)), att_vec_v=shape((VECTOR_ROWS, D), f32), start_v=shape((L, D)), grad_out_v=shape((L, D)),
            value_v=shape((L, D)), d_rel_v=shape((2 * L, 2 * D), f32), d_rel_old=shape((2 * L, 2 * D), f32), rel_low=shape((2 * L, 2 * D)),
        )
        if row == ROWS - 1 and section == 0:
            outs.update(d_rows=shape((L, 2 * D)))
            del outs["input_grad"], outs["d_start"]
            scratch.update(
                tail_v=shape((TAIL_ROWS, D)),
                att_vec_old=shape((VECTOR_ROWS, D), f32), ffn_vec_v=shape((ROWS, VECTOR_ROWS, D), f32),
            )
        flops, traffic = flops + 1100000000, traffic + 8000000
    return run(partial(backward_body, row, section, parts), ctl, ins, outs, held, scratch, 56, flops, traffic, near=())


def tables_body(r):
    @pl.when(r.ctl[0] == 1)
    def _():
        loads = [
            r.copies.start(source, target)
            for source, target in (
                (r.d_start, r.start_v), (r.ffn_vec, r.ffn_vec_v), (r.att_vec, r.att_vec_v), (r.d_rel_low, r.rel_low), (r.w_in, r.wi)
            )
        ]
        wait_all(loads)
        vectors = r.ffn_vec_v[0] + r.ffn_vec_v[1] + r.att_vec_v[0] + r.att_vec_v[1]
        wait_all(tail_part(r, [r.start_v[0], r.start_v[1]], vectors))


def tables(ctl, w_in, held):
    ins = dict(w_in=w_in, **{name: held[name] for name in ("d_start", "ffn_vec", "att_vec", "d_rel_low")})
    outs = dict(att_own=shape((SWAP_ROWS, D)), att_other=shape((SWAP_ROWS, D)))
    scratch = dict(
        start_v=shape((ROWS, L, D)), ffn_vec_v=shape((ROWS, VECTOR_ROWS, D), f32), att_vec_v=shape((ROWS, VECTOR_ROWS, D), f32),
        rel_low=shape((2 * L, 2 * D)), wi=shape((D, 3 * D)), tail_v=shape((TAIL_ROWS, D)),
    )
    return run(tables_body, ctl, ins, outs, held, scratch, 8, 1000000000, 7000000)


def small_kernel(body, ctl, ins, outs):
    return pl.pallas_call(
        body,
        out_shape=outs,
        in_specs=[SMEM] + [VMEM] * len(ins),
        out_specs=(VMEM,) * len(outs),
        compiler_params=pltpu.CompilerParams(vmem_limit_bytes=16 * 2**20),
        cost_estimate=pl.CostEstimate(flops=0, bytes_accessed=2 * sum(value.size for value in ins) * 2, transcendentals=0),
    )(ctl, *ins)


def added(kept, received):
    return (kept.astype(f32) + received.astype(f32)).astype(bf16)


def split_sum(ctl, bit, kept, received):
    half = kept.shape[0] // 2
    if half % 16 != 0:
        total, at = kept + received, ctl[bit]
        return (lax.dynamic_slice_in_dim(total, part * half, half, 0) for part in (at, 1 - at))

    def body(ctl, kept, received, keep, send):
        low, high = (added(kept[at], received[at]) for at in (slice(0, half), slice(half, 2 * half)))
        first = ctl[bit] == 0
        keep[...] = jnp.where(first, low, high)
        send[...] = jnp.where(first, high, low)

    return small_kernel(body, ctl, (kept, received), (shape((half, D)),) * 2)


def in_order(ctl, bit, own, other):
    half = own.shape[0]
    if half % 16 != 0:
        pairs = jnp.concatenate([own, other], axis=0), jnp.concatenate([other, own], axis=0)
        return jnp.where(ctl[bit] == 0, *pairs)

    def body(ctl, own, other, out):
        first = ctl[bit] == 0
        out[:half] = jnp.where(first, own[...], other[...])
        out[half:] = jnp.where(first, other[...], own[...])

    return small_kernel(body, ctl, (own, other), (shape((2 * half, D)),))[0]


class Halves:
    def __init__(self, r, first_piece, half_rows):
        self.r, self.first_piece, self.half_rows, self.pending = r, first_piece, half_rows, []

    def store(self, first, rows):
        while rows > 0:
            index, inside = divmod(first, self.half_rows)
            count = min(rows, self.half_rows - inside)
            piece, half = index // 2, index % 2
            view, there = self.r.out_v.at[pl.ds(first, count)], pl.ds(inside, count)
            kept = self.r.copies.make(view, getattr(self.r, f"kept{piece}").at[there])
            sem = self.r.copies.sems.at[self.r.copies.used - 1]
            sent = pltpu.make_async_copy(view, getattr(self.r, f"sent{piece}").at[there], sem)
            mine = self.r.ctl[bit_at(self.first_piece + piece, False)] == half

            @pl.when(mine)
            def _():
                kept.start()

            @pl.when(jnp.logical_not(mine))
            def _():
                sent.start()

            self.pending.append(kept)
            first, rows = first + count, rows - count


def bit_at(piece, of_other_core):
    return 4 + 2 * piece + int(of_other_core)


def half_outputs(rows, pieces):
    half_rows = rows // pieces // 2
    return {f"{kind}{piece}": shape((half_rows, D)) for piece in range(pieces) for kind in ("kept", "sent")}


def load_acts(r, at, size, to):
    if not isinstance(at, int):
        at = pl.multiple_of(at, 128)
    return [
        r.copies.start(source.at[row, :, pl.ds(at, size)], r.acts_v.at[pl.ds((ROWS * core + row) * L, L), pl.ds(to, size)])
        for row in range(ROWS)
        for core, source in enumerate((r.acts, r.acts_sent))
    ]


def ffn_weights_body(r):
    core = r.ctl[1]
    loads = [r.copies.start(r.rows, r.rows_v.at[pl.ds(0, 2 * L)])] + load_acts(r, A_HID, D, 0)
    r.rows_v[2 * L :] = r.rows_sent[...]
    later = load_acts(r, A_ACT + core * 2 * D, 2 * D, D)
    last = load_acts(r, A_CTX + core * HALF, HALF, 3 * D) + load_acts(r, A_X + core * HALF, HALF, 3 * D + HALF)
    halves = Halves(r, 0, FFN_ROWS // FFN_PIECES // 2)

    def product(acts_at, rows_at):
        return tn(r.acts_v[:, acts_at], r.rows_v[:, rows_at]).astype(bf16)

    wait_all(loads)
    for block in range(2):
        r.out_v[block_at(block)] = product(block_at(0), block_at(block))
        halves.store(block * D, D)
    wait_all(later)
    for block in range(2, 4):
        r.out_v[block_at(block)] = product(block_at(block - 1), block_at(2))
        halves.store(block * D, D)
    wait_all(last)
    for part in range(2):
        to = slice(4 * D + part * HALF, 4 * D + (part + 1) * HALF)
        r.out_v[to] = product(slice(3 * D + part * HALF, 3 * D + (part + 1) * HALF), block_at(3 + part))
    halves.store(4 * D, D)
    wait_all(halves.pending)


def ffn_weights(ctl, **ins):
    scratch = dict(
        rows_v=shape((2 * ROWS * L, 5 * D)), acts_v=shape((2 * ROWS * L, 4 * D)),
        out_v=shape((FFN_ROWS, D)),
    )
    outs = half_outputs(FFN_ROWS, FFN_PIECES)
    return run(ffn_weights_body, ctl, ins, outs, {}, scratch, 36, 2 * 512 * 768 * FFN_ROWS, 14000000, ("rows_sent",))


def att_weights_body(r):
    loads = [r.copies.start(r.rows, r.rows_v), r.copies.start(r.table, r.table_v)]
    loads += load_acts(r, r.ctl[1] * D, D, 0)
    halves = Halves(r, FFN_PIECES, ATT_ROWS // ATT_PIECES // 2)
    wait_all(loads)
    total = tn(r.acts_v[...], jnp.concatenate([r.rows_v[: 2 * L], r.rows_sent[: 2 * L]], axis=0))
    far = (r.rows_v[2 * L : 4 * L].astype(f32) + r.rows_sent[2 * L : 4 * L].astype(f32)).astype(bf16)
    r.out_v[:D] = (total + tn(r.table_v[...], far)).astype(bf16)
    r.out_v[TAIL_AT:] = r.rows_v[4 * L :] + r.rows_sent[4 * L :]
    halves.store(0, ATT_ROWS)
    wait_all(halves.pending)


def att_weights(ctl, **ins):
    scratch = dict(
        rows_v=shape((SWAP_ROWS, D)), table_v=shape((2 * L, D)),
        acts_v=shape((2 * ROWS * L, D)), out_v=shape((ATT_ROWS, D)),
    )
    outs = half_outputs(ATT_ROWS, ATT_PIECES)
    return run(att_weights_body, ctl, ins, outs, {}, scratch, 16, 2 * 768 * 768 * 768, 6000000, ("rows_sent",))


def half_segments(layout, half_rows, piece, half):
    low = (2 * piece + half) * half_rows
    found, at = [], 0
    for target, rows, first, block in layout:
        start, stop = max(at, low), min(at + rows, low + half_rows)
        if start < stop:
            found.append((start - low, stop - start, target, first + start - at, block))
        at += rows
    return found


def assemble_body(kind, first_piece, layouts, half_rows, chosen, r):
    start_copy = r.copies.start
    core = r.ctl[1]
    blank = None
    if first_piece > 0 and kind == 0:
        r.blank[...] = jnp.zeros_like(r.blank)
        rest = 2 * SPAN - REL_FROM - REL_ROWS
        blank = [
            start_copy(r.blank, r.g_rel.at[pl.ds(0, REL_FROM)]),
            start_copy(r.blank.at[pl.ds(0, rest)], r.g_rel.at[pl.ds(REL_FROM + REL_ROWS, rest)]),
        ]
    branches = []
    chunk = half_rows // 2
    items = [(piece, origin) for piece in chosen for origin in ("own", "sent")]
    for index, (piece, origin) in enumerate(items):
        array = getattr(r, f"{origin}{piece}")
        bit = r.ctl[bit_at(first_piece + piece, origin == "sent")]
        maker = core if origin == "own" else 1 - core
        cases = [(made_by, half) for made_by in range(2) for half in range(2)]
        for at in range(0, half_rows, chunk):
            r.wide[index, at : at + chunk] = array[at : at + chunk].astype(f32)
            first_copy = last_copy = r.copies.used
            for made_by, half in cases:
                r.copies.used = first_copy
                copies = []
                for inside, count, name, start, block in half_segments(layouts[made_by], half_rows, piece, half):
                    low, high = max(inside, at), min(inside + count, at + chunk)
                    if low < high and name not in ("", "vectors"):
                        target = getattr(r, name).at[pl.ds(start + low - inside, high - low), pl.ds(block * D, D)]
                        copies.append(r.copies.make(r.wide.at[index, pl.ds(low, high - low)], target))
                last_copy = max(last_copy, r.copies.used)
                here = (maker == made_by) & (bit == (half if kind == 0 else 1 - half))
                branches.append((here, copies))

                @pl.when(here)
                def _():
                    for copy in copies:
                        copy.start()

            r.copies.used = last_copy
        for made_by, half in cases:
            for inside, count, name, _, _ in half_segments(layouts[made_by], half_rows, piece, half):
                if name == "vectors":

                    @pl.when((maker == made_by) & (bit == (half if kind == 0 else 1 - half)))
                    def _():
                        vectors = r.wide[index, inside : inside + count, :]
                        for part in range(3):
                            r.b_in_v[:, block_at(part)] = vectors[part : part + 1]
                        for part in range(4):
                            r.b_up_v[:, block_at(part)] = vectors[3 + part : 4 + part]
                        r.gains_v[...] = vectors[7:9]
                        r.biases_v[...] = vectors[9:13]
                        wait_all([
                            start_copy(r.b_in_v, r.g_b_in), start_copy(r.b_up_v, r.g_b_up),
                            start_copy(r.gains_v, r.g_gains), start_copy(r.biases_v, r.g_biases),
                        ])

    wait_all(blank or [])
    for here, copies in branches:

        @pl.when(here)
        def _():
            wait_all(copies)


def assemble(kind, first_piece, layouts, rows, pieces, chosen, ctl, own, sent, shapes, held):
    ins = {f"own{i}": value for i, value in zip(chosen, own)}
    ins.update({f"sent{i}": value for i, value in zip(chosen, sent)})
    outs = {name: shape(dims, f32) for name, dims in shapes.items()}
    half_rows = rows // pieces // 2
    scratch = dict(wide=shape((len(ins), half_rows, D), f32))
    if first_piece > 0:
        scratch.update(
            blank=shape((REL_FROM, D), f32), b_in_v=shape((1, 3 * D), f32), b_up_v=shape((1, FF), f32),
            gains_v=shape((2, D), f32), biases_v=shape((4, D), f32),
        )
    body = partial(assemble_body, kind, first_piece, layouts, half_rows, chosen)
    return run(body, ctl, ins, outs, held, scratch, 96, 0, len(ins) * half_rows * D * 6, tuple(ins), 44 * 2**20)


FFN_SHAPES = dict(g_up=(D, FF), g_down=(FF, D), g_out=(D, D), g_in=(D, 3 * D))
ATT_SHAPES = dict(
    g_in=(D, 3 * D), g_rel=(2 * SPAN, D), g_abs=(ABS_ROWS, D),
    g_b_in=(1, 3 * D), g_b_up=(1, FF), g_gains=(2, D), g_biases=(4, D),
)


SQUARE = ((0, 0), (1, 0), (1, 1), (0, 1))


def dp_place(index):
    return {"core": index % 2, "x": index // 2 % 4, "y": index // 8 % 2, "z": index // 16}


def dp_index(place):
    return ((place["z"] * 2 + place["y"]) * 4 + place["x"]) * 2 + place["core"]


def partner(index, dim):
    place = dp_place(index)
    if len(dim) == 2:
        bits = list(SQUARE[place[dim[0]]])
        bits[int(dim[1])] ^= 1
        place[dim[0]] = SQUARE.index(tuple(bits))
    else:
        place[dim] ^= 1
    return dp_index(place)


def swap(value, dims):
    peers = lax.axis_size("dp")
    return lax.ppermute(value, "dp", [(i, partner(i, dims[i % 2])) for i in range(peers)])


BETWEEN_CORES = ("core", "core")


def side_along(dim):
    place = dp_place(lax.axis_index("dp"))
    if dim == "y":
        return place[dim].astype(jnp.int32)
    at = place[dim[0]]
    if dim[1] == "0":
        return ((at == 1) | (at == 2)).astype(jnp.int32)
    return (at >= 2).astype(jnp.int32)


def this_core():
    return (lax.axis_index("dp") % 2).astype(jnp.int32)


def side(dims):
    return jnp.where(this_core() == 0, side_along(dims[0]), side_along(dims[1]))


ORDERS = [
    [("x0", "y"), ("z0", "x1"), ("x1", "z1"), ("y", "z0"), ("z1", "x0")],
    [("x1", "z0"), ("x0", "z1"), ("y", "x0"), ("z1", "x1"), ("z0", "y")],
    [("z1", "y"), ("x1", "z1"), ("y", "z0"), ("x0", "x1"), ("z0", "x0")],
]
BITS_AT = 4 + 2 * (FFN_PIECES + ATT_PIECES)
SPLIT_STEPS = 3


def bit_of(piece, step):
    return BITS_AT + 2 * piece + step - 1


def is_table_row(chunk):
    piece = FFN_PIECES
    first_row, span = 0, ATT_ROWS
    for dims in ORDERS[piece][:SPLIT_STEPS]:
        span //= 2
        first_row = first_row + side(dims) * span
    row_at = first_row + lax.broadcasted_iota(jnp.int32, chunk.shape, 0) - TAIL_AT
    return (row_at >= 0) & (row_at + this_core() * TAIL_HALF < TABLE_ROWS)


class Sequence:
    def __init__(self, last):
        self.last = last

    def after(self, *values):
        values = lax.optimization_barrier((*values, self.last))[:-1]
        return values[0] if len(values) == 1 else values


class Pieces:
    def __init__(self, ctl, seq):
        self.ctl, self.seq = ctl, seq
        self.kept, self.received, self.mine, self.mine_sent, self.partners, self.partners_sent = ({} for _ in range(6))

    def begin(self, piece, kept, sent):
        self.kept[piece], self.received[piece] = kept, swap(sent, ORDERS[piece][0])

    def inputs(self, piece):
        return self.seq.after(self.kept[piece], self.received[piece])

    def hold(self, piece, chunk):
        self.kept[piece] = self.seq.last = chunk

    def land(self, piece):
        self.received[piece] = self.seq.last = self.seq.after(self.received[piece])

    def split(self, piece, step):
        kept, sent = split_sum(self.ctl, bit_of(piece, step), *self.inputs(piece))
        self.hold(piece, kept)
        self.received[piece] = swap(sent, ORDERS[piece][step])

    def add(self, piece, step):
        kept, received = self.inputs(piece)
        self.hold(piece, kept + received)
        self.received[piece] = swap(self.kept[piece], ORDERS[piece][step])

    def add_for_section(self, piece):
        kept, received = self.inputs(piece)
        self.hold(piece, kept + received)
        self.received[piece] = lax.ppermute(self.kept[piece], "section", [(0, 1), (1, 0)])

    def add_tables(self, piece, step):
        kept, received = self.inputs(piece)
        self.hold(piece, jnp.where(is_table_row(kept), kept + received, kept))
        self.received[piece] = swap(self.kept[piece], ORDERS[piece][step])

    def join(self, piece, step):
        self.hold(piece, in_order(self.ctl, bit_of(piece, step), *self.inputs(piece)))
        self.received[piece] = swap(self.kept[piece], ORDERS[piece][step - 1])

    def cross(self, piece):
        self.mine[piece] = self.seq.last = self.seq.after(self.kept[piece])
        self.mine_sent[piece] = swap(self.mine[piece], BETWEEN_CORES)

    def arrive(self, piece):
        self.partners[piece] = self.seq.last = self.seq.after(self.received[piece])
        self.partners_sent[piece] = swap(self.partners[piece], BETWEEN_CORES)


def per_device(
    hidden_in,
    cotangent,
    segment_ids,
    positions,
    w_in,
    b_in,
    w_out,
    w_up,
    b_up,
    w_down,
    gains,
    biases,
    rel_table,
    abs_table,
):
    section = lax.axis_index("section").astype(jnp.int32)
    firsts = jnp.where(section == 1, positions[:, 0], 8 * ABS_ROWS)
    bits = [side(dims) for order in ORDERS for dims in (order[0], order[0][::-1])]
    bits += [side(order[step]) for order in ORDERS for step in range(1, SPLIT_STEPS)]
    ctl = jnp.stack([section, this_core(), firsts[0], firsts[1], *bits])
    weights = dict(w_in=w_in[0], w_out=w_out[0], w_up=w_up[0], w_down=w_down[0], gains=gains[0])
    common = dict(
        weights, hidden_in=hidden_in, segment_ids=segment_ids, biases=biases[0], b_in=b_in, b_up=b_up, abs_table=abs_table
    )

    out = forward(0, 0, ctl, dict(common, rel_table=rel_table), {})
    rel, rel_rows = out["rel"], out["rel_rows"]
    common["rel"] = rel
    received = []
    for row in range(ROWS):
        if row > 0:
            out = forward(row, 0, ctl, common, out)
        received.append(lax.ppermute(out["sent"], "section", [(0, 1)]))
    ready = {name: out[name] for name in ("keep", "resid")}
    back_ins = dict(common, cotangent=cotangent)
    grads = []
    for row in range(ROWS):
        turned = {name: out[name] for name in ("w_up_t", "w_down_t")} if row > 0 else {}
        out = {**out, **forward(row, 1, ctl, dict(back_ins, **turned, received=received[row]), out)}
        grads.append(lax.ppermute(out["sent"], "section", [(1, 0)]))
        if row < ROWS - 1:
            received[row + 1], grads[row] = lax.optimization_barrier((received[row + 1], grads[row]))
    acts, section_out = out["acts"], out["section_out"]
    acts_sent = swap(acts, BETWEEN_CORES)
    turned = {name: out[name] for name in ("w_up_t", "w_down_t")}
    common = dict(weights, **ready, **turned, rel=rel)
    received = grads
    out.update(tables(ctl, weights["w_in"], out))
    out = backward(0, 0, "both", ctl, dict(common, received=received[0]), out)
    early = out
    ffn = backward(1, 0, "ffn", ctl, dict(common, received=received[1]), early)
    ffn_sent = swap(ffn["ffn_other"], BETWEEN_CORES)
    seq = Sequence(ffn["ffn_own"])
    pieces = Pieces(ctl, seq)
    grads = {}

    def write(kind, group, *chosen):
        own, sent = ((pieces.mine, pieces.mine_sent), (pieces.partners, pieces.partners_sent))[kind]
        first, count, layout, rows, shapes = group
        first_own, *own = [own[first + i] for i in chosen]
        sent = [sent[first + i] for i in chosen]
        result = assemble(kind, first, layout, rows, count, chosen, ctl, [seq.after(first_own), *own], sent, shapes, grads)
        grads.update(result)
        seq.last = result["g_biases"] if first > 0 else result["g_out"]

    ffn_group = 0, FFN_PIECES, FFN_LAYOUT, FFN_ROWS, FFN_SHAPES
    att_group = FFN_PIECES, ATT_PIECES, ATT_LAYOUT, ATT_ROWS, ATT_SHAPES
    ins = dict(common, d_resid=seq.after(ffn["d_resid"]), d_context=ffn["d_context"], ffn_vec=ffn["ffn_vec"])
    out = backward(1, 0, "att", ctl, ins, early)
    att_sent = swap(out["att_other"], BETWEEN_CORES)
    seq.last = out["att_own"]
    halves = ffn_weights(ctl, acts=acts, acts_sent=acts_sent, rows=seq.after(ffn["ffn_own"]), rows_sent=ffn_sent)
    for piece in range(FFN_PIECES):
        pieces.begin(piece, halves[f"kept{piece}"], halves[f"sent{piece}"])
    seq.last = halves["kept0"]
    halves = att_weights(
        ctl, acts=acts, acts_sent=acts_sent, rows=seq.after(out["att_own"]), rows_sent=att_sent, table=rel_rows
    )
    pieces.begin(FFN_PIECES, halves["kept0"], halves["sent0"])
    seq.last = halves["kept0"]
    input_grad = finish(
        ctl, early, d_resid=ffn["d_resid"], d_rows=seq.after(out["d_rows"]), d_context=ffn["d_context"], w_in=weights["w_in"]
    )
    seq.last = input_grad
    pieces.split(0, 1)
    pieces.split(1, 1)
    pieces.land(2)
    pieces.split(0, 2)
    pieces.split(1, 2)
    pieces.split(2, 1)
    pieces.add(0, 3)
    pieces.add(1, 3)
    pieces.split(2, 2)
    pieces.add(0, 4)
    pieces.add(1, 4)
    pieces.add(2, 3)
    pieces.add(0, 2)
    pieces.land(1)
    pieces.add(2, 4)
    pieces.add(1, 2)
    pieces.join(0, 2)
    pieces.add_for_section(2)
    pieces.join(1, 2)
    pieces.add_tables(2, 2)
    pieces.join(0, 1)
    pieces.cross(0)
    pieces.join(2, 2)
    pieces.join(1, 1)
    pieces.cross(1)
    pieces.join(2, 1)
    pieces.cross(2)
    write(0, att_group, 0)
    pieces.arrive(0)
    write(0, ffn_group, 0, 1)
    pieces.arrive(1)
    pieces.arrive(2)
    write(1, ffn_group, 0, 1)
    write(1, att_group, 0)
    return (
        section_out[None],
        input_grad[None],
        grads["g_in"][None],
        grads["g_b_in"],
        grads["g_out"][None],
        grads["g_up"][None],
        grads["g_b_up"],
        grads["g_down"][None],
        grads["g_gains"][None],
        grads["g_biases"][None],
        grads["g_rel"],
        grads["g_abs"],
    )


def solution(mesh):
    in_specs = (
        P("dp", None, None),
        P("dp", None, None),
        P("dp", None),
        P("dp", None),
        P("section", None, None),
        P("section", None),
        P("section", None, None),
        P("section", None, None),
        P("section", None),
        P("section", None, None),
        P("section", None, None),
        P("section", None, None),
        P(),
        P(),
    )
    out_specs = (
        P("section", "dp", None, None),
        P("section", "dp", None, None),
        P("section", None, None),
        P("section", None),
        P("section", None, None),
        P("section", None, None),
        P("section", None),
        P("section", None, None),
        P("section", None, None),
        P("section", None, None),
        P(),
        P(),
    )
    return jax.shard_map(
        per_device, mesh=mesh, in_specs=in_specs, out_specs=out_specs, check_vma=False
    )
```
